32 devices in a mesh: groups: 2 (over y), node: 4 (over z), tensor: 4 (over x, core).
Axes of the slice: x: 2, y: 2, z: 4, core: 2. Of those that a mesh axis runs over, the one named last changes fastest.
Arguments:
- queries: bfloat16 [6144, 5120], P(('groups', 'node'), 'tensor'), parts along dimension 0, may hold values from -90 to 90
- keys: bfloat16 [6144, 1024], P(('groups', 'node'), 'tensor'), parts along dimension 0, may hold values from -4.1 to 4.1
- values: bfloat16 [6144, 1024], P(('groups', 'node'), 'tensor'), parts along dimension 0, may hold values from -4 to 4
- out_weight: bfloat16 [5120, 5120], P('node', 'tensor'), may hold values from -0.59765625 to 0.59765625
- slot_nodes: int32 [48], P('groups'), parts along dimension 0, may hold values from 0 to 23, as said below
- ancestors: int32 [48, 7], P('groups'), parts along dimension 0, may hold values from -1 to 23, as said below
- depth: int32 [48], P('groups'), parts along dimension 0, may hold values from 0 to 7, as said below
Outputs:
- projected: bfloat16 [6144, 5120], P(('groups', 'node', 'tensor')), parts along dimension 0
The draws below stay inside these ranges and needn't reach their ends.
There are 2 independent parts, one for each index of `groups`. The reference program is written for one: setup_inputs(seed, part) draws one part's arguments, and reference() takes and returns one part's arrays. A program takes and returns all parts, laid end to end along the dimension named above; an argument that names none is the same for every part. Nothing has to cross between parts.
Inputs may be any that keep to these rules, and one draw needn't show every extreme that they name: `slot_nodes`: every node is held in exactly one slot. `ancestors`: every device holds one subtree: a node whose parent, if any, lies on another device, and its 5 children. When a node's parent lies on another device, that parent is one of the children of its device's subtree, and all nodes of other devices below a device hang below the same one of its children. Above any device lie at most 3 other devices. depth counts the entries of a row of ancestors that are not -1.
All inputs are finite; a program needn't handle non-finite values.
Results may differ from the reference program's by a relative error of at most 0.009.
Values may be sent and summed in bfloat16 or wider, within the bound.
No kernel may reach another device: no remote copies, remote signals or barrier semaphores. Data moves between devices by JAX's collectives and lax.ppermute only.
A program may use at most 128 MiB of HBM per device.

```python
import math
import jax
import jax.numpy as jnp
from jax import lax

D = 5120
HEADS = 40
KV_HEADS = 8
HEAD = 128
NODE_TOK = 128
NODES_DEV = 6
DEV_LEVELS = 3
A_MAX = 7
NODES = 24
TOKENS = 3072
N_TENSOR = 4


def base_keys(key):
    drawn = jax.random.normal(key, (TOKENS, KV_HEADS * HEAD), jnp.float32)
    return jnp.clip(drawn, -4.0, 4.0)


def tree_tables(key):
    devices = NODES // NODES_DEV
    k_order, k_parent, k_attach, k_local, k_label = jax.random.split(key, 5)
    order = jax.random.permutation(k_order, devices).astype(jnp.int32)
    position = jnp.arange(devices, dtype=jnp.int32)
    level = jnp.where(position == 0, 0, 1 + (position - 1) % DEV_LEVELS)
    span = jnp.maximum((position - 1) // DEV_LEVELS, 0) + 1
    pick = jax.random.randint(k_parent, (devices,), 0, span)
    upper = jnp.where(level <= 1, 0, level - 1 + DEV_LEVELS * pick).astype(jnp.int32)
    attach = jax.random.randint(k_attach, (devices,), 1, NODES_DEV).astype(jnp.int32)
    entries = []
    current = position
    for step in range(DEV_LEVELS):
        alive = level > step
        current = upper[current]
        entries.append(jnp.where(alive, current * NODES_DEV + attach[current], -1))
        entries.append(jnp.where(alive, current * NODES_DEV, -1))
    chain = jnp.stack(entries, 1)
    local = jnp.arange(NODES_DEV, dtype=jnp.int32)
    is_child = local > 0
    with_root = jnp.concatenate([(position * NODES_DEV)[:, None], chain], 1)
    no_root = jnp.concatenate([chain, -jnp.ones((devices, 1), jnp.int32)], 1)
    table = jnp.where(is_child[None, :, None], with_root[:, None, :], no_root[:, None, :])
    counts = 2 * level[:, None] + is_child[None, :].astype(jnp.int32)
    label = jax.random.permutation(k_label, NODES).astype(jnp.int32)
    flat = table.reshape(NODES, A_MAX)
    mapped = jnp.where(flat >= 0, label[jnp.clip(flat, 0, NODES - 1)], -1)
    ancestors = jnp.zeros((NODES, A_MAX), jnp.int32).at[label].set(mapped)
    depth = jnp.zeros((NODES,), jnp.int32).at[label].set(counts.reshape(NODES))
    local_keys = jax.random.split(k_local, devices)
    local_order = jax.vmap(lambda one_key: jax.random.permutation(one_key, NODES_DEV))(local_keys).astype(jnp.int32)
    slot_table = order[:, None] * NODES_DEV + local_order
    slot_nodes = jnp.zeros((NODES,), jnp.int32).at[slot_table.reshape(NODES)].set(label)
    return (slot_nodes, ancestors, depth)


def draw_slot_nodes(key, part):
    tables = tree_tables(key)
    return tables[0]


def draw_ancestors(key, part):
    tables = tree_tables(key)
    return tables[1]


def draw_depth(key, part):
    tables = tree_tables(key)
    return tables[2]


def draw_keys(key, part):
    shared = base_keys(key)
    return shared.astype(jnp.bfloat16)


def draw_queries(key, part):
    key = jax.random.fold_in(key, 32)
    drawn = jnp.clip(jax.random.normal(key, (TOKENS, HEADS * HEAD), jnp.float32), -4.0, 4.0)
    return drawn.astype(jnp.bfloat16)


def shard_levels(own_key, shape, shards, low, high):
    factor_of, own = 1.0, jax.random.fold_in(own_key, 6)
    for dim, blocks in shards:
        steps = jnp.exp(jax.random.uniform(jax.random.fold_in(own, dim), (blocks,), jnp.float32, low / len(shards), high / len(shards)))
        factor_of = factor_of * jnp.repeat(steps, shape[dim] // blocks).reshape([-1 if axis == dim else 1 for axis in range(len(shape))])
    return factor_of


def normal_values(stream_key, extent, scale, limit, cuts=(), held_as=jnp.bfloat16):
    values = scale * jax.random.normal(stream_key, extent, jnp.float32)
    if cuts:
        values = values * shard_levels(stream_key, extent, cuts, -0.22, 0.18)
    return jnp.clip(values, -limit, limit).astype(held_as)


def setup_inputs(seed: int = 0, part: int = 0) -> dict:
    streams_of = jax.random.split(jax.random.key(seed), 8)
    part_keys = jax.random.split(jax.random.fold_in(streams_of[7], part), 8)
    return {
        "queries": draw_queries(jax.random.fold_in(jax.random.fold_in(streams_of[7], part), 71), part),
        "keys": draw_keys(jax.random.fold_in(jax.random.fold_in(streams_of[7], part), 71), part),
        "values": normal_values(part_keys[2], (TOKENS, KV_HEADS * HEAD), 1.0, 4.0, ((0, 4), (1, 4))),
        "out_weight": normal_values(streams_of[3], (D, HEADS * HEAD), 0.14, 0.59765625, ((0, 4), (1, 4))),
        "slot_nodes": draw_slot_nodes(jax.random.fold_in(jax.random.fold_in(streams_of[7], part), 71), part),
        "ancestors": draw_ancestors(jax.random.fold_in(jax.random.fold_in(streams_of[7], part), 71), part),
        "depth": draw_depth(jax.random.fold_in(jax.random.fold_in(streams_of[7], part), 71), part),
    }


def attend_block(query_rows, ancestor_keys, ancestor_values, ancestor_live, own_keys, own_values):
    block_rows = own_keys.shape[0]
    key_width = own_keys.shape[1]
    kv_count = key_width // HEAD
    group = query_rows.shape[1] // HEAD // kv_count
    ancestor_count = ancestor_keys.shape[0]
    shaped_query = query_rows.reshape(block_rows, kv_count, group, HEAD).astype(jnp.float32)
    all_keys = jnp.concatenate([ancestor_keys.reshape(ancestor_count * block_rows, key_width), own_keys], 0)
    all_values = jnp.concatenate([ancestor_values.reshape(ancestor_count * block_rows, key_width), own_values], 0)
    all_keys = all_keys.reshape(-1, kv_count, HEAD).astype(jnp.float32)
    all_values = all_values.reshape(-1, kv_count, HEAD).astype(jnp.float32)
    scores = jnp.einsum('tghd,sgd->ghts', shaped_query, all_keys) * (1.0 / math.sqrt(HEAD))
    key_live = jnp.concatenate([jnp.repeat(ancestor_live, block_rows), jnp.ones((block_rows,), bool)])
    key_index = jnp.arange(all_keys.shape[0], dtype=jnp.int32) - ancestor_count * block_rows
    query_index = jnp.arange(block_rows, dtype=jnp.int32)
    visible = key_live[None, :] & (key_index[None, :] <= query_index[:, None])
    scores = jnp.where(visible[None, None], scores, jnp.float32(-1e+30))
    largest = lax.optimization_barrier(jnp.max(scores, axis=-1, keepdims=True))
    expo = jnp.exp(scores - largest)
    weights = (expo / lax.optimization_barrier(jnp.sum(expo, axis=-1, keepdims=True))).astype(jnp.bfloat16)
    mixed = jnp.einsum('ghts,sgd->tghd', weights.astype(jnp.float32), all_values)
    return mixed.reshape(block_rows, -1).astype(jnp.bfloat16)

def reference(queries, keys, values, out_weight, slot_nodes, ancestors, depth):
    slots = jnp.arange(NODES, dtype=jnp.int32)
    slot_of = jnp.zeros((NODES,), jnp.int32).at[slot_nodes].set(slots)
    key_blocks = keys.reshape(NODES, NODE_TOK, -1)
    value_blocks = values.reshape(NODES, NODE_TOK, -1)
    query_blocks = queries.reshape(NODES, NODE_TOK, -1)

    def one_slot(slot_index):
        node_id = slot_nodes[slot_index]
        listed = jnp.clip(ancestors[node_id], 0, NODES - 1)
        live = jnp.arange(A_MAX, dtype=jnp.int32) < depth[node_id]
        above = slot_of[listed]
        return attend_block(query_blocks[slot_index], key_blocks[above], value_blocks[above], live, key_blocks[slot_index], value_blocks[slot_index])
    attended = lax.map(one_slot, slots).reshape(TOKENS, HEADS * HEAD)
    width = HEADS * HEAD // N_TENSOR
    total = jnp.zeros((TOKENS, D), jnp.float32)
    for block in range(N_TENSOR):
        partial_value = lax.dot_general(attended[:, block * width:(block + 1) * width], out_weight[:, block * width:(block + 1) * width], (((1,), (1,)), ((), ())), preferred_element_type=jnp.float32)
        rounded = lax.optimization_barrier(partial_value.astype(jnp.bfloat16))
        total = total + rounded.astype(jnp.float32)
    return total.astype(jnp.bfloat16)
```

```python
import functools
import math

import jax
import jax.numpy as jnp
from jax import lax
from jax.experimental import pallas as pl
from jax.experimental.pallas import tpu as pltpu
from jax.sharding import PartitionSpec as P

HEAD = 128
NODE_TOK = 128
A_MAX = 7
CHAIN = A_MAX - 1
EXPORTS = 2
SCALE = math.log2(math.e) / math.sqrt(HEAD)
DEAD = -1e30
VMEM_LIMIT = 40 * 1024 * 1024


def prepare_body(nodes, slot_nodes, ancestors, depth, keys, values, exported, table, slot_of, sem):
    slots = slot_nodes.shape[0]
    me = lax.axis_index("node")

    def place(slot, carry):
        slot_of[slot_nodes[slot]] = slot
        return carry

    lax.fori_loop(0, slots, place, 0)

    def find_root(index, root):
        return jnp.where(depth[slot_nodes[me * nodes + index]] % 2 == 0, index, root)

    root = lax.fori_loop(0, nodes, find_root, jnp.int32(0))

    def find_attach(slot, attach):
        node = slot_nodes[slot]
        level = depth[node]
        for step in range(0, CHAIN, 2):
            holder = slot_of[jnp.maximum(ancestors[node, step], 0)]
            hit = (level % 2 == 0) & (step < level) & (holder // nodes == me)
            attach = jnp.where(hit, holder % nodes, attach)
        return attach

    attach = lax.fori_loop(0, slots, find_attach, jnp.int32(0))
    copies = []
    for position, (source, index) in enumerate(
        ((keys, root), (keys, attach), (values, root), (values, attach))
    ):
        rows = pl.ds(pl.multiple_of(index * NODE_TOK, NODE_TOK), NODE_TOK)
        copies.append(
            pltpu.make_async_copy(source.at[rows, :], exported.at[position], sem.at[position])
        )
    for copy in copies:
        copy.start()
    root_node = slot_nodes[me * nodes + root]
    count = depth[root_node]
    table[0] = root
    table[1] = count
    for step in range(CHAIN):
        holder = slot_of[jnp.maximum(ancestors[root_node, step], 0)] // nodes
        entry = holder * (2 * EXPORTS) + (1 if step % 2 == 0 else 0)
        table[2 + step] = jnp.where(step < count, entry, 0)
    for copy in copies:
        copy.wait()


def prepare(slot_nodes, ancestors, depth, keys, values):
    nodes = keys.shape[0] // NODE_TOK
    smem = pl.BlockSpec(memory_space=pltpu.SMEM)
    hbm = pl.BlockSpec(memory_space=pl.ANY)
    return pl.pallas_call(
        functools.partial(prepare_body, nodes),
        out_shape=(
            jax.ShapeDtypeStruct((2 * EXPORTS, NODE_TOK, keys.shape[1]), keys.dtype),
            jax.ShapeDtypeStruct((2 + CHAIN,), jnp.int32),
        ),
        in_specs=[smem, smem, smem, hbm, hbm],
        out_specs=(hbm, smem),
        scratch_shapes=[
            pltpu.SMEM((slot_nodes.shape[0],), jnp.int32),
            pltpu.SemaphoreType.DMA((2 * EXPORTS,)),
        ],
        name="prepare",
    )(slot_nodes, ancestors, depth, keys, values)


def attend_body(parts, per_part, table, *refs):
    query, own_key, own_value, root_key, root_value = refs[:5]
    chain_keys = refs[5 : 5 + CHAIN]
    chain_values = refs[5 + CHAIN : 5 + 2 * CHAIN]
    out, all_keys, all_values, bias = refs[5 + 2 * CHAIN :]
    node = pl.program_id(0)
    kv_count = own_key.shape[1] // HEAD
    group = query.shape[1] // HEAD // kv_count
    above = CHAIN * NODE_TOK
    root_rows = pl.ds(above, NODE_TOK)
    own_rows = pl.ds(above + NODE_TOK, NODE_TOK)

    @pl.when(node == 0)
    def _():
        all_values[:, :, HEAD:] = jnp.ones_like(all_values[:, :, HEAD:])
        for kv in range(kv_count):
            lanes = pl.ds(kv * HEAD, HEAD)
            for step in range(CHAIN):
                rows = pl.ds(step * NODE_TOK, NODE_TOK)
                all_keys[kv, rows, :] = chain_keys[step][0, :, lanes]
                all_values[kv, rows, :HEAD] = chain_values[step][0, :, lanes]
            all_keys[kv, root_rows, :] = root_key[:, lanes]
            all_values[kv, root_rows, :HEAD] = root_value[:, lanes]
        for step in range(CHAIN):
            live = step < table[1]
            bias[:, step * NODE_TOK : (step + 1) * NODE_TOK] = jnp.full(
                (8, NODE_TOK), jnp.where(live, 0.0, DEAD), jnp.float32
            )

    for kv in range(kv_count):
        lanes = pl.ds(kv * HEAD, HEAD)
        all_keys[kv, own_rows, :] = own_key[:, lanes]
        all_values[kv, own_rows, :HEAD] = own_value[:, lanes]

    root_bias = jnp.where(node == table[0], DEAD, 0.0)
    query_index = lax.broadcasted_iota(jnp.int32, (NODE_TOK, NODE_TOK), 0)
    key_index = lax.broadcasted_iota(jnp.int32, (NODE_TOK, NODE_TOK), 1)
    own_bias = jnp.where(key_index <= query_index, 0.0, DEAD)
    piece = math.gcd(NODE_TOK, per_part)
    pieces_part = per_part // piece
    me = lax.axis_index("tensor")
    contract = (((1,), (1,)), ((), ()))
    for kv in range(kv_count):
        heads = range(kv * group, (kv + 1) * group)
        stacked = jnp.concatenate([query[:, h * HEAD : (h + 1) * HEAD] for h in heads], 0)
        scores = lax.dot_general(
            stacked, all_keys[kv], contract, preferred_element_type=jnp.float32
        )
        chain = scores[:, :above] + bias[0:1, :]
        root = scores[:, above : above + NODE_TOK] + root_bias
        own = scores[:, above + NODE_TOK :] + jnp.concatenate([own_bias] * group, 0)
        masked = jnp.concatenate([chain, root, own], 1)
        largest = jnp.max(masked, axis=1, keepdims=True)
        expo = jnp.exp2((masked - largest) * SCALE).astype(jnp.bfloat16)
        mixed = jnp.dot(expo, all_values[kv], preferred_element_type=jnp.float32)
        result = (mixed[:, :HEAD] / mixed[:, HEAD:]).astype(jnp.bfloat16)
        for order, h in enumerate(heads):
            for part in range(NODE_TOK // piece):
                block = node * (NODE_TOK // piece) + part
                target = slot_position(parts, (block // pieces_part) ^ me)
                first = order * NODE_TOK + part * piece
                rows = pl.ds(pl.multiple_of((block % pieces_part) * piece, piece), piece)
                out[target, rows, h * HEAD : (h + 1) * HEAD] = result[first : first + piece]


def slot_position(parts, distance):
    half = parts // 2
    return jnp.where(distance % 2 == 1, distance // 2, half + distance // 2)


def attend(table, queries, keys, values, got, parts):
    rows, width = queries.shape
    key_width = keys.shape[1]
    nodes = rows // NODE_TOK
    kv_count = key_width // HEAD
    total = (CHAIN + 2) * NODE_TOK
    own = pl.BlockSpec((NODE_TOK, key_width), lambda node, table: (node, 0))
    root = pl.BlockSpec((NODE_TOK, key_width), lambda node, table: (table[0], 0))

    def chain_spec(step, offset):
        return pl.BlockSpec(
            (1, NODE_TOK, key_width), lambda node, table: (table[2 + step] + offset, 0, 0)
        )

    return pl.pallas_call(
        functools.partial(attend_body, parts, rows // parts),
        out_shape=jax.ShapeDtypeStruct((parts, rows // parts, width), queries.dtype),
        grid_spec=pltpu.PrefetchScalarGridSpec(
            num_scalar_prefetch=1,
            grid=(nodes,),
            in_specs=[
                pl.BlockSpec((NODE_TOK, width), lambda node, table: (node, 0)),
                own,
                own,
                root,
                root,
            ]
            + [chain_spec(step, 0) for step in range(CHAIN)]
            + [chain_spec(step, EXPORTS) for step in range(CHAIN)],
            out_specs=pl.BlockSpec(
                (parts, rows // parts, width), lambda node, table: (0, 0, 0)
            ),
            scratch_shapes=[
                pltpu.VMEM((kv_count, total, HEAD), keys.dtype),
                pltpu.VMEM((kv_count, total, 2 * HEAD), keys.dtype),
                pltpu.VMEM((8, CHAIN * NODE_TOK), jnp.float32),
            ],
        ),
        compiler_params=pltpu.CompilerParams(
            dimension_semantics=("arbitrary",), vmem_limit_bytes=VMEM_LIMIT
        ),
        cost_estimate=pl.CostEstimate(
            flops=rows * (width // HEAD) * total * HEAD * 6,
            bytes_accessed=rows * width * 4 + rows * key_width * 8,
            transcendentals=rows * (width // HEAD) * total,
        ),
        name="attend",
    )(table, queries, keys, values, keys, values, *([got] * (2 * CHAIN)))


def swap(array, axis, distance):
    size = lax.axis_size(axis)
    return lax.ppermute(array, axis, [(i, i ^ distance) for i in range(size)])


def times(rows, weight):
    return lax.dot_general(
        rows, weight, (((1,), (1,)), ((), ())), preferred_element_type=jnp.float32
    )


def project_rows(attended, weight):
    parts, per_part, width = attended.shape
    half = parts // 2
    sent = times(attended[:half].reshape(half * per_part, width), weight)
    from_core = swap(sent.astype(jnp.bfloat16), "tensor", 1).reshape(half, per_part, -1)
    away = times(attended[half + 1], weight) + from_core[1].astype(jnp.float32)
    from_chip = swap(away.astype(jnp.bfloat16), "tensor", 2)
    kept = times(attended[half], weight) + from_core[0].astype(jnp.float32)
    return (kept + from_chip.astype(jnp.float32)).astype(jnp.bfloat16)


def place_body(sizes, devices, features, *refs):
    out = refs[-1]
    count = len(sizes)
    mine = lax.axis_index("groups")
    half = features // 2
    for group in range(2):

        @pl.when(mine == group)
        def _():
            for which in range(2):
                column = (group if which == 0 else 1 - group) * half
                for part, size in enumerate(sizes):
                    source = refs[which * count + part]
                    for device in range(devices):
                        first = device * features + column
                        out[:, first : first + size] = source[:, device * size : (device + 1) * size]
                    column += size


def place(own, other, sizes, devices, features):
    rows = own[0].shape[0]
    return pl.pallas_call(
        functools.partial(place_body, sizes, devices, features),
        out_shape=jax.ShapeDtypeStruct((rows, devices * features), own[0].dtype),
        compiler_params=pltpu.CompilerParams(vmem_limit_bytes=VMEM_LIMIT),
        name="place",
    )(*own, *other)


def chunk_sizes(half):
    tiles = half // HEAD
    sizes = [2 * HEAD] * (tiles // 2) + [HEAD] * (tiles % 2)
    return sizes


def project_split(attended, out_weight):
    devices = lax.axis_size("node")
    features = out_weight.shape[0]
    half = features // 2
    first = lax.axis_index("groups") * half
    other = swap(attended, "groups", 1)
    own_done, other_done = [], []
    sizes = chunk_sizes(half)
    for size in sizes:
        piece = lax.dynamic_slice_in_dim(out_weight, first, size, 0)
        first = first + size
        weight = lax.all_gather(piece, "node", axis=0, tiled=True)
        own_done.append(project_rows(attended, weight))
        other_done.append(swap(project_rows(other, weight), "groups", 1))
    return place(own_done, other_done, sizes, devices, features)


def project_plain(attended, out_weight):
    parts, per_part, width = attended.shape
    me = lax.axis_index("tensor")
    order = slot_position(parts, jnp.arange(parts, dtype=jnp.int32) ^ me)
    rows = attended[order].reshape(parts * per_part, width)
    weight = lax.all_gather(out_weight, "node", axis=0, tiled=True)
    terms = times(rows, weight).astype(jnp.bfloat16)
    return lax.psum_scatter(terms, "tensor", scatter_dimension=0, tiled=True)


def local(queries, keys, values, out_weight, slot_nodes, ancestors, depth):
    parts = lax.axis_size("tensor")
    exported, table = prepare(slot_nodes, ancestors, depth, keys, values)
    got = lax.all_gather(exported, "node", axis=0, tiled=True)
    attended = attend(table, queries, keys, values, got, parts)
    if parts == 4 and lax.axis_size("groups") == 2 and out_weight.shape[0] % (2 * HEAD) == 0:
        return project_split(attended, out_weight)
    return project_plain(attended, out_weight)


def solution(mesh):
    placed = (
        P(("groups", "node"), "tensor"),
        P(("groups", "node"), "tensor"),
        P(("groups", "node"), "tensor"),
        P("node", "tensor"),
        P("groups"),
        P("groups", None),
        P("groups"),
    )
    return jax.shard_map(
        local,
        mesh=mesh,
        in_specs=placed,
        out_specs=P(("groups", "node", "tensor"), None),
        check_vma=False,
    )
```

```python
import functools
import math

import jax
import jax.numpy as jnp
from jax import lax
from jax.experimental import pallas as pl
from jax.experimental.pallas import tpu as pltpu
from jax.sharding import PartitionSpec as P

HEAD = 128
NODE_TOK = 128
A_MAX = 7
CHAIN = A_MAX - 1
EXPORTS = 2
SCALE = math.log2(math.e) / math.sqrt(HEAD)
DEAD = -1e30
VMEM_LIMIT = 40 * 1024 * 1024


def prepare_body(
    nodes, slot_nodes, ancestors, depth, keys, values, exported, table, holder, within, roots, sem
):
    devices = slot_nodes.shape[0] // nodes
    me = lax.axis_index("node")

    def place(device, mine):
        root, root_index = jnp.int32(0), jnp.int32(0)
        for index in range(nodes):
            node = slot_nodes[device * nodes + index]
            holder[node] = device
            within[node] = index
            even = (depth[node] & 1) == 0
            root = jnp.where(even, node, root)
            root_index = jnp.where(even, index, root_index)
        roots[device] = root
        return jnp.where(device == me, root_index, mine)

    root = lax.fori_loop(0, devices, place, jnp.int32(0))

    def find_attach(device, attach):
        node = roots[device]
        level = depth[node]
        for step in range(0, CHAIN, 2):
            above = jnp.maximum(ancestors[step, node], 0)
            hit = (step < level) & (holder[above] == me)
            attach = jnp.where(hit, within[above], attach)
        return attach

    attach = lax.fori_loop(0, devices, find_attach, jnp.int32(0))
    copies = []
    for position, (source, index) in enumerate(
        ((keys, root), (keys, attach), (values, root), (values, attach))
    ):
        rows = pl.ds(pl.multiple_of(index * NODE_TOK, NODE_TOK), NODE_TOK)
        copies.append(
            pltpu.make_async_copy(source.at[rows, :], exported.at[position], sem.at[position])
        )
    for copy in copies:
        copy.start()
    root_node = roots[me]
    count = depth[root_node]
    table[0] = root
    table[1] = count
    for step in range(CHAIN):
        above = jnp.maximum(ancestors[step, root_node], 0)
        entry = holder[above] * (2 * EXPORTS) + (1 if step % 2 == 0 else 0)
        table[2 + step] = jnp.where(step < count, entry, 0)
    for copy in copies:
        copy.wait()


def prepare(slot_nodes, ancestors, depth, keys, values):
    nodes = keys.shape[0] // NODE_TOK
    slots = slot_nodes.shape[0]
    smem = pl.BlockSpec(memory_space=pltpu.SMEM)
    hbm = pl.BlockSpec(memory_space=pl.ANY)
    return pl.pallas_call(
        functools.partial(prepare_body, nodes),
        out_shape=(
            jax.ShapeDtypeStruct((2 * EXPORTS, NODE_TOK, keys.shape[1]), keys.dtype),
            jax.ShapeDtypeStruct((2 + CHAIN,), jnp.int32),
        ),
        in_specs=[smem, smem, smem, hbm, hbm],
        out_specs=(hbm, smem),
        scratch_shapes=[
            pltpu.SMEM((slots,), jnp.int32),
            pltpu.SMEM((slots,), jnp.int32),
            pltpu.SMEM((slots // nodes,), jnp.int32),
            pltpu.SemaphoreType.DMA((2 * EXPORTS,)),
        ],
        name="prepare",
    )(slot_nodes, ancestors.T, depth, keys, values)


def attend_body(parts, per_part, table, *refs):
    query, own_key, own_value, root_key, root_value = refs[:5]
    chain_keys = refs[5 : 5 + CHAIN]
    chain_values = refs[5 + CHAIN : 5 + 2 * CHAIN]
    out, all_keys, all_values, bias = refs[5 + 2 * CHAIN :]
    node = pl.program_id(0)
    kv_count = own_key.shape[1] // HEAD
    group = query.shape[1] // HEAD // kv_count
    above = CHAIN * NODE_TOK
    root_rows = pl.ds(above, NODE_TOK)
    own_rows = pl.ds(above + NODE_TOK, NODE_TOK)

    @pl.when(node == 0)
    def _():
        all_values[:, :, HEAD:] = jnp.ones_like(all_values[:, :, HEAD:])
        for kv in range(kv_count):
            lanes = pl.ds(kv * HEAD, HEAD)
            for step in range(CHAIN):
                rows = pl.ds(step * NODE_TOK, NODE_TOK)
                all_keys[kv, rows, :] = chain_keys[step][0, :, lanes]
                all_values[kv, rows, :HEAD] = chain_values[step][0, :, lanes]
            all_keys[kv, root_rows, :] = root_key[:, lanes]
            all_values[kv, root_rows, :HEAD] = root_value[:, lanes]
        for step in range(CHAIN):
            live = step < table[1]
            bias[:, step * NODE_TOK : (step + 1) * NODE_TOK] = jnp.full(
                (8, NODE_TOK), jnp.where(live, 0.0, DEAD), jnp.float32
            )

    for kv in range(kv_count):
        lanes = pl.ds(kv * HEAD, HEAD)
        all_keys[kv, own_rows, :] = own_key[:, lanes]
        all_values[kv, own_rows, :HEAD] = own_value[:, lanes]

    root_bias = jnp.where(node == table[0], DEAD, 0.0)
    query_index = lax.broadcasted_iota(jnp.int32, (NODE_TOK, NODE_TOK), 0)
    key_index = lax.broadcasted_iota(jnp.int32, (NODE_TOK, NODE_TOK), 1)
    own_bias = jnp.where(key_index <= query_index, 0.0, DEAD)
    piece = math.gcd(NODE_TOK, per_part)
    pieces_part = per_part // piece
    me = lax.axis_index("tensor")
    contract = (((1,), (1,)), ((), ()))
    for kv in range(kv_count):
        heads = range(kv * group, (kv + 1) * group)
        stacked = jnp.concatenate([query[:, h * HEAD : (h + 1) * HEAD] for h in heads], 0)
        scores = lax.dot_general(
            stacked, all_keys[kv], contract, preferred_element_type=jnp.float32
        )
        chain = scores[:, :above] + bias[0:1, :]
        root = scores[:, above : above + NODE_TOK] + root_bias
        own = scores[:, above + NODE_TOK :] + jnp.concatenate([own_bias] * group, 0)
        masked = jnp.concatenate([chain, root, own], 1)
        largest = jnp.max(masked, axis=1, keepdims=True)
        expo = jnp.exp2((masked - largest) * SCALE).astype(jnp.bfloat16)
        mixed = jnp.dot(expo, all_values[kv], preferred_element_type=jnp.float32)
        result = (mixed[:, :HEAD] / mixed[:, HEAD:]).astype(jnp.bfloat16)
        for order, h in enumerate(heads):
            for part in range(NODE_TOK // piece):
                block = node * (NODE_TOK // piece) + part
                target = slot_position(parts, (block // pieces_part) ^ me)
                first = order * NODE_TOK + part * piece
                rows = pl.ds(pl.multiple_of((block % pieces_part) * piece, piece), piece)
                out[target, rows, h * HEAD : (h + 1) * HEAD] = result[first : first + piece]


def slot_position(parts, distance):
    half = parts // 2
    return jnp.where(distance % 2 == 1, distance // 2, half + distance // 2)


def attend(table, queries, keys, values, got, parts):
    rows, width = queries.shape
    key_width = keys.shape[1]
    nodes = rows // NODE_TOK
    kv_count = key_width // HEAD
    total = (CHAIN + 2) * NODE_TOK
    own = pl.BlockSpec((NODE_TOK, key_width), lambda node, table: (node, 0))
    root = pl.BlockSpec((NODE_TOK, key_width), lambda node, table: (table[0], 0))

    def chain_spec(step, offset):
        return pl.BlockSpec(
            (1, NODE_TOK, key_width), lambda node, table: (table[2 + step] + offset, 0, 0)
        )

    return pl.pallas_call(
        functools.partial(attend_body, parts, rows // parts),
        out_shape=jax.ShapeDtypeStruct((parts, rows // parts, width), queries.dtype),
        grid_spec=pltpu.PrefetchScalarGridSpec(
            num_scalar_prefetch=1,
            grid=(nodes,),
            in_specs=[
                pl.BlockSpec((NODE_TOK, width), lambda node, table: (node, 0)),
                own,
                own,
                root,
                root,
            ]
            + [chain_spec(step, 0) for step in range(CHAIN)]
            + [chain_spec(step, EXPORTS) for step in range(CHAIN)],
            out_specs=pl.BlockSpec(
                (parts, rows // parts, width), lambda node, table: (0, 0, 0)
            ),
            scratch_shapes=[
                pltpu.VMEM((kv_count, total, HEAD), keys.dtype),
                pltpu.VMEM((kv_count, total, 2 * HEAD), keys.dtype),
                pltpu.VMEM((8, CHAIN * NODE_TOK), jnp.float32),
            ],
        ),
        compiler_params=pltpu.CompilerParams(
            dimension_semantics=("arbitrary",), vmem_limit_bytes=VMEM_LIMIT
        ),
        cost_estimate=pl.CostEstimate(
            flops=rows * (width // HEAD) * total * HEAD * 6,
            bytes_accessed=rows * width * 4 + rows * key_width * 8,
            transcendentals=rows * (width // HEAD) * total,
        ),
        name="attend",
    )(table, queries, keys, values, keys, values, *([got] * (2 * CHAIN)))


def swap(array, axis, distance):
    size = lax.axis_size(axis)
    return lax.ppermute(array, axis, [(i, i ^ distance) for i in range(size)])


def times(rows, weight):
    return lax.dot_general(
        rows, weight, (((1,), (1,)), ((), ())), preferred_element_type=jnp.float32
    )


def is_middle(index):
    return (index == 1) | (index == 2)


def multiply_body(groups, pairs, *refs):
    rows = refs[:groups]
    weights = refs[groups:-2]
    outs = refs[-2:]
    middle = is_middle(lax.axis_index("node"))
    half = rows[0].shape[0] // 2
    column = 0
    cursor = 0
    for paired in pairs:
        size = weights[cursor].shape[0]

        def product(weight, column=column, size=size):
            for out, first in zip(outs, (0, half)):
                for group in range(groups):
                    out[group, :, column : column + size] = times(
                        rows[group][first : first + half, :], weight[...]
                    ).astype(out.dtype)

        if paired:
            pl.when(middle)(functools.partial(product, weights[cursor]))
            pl.when(jnp.logical_not(middle))(functools.partial(product, weights[cursor + 1]))
        else:
            product(weights[cursor])
        cursor += 2 if paired else 1
        column += size


def multiply(rows, weights):
    pairs = [isinstance(weight, tuple) for weight in weights]
    flat = [w for weight in weights for w in (weight if isinstance(weight, tuple) else (weight,))]
    total = sum((w[0] if isinstance(w, tuple) else w).shape[0] for w in weights)
    height, depth = rows[0].shape
    shape = jax.ShapeDtypeStruct((len(rows), height // 2, total), rows[0].dtype)
    return pl.pallas_call(
        functools.partial(multiply_body, len(rows), pairs),
        out_shape=(shape, shape),
        compiler_params=pltpu.CompilerParams(vmem_limit_bytes=VMEM_LIMIT),
        cost_estimate=pl.CostEstimate(
            flops=4 * len(rows) * height * depth * total,
            bytes_accessed=2 * depth * (height + total) + 2 * height * total,
            transcendentals=0,
        ),
        name="multiply",
    )(*rows, *flat)


def project_rows(rows, weights):
    sent, kept = multiply(rows, weights)
    per_part = kept.shape[1] // 2
    from_core = swap(sent, "tensor", 1)
    kept, from_core = kept.astype(jnp.float32), from_core.astype(jnp.float32)
    summed = kept + from_core
    away = summed[:, per_part:].astype(sent.dtype)
    from_chip = swap(away, "tensor", 2)
    return [
        (summed[group, :per_part] + from_chip[group].astype(jnp.float32)).astype(sent.dtype)
        for group in range(len(rows))
    ]


def relay(piece):
    pairs = [(0, 1), (1, 0), (2, 3), (3, 2)]
    middle = [(1, 2), (2, 1)]
    outward = [(1, 0), (2, 3)]
    near = lax.ppermute(piece, "node", pairs)
    across = lax.ppermute(piece, "node", middle)
    across_out = lax.ppermute(across, "node", outward)
    near_across = lax.ppermute(near, "node", middle)
    far_out = lax.ppermute(near_across, "node", outward)
    return near, (near_across, across_out), (across, far_out)


def place_body(spots, features, *refs):
    out = refs[-1]
    half = features // 2
    device = lax.axis_index("node")
    mine = lax.axis_index("groups")
    for source, parts in zip(refs[:-1], spots):
        start = 0
        for size, distance, own, offset in parts:
            group = mine if own else 1 - mine
            column = pl.multiple_of((device ^ distance) * features + group * half + offset, HEAD)
            out[:, pl.ds(column, size)] = source[:, start : start + size]
            start += size


def place(sources, spots, devices, features):
    rows = sources[0].shape[0]
    return pl.pallas_call(
        functools.partial(place_body, spots, features),
        out_shape=jax.ShapeDtypeStruct((rows, devices * features), sources[0].dtype),
        compiler_params=pltpu.CompilerParams(vmem_limit_bytes=VMEM_LIMIT),
        name="place",
    )(*sources)


def split_weight(out_weight):
    half = out_weight.shape[0] // 2
    tiles = half // HEAD
    sizes = [(tiles + 1) // 2 * HEAD, tiles // 2 * HEAD]
    first = lax.axis_index("groups") * half
    pieces = []
    for size in sizes:
        pieces.append(lax.dynamic_slice_in_dim(out_weight, first, size, 0))
        first = first + size
    return sizes, pieces, [relay(piece) for piece in pieces]


def project_split(attended, split, devices, features):
    sizes, pieces, relayed = split
    parts, per_part, width = attended.shape
    rows = attended.reshape(parts * per_part, width)
    other = swap(rows, "groups", 1)
    sources, spots = [], []

    def spot(own, items):
        spots.append(
            tuple((sizes[c], distance, own, sum(sizes[:c])) for c, distance in items)
        )

    def run(own, weights, items):
        (done,) = project_rows([rows if own else other], weights)
        sources.append(done if own else swap(done, "groups", 1))
        spot(own, items)

    def run_both(weights, items):
        done = project_rows([rows, other], weights)
        sources.append(done[0])
        spot(True, items)
        sources.append(swap(done[1], "groups", 1))
        spot(False, items)

    near = [pieces[0], pieces[1], relayed[0][0], relayed[1][0]]
    near_items = [(0, 0), (1, 0), (0, 1), (1, 1)]
    second = [relayed[0][1], relayed[1][1]]
    second_items = [(0, 2), (1, 2)]
    run(True, near, near_items)
    run(True, second, second_items)
    run(False, near, near_items)
    run(False, second, second_items)
    run_both([relayed[0][2]], [(0, 3)])
    run_both([relayed[1][2]], [(1, 3)])
    return place(sources, spots, devices, features)


def project_plain(attended, out_weight):
    parts, per_part, width = attended.shape
    me = lax.axis_index("tensor")
    order = slot_position(parts, jnp.arange(parts, dtype=jnp.int32) ^ me)
    rows = attended[order].reshape(parts * per_part, width)
    weight = lax.all_gather(out_weight, "node", axis=0, tiled=True)
    terms = times(rows, weight).astype(jnp.bfloat16)
    return lax.psum_scatter(terms, "tensor", scatter_dimension=0, tiled=True)


def local(queries, keys, values, out_weight, slot_nodes, ancestors, depth):
    parts = lax.axis_size("tensor")
    devices = lax.axis_size("node")
    features = out_weight.shape[0]
    split = None
    if (
        devices == 4
        and parts == 4
        and lax.axis_size("groups") == 2
        and features % (4 * HEAD) == 2 * HEAD
    ):
        split = split_weight(out_weight)
    exported, table = prepare(slot_nodes, ancestors, depth, keys, values)
    got = lax.all_gather(exported, "node", axis=0, tiled=True)
    attended = attend(table, queries, keys, values, got, parts)
    if split is None:
        return project_plain(attended, out_weight)
    return project_split(attended, split, devices, features)


def solution(mesh):
    placed = (
        P(("groups", "node"), "tensor"),
        P(("groups", "node"), "tensor"),
        P(("groups", "node"), "tensor"),
        P("node", "tensor"),
        P("groups"),
        P("groups", None),
        P("groups"),
    )
    return jax.shard_map(
        local,
        mesh=mesh,
        in_specs=placed,
        out_specs=P(("groups", "node", "tensor"), None),
        check_vma=False,
    )
```

```python
import functools
import math

import jax
import jax.numpy as jnp
from jax import lax
from jax.experimental import pallas as pl
from jax.experimental.pallas import tpu as pltpu
from jax.sharding import PartitionSpec as P

HEAD = 128
NODE_TOK = 128
A_MAX = 7
CHAIN = A_MAX - 1
EXPORTS = 2
SCALE = math.log2(math.e) / math.sqrt(HEAD)
DEAD = -1e30
LIGHT = pl.CostEstimate(flops=1, bytes_accessed=1, transcendentals=0)
VMEM_LIMIT = 40 * 1024 * 1024
ATTEND_LIMIT = 56 * 1024 * 1024


def prepare_body(nodes, relative, *refs):
    slot_hbm, ancestors_hbm, depth_hbm, keys, values, exported, table_hbm = refs[:7]
    slot_nodes, ancestors, depth, table, holder, within, roots, sem = refs[7:]
    devices = slot_nodes.shape[0] // nodes
    me = lax.axis_index("node")
    fetches = [
        pltpu.make_async_copy(source, target, sem.at[2 * EXPORTS + 1 + order])
        for order, (source, target) in enumerate(
            ((slot_hbm, slot_nodes), (ancestors_hbm, ancestors), (depth_hbm, depth))
        )
    ]
    for fetch in fetches:
        fetch.start()
    for fetch in fetches:
        fetch.wait()

    def place(device, mine):
        root, root_index = jnp.int32(0), jnp.int32(0)
        for index in range(nodes):
            node = slot_nodes[device * nodes + index]
            holder[node] = device
            within[node] = index
            even = (depth[node] & 1) == 0
            root = jnp.where(even, node, root)
            root_index = jnp.where(even, index, root_index)
        roots[device] = root
        return jnp.where(device == me, root_index, mine)

    root = lax.fori_loop(0, devices, place, jnp.int32(0))

    def find_attach(device, attach):
        node = roots[device]
        level = depth[node]
        for step in range(0, CHAIN, 2):
            above = jnp.maximum(ancestors[step, node], 0)
            hit = (step < level) & (holder[above] == me)
            attach = jnp.where(hit, within[above], attach)
        return attach

    attach = lax.fori_loop(0, devices, find_attach, jnp.int32(0))
    copies = []
    for position, (source, index) in enumerate(
        ((keys, root), (keys, attach), (values, root), (values, attach))
    ):
        rows = pl.ds(pl.multiple_of(index * NODE_TOK, NODE_TOK), NODE_TOK)
        copies.append(
            pltpu.make_async_copy(source.at[rows, :], exported.at[position], sem.at[position])
        )
    for copy in copies:
        copy.start()
    root_node = roots[me]
    count = depth[root_node]
    table[0] = root
    table[1] = count
    for step in range(CHAIN):
        above = jnp.maximum(ancestors[step, root_node], 0)
        where = ((holder[above] ^ me) - 1) if relative else holder[above]
        entry = where * (2 * EXPORTS) + (1 if step % 2 == 0 else 0)
        table[2 + step] = jnp.where(step < count, entry, 0)
    store = pltpu.make_async_copy(table, table_hbm, sem.at[2 * EXPORTS])
    store.start()
    for copy in copies:
        copy.wait()
    store.wait()


def prepare(slot_nodes, ancestors, depth, keys, values, relative):
    nodes = keys.shape[0] // NODE_TOK
    slots = slot_nodes.shape[0]
    hbm = pl.BlockSpec(memory_space=pl.ANY)
    return pl.pallas_call(
        functools.partial(prepare_body, nodes, relative),
        out_shape=(
            jax.ShapeDtypeStruct((2 * EXPORTS, NODE_TOK, keys.shape[1]), keys.dtype),
            jax.ShapeDtypeStruct((2 + CHAIN,), jnp.int32),
        ),
        in_specs=[hbm] * 5,
        out_specs=(hbm, hbm),
        scratch_shapes=[
            pltpu.SMEM((slots,), jnp.int32),
            pltpu.SMEM((A_MAX, slots), jnp.int32),
            pltpu.SMEM((slots,), jnp.int32),
            pltpu.SMEM((2 + CHAIN,), jnp.int32),
            pltpu.SMEM((slots,), jnp.int32),
            pltpu.SMEM((slots,), jnp.int32),
            pltpu.SMEM((slots // nodes,), jnp.int32),
            pltpu.SemaphoreType.DMA((2 * EXPORTS + 4,)),
        ],
        name="prepare",
    )(slot_nodes, ancestors.T, depth, keys, values)


def attend_body(parts, per_part, table, *refs):
    query, own_key, own_value, root_key, root_value = refs[:5]
    chain_keys = refs[5 : 5 + CHAIN]
    chain_values = refs[5 + CHAIN : 5 + 2 * CHAIN]
    out, all_keys, all_values, bias = refs[-4:]
    node = pl.program_id(0)
    kv_count = own_key.shape[1] // HEAD
    group = query.shape[1] // HEAD // kv_count
    above = CHAIN * NODE_TOK
    root_rows = pl.ds(above, NODE_TOK)
    own_rows = pl.ds(above + NODE_TOK, NODE_TOK)

    @pl.when(node == 0)
    def _():
        all_values[:, :, HEAD:] = jnp.ones_like(all_values[:, :, HEAD:])
        for kv in range(kv_count):
            lanes = pl.ds(kv * HEAD, HEAD)
            for step in range(CHAIN):
                rows = pl.ds(step * NODE_TOK, NODE_TOK)
                all_keys[kv, rows, :] = chain_keys[step][0, :, lanes]
                all_values[kv, rows, :HEAD] = chain_values[step][0, :, lanes]
            all_keys[kv, root_rows, :] = root_key[:, lanes]
            all_values[kv, root_rows, :HEAD] = root_value[:, lanes]
        for step in range(CHAIN):
            live = step < table[1]
            bias[:, step * NODE_TOK : (step + 1) * NODE_TOK] = jnp.full(
                (8, NODE_TOK), jnp.where(live, 0.0, DEAD), jnp.float32
            )

    for kv in range(kv_count):
        lanes = pl.ds(kv * HEAD, HEAD)
        all_keys[kv, own_rows, :] = own_key[:, lanes]
        all_values[kv, own_rows, :HEAD] = own_value[:, lanes]

    root_bias = jnp.where(node == table[0], DEAD, 0.0)
    query_index = lax.broadcasted_iota(jnp.int32, (NODE_TOK, NODE_TOK), 0)
    key_index = lax.broadcasted_iota(jnp.int32, (NODE_TOK, NODE_TOK), 1)
    own_bias = jnp.where(key_index <= query_index, 0.0, DEAD)
    piece = math.gcd(NODE_TOK, per_part)
    pieces_part = per_part // piece
    me = lax.axis_index("tensor")
    contract = (((1,), (1,)), ((), ()))
    for kv in range(kv_count):
        heads = range(kv * group, (kv + 1) * group)
        stacked = jnp.concatenate([query[:, h * HEAD : (h + 1) * HEAD] for h in heads], 0)
        scores = lax.dot_general(
            stacked, all_keys[kv], contract, preferred_element_type=jnp.float32
        )
        chain = scores[:, :above] + bias[0:1, :]
        root = scores[:, above : above + NODE_TOK] + root_bias
        own = scores[:, above + NODE_TOK :] + jnp.concatenate([own_bias] * group, 0)
        masked = jnp.concatenate([chain, root, own], 1)
        largest = jnp.max(masked, axis=1, keepdims=True)
        expo = jnp.exp2((masked - largest) * SCALE).astype(jnp.bfloat16)
        mixed = jnp.dot(expo, all_values[kv], preferred_element_type=jnp.float32)
        result = (mixed[:, :HEAD] / mixed[:, HEAD:]).astype(jnp.bfloat16)
        for order, h in enumerate(heads):
            for part in range(NODE_TOK // piece):
                block = node * (NODE_TOK // piece) + part
                target = slot_position(parts, (block // pieces_part) ^ me)
                first = order * NODE_TOK + part * piece
                rows = pl.ds(pl.multiple_of((block % pieces_part) * piece, piece), piece)
                out[target, rows, h * HEAD : (h + 1) * HEAD] = result[first : first + piece]


def slot_position(parts, distance):
    half = parts // 2
    return jnp.where(distance % 2 == 1, distance // 2, half + distance // 2)


def attend(table, queries, keys, values, got, parts):
    rows, width = queries.shape
    key_width = keys.shape[1]
    nodes = rows // NODE_TOK
    kv_count = key_width // HEAD
    total = (CHAIN + 2) * NODE_TOK
    own = pl.BlockSpec((NODE_TOK, key_width), lambda node, table: (node, 0))
    root = pl.BlockSpec((NODE_TOK, key_width), lambda node, table: (table[0], 0))

    def chain_spec(step, offset):
        return pl.BlockSpec(
            (1, NODE_TOK, key_width), lambda node, table: (table[2 + step] + offset, 0, 0)
        )

    return pl.pallas_call(
        functools.partial(attend_body, parts, rows // parts),
        out_shape=jax.ShapeDtypeStruct((parts, rows // parts, width), queries.dtype),
        grid_spec=pltpu.PrefetchScalarGridSpec(
            num_scalar_prefetch=1,
            grid=(nodes,),
            in_specs=[
                pl.BlockSpec((NODE_TOK, width), lambda node, table: (node, 0)),
                own,
                own,
                root,
                root,
            ]
            + [chain_spec(step, 0) for step in range(CHAIN)]
            + [chain_spec(step, EXPORTS) for step in range(CHAIN)],
            out_specs=pl.BlockSpec(
                (parts, rows // parts, width), lambda node, table: (0, 0, 0)
            ),
            scratch_shapes=[
                pltpu.VMEM((kv_count, total, HEAD), keys.dtype),
                pltpu.VMEM((kv_count, total, 2 * HEAD), keys.dtype),
                pltpu.VMEM((8, CHAIN * NODE_TOK), jnp.float32),
            ],
        ),
        compiler_params=pltpu.CompilerParams(
            dimension_semantics=("arbitrary",), vmem_limit_bytes=ATTEND_LIMIT
        ),
        cost_estimate=LIGHT,
        name="attend",
    )(table, queries, keys, values, keys, values, *([got] * (2 * CHAIN)))


def swap(array, axis, distance):
    size = lax.axis_size(axis)
    return lax.ppermute(array, axis, [(i, i ^ distance) for i in range(size)])


def times(rows, weight):
    return lax.dot_general(
        rows, weight, (((1,), (1,)), ((), ())), preferred_element_type=jnp.float32
    )


def multiply_body(groups, sizes, *refs):
    rows = refs[:groups]
    weights = refs[groups : groups + len(sizes)]
    outs = refs[-2:]
    me = lax.axis_index("node")
    half = rows[0].shape[0] // 2
    column = 0
    for weight, size in zip(weights, sizes):
        taken = [weight]
        if size:
            taken = [
                weight.at[pl.ds(pl.multiple_of((me ^ distance) * size, size), size), :]
                for distance in range(1, weight.shape[0] // size)
            ]
        for block in taken:
            width = block.shape[0]
            for out, first in zip(outs, (0, half)):
                for group in range(groups):
                    out[group, :, column : column + width] = times(
                        rows[group][first : first + half, :], block[...]
                    ).astype(out.dtype)
            column += width


def multiply(rows, weights, sizes, after):
    total = sum(weight.shape[0] - size for weight, size in zip(weights, sizes))
    height, depth = rows[0].shape
    shape = jax.ShapeDtypeStruct((len(rows), height // 2, total), rows[0].dtype)
    return pl.pallas_call(
        functools.partial(multiply_body, len(rows), sizes),
        out_shape=(shape, shape),
        in_specs=[pl.BlockSpec(memory_space=pltpu.VMEM)] * (len(rows) + len(weights))
        + [pl.BlockSpec(memory_space=pl.ANY)] * len(after),
        compiler_params=pltpu.CompilerParams(vmem_limit_bytes=VMEM_LIMIT),
        cost_estimate=LIGHT,
        name="multiply",
    )(*rows, *weights, *after)


def project_rows(rows, weights, sizes, after):
    sent, kept = multiply(rows, weights, sizes, after)
    per_part = kept.shape[1] // 2
    from_core = swap(sent, "tensor", 1)
    kept, from_core = kept.astype(jnp.float32), from_core.astype(jnp.float32)
    summed = kept + from_core
    away = summed[:, per_part:].astype(sent.dtype)
    from_chip = swap(away, "tensor", 2)
    return sent, [
        (summed[group, :per_part] + from_chip[group].astype(jnp.float32)).astype(sent.dtype)
        for group in range(len(rows))
    ]


def place_body(spots, features, *refs):
    out = refs[-1]
    half = features // 2
    device = lax.axis_index("node")
    mine = lax.axis_index("groups")
    for source, parts in zip(refs[:-1], spots):
        start = 0
        for size, distance, side, offset in parts:
            group = {"own": mine, "other": 1 - mine, "all": 0}[side]
            column = pl.multiple_of((device ^ distance) * features + group * half + offset, HEAD)
            out[:, pl.ds(column, size)] = source[:, start : start + size]
            start += size


def place(sources, spots, devices, features):
    rows = sources[0].shape[0]
    return pl.pallas_call(
        functools.partial(place_body, spots, features),
        out_shape=jax.ShapeDtypeStruct((rows, devices * features), sources[0].dtype),
        compiler_params=pltpu.CompilerParams(vmem_limit_bytes=VMEM_LIMIT),
        name="place",
    )(*sources)


def split_weight(out_weight):
    half = out_weight.shape[0] // 2
    first_size = (half // HEAD + 1) // 2 * HEAD
    sizes = [first_size, half - first_size]
    first = lax.axis_index("groups") * half
    gathered = []
    for size in sizes:
        piece = lax.dynamic_slice_in_dim(out_weight, first, size, 0)
        gathered.append(lax.all_gather(piece, "node", axis=0, tiled=True))
        first = first + size
    return sizes, gathered


def project_split(attended, split, out_weight):
    sizes, gathered = split
    features = out_weight.shape[0]
    devices = lax.axis_size("node")
    parts, per_part, width = attended.shape
    rows = attended.reshape(parts * per_part, width)
    other = swap(rows, "groups", 1)

    sent, (done,) = project_rows([rows], [out_weight], [0], [])
    sources = [done]
    spots = [((features, 0, "all", 0),)]

    offset = 0
    for size, weight in zip(sizes, gathered):
        earlier = sources[-2:]
        for side, chosen in (("own", rows), ("other", other)):
            sent, (done,) = project_rows([chosen], [weight], [size], [sent, earlier.pop(0)])
            earlier = earlier or [sent]
            sources.append(done if side == "own" else swap(done, "groups", 1))
            spots.append(
                tuple((size, distance, side, offset) for distance in range(1, devices))
            )
        offset += size
    return place(sources, spots, devices, features)


def project_plain(attended, out_weight):
    parts, per_part, width = attended.shape
    me = lax.axis_index("tensor")
    order = slot_position(parts, jnp.arange(parts, dtype=jnp.int32) ^ me)
    rows = attended[order].reshape(parts * per_part, width)
    weight = lax.all_gather(out_weight, "node", axis=0, tiled=True)
    terms = times(rows, weight).astype(jnp.bfloat16)
    return lax.psum_scatter(terms, "tensor", scatter_dimension=0, tiled=True)


def local(queries, keys, values, out_weight, slot_nodes, ancestors, depth):
    parts = lax.axis_size("tensor")
    devices = lax.axis_size("node")
    features = out_weight.shape[0]
    split = None
    relative = devices == 4
    if (
        devices == 4
        and parts == 4
        and lax.axis_size("groups") == 2
        and features % (2 * HEAD) == 0
        and features >= 4 * HEAD
    ):
        split = split_weight(out_weight)
    exported, table = prepare(slot_nodes, ancestors, depth, keys, values, relative)
    if relative:
        got = jnp.concatenate([swap(exported, "node", distance) for distance in (1, 2, 3)], 0)
    else:
        got = lax.all_gather(exported, "node", axis=0, tiled=True)
    attended = attend(table, queries, keys, values, got, parts)
    if split is None:
        return project_plain(attended, out_weight)
    return project_split(attended, split, out_weight)


def solution(mesh):
    placed = (
        P(("groups", "node"), "tensor"),
        P(("groups", "node"), "tensor"),
        P(("groups", "node"), "tensor"),
        P("node", "tensor"),
        P("groups"),
        P("groups", None),
        P("groups"),
    )
    return jax.shard_map(
        local,
        mesh=mesh,
        in_specs=placed,
        out_specs=P(("groups", "node", "tensor"), None),
        check_vma=False,
    )
```

```python
import functools
import math

import jax
import jax.numpy as jnp
from jax import lax
from jax.experimental import pallas as pl
from jax.experimental.pallas import tpu as pltpu
from jax.sharding import PartitionSpec as P

HEAD = 128
NODE_TOK = 128
A_MAX = 7
CHAIN = A_MAX - 1
EXPORTS = 2
SCALE = math.log2(math.e) / math.sqrt(HEAD)
DEAD = -1e30
LIGHT = pl.CostEstimate(flops=1, bytes_accessed=1, transcendentals=0)
VMEM_LIMIT = 40 * 1024 * 1024
ATTEND_LIMIT = 56 * 1024 * 1024


def prepare_body(nodes, *refs):
    slot_hbm, ancestors_hbm, depth_hbm, keys, values, exported, table_hbm = refs[:7]
    slot_nodes, ancestors, depth, table, holder, within, roots, sem = refs[7:]
    devices = slot_nodes.shape[0] // nodes
    me = lax.axis_index("node")
    fetches = [
        pltpu.make_async_copy(source, target, sem.at[2 * EXPORTS + 1 + order])
        for order, (source, target) in enumerate(
            ((slot_hbm, slot_nodes), (ancestors_hbm, ancestors), (depth_hbm, depth))
        )
    ]
    for fetch in fetches:
        fetch.start()
    for fetch in fetches:
        fetch.wait()

    def place(device, mine):
        root, root_index = jnp.int32(0), jnp.int32(0)
        for index in range(nodes):
            node = slot_nodes[device * nodes + index]
            holder[node] = device
            within[node] = index
            even = (depth[node] & 1) == 0
            root = jnp.where(even, node, root)
            root_index = jnp.where(even, index, root_index)
        roots[device] = root
        return jnp.where(device == me, root_index, mine)

    root = lax.fori_loop(0, devices, place, jnp.int32(0))

    def find_attach(device, attach):
        node = roots[device]
        level = depth[node]
        for step in range(0, CHAIN, 2):
            above = jnp.maximum(ancestors[step, node], 0)
            hit = (step < level) & (holder[above] == me)
            attach = jnp.where(hit, within[above], attach)
        return attach

    attach = lax.fori_loop(0, devices, find_attach, jnp.int32(0))
    copies = []
    for position, (source, index) in enumerate(
        ((keys, root), (keys, attach), (values, root), (values, attach))
    ):
        rows = pl.ds(pl.multiple_of(index * NODE_TOK, NODE_TOK), NODE_TOK)
        copies.append(
            pltpu.make_async_copy(source.at[rows, :], exported.at[position], sem.at[position])
        )
    for copy in copies:
        copy.start()
    root_node = roots[me]
    count = depth[root_node]
    table[0] = root
    table[1] = count
    for step in range(CHAIN):
        above = jnp.maximum(ancestors[step, root_node], 0)
        entry = holder[above] * (2 * EXPORTS) + (1 if step % 2 == 0 else 0)
        table[2 + step] = jnp.where(step < count, entry, 0)
    store = pltpu.make_async_copy(table, table_hbm, sem.at[2 * EXPORTS])
    store.start()
    for copy in copies:
        copy.wait()
    store.wait()


def prepare(slot_nodes, ancestors, depth, keys, values):
    nodes = keys.shape[0] // NODE_TOK
    slots = slot_nodes.shape[0]
    hbm = pl.BlockSpec(memory_space=pl.ANY)
    return pl.pallas_call(
        functools.partial(prepare_body, nodes),
        out_shape=(
            jax.ShapeDtypeStruct((2 * EXPORTS, NODE_TOK, keys.shape[1]), keys.dtype),
            jax.ShapeDtypeStruct((2 + CHAIN,), jnp.int32),
        ),
        in_specs=[hbm] * 5,
        out_specs=(hbm, hbm),
        scratch_shapes=[
            pltpu.SMEM((slots,), jnp.int32),
            pltpu.SMEM((A_MAX, slots), jnp.int32),
            pltpu.SMEM((slots,), jnp.int32),
            pltpu.SMEM((2 + CHAIN,), jnp.int32),
            pltpu.SMEM((slots,), jnp.int32),
            pltpu.SMEM((slots,), jnp.int32),
            pltpu.SMEM((slots // nodes,), jnp.int32),
            pltpu.SemaphoreType.DMA((2 * EXPORTS + 4,)),
        ],
        name="prepare",
    )(slot_nodes, ancestors.T, depth, keys, values)


def attend_body(parts, per_part, table, *refs):
    query, own_key, own_value, root_key, root_value = refs[:5]
    chain_keys = refs[5 : 5 + CHAIN]
    chain_values = refs[5 + CHAIN : 5 + 2 * CHAIN]
    out, all_keys, all_values, bias = refs[-4:]
    node = pl.program_id(0)
    kv_count = own_key.shape[1] // HEAD
    group = query.shape[1] // HEAD // kv_count
    above = CHAIN * NODE_TOK
    root_rows = pl.ds(above, NODE_TOK)
    own_rows = pl.ds(above + NODE_TOK, NODE_TOK)

    @pl.when(node == 0)
    def _():
        all_values[:, :, HEAD:] = jnp.ones_like(all_values[:, :, HEAD:])
        for kv in range(kv_count):
            lanes = pl.ds(kv * HEAD, HEAD)
            for step in range(CHAIN):
                rows = pl.ds(step * NODE_TOK, NODE_TOK)
                all_keys[kv, rows, :] = chain_keys[step][0, :, lanes]
                all_values[kv, rows, :HEAD] = chain_values[step][0, :, lanes]
            all_keys[kv, root_rows, :] = root_key[:, lanes]
            all_values[kv, root_rows, :HEAD] = root_value[:, lanes]
        for step in range(CHAIN):
            live = step < table[1]
            bias[:, step * NODE_TOK : (step + 1) * NODE_TOK] = jnp.full(
                (8, NODE_TOK), jnp.where(live, 0.0, DEAD), jnp.float32
            )

    for kv in range(kv_count):
        lanes = pl.ds(kv * HEAD, HEAD)
        all_keys[kv, own_rows, :] = own_key[:, lanes]
        all_values[kv, own_rows, :HEAD] = own_value[:, lanes]

    root_bias = jnp.where(node == table[0], DEAD, 0.0)
    query_index = lax.broadcasted_iota(jnp.int32, (NODE_TOK, NODE_TOK), 0)
    key_index = lax.broadcasted_iota(jnp.int32, (NODE_TOK, NODE_TOK), 1)
    own_bias = jnp.where(key_index <= query_index, 0.0, DEAD)
    piece = math.gcd(NODE_TOK, per_part)
    pieces_part = per_part // piece
    me = lax.axis_index("tensor")
    contract = (((1,), (1,)), ((), ()))
    for kv in range(kv_count):
        heads = range(kv * group, (kv + 1) * group)
        stacked = jnp.concatenate([query[:, h * HEAD : (h + 1) * HEAD] for h in heads], 0)
        scores = lax.dot_general(
            stacked, all_keys[kv], contract, preferred_element_type=jnp.float32
        )
        chain = scores[:, :above] + bias[0:1, :]
        root = scores[:, above : above + NODE_TOK] + root_bias
        own = scores[:, above + NODE_TOK :] + jnp.concatenate([own_bias] * group, 0)
        masked = jnp.concatenate([chain, root, own], 1)
        largest = jnp.max(masked, axis=1, keepdims=True)
        expo = jnp.exp2((masked - largest) * SCALE).astype(jnp.bfloat16)
        mixed = jnp.dot(expo, all_values[kv], preferred_element_type=jnp.float32)
        result = (mixed[:, :HEAD] / mixed[:, HEAD:]).astype(jnp.bfloat16)
        for order, h in enumerate(heads):
            for part in range(NODE_TOK // piece):
                block = node * (NODE_TOK // piece) + part
                target = slot_position(parts, (block // pieces_part) ^ me)
                first = order * NODE_TOK + part * piece
                rows = pl.ds(pl.multiple_of((block % pieces_part) * piece, piece), piece)
                out[target, rows, h * HEAD : (h + 1) * HEAD] = result[first : first + piece]


def slot_position(parts, distance):
    half = parts // 2
    return jnp.where(distance % 2 == 1, distance // 2, half + distance // 2)


def attend(table, queries, keys, values, got, parts, after):
    rows, width = queries.shape
    key_width = keys.shape[1]
    nodes = rows // NODE_TOK
    kv_count = key_width // HEAD
    total = (CHAIN + 2) * NODE_TOK
    own = pl.BlockSpec((NODE_TOK, key_width), lambda node, table: (node, 0))
    root = pl.BlockSpec((NODE_TOK, key_width), lambda node, table: (table[0], 0))

    def chain_spec(step, offset):
        return pl.BlockSpec(
            (1, NODE_TOK, key_width), lambda node, table: (table[2 + step] + offset, 0, 0)
        )

    return pl.pallas_call(
        functools.partial(attend_body, parts, rows // parts),
        out_shape=jax.ShapeDtypeStruct((parts, rows // parts, width), queries.dtype),
        grid_spec=pltpu.PrefetchScalarGridSpec(
            num_scalar_prefetch=1,
            grid=(nodes,),
            in_specs=[
                pl.BlockSpec((NODE_TOK, width), lambda node, table: (node, 0)),
                own,
                own,
                root,
                root,
            ]
            + [chain_spec(step, 0) for step in range(CHAIN)]
            + [chain_spec(step, EXPORTS) for step in range(CHAIN)]
            + [pl.BlockSpec(memory_space=pl.ANY)] * len(after),
            out_specs=pl.BlockSpec(
                (parts, rows // parts, width), lambda node, table: (0, 0, 0)
            ),
            scratch_shapes=[
                pltpu.VMEM((kv_count, total, HEAD), keys.dtype),
                pltpu.VMEM((kv_count, total, 2 * HEAD), keys.dtype),
                pltpu.VMEM((8, CHAIN * NODE_TOK), jnp.float32),
            ],
        ),
        compiler_params=pltpu.CompilerParams(
            dimension_semantics=("arbitrary",), vmem_limit_bytes=ATTEND_LIMIT
        ),
        cost_estimate=LIGHT,
        name="attend",
    )(table, queries, keys, values, keys, values, *([got] * (2 * CHAIN)), *after)


def swap(array, axis, distance):
    size = lax.axis_size(axis)
    return lax.ppermute(array, axis, [(i, i ^ distance) for i in range(size)])


def times(rows, weight):
    return lax.dot_general(
        rows, weight, (((1,), (1,)), ((), ())), preferred_element_type=jnp.float32
    )


def is_middle(index):
    return (index == 1) | (index == 2)


def step_body(row_count, pairs, core_count, chip_count, outputs, *refs):
    refs = list(refs)
    outs = refs[len(refs) - outputs :]
    rows = [refs.pop(0) for _ in range(row_count)]
    weights = [[refs.pop(0) for _ in range(2 if paired else 1)] for paired in pairs]
    middle = is_middle(lax.axis_index("node"))

    def product(column, weight):
        half = rows[0].shape[0] // 2
        for out, start in zip(outs, (0, half)):
            out[:, column : column + weight.shape[0]] = times(
                rows[0][start : start + half, :], weight[...]
            ).astype(out.dtype)

    column = 0
    for choice in weights:
        if len(choice) == 2:
            pl.when(middle)(functools.partial(product, column, choice[0]))
            pl.when(jnp.logical_not(middle))(functools.partial(product, column, choice[1]))
        else:
            product(column, choice[0])
        column += choice[0].shape[0]
    outs = outs[2 if weights else 0 :]
    for _ in range(core_count):
        kept, from_core = refs.pop(0), refs.pop(0)
        half = kept.shape[0] // 2
        out = outs.pop(0)
        out[...] = (
            kept[half:, :].astype(jnp.float32) + from_core[half:, :].astype(jnp.float32)
        ).astype(out.dtype)
    for _ in range(chip_count):
        kept, from_core, from_chip = refs.pop(0), refs.pop(0), refs.pop(0)
        out = outs.pop(0)
        out[...] = chip_sum(kept, from_core, from_chip).astype(out.dtype)


def chip_sum(kept, from_core, from_chip):
    half = kept.shape[0] // 2
    first = kept[:half, :].astype(jnp.float32) + from_core[:half, :].astype(jnp.float32)
    return first + from_chip[...].astype(jnp.float32)


def step(rows=(), weights=(), cores=(), chips=(), after=()):
    pairs = [isinstance(weight, tuple) for weight in weights]
    flat = [w for weight in weights for w in (weight if isinstance(weight, tuple) else (weight,))]
    dtype = (cores or chips)[0][0].dtype if not rows else rows[0].dtype
    shapes = []
    if rows:
        total = sum((w[0] if isinstance(w, tuple) else w).shape[0] for w in weights)
        height = sum(block.shape[0] for block in rows) // 2
        shapes += [(height, total)] * 2
    shapes += [(kept.shape[0] // 2, kept.shape[1]) for kept, _ in cores]
    shapes += [(kept.shape[0] // 2, kept.shape[1]) for kept, _, _ in chips]
    read = [*rows, *flat, *[x for item in (*cores, *chips) for x in item]]
    return pl.pallas_call(
        functools.partial(step_body, len(rows), pairs, len(cores), len(chips), len(shapes)),
        out_shape=[jax.ShapeDtypeStruct(shape, dtype) for shape in shapes],
        in_specs=[pl.BlockSpec(memory_space=pltpu.VMEM)] * len(read)
        + [pl.BlockSpec(memory_space=pl.ANY)] * len(after),
        compiler_params=pltpu.CompilerParams(vmem_limit_bytes=VMEM_LIMIT),
        cost_estimate=LIGHT,
        name="step",
    )(*read, *after)


def relay(piece):
    pairs = [(0, 1), (1, 0), (2, 3), (3, 2)]
    middle = [(1, 2), (2, 1)]
    outward = [(1, 0), (2, 3)]
    near = lax.ppermute(piece, "node", pairs)
    across = lax.ppermute(piece, "node", middle)
    across_out = lax.ppermute(across, "node", outward)
    near_across = lax.ppermute(near, "node", middle)
    far_out = lax.ppermute(near_across, "node", outward)
    return near, (near_across, across_out), (across, far_out)


def place_body(spots, features, *refs):
    out = refs[-1]
    half = features // 2
    device = lax.axis_index("node")
    mine = lax.axis_index("groups")
    last = chip_sum(*refs[:3]).astype(out.dtype)
    for source, parts in zip((last, *refs[3:-1]), spots):
        start = 0
        for size, distance, side in parts:
            group = {"own": mine, "other": 1 - mine, "all": 0}[side]
            column = pl.multiple_of((device ^ distance) * features + group * half, HEAD)
            out[:, pl.ds(column, size)] = source[:, start : start + size]
            start += size


def place(last, sources, spots, devices, features):
    return pl.pallas_call(
        functools.partial(place_body, spots, features),
        out_shape=jax.ShapeDtypeStruct((last[2].shape[0], devices * features), last[2].dtype),
        compiler_params=pltpu.CompilerParams(vmem_limit_bytes=VMEM_LIMIT),
        name="place",
    )(*last, *sources)


def split_weight(out_weight):
    half = out_weight.shape[0] // 2
    first = lax.axis_index("groups") * half
    return relay(lax.dynamic_slice_in_dim(out_weight, first, half, 0))


def project_split(attended, relayed, out_weight):
    features = out_weight.shape[0]
    half = features // 2
    parts, per_part, width = attended.shape
    rows = attended.reshape(parts * per_part, width)
    other = swap(rows, "groups", 1)
    near, second, far = relayed

    def core(sent):
        return swap(sent, "tensor", 1)

    def chip(away):
        return swap(away, "tensor", 2)

    sent, kept_0 = step([rows], [out_weight])
    core_0 = core(sent)
    sent, kept_1 = step([rows], [near], after=[sent])
    core_1 = core(sent)
    sent, kept_2, away_0, away_1 = step(
        [rows], [second], cores=[(kept_0, core_0), (kept_1, core_1)]
    )
    core_2, chip_0, chip_1 = core(sent), chip(away_0), chip(away_1)
    sent, kept_3, away_2, done_0 = step(
        [other],
        [near, second],
        cores=[(kept_2, core_2)],
        chips=[(kept_0, core_0, chip_0)],
    )
    core_3, chip_2 = core(sent), chip(away_2)
    away_3, done_1 = step(cores=[(kept_3, core_3)], chips=[(kept_1, core_1, chip_1)])
    chip_3 = chip(away_3)
    sent, kept_4 = step([other], [far], after=[away_3])
    core_4 = core(sent)
    sent, kept_5, away_4, done_2 = step(
        [rows], [far], cores=[(kept_4, core_4)], chips=[(kept_2, core_2, chip_2)]
    )
    core_5, chip_4 = core(sent), chip(away_4)
    away_5, done_3 = step(cores=[(kept_5, core_5)], chips=[(kept_3, core_3, chip_3)])
    chip_5, group_3 = chip(away_5), swap(done_3, "groups", 1)
    (done_4,) = step(chips=[(kept_4, core_4, chip_4)])
    group_4 = swap(done_4, "groups", 1)
    return place(
        (kept_5, core_5, chip_5),
        (done_0, done_1, done_2, group_3, group_4),
        (
            ((half, 3, "own"),),
            ((features, 0, "all"),),
            ((half, 1, "own"),),
            ((half, 2, "own"),),
            ((half, 1, "other"), (half, 2, "other")),
            ((half, 3, "other"),),
        ),
        lax.axis_size("node"),
        features,
    )


def project_plain(attended, out_weight):
    parts, per_part, width = attended.shape
    me = lax.axis_index("tensor")
    order = slot_position(parts, jnp.arange(parts, dtype=jnp.int32) ^ me)
    rows = attended[order].reshape(parts * per_part, width)
    weight = lax.all_gather(out_weight, "node", axis=0, tiled=True)
    terms = times(rows, weight).astype(jnp.bfloat16)
    return lax.psum_scatter(terms, "tensor", scatter_dimension=0, tiled=True)


def local(queries, keys, values, out_weight, slot_nodes, ancestors, depth):
    parts = lax.axis_size("tensor")
    devices = lax.axis_size("node")
    features = out_weight.shape[0]
    relayed, after = None, []
    if (
        devices == 4
        and parts == 4
        and lax.axis_size("groups") == 2
        and features % (2 * HEAD) == 0
    ):
        relayed = split_weight(out_weight)
        after = [relayed[0], relayed[2][0]]
    exported, table = prepare(slot_nodes, ancestors, depth, keys, values)
    got = lax.all_gather(exported, "node", axis=0, tiled=True)
    attended = attend(table, queries, keys, values, got, parts, after)
    if relayed is None:
        return project_plain(attended, out_weight)
    return project_split(attended, relayed, out_weight)


def solution(mesh):
    placed = (
        P(("groups", "node"), "tensor"),
        P(("groups", "node"), "tensor"),
        P(("groups", "node"), "tensor"),
        P("node", "tensor"),
        P("groups"),
        P("groups", None),
        P("groups"),
    )
    return jax.shard_map(
        local,
        mesh=mesh,
        in_specs=placed,
        out_specs=P(("groups", "node", "tensor"), None),
        check_vma=False,
    )
```

```python
import functools
import math

import jax
import jax.numpy as jnp
from jax import lax
from jax.experimental import pallas as pl
from jax.experimental.pallas import tpu as pltpu
from jax.sharding import PartitionSpec as P

HEAD = 128
NODE_TOK = 128
A_MAX = 7
CHAIN = A_MAX - 1
EXPORTS = 2
SCALE = math.log2(math.e) / math.sqrt(HEAD)
DEAD = -1e30
LIGHT = pl.CostEstimate(flops=1, bytes_accessed=1, transcendentals=0)
VMEM_LIMIT = 56 * 1024 * 1024


def prepare_body(nodes, *refs):
    slot_hbm, ancestors_hbm, depth_hbm, keys, values, exported, table_hbm = refs[:7]
    slot_nodes, ancestors, depth, table, holder, within, roots, sem = refs[7:]
    devices = slot_nodes.shape[0] // nodes
    me = lax.axis_index("node")
    fetches = [
        pltpu.make_async_copy(source, target, sem.at[2 * EXPORTS + 1 + order])
        for order, (source, target) in enumerate(
            ((slot_hbm, slot_nodes), (ancestors_hbm, ancestors), (depth_hbm, depth))
        )
    ]
    for fetch in fetches:
        fetch.start()
    for fetch in fetches:
        fetch.wait()

    def place(device, mine):
        root, root_index = jnp.int32(0), jnp.int32(0)
        for index in range(nodes):
            node = slot_nodes[device * nodes + index]
            holder[node] = device
            within[node] = index
            even = (depth[node] & 1) == 0
            root = jnp.where(even, node, root)
            root_index = jnp.where(even, index, root_index)
        roots[device] = root
        return jnp.where(device == me, root_index, mine)

    root = lax.fori_loop(0, devices, place, jnp.int32(0))

    def find_attach(device, attach):
        node = roots[device]
        level = depth[node]
        for step in range(0, CHAIN, 2):
            above = jnp.maximum(ancestors[step, node], 0)
            hit = (step < level) & (holder[above] == me)
            attach = jnp.where(hit, within[above], attach)
        return attach

    attach = lax.fori_loop(0, devices, find_attach, jnp.int32(0))
    copies = []
    for position, (source, index) in enumerate(
        ((keys, root), (keys, attach), (values, root), (values, attach))
    ):
        rows = pl.ds(pl.multiple_of(index * NODE_TOK, NODE_TOK), NODE_TOK)
        copies.append(
            pltpu.make_async_copy(source.at[rows, :], exported.at[position], sem.at[position])
        )
    for copy in copies:
        copy.start()
    root_node = roots[me]
    count = depth[root_node]
    table[0] = root
    table[1] = count
    for step in range(CHAIN):
        above = jnp.maximum(ancestors[step, root_node], 0)
        entry = holder[above] * (2 * EXPORTS) + (1 if step % 2 == 0 else 0)
        table[2 + step] = jnp.where(step < count, entry, 0)
    store = pltpu.make_async_copy(table, table_hbm, sem.at[2 * EXPORTS])
    store.start()
    for copy in copies:
        copy.wait()
    store.wait()


def prepare(slot_nodes, ancestors, depth, keys, values):
    nodes = keys.shape[0] // NODE_TOK
    slots = slot_nodes.shape[0]
    hbm = pl.BlockSpec(memory_space=pl.ANY)
    return pl.pallas_call(
        functools.partial(prepare_body, nodes),
        out_shape=(
            jax.ShapeDtypeStruct((2 * EXPORTS, NODE_TOK, keys.shape[1]), keys.dtype),
            jax.ShapeDtypeStruct((2 + CHAIN,), jnp.int32),
        ),
        in_specs=[hbm] * 5,
        out_specs=(hbm, hbm),
        scratch_shapes=[
            pltpu.SMEM((slots,), jnp.int32),
            pltpu.SMEM((A_MAX, slots), jnp.int32),
            pltpu.SMEM((slots,), jnp.int32),
            pltpu.SMEM((2 + CHAIN,), jnp.int32),
            pltpu.SMEM((slots,), jnp.int32),
            pltpu.SMEM((slots,), jnp.int32),
            pltpu.SMEM((slots // nodes,), jnp.int32),
            pltpu.SemaphoreType.DMA((2 * EXPORTS + 4,)),
        ],
        name="prepare",
    )(slot_nodes, ancestors.T, depth, keys, values)


def attend_body(parts, per_part, table, *refs):
    query, own_key, own_value, root_key, root_value = refs[:5]
    chain_keys = refs[5 : 5 + CHAIN]
    chain_values = refs[5 + CHAIN : 5 + 2 * CHAIN]
    out, all_keys, all_values, bias = refs[-4:]
    node = pl.program_id(0)
    group = query.shape[1] // HEAD
    above = CHAIN * NODE_TOK
    root_rows = pl.ds(above, NODE_TOK)
    own_rows = pl.ds(above + NODE_TOK, NODE_TOK)

    @pl.when(node == 0)
    def _():
        all_values[:, HEAD:] = jnp.ones_like(all_values[:, HEAD:])
        for step in range(CHAIN):
            rows = pl.ds(step * NODE_TOK, NODE_TOK)
            all_keys[rows, :] = chain_keys[step][0]
            all_values[rows, :HEAD] = chain_values[step][0]
            bias[:, step * NODE_TOK : (step + 1) * NODE_TOK] = jnp.full(
                (8, NODE_TOK), jnp.where(step < table[1], 0.0, DEAD), jnp.float32
            )
        all_keys[root_rows, :] = root_key[...]
        all_values[root_rows, :HEAD] = root_value[...]

    all_keys[own_rows, :] = own_key[...]
    all_values[own_rows, :HEAD] = own_value[...]
    root_bias = jnp.where(node == table[0], DEAD, 0.0)
    query_index = lax.broadcasted_iota(jnp.int32, (NODE_TOK, NODE_TOK), 0)
    key_index = lax.broadcasted_iota(jnp.int32, (NODE_TOK, NODE_TOK), 1)
    own_bias = jnp.where(key_index <= query_index, 0.0, DEAD)
    piece = math.gcd(NODE_TOK, per_part)
    pieces_part = per_part // piece
    me = lax.axis_index("tensor")
    contract = (((1,), (1,)), ((), ()))
    stacked = jnp.concatenate([query[:, h * HEAD : (h + 1) * HEAD] for h in range(group)], 0)
    scores = lax.dot_general(
        stacked, all_keys[...], contract, preferred_element_type=jnp.float32
    )
    chain = scores[:, :above] + bias[0:1, :]
    root = scores[:, above : above + NODE_TOK] + root_bias
    own = scores[:, above + NODE_TOK :] + jnp.concatenate([own_bias] * group, 0)
    masked = jnp.concatenate([chain, root, own], 1)
    largest = jnp.max(masked, axis=1, keepdims=True)
    expo = jnp.exp2((masked - largest) * SCALE).astype(jnp.bfloat16)
    mixed = jnp.dot(expo, all_values[...], preferred_element_type=jnp.float32)
    result = (mixed[:, :HEAD] / mixed[:, HEAD:]).astype(jnp.bfloat16)
    for h in range(group):
        for part in range(NODE_TOK // piece):
            block = node * (NODE_TOK // piece) + part
            target = slot_position(parts, (block // pieces_part) ^ me)
            first = h * NODE_TOK + part * piece
            rows = pl.ds(pl.multiple_of((block % pieces_part) * piece, piece), piece)
            out[target, rows, h * HEAD : (h + 1) * HEAD] = result[first : first + piece]


def slot_position(parts, distance):
    half = parts // 2
    return jnp.where(distance % 2 == 1, distance // 2, half + distance // 2)


def attend(kv, table, queries, keys, values, got, parts, after):
    rows = queries.shape[0]
    width = queries.shape[1] // (keys.shape[1] // HEAD)
    nodes = rows // NODE_TOK
    total = (CHAIN + 2) * NODE_TOK
    own = pl.BlockSpec((NODE_TOK, HEAD), lambda node, table: (node, kv))
    root = pl.BlockSpec((NODE_TOK, HEAD), lambda node, table: (table[0], kv))

    def chain_spec(step, offset):
        return pl.BlockSpec(
            (1, NODE_TOK, HEAD), lambda node, table: (table[2 + step] + offset, 0, kv)
        )

    return pl.pallas_call(
        functools.partial(attend_body, parts, rows // parts),
        out_shape=jax.ShapeDtypeStruct((parts, rows // parts, width), queries.dtype),
        grid_spec=pltpu.PrefetchScalarGridSpec(
            num_scalar_prefetch=1,
            grid=(nodes,),
            in_specs=[
                pl.BlockSpec((NODE_TOK, width), lambda node, table: (node, kv)),
                own,
                own,
                root,
                root,
            ]
            + [chain_spec(step, 0) for step in range(CHAIN)]
            + [chain_spec(step, EXPORTS) for step in range(CHAIN)]
            + [pl.BlockSpec(memory_space=pl.ANY)] * len(after),
            out_specs=pl.BlockSpec(
                (parts, rows // parts, width), lambda node, table: (0, 0, 0)
            ),
            scratch_shapes=[
                pltpu.VMEM((total, HEAD), keys.dtype),
                pltpu.VMEM((total, 2 * HEAD), keys.dtype),
                pltpu.VMEM((8, CHAIN * NODE_TOK), jnp.float32),
            ],
        ),
        compiler_params=pltpu.CompilerParams(
            dimension_semantics=("arbitrary",), vmem_limit_bytes=VMEM_LIMIT
        ),
        cost_estimate=LIGHT,
        name="attend",
    )(table, queries, keys, values, keys, values, *([got] * (2 * CHAIN)), *after)


def swap(array, axis, distance):
    size = lax.axis_size(axis)
    return lax.ppermute(array, axis, [(i, i ^ distance) for i in range(size)])


def times(rows, weight):
    return lax.dot_general(
        rows, weight, (((1,), (1,)), ((), ())), preferred_element_type=jnp.float32
    )


def is_middle(index):
    return (index == 1) | (index == 2)


def product(rows, weight, outs):
    half = rows[0].shape[0] // 2
    for order, pair in enumerate(outs):
        width = pair[0].shape[1]
        features = slice(order * width, (order + 1) * width)
        for out, start in zip(pair, (0, half)):
            total, first = None, 0
            for part in rows:
                depth = part.shape[1]
                term = times(part[start : start + half, :], weight[features, first : first + depth])
                total = term if total is None else total + term
                first += depth
            out[...] = total.astype(out.dtype)


def core_sums(pairs, upper):
    half = pairs[0][0].shape[0] // 2
    rows = slice(half, 2 * half) if upper else slice(0, half)
    return jnp.concatenate(
        [k[rows, :].astype(jnp.float32) + c[rows, :].astype(jnp.float32) for k, c in pairs], 1
    )


def step_body(row_count, pairs, width, core_count, chip_count, outputs, *refs):
    refs = list(refs)
    outs = refs[len(refs) - outputs :]
    rows = [refs.pop(0) for _ in range(row_count)]
    middle = is_middle(lax.axis_index("node"))
    for paired in pairs:
        choice = [refs.pop(0) for _ in range(2 if paired else 1)]
        mine = [(outs.pop(0), outs.pop(0)) for _ in range(choice[0].shape[0] // width)]
        if paired:
            pl.when(middle)(functools.partial(product, rows, choice[0], mine))
            pl.when(jnp.logical_not(middle))(functools.partial(product, rows, choice[1], mine))
        else:
            product(rows, choice[0], mine)
    if core_count:
        items = [(refs.pop(0), refs.pop(0)) for _ in range(core_count)]
        out = outs.pop(0)
        out[...] = core_sums(items, True).astype(out.dtype)
    if chip_count:
        items = [(refs.pop(0), refs.pop(0)) for _ in range(chip_count)]
        from_chip, out = refs.pop(0), outs.pop(0)
        out[...] = (core_sums(items, False) + from_chip[...].astype(jnp.float32)).astype(out.dtype)


def step(rows=(), weights=(), cores=(), chips=(), after=(), width=0):
    pairs = [isinstance(weight, tuple) for weight in weights]
    flat = [w for weight in weights for w in (weight if isinstance(weight, tuple) else (weight,))]
    shapes = []
    for weight in weights:
        features = (weight[0] if isinstance(weight, tuple) else weight).shape[0]
        shapes += [(rows[0].shape[0] // 2, width)] * (2 * (features // width))
    for items in (cores, chips[:-1]):
        if items:
            features = sum(kept.shape[1] for kept, _ in items)
            shapes.append((items[0][0].shape[0] // 2, features))
    read = [*rows, *flat, *[x for item in (*cores, *chips[:-1]) for x in item], *chips[-1:]]
    return pl.pallas_call(
        functools.partial(
            step_body, len(rows), pairs, width, len(cores), len(chips[:-1]), len(shapes)
        ),
        out_shape=[jax.ShapeDtypeStruct(shape, read[0].dtype) for shape in shapes],
        in_specs=[pl.BlockSpec(memory_space=pltpu.VMEM)] * len(read)
        + [pl.BlockSpec(memory_space=pl.ANY)] * len(after),
        compiler_params=pltpu.CompilerParams(vmem_limit_bytes=VMEM_LIMIT),
        cost_estimate=LIGHT,
        name="step",
    )(*read, *after)


def relay(piece, exported):
    pairs = [(0, 1), (1, 0), (2, 3), (3, 2)]
    middle = [(1, 2), (2, 1)]
    outward = [(1, 0), (2, 3)]
    near = lax.ppermute(piece, "node", pairs)
    across = lax.ppermute(piece, "node", middle)
    near, across, exported = lax.optimization_barrier((near, across, exported))
    across_out = lax.ppermute(across, "node", outward)
    near_across = lax.ppermute(near, "node", middle)
    far_out = lax.ppermute(near_across, "node", outward)
    return exported, (near, (near_across, across_out), (across, far_out))


def place_body(spots, features, *refs):
    out = refs[-1]
    half = features // 2
    device = lax.axis_index("node")
    mine = lax.axis_index("groups")
    last = (core_sums([refs[:2]], False) + refs[2][...].astype(jnp.float32)).astype(out.dtype)
    for source, parts in zip((last, *refs[3:-1]), spots):
        start = 0
        for size, distance, side in parts:
            group = {"own": mine, "other": 1 - mine, "all": 0}[side]
            column = pl.multiple_of((device ^ distance) * features + group * half, HEAD)
            out[:, pl.ds(column, size)] = source[:, start : start + size]
            start += size


def place(last, sources, spots, devices, features):
    return pl.pallas_call(
        functools.partial(place_body, spots, features),
        out_shape=jax.ShapeDtypeStruct((last[2].shape[0], devices * features), last[2].dtype),
        compiler_params=pltpu.CompilerParams(vmem_limit_bytes=VMEM_LIMIT),
        name="place",
    )(*last, *sources)


def split_weight(out_weight, exported):
    half = out_weight.shape[0] // 2
    first = lax.axis_index("groups") * half
    return relay(lax.dynamic_slice_in_dim(out_weight, first, half, 0), exported)


def project_split(halves, relayed, out_weight):
    features = out_weight.shape[0]
    half = features // 2
    rows = [part.reshape(-1, part.shape[-1]) for part in halves]
    other = [swap(part, "groups", 1) for part in rows]
    near, second, far = relayed

    def core(sent):
        return swap(sent, "tensor", 1)

    def chip(away):
        return swap(away, "tensor", 2)

    def multiply(rows, weights, after=(), cores=()):
        return step(rows, weights, cores=cores, after=after, width=half)

    sent_a, kept_a, sent_b, kept_b = multiply(rows, [out_weight])
    sent_1, kept_1 = multiply(rows, [near], [sent_b, other[0]])
    first = [(kept_a, core(sent_a)), (kept_b, core(sent_b)), (kept_1, core(sent_1))]
    (away,) = step(cores=first, after=second)
    first.append(chip(away))
    sent_2, kept_2 = multiply(rows, [second], [sent_1])
    sent_3, kept_3, sent_4, kept_4 = multiply(other, [near, second], [sent_2])
    then = [(kept_2, core(sent_2)), (kept_3, core(sent_3)), (kept_4, core(sent_4))]
    away, first_done = step(cores=then, chips=first)
    then.append(chip(away))
    sent_5, kept_5 = multiply(other, [far], [away])
    last_other = [(kept_5, core(sent_5))]
    sent_6, kept_6, away = multiply(rows, [far], (), last_other)
    last_other.append(chip(away))
    last = [(kept_6, core(sent_6))]
    away, then_done = step(cores=last, chips=then)
    last.append(chip(away))
    then_other = swap(then_done[:, half:], "groups", 1)
    (last_done,) = step(chips=last_other)
    last_other = swap(last_done, "groups", 1)
    return place(
        (*last[0], last[1]),
        (first_done, then_done, then_other, last_other),
        (
            ((half, 3, "own"),),
            ((features, 0, "all"), (half, 1, "own")),
            ((half, 2, "own"),),
            ((half, 1, "other"), (half, 2, "other")),
            ((half, 3, "other"),),
        ),
        lax.axis_size("node"),
        features,
    )


def project_plain(halves, out_weight):
    attended = jnp.concatenate(halves, 2)
    parts, per_part, width = attended.shape
    me = lax.axis_index("tensor")
    order = slot_position(parts, jnp.arange(parts, dtype=jnp.int32) ^ me)
    rows = attended[order].reshape(parts * per_part, width)
    weight = lax.all_gather(out_weight, "node", axis=0, tiled=True)
    terms = times(rows, weight).astype(jnp.bfloat16)
    return lax.psum_scatter(terms, "tensor", scatter_dimension=0, tiled=True)


def local(queries, keys, values, out_weight, slot_nodes, ancestors, depth):
    parts = lax.axis_size("tensor")
    devices = lax.axis_size("node")
    features = out_weight.shape[0]
    kv_count = keys.shape[1] // HEAD
    relayed, after = None, []
    exported, table = prepare(slot_nodes, ancestors, depth, keys, values)
    got = lax.all_gather(exported, "node", axis=0, tiled=True)
    if (
        devices == 4
        and parts == 4
        and lax.axis_size("groups") == 2
        and features % (2 * HEAD) == 0
    ):
        _, relayed = split_weight(out_weight, exported)
        after = [relayed[0], relayed[2][0]]
    halves = []
    for kv in range(kv_count):
        halves.append(attend(kv, table, queries, keys, values, got, parts, after))
        after = halves[-1:]
    if relayed is None:
        return project_plain(halves, out_weight)
    return project_split(halves, relayed, out_weight)


def solution(mesh):
    placed = (
        P(("groups", "node"), "tensor"),
        P(("groups", "node"), "tensor"),
        P(("groups", "node"), "tensor"),
        P("node", "tensor"),
        P("groups"),
        P("groups", None),
        P("groups"),
    )
    return jax.shard_map(
        local,
        mesh=mesh,
        in_specs=placed,
        out_specs=P(("groups", "node", "tensor"), None),
        check_vma=False,
    )
```

```python
import functools
import math

import jax
import jax.numpy as jnp
from jax import lax
from jax.experimental import pallas as pl
from jax.experimental.pallas import tpu as pltpu
from jax.sharding import PartitionSpec as P

HEAD = 128
NODE_TOK = 128
A_MAX = 7
CHAIN = A_MAX - 1
EXPORTS = 2
SCALE = math.log2(math.e) / math.sqrt(HEAD)
DEAD = -1e30
LIGHT = pl.CostEstimate(flops=1, bytes_accessed=1, transcendentals=0)
VMEM_LIMIT = 20 * 1024 * 1024


def prepare_body(nodes, *refs):
    slot_hbm, ancestors_hbm, depth_hbm, keys, values, exported, table_hbm = refs[:7]
    slot_nodes, ancestors, depth, table, holder, within, roots, sem = refs[7:]
    devices = slot_nodes.shape[0] // nodes
    me = lax.axis_index("node")
    fetches = [
        pltpu.make_async_copy(source, target, sem.at[2 * EXPORTS + 1 + order])
        for order, (source, target) in enumerate(
            ((slot_hbm, slot_nodes), (ancestors_hbm, ancestors), (depth_hbm, depth))
        )
    ]
    for fetch in fetches:
        fetch.start()
    for fetch in fetches:
        fetch.wait()

    def place(device, mine):
        root, root_index = jnp.int32(0), jnp.int32(0)
        for index in range(nodes):
            node = slot_nodes[device * nodes + index]
            holder[node] = device
            within[node] = index
            even = (depth[node] & 1) == 0
            root = jnp.where(even, node, root)
            root_index = jnp.where(even, index, root_index)
        roots[device] = root
        return jnp.where(device == me, root_index, mine)

    root = lax.fori_loop(0, devices, place, jnp.int32(0))

    def find_attach(device, attach):
        node = roots[device]
        level = depth[node]
        for step in range(0, CHAIN, 2):
            above = jnp.maximum(ancestors[step, node], 0)
            hit = (step < level) & (holder[above] == me)
            attach = jnp.where(hit, within[above], attach)
        return attach

    attach = lax.fori_loop(0, devices, find_attach, jnp.int32(0))
    copies = []
    for position, (source, index) in enumerate(
        ((keys, root), (keys, attach), (values, root), (values, attach))
    ):
        rows = pl.ds(pl.multiple_of(index * NODE_TOK, NODE_TOK), NODE_TOK)
        copies.append(
            pltpu.make_async_copy(source.at[rows, :], exported.at[position], sem.at[position])
        )
    for copy in copies:
        copy.start()
    root_node = roots[me]
    count = depth[root_node]
    table[0] = root
    table[1] = count
    for step in range(CHAIN):
        above = jnp.maximum(ancestors[step, root_node], 0)
        entry = holder[above] * (2 * EXPORTS) + (1 if step % 2 == 0 else 0)
        table[2 + step] = jnp.where(step < count, entry, 0)
    store = pltpu.make_async_copy(table, table_hbm, sem.at[2 * EXPORTS])
    store.start()
    for copy in copies:
        copy.wait()
    store.wait()


def prepare(slot_nodes, ancestors, depth, keys, values):
    nodes = keys.shape[0] // NODE_TOK
    slots = slot_nodes.shape[0]
    hbm = pl.BlockSpec(memory_space=pltpu.HBM)
    return pl.pallas_call(
        functools.partial(prepare_body, nodes),
        out_shape=(
            jax.ShapeDtypeStruct((2 * EXPORTS, NODE_TOK, keys.shape[1]), keys.dtype),
            jax.ShapeDtypeStruct((2 + CHAIN,), jnp.int32),
        ),
        in_specs=[hbm] * 5,
        out_specs=(hbm, hbm),
        scratch_shapes=[
            pltpu.SMEM((slots,), jnp.int32),
            pltpu.SMEM((A_MAX, slots), jnp.int32),
            pltpu.SMEM((slots,), jnp.int32),
            pltpu.SMEM((2 + CHAIN,), jnp.int32),
            pltpu.SMEM((slots,), jnp.int32),
            pltpu.SMEM((slots,), jnp.int32),
            pltpu.SMEM((slots // nodes,), jnp.int32),
            pltpu.SemaphoreType.DMA((2 * EXPORTS + 4,)),
        ],
        name="prepare",
    )(slot_nodes, ancestors.T, depth, keys, values)


def attend_body(kv, parts, table, query_hbm, keys_hbm, values_hbm, got, *refs):
    out, query, keys, values, all_keys, all_values, bias, query_sem, sem = refs[-9:]
    nodes = query.shape[0] // NODE_TOK
    group = query.shape[1] // HEAD
    per_part = query.shape[0] // parts
    above = CHAIN * NODE_TOK
    lanes = pl.ds(kv * HEAD, HEAD)
    root_rows = pl.ds(above, NODE_TOK)
    own_rows = pl.ds(above + NODE_TOK, NODE_TOK)
    root = pl.ds(pl.multiple_of(table[0] * NODE_TOK, NODE_TOK), NODE_TOK)

    def node_rows(node):
        return pl.ds(pl.multiple_of(node * NODE_TOK, NODE_TOK), NODE_TOK)

    def fetch_query(node):
        return pltpu.make_async_copy(
            query_hbm.at[node_rows(node), pl.ds(kv * group * HEAD, group * HEAD)],
            query.at[node_rows(node), :],
            query_sem.at[node],
        )

    pairs = [
        (keys_hbm.at[root, lanes], all_keys.at[root_rows, :]),
        (values_hbm.at[root, lanes], all_values.at[root_rows, pl.ds(0, HEAD)]),
        (keys_hbm.at[:, lanes], keys),
        (values_hbm.at[:, lanes], values),
    ]
    for step in range(CHAIN):
        rows = pl.ds(step * NODE_TOK, NODE_TOK)
        entry = table[2 + step]
        pairs.append((got.at[entry, :, lanes], all_keys.at[rows, :]))
        pairs.append((got.at[entry + EXPORTS, :, lanes], all_values.at[rows, pl.ds(0, HEAD)]))
    copies = [
        pltpu.make_async_copy(source, target, sem.at[order])
        for order, (source, target) in enumerate(pairs)
    ]
    for copy in copies:
        copy.start()
    for node in range(nodes):
        fetch_query(node).start()
    all_values[:, HEAD:] = jnp.ones_like(all_values[:, HEAD:])
    for step in range(CHAIN):
        bias[:, step * NODE_TOK : (step + 1) * NODE_TOK] = jnp.full(
            (8, NODE_TOK), jnp.where(step < table[1], 0.0, DEAD), jnp.float32
        )
    query_index = lax.broadcasted_iota(jnp.int32, (NODE_TOK, NODE_TOK), 0)
    key_index = lax.broadcasted_iota(jnp.int32, (NODE_TOK, NODE_TOK), 1)
    own_bias = jnp.where(key_index <= query_index, 0.0, DEAD)
    piece = math.gcd(NODE_TOK, per_part)
    pieces_part = per_part // piece
    me = lax.axis_index("tensor")
    for copy in copies:
        copy.wait()

    def one_node(node, carry):
        fetch_query(node).wait()
        rows = node_rows(node)
        all_keys[own_rows, :] = keys[rows, :]
        all_values[own_rows, :HEAD] = values[rows, :]
        root_bias = jnp.where(node == table[0], DEAD, 0.0)
        stacked = jnp.concatenate(
            [query[rows, h * HEAD : (h + 1) * HEAD] for h in range(group)], 0
        )
        scores = times(stacked, all_keys[...])
        chain = scores[:, :above] + bias[0:1, :]
        root = scores[:, above : above + NODE_TOK] + root_bias
        own = scores[:, above + NODE_TOK :] + jnp.concatenate([own_bias] * group, 0)
        masked = jnp.concatenate([chain, root, own], 1)
        largest = jnp.max(masked, axis=1, keepdims=True)
        expo = jnp.exp2((masked - largest) * SCALE).astype(jnp.bfloat16)
        mixed = jnp.dot(expo, all_values[...], preferred_element_type=jnp.float32)
        result = (mixed[:, :HEAD] / mixed[:, HEAD:]).astype(jnp.bfloat16)
        for part in range(NODE_TOK // piece):
            block = node * (NODE_TOK // piece) + part
            owner = block // pieces_part
            target = slot_position(parts, owner ^ me)
            inner = (block - owner * pieces_part) * piece
            to = pl.ds(pl.multiple_of(inner, piece), piece)
            for h in range(group):
                first = h * NODE_TOK + part * piece
                out[target, to, h * HEAD : (h + 1) * HEAD] = result[first : first + piece]
        return carry

    lax.fori_loop(0, nodes, one_node, 0)


def slot_position(parts, distance):
    half = parts // 2
    return jnp.where(distance % 2 == 1, distance // 2, half + distance // 2)


def attend(kv, table, queries, keys, values, got, parts, after):
    rows = queries.shape[0]
    width = queries.shape[1] // (keys.shape[1] // HEAD)
    nodes = rows // NODE_TOK
    total = (CHAIN + 2) * NODE_TOK
    hbm = pl.BlockSpec(memory_space=pltpu.HBM)
    return pl.pallas_call(
        functools.partial(attend_body, kv, parts),
        out_shape=jax.ShapeDtypeStruct((parts, rows // parts, width), queries.dtype),
        in_specs=[pl.BlockSpec(memory_space=pltpu.SMEM)]
        + [hbm] * 4
        + [pl.BlockSpec(memory_space=pl.ANY)] * len(after),
        scratch_shapes=[
            pltpu.VMEM((rows, width), queries.dtype),
            pltpu.VMEM((rows, HEAD), keys.dtype),
            pltpu.VMEM((rows, HEAD), keys.dtype),
            pltpu.VMEM((total, HEAD), keys.dtype),
            pltpu.VMEM((total, 2 * HEAD), keys.dtype),
            pltpu.VMEM((8, CHAIN * NODE_TOK), jnp.float32),
            pltpu.SemaphoreType.DMA((nodes,)),
            pltpu.SemaphoreType.DMA((4 + 2 * CHAIN,)),
        ],
        compiler_params=pltpu.CompilerParams(vmem_limit_bytes=VMEM_LIMIT),
        cost_estimate=LIGHT,
        name="attend",
    )(table, queries, keys, values, got, *after)


def swap(array, axis, distance):
    size = lax.axis_size(axis)
    return lax.ppermute(array, axis, [(i, i ^ distance) for i in range(size)])


def times(rows, weight):
    return lax.dot_general(
        rows, weight, (((1,), (1,)), ((), ())), preferred_element_type=jnp.float32
    )


def is_middle(index):
    return (index == 1) | (index == 2)


def product(rows, weight, outs):
    half = rows[0].shape[0] // 2
    for order, pair in enumerate(outs):
        width = pair[0].shape[1]
        features = slice(order * width, (order + 1) * width)
        for out, start in zip(pair, (0, half)):
            total, first = None, 0
            for part in rows:
                depth = part.shape[1]
                term = times(part[start : start + half, :], weight[features, first : first + depth])
                total = term if total is None else total + term
                first += depth
            out[...] = total.astype(out.dtype)


def core_sums(pairs, upper):
    half = pairs[0][0].shape[0] // 2
    rows = slice(half, 2 * half) if upper else slice(0, half)
    return jnp.concatenate(
        [k[rows, :].astype(jnp.float32) + c[rows, :].astype(jnp.float32) for k, c in pairs], 1
    )


def step_body(row_count, pairs, width, core_count, chip_count, outputs, *refs):
    refs = list(refs)
    outs = refs[len(refs) - outputs :]
    rows = [refs.pop(0) for _ in range(row_count)]
    middle = is_middle(lax.axis_index("node"))
    for paired in pairs:
        choice = [refs.pop(0) for _ in range(2 if paired else 1)]
        mine = [(outs.pop(0), outs.pop(0)) for _ in range(choice[0].shape[0] // width)]
        if paired:
            pl.when(middle)(functools.partial(product, rows, choice[0], mine))
            pl.when(jnp.logical_not(middle))(functools.partial(product, rows, choice[1], mine))
        else:
            product(rows, choice[0], mine)
    if core_count:
        items = [(refs.pop(0), refs.pop(0)) for _ in range(core_count)]
        out = outs.pop(0)
        out[...] = core_sums(items, True).astype(out.dtype)
    if chip_count:
        items = [(refs.pop(0), refs.pop(0)) for _ in range(chip_count)]
        from_chip, out = refs.pop(0), outs.pop(0)
        out[...] = (core_sums(items, False) + from_chip[...].astype(jnp.float32)).astype(out.dtype)


def step(rows=(), weights=(), cores=(), chips=(), after=(), width=0):
    pairs = [isinstance(weight, tuple) for weight in weights]
    flat = [w for weight in weights for w in (weight if isinstance(weight, tuple) else (weight,))]
    shapes = []
    for weight in weights:
        features = (weight[0] if isinstance(weight, tuple) else weight).shape[0]
        shapes += [(rows[0].shape[0] // 2, width)] * (2 * (features // width))
    for items in (cores, chips[:-1]):
        if items:
            features = sum(kept.shape[1] for kept, _ in items)
            shapes.append((items[0][0].shape[0] // 2, features))
    read = [*rows, *flat, *[x for item in (*cores, *chips[:-1]) for x in item], *chips[-1:]]
    return pl.pallas_call(
        functools.partial(
            step_body, len(rows), pairs, width, len(cores), len(chips[:-1]), len(shapes)
        ),
        out_shape=[jax.ShapeDtypeStruct(shape, read[0].dtype) for shape in shapes],
        in_specs=[pl.BlockSpec(memory_space=pltpu.VMEM)] * len(read)
        + [pl.BlockSpec(memory_space=pl.ANY)] * len(after),
        compiler_params=pltpu.CompilerParams(vmem_limit_bytes=VMEM_LIMIT),
        cost_estimate=LIGHT,
        name="step",
    )(*read, *after)


def relay(piece, exported):
    pairs = [(0, 1), (1, 0), (2, 3), (3, 2)]
    middle = [(1, 2), (2, 1)]
    outward = [(1, 0), (2, 3)]
    near = lax.ppermute(piece, "node", pairs)
    across = lax.ppermute(piece, "node", middle)
    near, across, exported = lax.optimization_barrier((near, across, exported))
    across_out = lax.ppermute(across, "node", outward)
    near_across = lax.ppermute(near, "node", middle)
    far_out = lax.ppermute(near_across, "node", outward)
    return exported, (near, (near_across, across_out), (across, far_out))


def place_body(spots, features, *refs):
    out = refs[-1]
    half = features // 2
    device = lax.axis_index("node")
    mine = lax.axis_index("groups")
    last = (core_sums([refs[:2]], False) + refs[2][...].astype(jnp.float32)).astype(out.dtype)
    for source, parts in zip((last, *refs[3:-1]), spots):
        start = 0
        for size, distance, side in parts:
            group = {"own": mine, "other": 1 - mine, "all": 0}[side]
            column = pl.multiple_of((device ^ distance) * features + group * half, HEAD)
            out[:, pl.ds(column, size)] = source[:, start : start + size]
            start += size


def place(last, sources, spots, devices, features):
    return pl.pallas_call(
        functools.partial(place_body, spots, features),
        out_shape=jax.ShapeDtypeStruct((last[2].shape[0], devices * features), last[2].dtype),
        compiler_params=pltpu.CompilerParams(vmem_limit_bytes=VMEM_LIMIT),
        name="place",
    )(*last, *sources)


def split_weight(out_weight, exported):
    half = out_weight.shape[0] // 2
    first = lax.axis_index("groups") * half
    return relay(lax.dynamic_slice_in_dim(out_weight, first, half, 0), exported)


def project_split(halves, relayed, out_weight):
    features = out_weight.shape[0]
    half = features // 2
    rows = [part.reshape(-1, part.shape[-1]) for part in halves]
    other = [swap(part, "groups", 1) for part in rows]
    near, second, far = relayed

    def core(sent):
        return swap(sent, "tensor", 1)

    def chip(away):
        return swap(away, "tensor", 2)

    def multiply(rows, weights, after=(), cores=()):
        return step(rows, weights, cores=cores, after=after, width=half)

    sent_a, kept_a, sent_b, kept_b = multiply(rows, [out_weight])
    sent_1, kept_1 = multiply(rows, [near], [sent_b, other[0]])
    first = [(kept_a, core(sent_a)), (kept_b, core(sent_b)), (kept_1, core(sent_1))]
    (away,) = step(cores=first, after=second)
    first.append(chip(away))
    sent_2, kept_2 = multiply(rows, [second], [sent_1])
    sent_3, kept_3, sent_4, kept_4 = multiply(other, [near, second], [sent_2])
    then = [(kept_2, core(sent_2)), (kept_3, core(sent_3)), (kept_4, core(sent_4))]
    away, first_done = step(cores=then, chips=first)
    then.append(chip(away))
    sent_5, kept_5 = multiply(other, [far], [away])
    last_other = [(kept_5, core(sent_5))]
    sent_6, kept_6, away = multiply(rows, [far], (), last_other)
    last_other.append(chip(away))
    last = [(kept_6, core(sent_6))]
    away, then_done = step(cores=last, chips=then)
    last.append(chip(away))
    then_other = swap(then_done[:, half:], "groups", 1)
    (last_done,) = step(chips=last_other)
    last_other = swap(last_done, "groups", 1)
    return place(
        (*last[0], last[1]),
        (first_done, then_done, then_other, last_other),
        (
            ((half, 3, "own"),),
            ((features, 0, "all"), (half, 1, "own")),
            ((half, 2, "own"),),
            ((half, 1, "other"), (half, 2, "other")),
            ((half, 3, "other"),),
        ),
        lax.axis_size("node"),
        features,
    )


def project_plain(halves, out_weight):
    attended = jnp.concatenate(halves, 2)
    parts, per_part, width = attended.shape
    me = lax.axis_index("tensor")
    order = slot_position(parts, jnp.arange(parts, dtype=jnp.int32) ^ me)
    rows = attended[order].reshape(parts * per_part, width)
    weight = lax.all_gather(out_weight, "node", axis=0, tiled=True)
    terms = times(rows, weight).astype(jnp.bfloat16)
    return lax.psum_scatter(terms, "tensor", scatter_dimension=0, tiled=True)


def local(queries, keys, values, out_weight, slot_nodes, ancestors, depth):
    parts = lax.axis_size("tensor")
    devices = lax.axis_size("node")
    features = out_weight.shape[0]
    kv_count = keys.shape[1] // HEAD
    relayed, after = None, []
    exported, table = prepare(slot_nodes, ancestors, depth, keys, values)
    got = lax.all_gather(exported, "node", axis=0, tiled=True)
    if (
        devices == 4
        and parts == 4
        and lax.axis_size("groups") == 2
        and features % (2 * HEAD) == 0
    ):
        _, relayed = split_weight(out_weight, exported)
        after = [relayed[0], relayed[2][0]]
    halves = []
    for kv in range(kv_count):
        halves.append(attend(kv, table, queries, keys, values, got, parts, after))
        after = halves[-1:]
    if relayed is None:
        return project_plain(halves, out_weight)
    return project_split(halves, relayed, out_weight)


def solution(mesh):
    placed = (
        P(("groups", "node"), "tensor"),
        P(("groups", "node"), "tensor"),
        P(("groups", "node"), "tensor"),
        P("node", "tensor"),
        P("groups"),
        P("groups", None),
        P("groups"),
    )
    return jax.shard_map(
        local,
        mesh=mesh,
        in_specs=placed,
        out_specs=P(("groups", "node", "tensor"), None),
        check_vma=False,
    )
```

```python
import functools
import math

import jax
import jax.numpy as jnp
from jax import lax
from jax.experimental import pallas as pl
from jax.experimental.pallas import tpu as pltpu
from jax.sharding import PartitionSpec as P

HEAD = 128
NODE_TOK = 128
A_MAX = 7
CHAIN = A_MAX - 1
EXPORTS = 2
SCALE = math.log2(math.e) / math.sqrt(HEAD)
DEAD = -1e30
LIGHT = pl.CostEstimate(flops=1, bytes_accessed=1, transcendentals=0)
VMEM_LIMIT = 20 * 1024 * 1024


def prepare_body(nodes, *refs):
    slot_hbm, ancestors_hbm, depth_hbm, queries, keys, values = refs[:6]
    exported, table_hbm, *held = refs[6:11]
    slot_nodes, ancestors, depth, table, holder, within, roots, sem, held_sem = refs[11:]
    devices = slot_nodes.shape[0] // nodes
    me = lax.axis_index("node")
    fetches = [
        pltpu.make_async_copy(source, target, sem.at[2 * EXPORTS + 1 + order])
        for order, (source, target) in enumerate(
            ((slot_hbm, slot_nodes), (ancestors_hbm, ancestors), (depth_hbm, depth))
        )
    ]
    holds = [
        pltpu.make_async_copy(source, target, held_sem.at[order])
        for order, (source, target) in enumerate(zip((queries, keys, values), held))
    ]
    for fetch in (*fetches, *holds):
        fetch.start()
    for fetch in fetches:
        fetch.wait()

    def place(device, mine):
        root, root_index = jnp.int32(0), jnp.int32(0)
        for index in range(nodes):
            node = slot_nodes[device * nodes + index]
            holder[node] = device
            within[node] = index
            even = (depth[node] & 1) == 0
            root = jnp.where(even, node, root)
            root_index = jnp.where(even, index, root_index)
        roots[device] = root
        return jnp.where(device == me, root_index, mine)

    root = lax.fori_loop(0, devices, place, jnp.int32(0))

    def find_attach(device, attach):
        node = roots[device]
        level = depth[node]
        for step in range(0, CHAIN, 2):
            above = jnp.maximum(ancestors[step, node], 0)
            hit = (step < level) & (holder[above] == me)
            attach = jnp.where(hit, within[above], attach)
        return attach

    attach = lax.fori_loop(0, devices, find_attach, jnp.int32(0))
    copies = []
    for position, (source, index) in enumerate(
        ((keys, root), (keys, attach), (values, root), (values, attach))
    ):
        rows = pl.ds(pl.multiple_of(index * NODE_TOK, NODE_TOK), NODE_TOK)
        copies.append(
            pltpu.make_async_copy(source.at[rows, :], exported.at[position], sem.at[position])
        )
    for copy in copies:
        copy.start()
    root_node = roots[me]
    count = depth[root_node]
    table[0] = root
    table[1] = count
    for step in range(CHAIN):
        above = jnp.maximum(ancestors[step, root_node], 0)
        entry = holder[above] * (2 * EXPORTS) + (1 if step % 2 == 0 else 0)
        table[2 + step] = jnp.where(step < count, entry, 0)
    store = pltpu.make_async_copy(table, table_hbm, sem.at[2 * EXPORTS])
    store.start()
    for copy in (*copies, *holds, store):
        copy.wait()


def prepare(slot_nodes, ancestors, depth, queries, keys, values):
    nodes = keys.shape[0] // NODE_TOK
    slots = slot_nodes.shape[0]
    hbm = pl.BlockSpec(memory_space=pltpu.HBM)
    vmem = pl.BlockSpec(memory_space=pltpu.VMEM)
    return pl.pallas_call(
        functools.partial(prepare_body, nodes),
        out_shape=(
            jax.ShapeDtypeStruct((2 * EXPORTS, NODE_TOK, keys.shape[1]), keys.dtype),
            jax.ShapeDtypeStruct((2 + CHAIN,), jnp.int32),
            *[jax.ShapeDtypeStruct(x.shape, x.dtype) for x in (queries, keys, values)],
        ),
        in_specs=[hbm] * 6,
        out_specs=(hbm, hbm, vmem, vmem, vmem),
        scratch_shapes=[
            pltpu.SMEM((slots,), jnp.int32),
            pltpu.SMEM((A_MAX, slots), jnp.int32),
            pltpu.SMEM((slots,), jnp.int32),
            pltpu.SMEM((2 + CHAIN,), jnp.int32),
            pltpu.SMEM((slots,), jnp.int32),
            pltpu.SMEM((slots,), jnp.int32),
            pltpu.SMEM((slots // nodes,), jnp.int32),
            pltpu.SemaphoreType.DMA((2 * EXPORTS + 4,)),
            pltpu.SemaphoreType.DMA((3,)),
        ],
        compiler_params=pltpu.CompilerParams(vmem_limit_bytes=VMEM_LIMIT),
        name="prepare",
    )(slot_nodes, ancestors.T, depth, queries, keys, values)


def attend_body(kv, parts, table, query, keys, values, got, *refs):
    out, all_keys, all_values = refs[-3:]
    nodes = query.shape[0] // NODE_TOK
    group = query.shape[1] // keys.shape[1]
    per_part = query.shape[0] // parts
    lanes = pl.ds(kv * HEAD, HEAD)
    own_rows = pl.ds((CHAIN + 1) * NODE_TOK, NODE_TOK)
    ones = jnp.ones((NODE_TOK, HEAD), all_values.dtype)
    nothing = jnp.zeros((NODE_TOK, 2 * HEAD), all_values.dtype)
    query_index = lax.broadcasted_iota(jnp.int32, (NODE_TOK, NODE_TOK), 0)
    key_index = lax.broadcasted_iota(jnp.int32, (NODE_TOK, NODE_TOK), 1)
    own_bias = jnp.where(key_index <= query_index, 0.0, DEAD)
    piece = math.gcd(NODE_TOK, per_part)
    pieces_part = per_part // piece
    me = lax.axis_index("tensor")

    def node_rows(node):
        return pl.ds(pl.multiple_of(node * NODE_TOK, NODE_TOK), NODE_TOK)

    def put(order, key_block, value_block):
        rows = pl.ds(order * NODE_TOK, NODE_TOK)
        all_keys[rows, :] = key_block
        all_values[rows, :HEAD] = value_block
        all_values[rows, HEAD:] = ones

    def put_nothing(order, first_key):
        rows = pl.ds(order * NODE_TOK, NODE_TOK)
        all_keys[rows, :] = jnp.broadcast_to(first_key, (NODE_TOK, HEAD))
        all_values[rows, :] = nothing

    for step in range(CHAIN):
        entry = table[2 + step]
        put(step, got[entry, :, lanes], got[entry + EXPORTS, :, lanes])

    def one_node(node, carry):
        rows = node_rows(node)
        own_key = keys[rows, lanes]
        put(CHAIN + 1, own_key, values[rows, lanes])
        for step in range(CHAIN):
            pl.when(step >= table[1])(functools.partial(put_nothing, step, own_key[:1]))
        is_root = node == table[0]
        pl.when(is_root)(functools.partial(put_nothing, CHAIN, own_key[:1]))

        @pl.when(jnp.logical_not(is_root))
        def _():
            put(CHAIN, keys[node_rows(table[0]), lanes], values[node_rows(table[0]), lanes])

        first_head = kv * group
        stacked = jnp.concatenate(
            [query[rows, pl.ds((first_head + h) * HEAD, HEAD)] for h in range(group)], 0
        )
        scores = times(stacked, all_keys[...])
        above = (CHAIN + 1) * NODE_TOK
        own = scores[:, above:] + jnp.concatenate([own_bias] * group, 0)
        masked = jnp.concatenate([scores[:, :above], own], 1)
        largest = jnp.max(masked, axis=1, keepdims=True)
        expo = jnp.exp2((masked - largest) * SCALE).astype(jnp.bfloat16)
        mixed = jnp.dot(expo, all_values[...], preferred_element_type=jnp.float32)
        result = (mixed[:, :HEAD] / mixed[:, HEAD:]).astype(jnp.bfloat16)
        for part in range(NODE_TOK // piece):
            block = node * (NODE_TOK // piece) + part
            owner = block // pieces_part
            target = slot_position(parts, owner ^ me)
            inner = (block - owner * pieces_part) * piece
            to = pl.ds(pl.multiple_of(inner, piece), piece)
            for h in range(group):
                first = h * NODE_TOK + part * piece
                out[target, to, h * HEAD : (h + 1) * HEAD] = result[first : first + piece]
        return carry

    lax.fori_loop(0, nodes, one_node, 0)


def slot_position(parts, distance):
    half = parts // 2
    return jnp.where(distance % 2 == 1, distance // 2, half + distance // 2)


def attend(kv, table, queries, keys, values, got, parts, after):
    rows = queries.shape[0]
    width = queries.shape[1] // (keys.shape[1] // HEAD)
    total = (CHAIN + 2) * NODE_TOK
    return pl.pallas_call(
        functools.partial(attend_body, kv, parts),
        out_shape=jax.ShapeDtypeStruct((parts, rows // parts, width), queries.dtype),
        in_specs=[pl.BlockSpec(memory_space=pltpu.SMEM)]
        + [pl.BlockSpec(memory_space=pltpu.VMEM)] * 4
        + [pl.BlockSpec(memory_space=pl.ANY)] * len(after),
        scratch_shapes=[
            pltpu.VMEM((total, HEAD), keys.dtype),
            pltpu.VMEM((total, 2 * HEAD), keys.dtype),
        ],
        compiler_params=pltpu.CompilerParams(vmem_limit_bytes=VMEM_LIMIT),
        cost_estimate=LIGHT,
        name="attend",
    )(table, queries, keys, values, got, *after)


def swap(array, axis, distance):
    size = lax.axis_size(axis)
    return lax.ppermute(array, axis, [(i, i ^ distance) for i in range(size)])


def times(rows, weight):
    return lax.dot_general(
        rows, weight, (((1,), (1,)), ((), ())), preferred_element_type=jnp.float32
    )


def is_middle(index):
    return (index == 1) | (index == 2)


def product(rows, weight, outs):
    half = rows[0].shape[0] // 2
    for start in (0, half):
        whole = jnp.concatenate([part[start : start + half, :] for part in rows], 1)
        for order, pair in enumerate(outs):
            out = pair[start // half]
            width = out.shape[1]
            out[...] = times(whole, weight[order * width : (order + 1) * width, :]).astype(out.dtype)


def core_sums(pairs, upper):
    half = pairs[0][0].shape[0] // 2
    rows = slice(half, 2 * half) if upper else slice(0, half)
    return jnp.concatenate(
        [k[rows, :].astype(jnp.float32) + c[rows, :].astype(jnp.float32) for k, c in pairs], 1
    )


def step_body(row_count, pairs, width, core_count, chip_count, outputs, *refs):
    refs = list(refs)
    outs = refs[len(refs) - outputs :]
    rows = [refs.pop(0) for _ in range(row_count)]
    middle = is_middle(lax.axis_index("node"))
    for paired in pairs:
        choice = [refs.pop(0) for _ in range(2 if paired else 1)]
        mine = [(outs.pop(0), outs.pop(0)) for _ in range(choice[0].shape[0] // width)]
        if paired:
            pl.when(middle)(functools.partial(product, rows, choice[0], mine))
            pl.when(jnp.logical_not(middle))(functools.partial(product, rows, choice[1], mine))
        else:
            product(rows, choice[0], mine)
    if core_count:
        items = [(refs.pop(0), refs.pop(0)) for _ in range(core_count)]
        out = outs.pop(0)
        out[...] = core_sums(items, True).astype(out.dtype)
    if chip_count:
        items = [(refs.pop(0), refs.pop(0)) for _ in range(chip_count)]
        from_chip, out = refs.pop(0), outs.pop(0)
        out[...] = (core_sums(items, False) + from_chip[...].astype(jnp.float32)).astype(out.dtype)


def step(rows=(), weights=(), cores=(), chips=(), after=(), width=0):
    pairs = [isinstance(weight, tuple) for weight in weights]
    flat = [w for weight in weights for w in (weight if isinstance(weight, tuple) else (weight,))]
    shapes = []
    for weight in weights:
        features = (weight[0] if isinstance(weight, tuple) else weight).shape[0]
        shapes += [(rows[0].shape[0] // 2, width)] * (2 * (features // width))
    for items in (cores, chips[:-1]):
        if items:
            features = sum(kept.shape[1] for kept, _ in items)
            shapes.append((items[0][0].shape[0] // 2, features))
    read = [*rows, *flat, *[x for item in (*cores, *chips[:-1]) for x in item], *chips[-1:]]
    return pl.pallas_call(
        functools.partial(
            step_body, len(rows), pairs, width, len(cores), len(chips[:-1]), len(shapes)
        ),
        out_shape=[jax.ShapeDtypeStruct(shape, read[0].dtype) for shape in shapes],
        in_specs=[pl.BlockSpec(memory_space=pltpu.VMEM)] * len(read)
        + [pl.BlockSpec(memory_space=pl.ANY)] * len(after),
        compiler_params=pltpu.CompilerParams(vmem_limit_bytes=VMEM_LIMIT),
        cost_estimate=LIGHT,
        name="step",
    )(*read, *after)


def relay(piece, exported):
    pairs = [(0, 1), (1, 0), (2, 3), (3, 2)]
    middle = [(1, 2), (2, 1)]
    outward = [(1, 0), (2, 3)]
    near = lax.ppermute(piece, "node", pairs)
    across = lax.ppermute(piece, "node", middle)
    near, across, exported = lax.optimization_barrier((near, across, exported))
    across_out = lax.ppermute(across, "node", outward)
    near_across = lax.ppermute(near, "node", middle)
    far_out = lax.ppermute(near_across, "node", outward)
    return exported, (near, (near_across, across_out), (across, far_out))


def place_body(spots, features, *refs):
    out = refs[-1]
    half = features // 2
    device = lax.axis_index("node")
    mine = lax.axis_index("groups")
    last = (core_sums([refs[:2]], False) + refs[2][...].astype(jnp.float32)).astype(out.dtype)
    for source, parts in zip((last, *refs[3:-1]), spots):
        start = 0
        for size, distance, side in parts:
            group = {"own": mine, "other": 1 - mine, "all": 0}[side]
            column = pl.multiple_of((device ^ distance) * features + group * half, HEAD)
            out[:, pl.ds(column, size)] = source[:, start : start + size]
            start += size


def place(last, sources, spots, devices, features):
    return pl.pallas_call(
        functools.partial(place_body, spots, features),
        out_shape=jax.ShapeDtypeStruct((last[2].shape[0], devices * features), last[2].dtype),
        compiler_params=pltpu.CompilerParams(vmem_limit_bytes=VMEM_LIMIT),
        name="place",
    )(*last, *sources)


def split_weight(out_weight, exported):
    half = out_weight.shape[0] // 2
    first = lax.axis_index("groups") * half
    return relay(lax.dynamic_slice_in_dim(out_weight, first, half, 0), exported)


def project_split(halves, relayed, out_weight):
    features = out_weight.shape[0]
    half = features // 2
    rows = [part.reshape(-1, part.shape[-1]) for part in halves]
    other = [swap(part, "groups", 1) for part in rows]
    near, second, far = relayed

    def core(sent):
        return swap(sent, "tensor", 1)

    def chip(away):
        return swap(away, "tensor", 2)

    def multiply(rows, weights, after=(), cores=(), chips=()):
        return step(rows, weights, cores, chips, after, half)

    sent_a, kept_a, sent_b, kept_b = multiply(rows, [out_weight])
    sent_1, kept_1 = multiply(rows, [near], [sent_b, other[0]])
    one = [(kept_a, core(sent_a)), (kept_b, core(sent_b)), (kept_1, core(sent_1))]
    (away,) = step(cores=one, after=second)
    one.append(chip(away))
    sent_2, kept_2 = multiply(rows, [second], [sent_1])
    two = [(kept_2, core(sent_2))]
    sent_3, kept_3, sent_4, kept_4 = multiply(other, [near, second], [sent_2])
    three = [(kept_3, core(sent_3)), (kept_4, core(sent_4))]
    away, one_done = step(cores=three, chips=one)
    three.append(chip(away))
    sent_5, kept_5, away = multiply(other, [far], [away], two)
    two.append(chip(away))
    four = [(kept_5, core(sent_5))]
    sent_6, kept_6, three_done = multiply(rows, [far], [sent_5], (), three)
    three_other = swap(three_done, "groups", 1)
    five = [(kept_6, core(sent_6))]
    (away,) = step(cores=four, after=[sent_6])
    four.append(chip(away))
    away, two_done = step(cores=five, chips=two, after=[away])
    five.append(chip(away))
    (four_done,) = step(chips=four)
    four_other = swap(four_done, "groups", 1)
    return place(
        (*five[0], five[1]),
        (one_done, two_done, three_other, four_other),
        (
            ((half, 3, "own"),),
            ((features, 0, "all"), (half, 1, "own")),
            ((half, 2, "own"),),
            ((half, 1, "other"), (half, 2, "other")),
            ((half, 3, "other"),),
        ),
        lax.axis_size("node"),
        features,
    )


def project_plain(halves, out_weight):
    attended = jnp.concatenate(halves, 2)
    parts, per_part, width = attended.shape
    me = lax.axis_index("tensor")
    order = slot_position(parts, jnp.arange(parts, dtype=jnp.int32) ^ me)
    rows = attended[order].reshape(parts * per_part, width)
    weight = lax.all_gather(out_weight, "node", axis=0, tiled=True)
    terms = times(rows, weight).astype(jnp.bfloat16)
    return lax.psum_scatter(terms, "tensor", scatter_dimension=0, tiled=True)


def local(queries, keys, values, out_weight, slot_nodes, ancestors, depth):
    parts = lax.axis_size("tensor")
    devices = lax.axis_size("node")
    features = out_weight.shape[0]
    kv_count = keys.shape[1] // HEAD
    relayed, after = None, []
    exported, table, queries, keys, values = prepare(
        slot_nodes, ancestors, depth, queries, keys, values
    )
    got = lax.all_gather(exported, "node", axis=0, tiled=True)
    if (
        devices == 4
        and parts == 4
        and lax.axis_size("groups") == 2
        and features % (2 * HEAD) == 0
    ):
        _, relayed = split_weight(out_weight, exported)
        after = [relayed[0], relayed[2][0]]
    halves = []
    for kv in range(kv_count):
        halves.append(attend(kv, table, queries, keys, values, got, parts, after))
        after = halves[-1:]
    if relayed is None:
        return project_plain(halves, out_weight)
    return project_split(halves, relayed, out_weight)


def solution(mesh):
    placed = (
        P(("groups", "node"), "tensor"),
        P(("groups", "node"), "tensor"),
        P(("groups", "node"), "tensor"),
        P("node", "tensor"),
        P("groups"),
        P("groups", None),
        P("groups"),
    )
    return jax.shard_map(
        local,
        mesh=mesh,
        in_specs=placed,
        out_specs=P(("groups", "node", "tensor"), None),
        check_vma=False,
    )
```

```python
import functools
import math

import jax
import jax.numpy as jnp
from jax import lax
from jax.experimental import pallas as pl
from jax.experimental.pallas import tpu as pltpu
from jax.sharding import PartitionSpec as P

HEAD = 128
NODE_TOK = 128
A_MAX = 7
CHAIN = A_MAX - 1
EXPORTS = 2
SCALE = math.log2(math.e) / math.sqrt(HEAD)
DEAD = -1e30
LIGHT = pl.CostEstimate(flops=1, bytes_accessed=1, transcendentals=0)
VMEM_LIMIT = 20 * 1024 * 1024
ATTEND_LIMIT = 56 * 1024 * 1024


def prepare_body(nodes, *refs):
    slot_hbm, ancestors_hbm, depth_hbm, keys, values, exported, table_hbm = refs[:7]
    slot_nodes, ancestors, depth, table, holder, within, roots, sem = refs[7:]
    devices = slot_nodes.shape[0] // nodes
    me = lax.axis_index("node")
    fetches = [
        pltpu.make_async_copy(source, target, sem.at[2 * EXPORTS + 1 + order])
        for order, (source, target) in enumerate(
            ((slot_hbm, slot_nodes), (ancestors_hbm, ancestors), (depth_hbm, depth))
        )
    ]
    for fetch in fetches:
        fetch.start()
    for fetch in fetches:
        fetch.wait()

    def place(device, mine):
        root, root_index = jnp.int32(0), jnp.int32(0)
        for index in range(nodes):
            node = slot_nodes[device * nodes + index]
            holder[node] = device
            within[node] = index
            even = (depth[node] & 1) == 0
            root = jnp.where(even, node, root)
            root_index = jnp.where(even, index, root_index)
        roots[device] = root
        return jnp.where(device == me, root_index, mine)

    root = lax.fori_loop(0, devices, place, jnp.int32(0))

    def find_attach(device, attach):
        node = roots[device]
        level = depth[node]
        for step in range(0, CHAIN, 2):
            above = jnp.maximum(ancestors[step, node], 0)
            hit = (step < level) & (holder[above] == me)
            attach = jnp.where(hit, within[above], attach)
        return attach

    attach = lax.fori_loop(0, devices, find_attach, jnp.int32(0))
    copies = []
    for position, (source, index) in enumerate(
        ((keys, root), (keys, attach), (values, root), (values, attach))
    ):
        rows = pl.ds(pl.multiple_of(index * NODE_TOK, NODE_TOK), NODE_TOK)
        copies.append(
            pltpu.make_async_copy(source.at[rows, :], exported.at[position], sem.at[position])
        )
    for copy in copies:
        copy.start()
    root_node = roots[me]
    count = depth[root_node]
    table[0] = root
    table[1] = count
    for step in range(CHAIN):
        above = jnp.maximum(ancestors[step, root_node], 0)
        entry = holder[above] * (2 * EXPORTS) + (1 if step % 2 == 0 else 0)
        table[2 + step] = jnp.where(step < count, entry, 0)
    store = pltpu.make_async_copy(table, table_hbm, sem.at[2 * EXPORTS])
    store.start()
    for copy in (*copies, store):
        copy.wait()


def prepare(slot_nodes, ancestors, depth, keys, values):
    nodes = keys.shape[0] // NODE_TOK
    slots = slot_nodes.shape[0]
    hbm = pl.BlockSpec(memory_space=pltpu.HBM)
    vmem = pl.BlockSpec(memory_space=pltpu.VMEM)
    return pl.pallas_call(
        functools.partial(prepare_body, nodes),
        out_shape=(
            jax.ShapeDtypeStruct((2 * EXPORTS, NODE_TOK, keys.shape[1]), keys.dtype),
            jax.ShapeDtypeStruct((2 + CHAIN,), jnp.int32),
        ),
        in_specs=[hbm, hbm, hbm, vmem, vmem],
        out_specs=(hbm, hbm),
        scratch_shapes=[
            pltpu.SMEM((slots,), jnp.int32),
            pltpu.SMEM((A_MAX, slots), jnp.int32),
            pltpu.SMEM((slots,), jnp.int32),
            pltpu.SMEM((2 + CHAIN,), jnp.int32),
            pltpu.SMEM((slots,), jnp.int32),
            pltpu.SMEM((slots,), jnp.int32),
            pltpu.SMEM((slots // nodes,), jnp.int32),
            pltpu.SemaphoreType.DMA((2 * EXPORTS + 4,)),
        ],
        compiler_params=pltpu.CompilerParams(vmem_limit_bytes=VMEM_LIMIT),
        name="prepare",
    )(slot_nodes, ancestors.T, depth, keys, values)


def attend_body(kv, parts, table, query_hbm, keys_hbm, values_hbm, got, *refs):
    out, query, keys, values, above_keys, above_values, all_keys, all_values, sem = refs[-9:]
    nodes = query.shape[0] // NODE_TOK
    group = query.shape[1] // HEAD
    per_part = query.shape[0] // parts
    side = all_keys.shape[0]
    lanes = pl.ds(kv * HEAD, HEAD)
    pairs = [(keys_hbm.at[:, lanes], keys), (values_hbm.at[:, lanes], values)]
    for step in range(CHAIN):
        entry = table[2 + step]
        pairs.append((got.at[entry, :, lanes], above_keys.at[step]))
        pairs.append((got.at[entry + EXPORTS, :, lanes], above_values.at[step]))
    pairs.append((query_hbm.at[:, pl.ds(kv * group * HEAD, group * HEAD)], query))
    copies = [
        pltpu.make_async_copy(source, target, sem.at[order])
        for order, (source, target) in enumerate(pairs)
    ]
    for copy in copies:
        copy.start()
    ones = jnp.ones((NODE_TOK, HEAD), all_values.dtype)
    nothing = jnp.zeros((NODE_TOK, 2 * HEAD), all_values.dtype)
    query_index = lax.broadcasted_iota(jnp.int32, (NODE_TOK, NODE_TOK), 0)
    key_index = lax.broadcasted_iota(jnp.int32, (NODE_TOK, NODE_TOK), 1)
    own_bias = jnp.where(key_index <= query_index, 0.0, DEAD)
    piece = math.gcd(NODE_TOK, per_part)
    pieces_part = per_part // piece
    me = lax.axis_index("tensor")
    above = (CHAIN + 1) * NODE_TOK
    for copy in copies:
        copy.wait()

    def node_rows(node):
        return pl.ds(pl.multiple_of(node * NODE_TOK, NODE_TOK), NODE_TOK)

    def put(place, order, key_block, value_block):
        rows = pl.ds(order * NODE_TOK, NODE_TOK)
        all_keys[place, rows, :] = key_block
        all_values[place, rows, :HEAD] = value_block
        all_values[place, rows, HEAD:] = ones

    def put_nothing(place, order, first_key):
        rows = pl.ds(order * NODE_TOK, NODE_TOK)
        all_keys[place, rows, :] = jnp.broadcast_to(first_key, (NODE_TOK, HEAD))
        all_values[place, rows, :] = nothing

    for place in range(side):
        for step in range(CHAIN):
            put(place, step, above_keys[step], above_values[step])

    def lay_out(place, node):
        own_key = keys[node_rows(node), :]
        put(place, CHAIN + 1, own_key, values[node_rows(node), :])
        for step in range(CHAIN):
            pl.when(step >= table[1])(functools.partial(put_nothing, place, step, own_key[:1]))
        is_root = node == table[0]
        pl.when(is_root)(functools.partial(put_nothing, place, CHAIN, own_key[:1]))

        @pl.when(jnp.logical_not(is_root))
        def _():
            put(place, CHAIN, keys[node_rows(table[0]), :], values[node_rows(table[0]), :])

    def score(place, node):
        stacked = jnp.concatenate(
            [query[node_rows(node), h * HEAD : (h + 1) * HEAD] for h in range(group)], 0
        )
        return times(stacked, all_keys[place])

    def weigh(scores):
        own = scores[:, above:] + jnp.concatenate([own_bias] * group, 0)
        masked = jnp.concatenate([scores[:, :above], own], 1)
        largest = jnp.max(masked, axis=1, keepdims=True)
        return jnp.exp2((masked - largest) * SCALE).astype(jnp.bfloat16)

    def finish(place, node, expo):
        mixed = jnp.dot(expo, all_values[place], preferred_element_type=jnp.float32)
        result = (mixed[:, :HEAD] / mixed[:, HEAD:]).astype(jnp.bfloat16)
        for part in range(NODE_TOK // piece):
            block = node * (NODE_TOK // piece) + part
            owner = block // pieces_part
            target = slot_position(parts, owner ^ me)
            inner = (block - owner * pieces_part) * piece
            to = pl.ds(pl.multiple_of(inner, piece), piece)
            for h in range(group):
                first = h * NODE_TOK + part * piece
                out[target, to, h * HEAD : (h + 1) * HEAD] = result[first : first + piece]

    def some_nodes(turn, carry):
        mine = [(place, turn * side + place) for place in range(side)]
        for place, node in mine:
            lay_out(place, node)
        scores = [score(place, node) for place, node in mine]
        for (place, node), each in zip(mine, scores):
            finish(place, node, weigh(each))
        return carry

    lax.fori_loop(0, nodes // side, some_nodes, 0)


def slot_position(parts, distance):
    half = parts // 2
    return jnp.where(distance % 2 == 1, distance // 2, half + distance // 2)


def attend(kv, table, queries, keys, values, got, parts, after):
    rows = queries.shape[0]
    width = queries.shape[1] // (keys.shape[1] // HEAD)
    total = (CHAIN + 2) * NODE_TOK
    side = 2 if rows % (2 * NODE_TOK) == 0 else 1
    hbm = pl.BlockSpec(memory_space=pltpu.HBM)
    return pl.pallas_call(
        functools.partial(attend_body, kv, parts),
        out_shape=jax.ShapeDtypeStruct((parts, rows // parts, width), queries.dtype),
        in_specs=[pl.BlockSpec(memory_space=pltpu.SMEM)]
        + [hbm] * 4
        + [pl.BlockSpec(memory_space=pl.ANY)] * len(after),
        scratch_shapes=[
            pltpu.VMEM((rows, width), queries.dtype),
            pltpu.VMEM((rows, HEAD), keys.dtype),
            pltpu.VMEM((rows, HEAD), keys.dtype),
            pltpu.VMEM((CHAIN, NODE_TOK, HEAD), keys.dtype),
            pltpu.VMEM((CHAIN, NODE_TOK, HEAD), keys.dtype),
            pltpu.VMEM((side, total, HEAD), keys.dtype),
            pltpu.VMEM((side, total, 2 * HEAD), keys.dtype),
            pltpu.SemaphoreType.DMA((3 + 2 * CHAIN,)),
        ],
        compiler_params=pltpu.CompilerParams(vmem_limit_bytes=ATTEND_LIMIT),
        cost_estimate=LIGHT,
        name="attend",
    )(table, queries, keys, values, got, *after)


def swap(array, axis, distance):
    size = lax.axis_size(axis)
    return lax.ppermute(array, axis, [(i, i ^ distance) for i in range(size)])


def times(rows, weight):
    return lax.dot_general(
        rows, weight, (((1,), (1,)), ((), ())), preferred_element_type=jnp.float32
    )


def is_middle(index):
    return (index == 1) | (index == 2)


def product(rows, weight, outs):
    half = rows[0].shape[0] // 2
    for start in (0, half):
        whole = jnp.concatenate([part[start : start + half, :] for part in rows], 1)
        for order, pair in enumerate(outs):
            out = pair[start // half]
            width = out.shape[1]
            out[...] = times(whole, weight[order * width : (order + 1) * width, :]).astype(out.dtype)


def core_sums(pairs, upper):
    half = pairs[0][0].shape[0] // 2
    rows = slice(half, 2 * half) if upper else slice(0, half)
    return jnp.concatenate(
        [k[rows, :].astype(jnp.float32) + c[rows, :].astype(jnp.float32) for k, c in pairs], 1
    )


def step_body(plan, *refs):
    refs = list(refs)
    take = lambda count: [refs.pop(0) for _ in range(count)]
    rows = [take(count) for count in plan["rows"]]
    weights = [take(count) for count in plan["weights"]]
    cores = [[take(2) for _ in range(count)] for count in plan["cores"]]
    chips = [([take(2) for _ in range(count)], take(1)[0]) for count in plan["chips"]]
    take(plan["after"])
    outs = take(plan["outs"])
    chosen, sem = refs[-2:] if 2 in plan["weights"] else (None, None)
    middle = is_middle(lax.axis_index("node"))
    for bundle in weights:
        if len(bundle) == 2:
            for pick, source in zip((middle, jnp.logical_not(middle)), bundle):
                pl.when(pick)(pltpu.make_async_copy(source, chosen, sem).start)
    made = [outs.pop(0) for _ in rows for w in weights for _ in range(2 * plan["split"](w[0]))]
    for bundle in cores:
        out = outs.pop(0)
        out[...] = core_sums(bundle, True).astype(out.dtype)
    for bundle, from_chip in chips:
        out = outs.pop(0)
        out[...] = (core_sums(bundle, False) + from_chip[...].astype(jnp.float32)).astype(out.dtype)
    for weight in weights:
        source = weight[0]
        if len(weight) == 2:
            pltpu.make_async_copy(source, chosen, sem).wait()
            source = chosen
        for parts in rows:
            count = 2 * plan["split"](weight[0])
            product(parts, source, [made[i : i + 2] for i in range(0, count, 2)])
            made = made[count:]


def step(rows=(), weights=(), cores=(), chips=(), after=(), width=0):
    weights = [w if isinstance(w, tuple) else (w,) for w in weights]
    plan = {
        "rows": [len(parts) for parts in rows],
        "weights": [len(weight) for weight in weights],
        "cores": [len(bundle) for bundle in cores],
        "chips": [len(bundle) - 1 for bundle in chips],
        "after": len(after),
        "split": lambda weight: weight.shape[0] // width,
    }
    shapes = []
    for weight in weights:
        for parts in rows:
            shapes += [(parts[0].shape[0] // 2, width)] * (2 * plan["split"](weight[0]))
    for bundle in (*cores, *[bundle[:-1] for bundle in chips]):
        features = sum(kept.shape[1] for kept, _ in bundle)
        shapes.append((bundle[0][0].shape[0] // 2, features))
    plan["outs"] = len(shapes)
    vmem, hbm = pl.BlockSpec(memory_space=pltpu.VMEM), pl.BlockSpec(memory_space=pl.ANY)
    read = [(part, vmem) for parts in rows for part in parts]
    read += [(w, vmem if len(weight) == 1 else hbm) for weight in weights for w in weight]
    read += [(x, vmem) for bundle in cores for pair in bundle for x in pair]
    for bundle in chips:
        read += [(x, vmem) for pair in bundle[:-1] for x in pair] + [(bundle[-1], vmem)]
    read += [(x, hbm) for x in after]
    scratch = []
    if 2 in plan["weights"]:
        shape = [weight[0].shape for weight in weights if len(weight) == 2][0]
        scratch = [pltpu.VMEM(shape, read[0][0].dtype), pltpu.SemaphoreType.DMA]
    return pl.pallas_call(
        functools.partial(step_body, plan),
        out_shape=[jax.ShapeDtypeStruct(shape, read[0][0].dtype) for shape in shapes],
        in_specs=[spec for _, spec in read],
        scratch_shapes=scratch,
        compiler_params=pltpu.CompilerParams(vmem_limit_bytes=VMEM_LIMIT),
        cost_estimate=LIGHT,
        name="step",
    )(*[x for x, _ in read])


def relay(piece, exported):
    pairs = [(0, 1), (1, 0), (2, 3), (3, 2)]
    middle = [(1, 2), (2, 1)]
    outward = [(1, 0), (2, 3)]
    near = lax.ppermute(piece, "node", pairs)
    across = lax.ppermute(piece, "node", middle)
    near, across, exported = lax.optimization_barrier((near, across, exported))
    across_out = lax.ppermute(across, "node", outward)
    near_across = lax.ppermute(near, "node", middle)
    far_out = lax.ppermute(near_across, "node", outward)
    return exported, (near, (near_across, across_out), (across, far_out))


def place_body(spots, features, *refs):
    out = refs[-1]
    half = features // 2
    device = lax.axis_index("node")
    mine = lax.axis_index("groups")
    last = (core_sums([refs[:2]], False) + refs[2][...].astype(jnp.float32)).astype(out.dtype)
    for source, parts in zip((last, *refs[3:-1]), spots):
        start = 0
        for size, distance, side in parts:
            group = {"own": mine, "other": 1 - mine, "all": 0}[side]
            column = pl.multiple_of((device ^ distance) * features + group * half, HEAD)
            out[:, pl.ds(column, size)] = source[:, start : start + size]
            start += size


def place(last, sources, spots, devices, features):
    return pl.pallas_call(
        functools.partial(place_body, spots, features),
        out_shape=jax.ShapeDtypeStruct((last[2].shape[0], devices * features), last[2].dtype),
        compiler_params=pltpu.CompilerParams(vmem_limit_bytes=VMEM_LIMIT),
        name="place",
    )(*last, *sources)


def split_weight(out_weight, exported):
    half = out_weight.shape[0] // 2
    first = lax.axis_index("groups") * half
    return relay(lax.dynamic_slice_in_dim(out_weight, first, half, 0), exported)


def project_split(halves, relayed, out_weight):
    features = out_weight.shape[0]
    half = features // 2
    rows = [part.reshape(-1, part.shape[-1]) for part in halves]
    other = [swap(part, "groups", 1) for part in rows]
    near, second, far = relayed

    def core(sent):
        return swap(sent, "tensor", 1)

    def chip(away):
        return swap(away, "tensor", 2)

    def multiply(rows, weights, after=(), cores=(), chips=()):
        return step(rows, weights, cores, chips, after, half)

    sent_a, kept_a, sent_b, kept_b = multiply([rows], [out_weight])
    sent_1, kept_1 = multiply([rows], [near], [sent_b, other[0]])
    one = [(kept_a, core(sent_a)), (kept_b, core(sent_b)), (kept_1, core(sent_1))]
    (away,) = step(cores=[one], after=second)
    one.append(chip(away))
    sent_2, kept_2 = multiply([rows], [second], [sent_1])
    two = [(kept_2, core(sent_2))]
    sent_3, kept_3, sent_4, kept_4 = multiply([other], [near, second], [sent_2])
    three = [(kept_3, core(sent_3)), (kept_4, core(sent_4))]
    away, own_away, one_done = step(cores=[three, two], chips=[one])
    three.append(chip(away))
    two.append(chip(own_away))
    sent_5, kept_5, sent_6, kept_6, three_done = multiply([other, rows], [far], [away], (), [three])
    three_other = swap(three_done, "groups", 1)
    four = [(kept_5, core(sent_5))]
    five = [(kept_6, core(sent_6))]
    (away,) = step(cores=[four])
    four.append(chip(away))
    away, two_done = step(cores=[five], chips=[two], after=[away])
    five.append(chip(away))
    (four_done,) = step(chips=[four])
    four_other = swap(four_done, "groups", 1)
    return place(
        (*five[0], five[1]),
        (one_done, two_done, three_other, four_other),
        (
            ((half, 3, "own"),),
            ((features, 0, "all"), (half, 1, "own")),
            ((half, 2, "own"),),
            ((half, 1, "other"), (half, 2, "other")),
            ((half, 3, "other"),),
        ),
        lax.axis_size("node"),
        features,
    )


def project_plain(halves, out_weight):
    attended = jnp.concatenate(halves, 2)
    parts, per_part, width = attended.shape
    me = lax.axis_index("tensor")
    order = slot_position(parts, jnp.arange(parts, dtype=jnp.int32) ^ me)
    rows = attended[order].reshape(parts * per_part, width)
    weight = lax.all_gather(out_weight, "node", axis=0, tiled=True)
    terms = times(rows, weight).astype(jnp.bfloat16)
    return lax.psum_scatter(terms, "tensor", scatter_dimension=0, tiled=True)


def local(queries, keys, values, out_weight, slot_nodes, ancestors, depth):
    parts = lax.axis_size("tensor")
    devices = lax.axis_size("node")
    features = out_weight.shape[0]
    kv_count = keys.shape[1] // HEAD
    relayed, after = None, []
    exported, table = prepare(slot_nodes, ancestors, depth, keys, values)
    got = lax.all_gather(exported, "node", axis=0, tiled=True)
    if (
        devices == 4
        and parts == 4
        and lax.axis_size("groups") == 2
        and features % (2 * HEAD) == 0
    ):
        _, relayed = split_weight(out_weight, exported)
        after = [relayed[0], relayed[2][0]]
    halves = []
    for kv in range(kv_count):
        halves.append(attend(kv, table, queries, keys, values, got, parts, after))
        after = halves[-1:]
    if relayed is None:
        return project_plain(halves, out_weight)
    return project_split(halves, relayed, out_weight)


def solution(mesh):
    placed = (
        P(("groups", "node"), "tensor"),
        P(("groups", "node"), "tensor"),
        P(("groups", "node"), "tensor"),
        P("node", "tensor"),
        P("groups"),
        P("groups", None),
        P("groups"),
    )
    return jax.shard_map(
        local,
        mesh=mesh,
        in_specs=placed,
        out_specs=P(("groups", "node", "tensor"), None),
        check_vma=False,
    )
```

```python
import functools
import math

import jax
import jax.numpy as jnp
from jax import lax
from jax.experimental import pallas as pl
from jax.experimental.pallas import tpu as pltpu
from jax.sharding import PartitionSpec as P

HEAD = 128
NODE_TOK = 128
A_MAX = 7
CHAIN = A_MAX - 1
EXPORTS = 2
SCALE = math.log2(math.e) / math.sqrt(HEAD)
DEAD = -1e30
LIGHT = pl.CostEstimate(flops=1, bytes_accessed=1, transcendentals=0)
VMEM_LIMIT = 20 * 1024 * 1024
ATTEND_LIMIT = 56 * 1024 * 1024


def prepare_body(nodes, *refs):
    slot_hbm, ancestors_hbm, depth_hbm, keys, values, exported, table_hbm = refs[:7]
    slot_nodes, ancestors, depth, table, holder, within, roots, sem = refs[7:]
    devices = slot_nodes.shape[0] // nodes
    me = lax.axis_index("node")
    fetches = [
        pltpu.make_async_copy(source, target, sem.at[2 * EXPORTS + 1 + order])
        for order, (source, target) in enumerate(
            ((slot_hbm, slot_nodes), (ancestors_hbm, ancestors), (depth_hbm, depth))
        )
    ]
    for fetch in fetches:
        fetch.start()
    for fetch in fetches:
        fetch.wait()

    def place(device, mine):
        root, root_index = jnp.int32(0), jnp.int32(0)
        for index in range(nodes):
            node = slot_nodes[device * nodes + index]
            holder[node] = device
            within[node] = index
            even = (depth[node] & 1) == 0
            root = jnp.where(even, node, root)
            root_index = jnp.where(even, index, root_index)
        roots[device] = root
        return jnp.where(device == me, root_index, mine)

    root = lax.fori_loop(0, devices, place, jnp.int32(0))

    def find_attach(device, attach):
        node = roots[device]
        level = depth[node]
        for step in range(0, CHAIN, 2):
            above = jnp.maximum(ancestors[step, node], 0)
            hit = (step < level) & (holder[above] == me)
            attach = jnp.where(hit, within[above], attach)
        return attach

    attach = lax.fori_loop(0, devices, find_attach, jnp.int32(0))
    copies = []
    for position, (source, index) in enumerate(
        ((keys, root), (keys, attach), (values, root), (values, attach))
    ):
        rows = pl.ds(pl.multiple_of(index * NODE_TOK, NODE_TOK), NODE_TOK)
        copies.append(
            pltpu.make_async_copy(source.at[rows, :], exported.at[position], sem.at[position])
        )
    for copy in copies:
        copy.start()
    root_node = roots[me]
    count = depth[root_node]
    table[0] = root
    table[1] = count
    for step in range(CHAIN):
        above = jnp.maximum(ancestors[step, root_node], 0)
        entry = holder[above] * (2 * EXPORTS) + (1 if step % 2 == 0 else 0)
        table[2 + step] = jnp.where(step < count, entry, 0)
    store = pltpu.make_async_copy(table, table_hbm, sem.at[2 * EXPORTS])
    store.start()
    for copy in (*copies, store):
        copy.wait()


def prepare(slot_nodes, ancestors, depth, keys, values):
    nodes = keys.shape[0] // NODE_TOK
    slots = slot_nodes.shape[0]
    hbm = pl.BlockSpec(memory_space=pltpu.HBM)
    vmem = pl.BlockSpec(memory_space=pltpu.VMEM)
    return pl.pallas_call(
        functools.partial(prepare_body, nodes),
        out_shape=(
            jax.ShapeDtypeStruct((2 * EXPORTS, NODE_TOK, keys.shape[1]), keys.dtype),
            jax.ShapeDtypeStruct((2 + CHAIN,), jnp.int32),
        ),
        in_specs=[hbm, hbm, hbm, vmem, vmem],
        out_specs=(hbm, hbm),
        scratch_shapes=[
            pltpu.SMEM((slots,), jnp.int32),
            pltpu.SMEM((A_MAX, slots), jnp.int32),
            pltpu.SMEM((slots,), jnp.int32),
            pltpu.SMEM((2 + CHAIN,), jnp.int32),
            pltpu.SMEM((slots,), jnp.int32),
            pltpu.SMEM((slots,), jnp.int32),
            pltpu.SMEM((slots // nodes,), jnp.int32),
            pltpu.SemaphoreType.DMA((2 * EXPORTS + 4,)),
        ],
        compiler_params=pltpu.CompilerParams(vmem_limit_bytes=VMEM_LIMIT),
        name="prepare",
    )(slot_nodes, ancestors.T, depth, keys, values)


def attend_body(kv, parts, table, query_hbm, keys_hbm, values_hbm, got, *refs):
    out, query, keys, values, above_keys, above_values, all_keys, all_values, sem = refs[-9:]
    nodes = query.shape[0] // NODE_TOK
    group = query.shape[1] // HEAD
    per_part = query.shape[0] // parts
    side = all_keys.shape[0]
    lanes = pl.ds(kv * HEAD, HEAD)
    pairs = [(keys_hbm.at[:, lanes], keys), (values_hbm.at[:, lanes], values)]
    for step in range(CHAIN):
        entry = table[2 + step]
        pairs.append((got.at[entry, :, lanes], above_keys.at[step]))
        pairs.append((got.at[entry + EXPORTS, :, lanes], above_values.at[step]))
    pairs.append((query_hbm.at[:, pl.ds(kv * group * HEAD, group * HEAD)], query))
    copies = [
        pltpu.make_async_copy(source, target, sem.at[order])
        for order, (source, target) in enumerate(pairs)
    ]
    for copy in copies:
        copy.start()
    ones = jnp.ones((NODE_TOK, HEAD), all_values.dtype)
    nothing = jnp.zeros((NODE_TOK, 2 * HEAD), all_values.dtype)
    query_index = lax.broadcasted_iota(jnp.int32, (NODE_TOK, NODE_TOK), 0)
    key_index = lax.broadcasted_iota(jnp.int32, (NODE_TOK, NODE_TOK), 1)
    own_bias = jnp.where(key_index <= query_index, 0.0, DEAD)
    piece = math.gcd(NODE_TOK, per_part)
    pieces_part = per_part // piece
    me = lax.axis_index("tensor")
    above = (CHAIN + 1) * NODE_TOK
    for copy in copies:
        copy.wait()

    def node_rows(node):
        return pl.ds(pl.multiple_of(node * NODE_TOK, NODE_TOK), NODE_TOK)

    def put(place, order, key_block, value_block):
        rows = pl.ds(order * NODE_TOK, NODE_TOK)
        all_keys[place, rows, :] = key_block
        all_values[place, rows, :HEAD] = value_block
        all_values[place, rows, HEAD:] = ones

    def put_nothing(place, order, first_key):
        rows = pl.ds(order * NODE_TOK, NODE_TOK)
        all_keys[place, rows, :] = jnp.broadcast_to(first_key, (NODE_TOK, HEAD))
        all_values[place, rows, :] = nothing

    for place in range(side):
        for step in range(CHAIN):
            put(place, step, above_keys[step], above_values[step])

    def lay_out(place, node):
        own_key = keys[node_rows(node), :]
        put(place, CHAIN + 1, own_key, values[node_rows(node), :])
        for step in range(CHAIN):
            pl.when(step >= table[1])(functools.partial(put_nothing, place, step, own_key[:1]))
        is_root = node == table[0]
        pl.when(is_root)(functools.partial(put_nothing, place, CHAIN, own_key[:1]))

        @pl.when(jnp.logical_not(is_root))
        def _():
            put(place, CHAIN, keys[node_rows(table[0]), :], values[node_rows(table[0]), :])

    def score(place, node):
        stacked = jnp.concatenate(
            [query[node_rows(node), h * HEAD : (h + 1) * HEAD] for h in range(group)], 0
        )
        return times(stacked, all_keys[place])

    def weigh(scores):
        own = scores[:, above:] + jnp.concatenate([own_bias] * group, 0)
        masked = jnp.concatenate([scores[:, :above], own], 1)
        largest = jnp.max(masked, axis=1, keepdims=True)
        return jnp.exp2((masked - largest) * SCALE).astype(jnp.bfloat16)

    def finish(place, node, expo):
        mixed = jnp.dot(expo, all_values[place], preferred_element_type=jnp.float32)
        result = (mixed[:, :HEAD] / mixed[:, HEAD:]).astype(jnp.bfloat16)
        for part in range(NODE_TOK // piece):
            block = node * (NODE_TOK // piece) + part
            owner = block // pieces_part
            target = slot_position(parts, owner ^ me)
            inner = (block - owner * pieces_part) * piece
            to = pl.ds(pl.multiple_of(inner, piece), piece)
            for h in range(group):
                first = h * NODE_TOK + part * piece
                out[target, to, h * HEAD : (h + 1) * HEAD] = result[first : first + piece]

    def some_nodes(turn, carry):
        mine = [(place, turn * side + place) for place in range(side)]
        for place, node in mine:
            lay_out(place, node)
        scores = [score(place, node) for place, node in mine]
        for (place, node), each in zip(mine, scores):
            finish(place, node, weigh(each))
        return carry

    lax.fori_loop(0, nodes // side, some_nodes, 0)


def slot_position(parts, distance):
    half = parts // 2
    return jnp.where(distance % 2 == 1, distance // 2, half + distance // 2)


def attend(kv, table, queries, keys, values, got, parts, after):
    rows = queries.shape[0]
    width = queries.shape[1] // (keys.shape[1] // HEAD)
    total = (CHAIN + 2) * NODE_TOK
    side = 2 if rows % (2 * NODE_TOK) == 0 else 1
    hbm = pl.BlockSpec(memory_space=pltpu.HBM)
    return pl.pallas_call(
        functools.partial(attend_body, kv, parts),
        out_shape=jax.ShapeDtypeStruct((parts, rows // parts, width), queries.dtype),
        in_specs=[pl.BlockSpec(memory_space=pltpu.SMEM)]
        + [hbm] * 4
        + [pl.BlockSpec(memory_space=pl.ANY)] * len(after),
        scratch_shapes=[
            pltpu.VMEM((rows, width), queries.dtype),
            pltpu.VMEM((rows, HEAD), keys.dtype),
            pltpu.VMEM((rows, HEAD), keys.dtype),
            pltpu.VMEM((CHAIN, NODE_TOK, HEAD), keys.dtype),
            pltpu.VMEM((CHAIN, NODE_TOK, HEAD), keys.dtype),
            pltpu.VMEM((side, total, HEAD), keys.dtype),
            pltpu.VMEM((side, total, 2 * HEAD), keys.dtype),
            pltpu.SemaphoreType.DMA((3 + 2 * CHAIN,)),
        ],
        compiler_params=pltpu.CompilerParams(vmem_limit_bytes=ATTEND_LIMIT),
        cost_estimate=LIGHT,
        name="attend",
    )(table, queries, keys, values, got, *after)


def swap(array, axis, distance):
    size = lax.axis_size(axis)
    return lax.ppermute(array, axis, [(i, i ^ distance) for i in range(size)])


def times(rows, weight):
    return lax.dot_general(
        rows, weight, (((1,), (1,)), ((), ())), preferred_element_type=jnp.float32
    )


def is_middle(index):
    return (index == 1) | (index == 2)


def product(rows, weight, outs):
    half = rows[0].shape[0] // 2
    for start in (0, half):
        whole = jnp.concatenate([part[start : start + half, :] for part in rows], 1)
        for order, pair in enumerate(outs):
            out = pair[start // half]
            width = out.shape[1]
            out[...] = times(whole, weight[order * width : (order + 1) * width, :]).astype(out.dtype)


def core_sums(pairs, upper):
    half = pairs[0][0].shape[0] // 2
    rows = slice(half, 2 * half) if upper else slice(0, half)
    return jnp.concatenate(
        [k[rows, :].astype(jnp.float32) + c[rows, :].astype(jnp.float32) for k, c in pairs], 1
    )


def step_body(plan, *refs):
    refs = list(refs)
    take = lambda count: [refs.pop(0) for _ in range(count)]
    rows = [take(count) for count in plan["rows"]]
    weights = [take(count) for count in plan["weights"]]
    cores = [[take(2) for _ in range(count)] for count in plan["cores"]]
    chips = [([take(2) for _ in range(count)], take(1)[0]) for count in plan["chips"]]
    take(plan["after"])
    outs = take(plan["outs"])
    chosen, sem = refs[-2:] if 2 in plan["weights"] else (None, None)
    middle = is_middle(lax.axis_index("node"))
    for bundle in weights:
        if len(bundle) == 2:
            for pick, source in zip((middle, jnp.logical_not(middle)), bundle):
                pl.when(pick)(pltpu.make_async_copy(source, chosen, sem).start)
    made = [outs.pop(0) for _ in rows for w in weights for _ in range(2 * plan["split"](w[0]))]
    for bundle in cores:
        out = outs.pop(0)
        out[...] = core_sums(bundle, True).astype(out.dtype)
    for bundle, from_chip in chips:
        out = outs.pop(0)
        out[...] = (core_sums(bundle, False) + from_chip[...].astype(jnp.float32)).astype(out.dtype)
    for weight in weights:
        source = weight[0]
        if len(weight) == 2:
            pltpu.make_async_copy(source, chosen, sem).wait()
            source = chosen
        for parts in rows:
            count = 2 * plan["split"](weight[0])
            product(parts, source, [made[i : i + 2] for i in range(0, count, 2)])
            made = made[count:]


def step(rows=(), weights=(), cores=(), chips=(), after=(), width=0):
    weights = [w if isinstance(w, tuple) else (w,) for w in weights]
    plan = {
        "rows": [len(parts) for parts in rows],
        "weights": [len(weight) for weight in weights],
        "cores": [len(bundle) for bundle in cores],
        "chips": [len(bundle) - 1 for bundle in chips],
        "after": len(after),
        "split": lambda weight: weight.shape[0] // width,
    }
    shapes = []
    for weight in weights:
        for parts in rows:
            shapes += [(parts[0].shape[0] // 2, width)] * (2 * plan["split"](weight[0]))
    for bundle in (*cores, *[bundle[:-1] for bundle in chips]):
        features = sum(kept.shape[1] for kept, _ in bundle)
        shapes.append((bundle[0][0].shape[0] // 2, features))
    plan["outs"] = len(shapes)
    vmem, hbm = pl.BlockSpec(memory_space=pltpu.VMEM), pl.BlockSpec(memory_space=pl.ANY)
    read = [(part, vmem) for parts in rows for part in parts]
    read += [(w, vmem if len(weight) == 1 else hbm) for weight in weights for w in weight]
    read += [(x, vmem) for bundle in cores for pair in bundle for x in pair]
    for bundle in chips:
        read += [(x, vmem) for pair in bundle[:-1] for x in pair] + [(bundle[-1], vmem)]
    read += [(x, hbm) for x in after]
    scratch = []
    if 2 in plan["weights"]:
        shape = [weight[0].shape for weight in weights if len(weight) == 2][0]
        scratch = [pltpu.VMEM(shape, read[0][0].dtype), pltpu.SemaphoreType.DMA]
    return pl.pallas_call(
        functools.partial(step_body, plan),
        out_shape=[jax.ShapeDtypeStruct(shape, read[0][0].dtype) for shape in shapes],
        in_specs=[spec for _, spec in read],
        scratch_shapes=scratch,
        compiler_params=pltpu.CompilerParams(vmem_limit_bytes=VMEM_LIMIT),
        cost_estimate=LIGHT,
        name="step",
    )(*[x for x, _ in read])


PAIRS = [(0, 1), (1, 0), (2, 3), (3, 2)]
MIDDLE = [(1, 2), (2, 1)]
OUTWARD = [(1, 0), (2, 3)]


def relay(piece, exported):
    near = lax.ppermute(piece, "node", PAIRS)
    across = lax.ppermute(piece, "node", MIDDLE)
    near, across, exported = lax.optimization_barrier((near, across, exported))
    across_out = lax.ppermute(across, "node", OUTWARD)
    near_across = lax.ppermute(near, "node", MIDDLE)
    return near, across, near_across, across_out


def place_body(spots, features, *refs):
    out = refs[-1]
    half = features // 2
    device = lax.axis_index("node")
    mine = lax.axis_index("groups")
    last = (core_sums([refs[:2]], False) + refs[2][...].astype(jnp.float32)).astype(out.dtype)
    for source, parts in zip((last, *refs[3:-1]), spots):
        start = 0
        for size, distance, side in parts:
            group = {"own": mine, "other": 1 - mine, "all": 0}[side]
            column = pl.multiple_of((device ^ distance) * features + group * half, HEAD)
            out[:, pl.ds(column, size)] = source[:, start : start + size]
            start += size


def place(last, sources, spots, devices, features):
    return pl.pallas_call(
        functools.partial(place_body, spots, features),
        out_shape=jax.ShapeDtypeStruct((last[2].shape[0], devices * features), last[2].dtype),
        compiler_params=pltpu.CompilerParams(vmem_limit_bytes=VMEM_LIMIT),
        name="place",
    )(*last, *sources)


def split_weight(out_weight, exported):
    half = out_weight.shape[0] // 2
    first = lax.axis_index("groups") * half
    return relay(lax.dynamic_slice_in_dim(out_weight, first, half, 0), exported)


def project_split(halves, relayed, out_weight):
    features = out_weight.shape[0]
    half = features // 2
    rows = [part.reshape(-1, part.shape[-1]) for part in halves]
    other = [swap(part, "groups", 1) for part in rows]
    near, across, near_across, across_out = relayed
    second = (near_across, across_out)

    def core(sent):
        return swap(sent, "tensor", 1)

    def chip(away):
        return swap(away, "tensor", 2)

    def multiply(rows, weights, after=(), cores=(), chips=()):
        return step(rows, weights, cores, chips, after, half)

    far = (across, lax.ppermute(near_across, "node", OUTWARD))

    sent_a, kept_a, sent_b, kept_b = multiply([rows], [out_weight])
    sent_1, kept_1 = multiply([rows], [near], [sent_b, other[0]])
    one = [(kept_a, core(sent_a)), (kept_b, core(sent_b)), (kept_1, core(sent_1))]
    (away,) = step(cores=[one], after=second)
    one.append(chip(away))
    sent_2, kept_2 = multiply([rows], [second], [sent_1])
    two = [(kept_2, core(sent_2))]
    sent_3, kept_3, sent_4, kept_4 = multiply([other], [near, second], [sent_2])
    three = [(kept_3, core(sent_3)), (kept_4, core(sent_4))]
    away, own_away, one_done = step(cores=[three, two], chips=[one])
    three.append(chip(away))
    two.append(chip(own_away))
    sent_5, kept_5 = multiply([other], [far], [away])
    four = [(kept_5, core(sent_5))]
    three_done, two_done = step(chips=[three, two], after=[sent_5])
    three_other = swap(three_done, "groups", 1)
    sent_6, kept_6 = multiply([rows], [far], [three_done])
    five = [(kept_6, core(sent_6))]
    (away,) = step(cores=[four], after=[sent_6])
    four.append(chip(away))
    (away,) = step(cores=[five], after=[away])
    five.append(chip(away))
    (four_done,) = step(chips=[four], after=[three_other])
    four_other = swap(four_done, "groups", 1)
    return place(
        (*five[0], five[1]),
        (one_done, two_done, three_other, four_other),
        (
            ((half, 3, "own"),),
            ((features, 0, "all"), (half, 1, "own")),
            ((half, 2, "own"),),
            ((half, 1, "other"), (half, 2, "other")),
            ((half, 3, "other"),),
        ),
        lax.axis_size("node"),
        features,
    )


def project_plain(halves, out_weight):
    attended = jnp.concatenate(halves, 2)
    parts, per_part, width = attended.shape
    me = lax.axis_index("tensor")
    order = slot_position(parts, jnp.arange(parts, dtype=jnp.int32) ^ me)
    rows = attended[order].reshape(parts * per_part, width)
    weight = lax.all_gather(out_weight, "node", axis=0, tiled=True)
    terms = times(rows, weight).astype(jnp.bfloat16)
    return lax.psum_scatter(terms, "tensor", scatter_dimension=0, tiled=True)


def local(queries, keys, values, out_weight, slot_nodes, ancestors, depth):
    parts = lax.axis_size("tensor")
    devices = lax.axis_size("node")
    features = out_weight.shape[0]
    kv_count = keys.shape[1] // HEAD
    relayed, after = None, []
    exported, table = prepare(slot_nodes, ancestors, depth, keys, values)
    got = lax.all_gather(exported, "node", axis=0, tiled=True)
    if (
        devices == 4
        and parts == 4
        and lax.axis_size("groups") == 2
        and features % (2 * HEAD) == 0
    ):
        relayed = split_weight(out_weight, exported)
        after = relayed[:2]
    halves = []
    for kv in range(kv_count):
        halves.append(attend(kv, table, queries, keys, values, got, parts, after))
        after = halves[-1:]
    if relayed is None:
        return project_plain(halves, out_weight)
    return project_split(halves, relayed, out_weight)


def solution(mesh):
    placed = (
        P(("groups", "node"), "tensor"),
        P(("groups", "node"), "tensor"),
        P(("groups", "node"), "tensor"),
        P("node", "tensor"),
        P("groups"),
        P("groups", None),
        P("groups"),
    )
    return jax.shard_map(
        local,
        mesh=mesh,
        in_specs=placed,
        out_specs=P(("groups", "node", "tensor"), None),
        check_vma=False,
    )
```

```python
import functools
import math

import jax
import jax.numpy as jnp
from jax import lax
from jax.experimental import pallas as pl
from jax.experimental.pallas import tpu as pltpu
from jax.sharding import PartitionSpec as P

HEAD = 128
NODE_TOK = 128
A_MAX = 7
CHAIN = A_MAX - 1
EXPORTS = 2
SCALE = math.log2(math.e) / math.sqrt(HEAD)
DEAD = -1e30
LIGHT = pl.CostEstimate(flops=1, bytes_accessed=1, transcendentals=0)
VMEM_LIMIT = 20 * 1024 * 1024
ATTEND_LIMIT = 56 * 1024 * 1024


def prepare_body(nodes, *refs):
    slot_hbm, ancestors_hbm, depth_hbm, keys, values, exported, table_hbm = refs[:7]
    slot_nodes, ancestors, depth, table, holder, within, roots, sem = refs[7:]
    devices = slot_nodes.shape[0] // nodes
    me = lax.axis_index("node")
    fetches = [
        pltpu.make_async_copy(source, target, sem.at[2 * EXPORTS + 1 + order])
        for order, (source, target) in enumerate(
            ((slot_hbm, slot_nodes), (ancestors_hbm, ancestors), (depth_hbm, depth))
        )
    ]
    for fetch in fetches:
        fetch.start()
    for fetch in fetches:
        fetch.wait()

    def place(device, mine):
        root, root_index = jnp.int32(0), jnp.int32(0)
        for index in range(nodes):
            node = slot_nodes[device * nodes + index]
            holder[node] = device
            within[node] = index
            even = (depth[node] & 1) == 0
            root = jnp.where(even, node, root)
            root_index = jnp.where(even, index, root_index)
        roots[device] = root
        return jnp.where(device == me, root_index, mine)

    root = lax.fori_loop(0, devices, place, jnp.int32(0))

    def find_attach(device, attach):
        node = roots[device]
        level = depth[node]
        for step in range(0, CHAIN, 2):
            above = jnp.maximum(ancestors[step, node], 0)
            hit = (step < level) & (holder[above] == me)
            attach = jnp.where(hit, within[above], attach)
        return attach

    attach = lax.fori_loop(0, devices, find_attach, jnp.int32(0))
    copies = []
    for position, (source, index) in enumerate(
        ((keys, root), (keys, attach), (values, root), (values, attach))
    ):
        rows = pl.ds(pl.multiple_of(index * NODE_TOK, NODE_TOK), NODE_TOK)
        copies.append(
            pltpu.make_async_copy(source.at[rows, :], exported.at[position], sem.at[position])
        )
    for copy in copies:
        copy.start()
    root_node = roots[me]
    count = depth[root_node]
    table[0] = root
    table[1] = count
    for step in range(CHAIN):
        above = jnp.maximum(ancestors[step, root_node], 0)
        entry = holder[above] * (2 * EXPORTS) + (1 if step % 2 == 0 else 0)
        table[2 + step] = jnp.where(step < count, entry, 0)
    store = pltpu.make_async_copy(table, table_hbm, sem.at[2 * EXPORTS])
    store.start()
    for copy in (*copies, store):
        copy.wait()


def prepare(slot_nodes, ancestors, depth, keys, values):
    nodes = keys.shape[0] // NODE_TOK
    slots = slot_nodes.shape[0]
    hbm = pl.BlockSpec(memory_space=pltpu.HBM)
    vmem = pl.BlockSpec(memory_space=pltpu.VMEM)
    return pl.pallas_call(
        functools.partial(prepare_body, nodes),
        out_shape=(
            jax.ShapeDtypeStruct((2 * EXPORTS, NODE_TOK, keys.shape[1]), keys.dtype),
            jax.ShapeDtypeStruct((2 + CHAIN,), jnp.int32),
        ),
        in_specs=[hbm, hbm, hbm, vmem, vmem],
        out_specs=(hbm, hbm),
        scratch_shapes=[
            pltpu.SMEM((slots,), jnp.int32),
            pltpu.SMEM((A_MAX, slots), jnp.int32),
            pltpu.SMEM((slots,), jnp.int32),
            pltpu.SMEM((2 + CHAIN,), jnp.int32),
            pltpu.SMEM((slots,), jnp.int32),
            pltpu.SMEM((slots,), jnp.int32),
            pltpu.SMEM((slots // nodes,), jnp.int32),
            pltpu.SemaphoreType.DMA((2 * EXPORTS + 4,)),
        ],
        compiler_params=pltpu.CompilerParams(vmem_limit_bytes=VMEM_LIMIT),
        name="prepare",
    )(slot_nodes, ancestors.T, depth, keys, values)


def attend_body(kv, parts, table, query_hbm, keys_hbm, values_hbm, got, *refs):
    out, query, keys, values, above_keys, above_values, all_keys, all_values, sem = refs[-9:]
    nodes = query.shape[0] // NODE_TOK
    group = query.shape[1] // HEAD
    per_part = query.shape[0] // parts
    side = all_keys.shape[0]
    lanes = pl.ds(kv * HEAD, HEAD)
    pairs = [(keys_hbm.at[:, lanes], keys), (values_hbm.at[:, lanes], values)]
    for step in range(CHAIN):
        entry = table[2 + step]
        pairs.append((got.at[entry, :, lanes], above_keys.at[step]))
        pairs.append((got.at[entry + EXPORTS, :, lanes], above_values.at[step]))
    pairs.append((query_hbm.at[:, pl.ds(kv * group * HEAD, group * HEAD)], query))
    copies = [
        pltpu.make_async_copy(source, target, sem.at[order])
        for order, (source, target) in enumerate(pairs)
    ]
    for copy in copies:
        copy.start()
    ones = jnp.ones((NODE_TOK, HEAD), all_values.dtype)
    nothing = jnp.zeros((NODE_TOK, 2 * HEAD), all_values.dtype)
    query_index = lax.broadcasted_iota(jnp.int32, (NODE_TOK, NODE_TOK), 0)
    key_index = lax.broadcasted_iota(jnp.int32, (NODE_TOK, NODE_TOK), 1)
    own_bias = jnp.where(key_index <= query_index, 0.0, DEAD)
    piece = math.gcd(NODE_TOK, per_part)
    pieces_part = per_part // piece
    me = lax.axis_index("tensor")
    above = (CHAIN + 1) * NODE_TOK
    for copy in copies:
        copy.wait()

    def node_rows(node):
        return pl.ds(pl.multiple_of(node * NODE_TOK, NODE_TOK), NODE_TOK)

    def put(place, order, key_block, value_block):
        rows = pl.ds(order * NODE_TOK, NODE_TOK)
        all_keys[place, rows, :] = key_block
        all_values[place, rows, :HEAD] = value_block
        all_values[place, rows, HEAD:] = ones

    def put_nothing(place, order, first_key):
        rows = pl.ds(order * NODE_TOK, NODE_TOK)
        all_keys[place, rows, :] = jnp.broadcast_to(first_key, (NODE_TOK, HEAD))
        all_values[place, rows, :] = nothing

    for place in range(side):
        for step in range(CHAIN):
            put(place, step, above_keys[step], above_values[step])

    def lay_out(place, node):
        own_key = keys[node_rows(node), :]
        put(place, CHAIN + 1, own_key, values[node_rows(node), :])
        for step in range(CHAIN):
            pl.when(step >= table[1])(functools.partial(put_nothing, place, step, own_key[:1]))
        is_root = node == table[0]
        pl.when(is_root)(functools.partial(put_nothing, place, CHAIN, own_key[:1]))

        @pl.when(jnp.logical_not(is_root))
        def _():
            put(place, CHAIN, keys[node_rows(table[0]), :], values[node_rows(table[0]), :])

    def score(place, node):
        stacked = jnp.concatenate(
            [query[node_rows(node), h * HEAD : (h + 1) * HEAD] for h in range(group)], 0
        )
        return times(stacked, all_keys[place])

    def weigh(scores):
        own = scores[:, above:] + jnp.concatenate([own_bias] * group, 0)
        masked = jnp.concatenate([scores[:, :above], own], 1)
        largest = jnp.max(masked, axis=1, keepdims=True)
        return jnp.exp2((masked - largest) * SCALE).astype(jnp.bfloat16)

    def finish(place, node, expo):
        mixed = jnp.dot(expo, all_values[place], preferred_element_type=jnp.float32)
        result = (mixed[:, :HEAD] / mixed[:, HEAD:]).astype(jnp.bfloat16)
        for part in range(NODE_TOK // piece):
            block = node * (NODE_TOK // piece) + part
            owner = block // pieces_part
            target = slot_position(parts, owner ^ me)
            inner = (block - owner * pieces_part) * piece
            to = pl.ds(pl.multiple_of(inner, piece), piece)
            for h in range(group):
                first = h * NODE_TOK + part * piece
                out[target, to, h * HEAD : (h + 1) * HEAD] = result[first : first + piece]

    def some_nodes(turn, carry):
        mine = [(place, turn * side + place) for place in range(side)]
        for place, node in mine:
            lay_out(place, node)
        scores = [score(place, node) for place, node in mine]
        for (place, node), each in zip(mine, scores):
            finish(place, node, weigh(each))
        return carry

    lax.fori_loop(0, nodes // side, some_nodes, 0)


def slot_position(parts, distance):
    half = parts // 2
    return jnp.where(distance % 2 == 1, distance // 2, half + distance // 2)


def attend(kv, table, queries, keys, values, got, parts, after):
    rows = queries.shape[0]
    width = queries.shape[1] // (keys.shape[1] // HEAD)
    total = (CHAIN + 2) * NODE_TOK
    side = 2 if rows % (2 * NODE_TOK) == 0 else 1
    hbm = pl.BlockSpec(memory_space=pltpu.HBM)
    return pl.pallas_call(
        functools.partial(attend_body, kv, parts),
        out_shape=jax.ShapeDtypeStruct((parts, rows // parts, width), queries.dtype),
        in_specs=[pl.BlockSpec(memory_space=pltpu.SMEM)]
        + [hbm] * 4
        + [pl.BlockSpec(memory_space=pl.ANY)] * len(after),
        scratch_shapes=[
            pltpu.VMEM((rows, width), queries.dtype),
            pltpu.VMEM((rows, HEAD), keys.dtype),
            pltpu.VMEM((rows, HEAD), keys.dtype),
            pltpu.VMEM((CHAIN, NODE_TOK, HEAD), keys.dtype),
            pltpu.VMEM((CHAIN, NODE_TOK, HEAD), keys.dtype),
            pltpu.VMEM((side, total, HEAD), keys.dtype),
            pltpu.VMEM((side, total, 2 * HEAD), keys.dtype),
            pltpu.SemaphoreType.DMA((3 + 2 * CHAIN,)),
        ],
        compiler_params=pltpu.CompilerParams(vmem_limit_bytes=ATTEND_LIMIT),
        cost_estimate=LIGHT,
        name="attend",
    )(table, queries, keys, values, got, *after)


def swap(array, axis, distance):
    size = lax.axis_size(axis)
    return lax.ppermute(array, axis, [(i, i ^ distance) for i in range(size)])


def times(rows, weight):
    return lax.dot_general(
        rows, weight, (((1,), (1,)), ((), ())), preferred_element_type=jnp.float32
    )


def is_middle(index):
    return (index == 1) | (index == 2)


def product(rows, weight, outs):
    half = rows[0].shape[0] // 2
    for start in (0, half):
        whole = jnp.concatenate([part[start : start + half, :] for part in rows], 1)
        for order, pair in enumerate(outs):
            out = pair[start // half]
            width = out.shape[1]
            out[...] = times(whole, weight[order * width : (order + 1) * width, :]).astype(out.dtype)


def core_sums(pairs, upper):
    half = pairs[0][0].shape[0] // 2
    rows = slice(half, 2 * half) if upper else slice(0, half)
    return jnp.concatenate(
        [k[rows, :].astype(jnp.float32) + c[rows, :].astype(jnp.float32) for k, c in pairs], 1
    )


def step_body(plan, *refs):
    refs = list(refs)
    take = lambda count: [refs.pop(0) for _ in range(count)]
    rows = [take(count) for count in plan["rows"]]
    weights = [take(count) for count in plan["weights"]]
    cores = [[take(2) for _ in range(count)] for count in plan["cores"]]
    chips = [([take(2) for _ in range(count)], take(1)[0]) for count in plan["chips"]]
    take(plan["after"])
    outs = take(plan["outs"])
    chosen, sem = refs[-2:] if 2 in plan["weights"] else (None, None)
    middle = is_middle(lax.axis_index("node"))
    for out, part in zip(outs[len(outs) - plan["held"] :], [x for parts in rows for x in parts]):
        out[...] = part[...]
    for bundle in weights:
        if len(bundle) == 2:
            for pick, source in zip((middle, jnp.logical_not(middle)), bundle):
                pl.when(pick)(pltpu.make_async_copy(source, chosen, sem).start)
    made = [outs.pop(0) for _ in rows for w in weights for _ in range(2 * plan["split"](w[0]))]
    for bundle in cores:
        out = outs.pop(0)
        out[...] = core_sums(bundle, True).astype(out.dtype)
    for bundle, from_chip in chips:
        out = outs.pop(0)
        out[...] = (core_sums(bundle, False) + from_chip[...].astype(jnp.float32)).astype(out.dtype)
    for weight in weights:
        source = weight[0]
        if len(weight) == 2:
            pltpu.make_async_copy(source, chosen, sem).wait()
            source = chosen
        for parts in rows:
            count = 2 * plan["split"](weight[0])
            product(parts, source, [made[i : i + 2] for i in range(0, count, 2)])
            made = made[count:]


def step(rows=(), weights=(), cores=(), chips=(), after=(), width=0, hold=False):
    weights = [w if isinstance(w, tuple) else (w,) for w in weights]
    plan = {
        "rows": [len(parts) for parts in rows],
        "weights": [len(weight) for weight in weights],
        "cores": [len(bundle) for bundle in cores],
        "chips": [len(bundle) - 1 for bundle in chips],
        "after": len(after),
        "split": lambda weight: weight.shape[0] // width,
    }
    shapes = []
    for weight in weights:
        for parts in rows:
            shapes += [(parts[0].shape[0] // 2, width)] * (2 * plan["split"](weight[0]))
    for bundle in (*cores, *[bundle[:-1] for bundle in chips]):
        features = sum(kept.shape[1] for kept, _ in bundle)
        shapes.append((bundle[0][0].shape[0] // 2, features))
    held = [part.shape for parts in rows for part in parts] if hold else []
    shapes += held
    plan["outs"], plan["held"] = len(shapes), len(held)
    vmem, hbm = pl.BlockSpec(memory_space=pltpu.VMEM), pl.BlockSpec(memory_space=pl.ANY)
    read = [(part, vmem) for parts in rows for part in parts]
    read += [(w, vmem if len(weight) == 1 else hbm) for weight in weights for w in weight]
    read += [(x, vmem) for bundle in cores for pair in bundle for x in pair]
    for bundle in chips:
        read += [(x, vmem) for pair in bundle[:-1] for x in pair] + [(bundle[-1], vmem)]
    read += [(x, hbm) for x in after]
    scratch = []
    if 2 in plan["weights"]:
        shape = [weight[0].shape for weight in weights if len(weight) == 2][0]
        scratch = [pltpu.VMEM(shape, read[0][0].dtype), pltpu.SemaphoreType.DMA]
    return pl.pallas_call(
        functools.partial(step_body, plan),
        out_shape=[jax.ShapeDtypeStruct(shape, read[0][0].dtype) for shape in shapes],
        in_specs=[spec for _, spec in read],
        scratch_shapes=scratch,
        compiler_params=pltpu.CompilerParams(vmem_limit_bytes=VMEM_LIMIT),
        cost_estimate=LIGHT,
        name="step",
    )(*[x for x, _ in read])


PAIRS = [(0, 1), (1, 0), (2, 3), (3, 2)]
MIDDLE = [(1, 2), (2, 1)]
OUTWARD = [(1, 0), (2, 3)]


def relay(piece, exported):
    near = lax.ppermute(piece, "node", PAIRS)
    across = lax.ppermute(piece, "node", MIDDLE)
    near, across, exported = lax.optimization_barrier((near, across, exported))
    across_out = lax.ppermute(across, "node", OUTWARD)
    near_across = lax.ppermute(near, "node", MIDDLE)
    return near, across, near_across, across_out


def place_body(spots, features, *refs):
    out = refs[-1]
    half = features // 2
    device = lax.axis_index("node")
    mine = lax.axis_index("groups")
    last = (core_sums([refs[:2]], False) + refs[2][...].astype(jnp.float32)).astype(out.dtype)
    for source, parts in zip((last, *refs[3:-1]), spots):
        start = 0
        for size, distance, side in parts:
            group = {"own": mine, "other": 1 - mine, "all": 0}[side]
            column = pl.multiple_of((device ^ distance) * features + group * half, HEAD)
            out[:, pl.ds(column, size)] = source[:, start : start + size]
            start += size


def place(last, sources, spots, devices, features):
    return pl.pallas_call(
        functools.partial(place_body, spots, features),
        out_shape=jax.ShapeDtypeStruct((last[2].shape[0], devices * features), last[2].dtype),
        compiler_params=pltpu.CompilerParams(vmem_limit_bytes=VMEM_LIMIT),
        name="place",
    )(*last, *sources)


def split_weight(out_weight, exported):
    half = out_weight.shape[0] // 2
    first = lax.axis_index("groups") * half
    return relay(lax.dynamic_slice_in_dim(out_weight, first, half, 0), exported)


def project_split(halves, relayed, out_weight):
    features = out_weight.shape[0]
    half = features // 2
    rows = [part.reshape(-1, part.shape[-1]) for part in halves]
    other = [swap(part, "groups", 1) for part in rows]
    near, across, near_across, across_out = relayed
    second = (near_across, across_out)

    def core(sent):
        return swap(sent, "tensor", 1)

    def chip(away):
        return swap(away, "tensor", 2)

    def multiply(rows, weights, after=(), cores=(), chips=()):
        return step(rows, weights, cores, chips, after, half)

    far = (across, lax.ppermute(near_across, "node", OUTWARD))

    sent_a, kept_a, sent_b, kept_b, *rows = step([rows], [out_weight], width=half, hold=True)
    one = [(kept_a, core(sent_a)), (kept_b, core(sent_b))]
    (away,) = step(cores=[one])
    one.append(chip(away))
    sent_1, kept_1 = multiply([rows], [near], [sent_b, other[0]])
    sent_2, kept_2 = multiply([rows], [second], [sent_1])
    two = [(kept_1, core(sent_1)), (kept_2, core(sent_2))]
    away, one_done = step(cores=[two], chips=[one])
    two.append(chip(away))
    sent_3, kept_3, sent_4, kept_4 = multiply([other], [near, second], [away])
    three = [(kept_3, core(sent_3)), (kept_4, core(sent_4))]
    (away,) = step(cores=[three])
    three.append(chip(away))
    (three_done,) = step(chips=[three])
    three_other = swap(three_done, "groups", 1)
    sent_5, kept_5 = multiply([other], [far], [three_done])
    four = [(kept_5, core(sent_5))]
    sent_6, kept_6 = multiply([rows], [far], [sent_5])
    five = [(kept_6, core(sent_6))]
    away, two_done = step(cores=[four], chips=[two], after=[sent_6])
    four.append(chip(away))
    (away,) = step(cores=[five], after=[away, three_other])
    five.append(chip(away))
    (four_done,) = step(chips=[four])
    four_other = swap(four_done, "groups", 1)
    return place(
        (*five[0], five[1]),
        (one_done, two_done, three_other, four_other),
        (
            ((half, 3, "own"),),
            ((features, 0, "all"),),
            ((half, 1, "own"), (half, 2, "own")),
            ((half, 1, "other"), (half, 2, "other")),
            ((half, 3, "other"),),
        ),
        lax.axis_size("node"),
        features,
    )


def project_plain(halves, out_weight):
    attended = jnp.concatenate(halves, 2)
    parts, per_part, width = attended.shape
    me = lax.axis_index("tensor")
    order = slot_position(parts, jnp.arange(parts, dtype=jnp.int32) ^ me)
    rows = attended[order].reshape(parts * per_part, width)
    weight = lax.all_gather(out_weight, "node", axis=0, tiled=True)
    terms = times(rows, weight).astype(jnp.bfloat16)
    return lax.psum_scatter(terms, "tensor", scatter_dimension=0, tiled=True)


def local(queries, keys, values, out_weight, slot_nodes, ancestors, depth):
    parts = lax.axis_size("tensor")
    devices = lax.axis_size("node")
    features = out_weight.shape[0]
    kv_count = keys.shape[1] // HEAD
    relayed, after = None, []
    exported, table = prepare(slot_nodes, ancestors, depth, keys, values)
    got = lax.all_gather(exported, "node", axis=0, tiled=True)
    if (
        devices == 4
        and parts == 4
        and lax.axis_size("groups") == 2
        and features % (2 * HEAD) == 0
    ):
        relayed = split_weight(out_weight, exported)
        after = relayed[:2]
    halves = []
    for kv in range(kv_count):
        halves.append(attend(kv, table, queries, keys, values, got, parts, after))
        after = halves[-1:]
    if relayed is None:
        return project_plain(halves, out_weight)
    return project_split(halves, relayed, out_weight)


def solution(mesh):
    placed = (
        P(("groups", "node"), "tensor"),
        P(("groups", "node"), "tensor"),
        P(("groups", "node"), "tensor"),
        P("node", "tensor"),
        P("groups"),
        P("groups", None),
        P("groups"),
    )
    return jax.shard_map(
        local,
        mesh=mesh,
        in_specs=placed,
        out_specs=P(("groups", "node", "tensor"), None),
        check_vma=False,
    )
```

```python
import functools
import math

import jax
import jax.numpy as jnp
from jax import lax
from jax.experimental import pallas as pl
from jax.experimental.pallas import tpu as pltpu
from jax.sharding import PartitionSpec as P

HEAD = 128
NODE_TOK = 128
A_MAX = 7
CHAIN = A_MAX - 1
EXPORTS = 2
SCALE = math.log2(math.e) / math.sqrt(HEAD)
DEAD = -1e30
LIGHT = pl.CostEstimate(flops=1, bytes_accessed=1, transcendentals=0)
VMEM_LIMIT = 20 * 1024 * 1024
ATTEND_LIMIT = 56 * 1024 * 1024


def prepare_body(nodes, *refs):
    slot_hbm, ancestors_hbm, depth_hbm, keys, values, exported, table_hbm = refs[:7]
    slot_nodes, ancestors, depth, table, holder, within, roots, sem = refs[7:]
    devices = slot_nodes.shape[0] // nodes
    me = lax.axis_index("node")
    fetches = [
        pltpu.make_async_copy(source, target, sem.at[2 * EXPORTS + 1 + order])
        for order, (source, target) in enumerate(
            ((slot_hbm, slot_nodes), (ancestors_hbm, ancestors), (depth_hbm, depth))
        )
    ]
    for fetch in fetches:
        fetch.start()
    for fetch in fetches:
        fetch.wait()

    def place(device, mine):
        root, root_index = jnp.int32(0), jnp.int32(0)
        for index in range(nodes):
            node = slot_nodes[device * nodes + index]
            holder[node] = device
            within[node] = index
            even = (depth[node] & 1) == 0
            root = jnp.where(even, node, root)
            root_index = jnp.where(even, index, root_index)
        roots[device] = root
        return jnp.where(device == me, root_index, mine)

    root = lax.fori_loop(0, devices, place, jnp.int32(0))

    def find_attach(device, attach):
        node = roots[device]
        level = depth[node]
        for step in range(0, CHAIN, 2):
            above = jnp.maximum(ancestors[step, node], 0)
            hit = (step < level) & (holder[above] == me)
            attach = jnp.where(hit, within[above], attach)
        return attach

    attach = lax.fori_loop(0, devices, find_attach, jnp.int32(0))
    copies = []
    for position, (source, index) in enumerate(
        ((keys, root), (keys, attach), (values, root), (values, attach))
    ):
        rows = pl.ds(pl.multiple_of(index * NODE_TOK, NODE_TOK), NODE_TOK)
        copies.append(
            pltpu.make_async_copy(source.at[rows, :], exported.at[position], sem.at[position])
        )
    for copy in copies:
        copy.start()
    root_node = roots[me]
    count = depth[root_node]
    table[0] = root
    table[1] = count
    for step in range(CHAIN):
        above = jnp.maximum(ancestors[step, root_node], 0)
        entry = holder[above] * (2 * EXPORTS) + (1 if step % 2 == 0 else 0)
        table[2 + step] = jnp.where(step < count, entry, 0)
    store = pltpu.make_async_copy(table, table_hbm, sem.at[2 * EXPORTS])
    store.start()
    for copy in (*copies, store):
        copy.wait()


def prepare(slot_nodes, ancestors, depth, keys, values):
    nodes = keys.shape[0] // NODE_TOK
    slots = slot_nodes.shape[0]
    hbm = pl.BlockSpec(memory_space=pltpu.HBM)
    vmem = pl.BlockSpec(memory_space=pltpu.VMEM)
    return pl.pallas_call(
        functools.partial(prepare_body, nodes),
        out_shape=(
            jax.ShapeDtypeStruct((2 * EXPORTS, NODE_TOK, keys.shape[1]), keys.dtype),
            jax.ShapeDtypeStruct((2 + CHAIN,), jnp.int32),
        ),
        in_specs=[hbm, hbm, hbm, vmem, vmem],
        out_specs=(hbm, hbm),
        scratch_shapes=[
            pltpu.SMEM((slots,), jnp.int32),
            pltpu.SMEM((A_MAX, slots), jnp.int32),
            pltpu.SMEM((slots,), jnp.int32),
            pltpu.SMEM((2 + CHAIN,), jnp.int32),
            pltpu.SMEM((slots,), jnp.int32),
            pltpu.SMEM((slots,), jnp.int32),
            pltpu.SMEM((slots // nodes,), jnp.int32),
            pltpu.SemaphoreType.DMA((2 * EXPORTS + 4,)),
        ],
        compiler_params=pltpu.CompilerParams(vmem_limit_bytes=VMEM_LIMIT),
        name="prepare",
    )(slot_nodes, ancestors.T, depth, keys, values)


def attend_body(kv, parts, table, query_hbm, keys_hbm, values_hbm, got, *refs):
    out, query, keys, values, above_keys, above_values, all_keys, all_values, sem = refs[-9:]
    nodes = query.shape[0] // NODE_TOK
    group = query.shape[1] // HEAD
    per_part = query.shape[0] // parts
    side = all_keys.shape[0]
    lanes = pl.ds(kv * HEAD, HEAD)
    pairs = [(keys_hbm.at[:, lanes], keys), (values_hbm.at[:, lanes], values)]
    for step in range(CHAIN):
        entry = table[2 + step]
        pairs.append((got.at[entry, :, lanes], above_keys.at[step]))
        pairs.append((got.at[entry + EXPORTS, :, lanes], above_values.at[step]))
    pairs.append((query_hbm.at[:, pl.ds(kv * group * HEAD, group * HEAD)], query))
    copies = [
        pltpu.make_async_copy(source, target, sem.at[order])
        for order, (source, target) in enumerate(pairs)
    ]
    for copy in copies:
        copy.start()
    ones = jnp.ones((NODE_TOK, HEAD), all_values.dtype)
    nothing = jnp.zeros((NODE_TOK, 2 * HEAD), all_values.dtype)
    query_index = lax.broadcasted_iota(jnp.int32, (NODE_TOK, NODE_TOK), 0)
    key_index = lax.broadcasted_iota(jnp.int32, (NODE_TOK, NODE_TOK), 1)
    own_bias = jnp.where(key_index <= query_index, 0.0, DEAD)
    piece = math.gcd(NODE_TOK, per_part)
    pieces_part = per_part // piece
    me = lax.axis_index("tensor")
    above = (CHAIN + 1) * NODE_TOK
    for copy in copies:
        copy.wait()

    def node_rows(node):
        return pl.ds(pl.multiple_of(node * NODE_TOK, NODE_TOK), NODE_TOK)

    def put(place, order, key_block, value_block):
        rows = pl.ds(order * NODE_TOK, NODE_TOK)
        all_keys[place, rows, :] = key_block
        all_values[place, rows, :HEAD] = value_block
        all_values[place, rows, HEAD:] = ones

    def put_nothing(place, order, first_key):
        rows = pl.ds(order * NODE_TOK, NODE_TOK)
        all_keys[place, rows, :] = jnp.broadcast_to(first_key, (NODE_TOK, HEAD))
        all_values[place, rows, :] = nothing

    for place in range(side):
        for step in range(CHAIN):
            put(place, step, above_keys[step], above_values[step])

    def lay_out(place, node):
        own_key = keys[node_rows(node), :]
        put(place, CHAIN + 1, own_key, values[node_rows(node), :])
        for step in range(CHAIN):
            pl.when(step >= table[1])(functools.partial(put_nothing, place, step, own_key[:1]))
        is_root = node == table[0]
        pl.when(is_root)(functools.partial(put_nothing, place, CHAIN, own_key[:1]))

        @pl.when(jnp.logical_not(is_root))
        def _():
            put(place, CHAIN, keys[node_rows(table[0]), :], values[node_rows(table[0]), :])

    def score(place, node):
        stacked = jnp.concatenate(
            [query[node_rows(node), h * HEAD : (h + 1) * HEAD] for h in range(group)], 0
        )
        return times(stacked, all_keys[place])

    def weigh(scores):
        own = scores[:, above:] + jnp.concatenate([own_bias] * group, 0)
        masked = jnp.concatenate([scores[:, :above], own], 1)
        largest = jnp.max(masked, axis=1, keepdims=True)
        return jnp.exp2((masked - largest) * SCALE).astype(jnp.bfloat16)

    def finish(place, node, expo):
        mixed = jnp.dot(expo, all_values[place], preferred_element_type=jnp.float32)
        result = (mixed[:, :HEAD] / mixed[:, HEAD:]).astype(jnp.bfloat16)
        for part in range(NODE_TOK // piece):
            block = node * (NODE_TOK // piece) + part
            owner = block // pieces_part
            target = slot_position(parts, owner ^ me)
            inner = (block - owner * pieces_part) * piece
            to = pl.ds(pl.multiple_of(inner, piece), piece)
            for h in range(group):
                first = h * NODE_TOK + part * piece
                out[target, to, h * HEAD : (h + 1) * HEAD] = result[first : first + piece]

    def some_nodes(turn, carry):
        mine = [(place, turn * side + place) for place in range(side)]
        for place, node in mine:
            lay_out(place, node)
        scores = [score(place, node) for place, node in mine]
        for (place, node), each in zip(mine, scores):
            finish(place, node, weigh(each))
        return carry

    lax.fori_loop(0, nodes // side, some_nodes, 0)


def slot_position(parts, distance):
    half = parts // 2
    return jnp.where(distance % 2 == 1, distance // 2, half + distance // 2)


def attend(kv, table, queries, keys, values, got, parts, after):
    rows = queries.shape[0]
    width = queries.shape[1] // (keys.shape[1] // HEAD)
    total = (CHAIN + 2) * NODE_TOK
    side = 2 if rows % (2 * NODE_TOK) == 0 else 1
    hbm = pl.BlockSpec(memory_space=pltpu.HBM)
    return pl.pallas_call(
        functools.partial(attend_body, kv, parts),
        out_shape=jax.ShapeDtypeStruct((parts, rows // parts, width), queries.dtype),
        in_specs=[pl.BlockSpec(memory_space=pltpu.SMEM)]
        + [hbm] * 4
        + [pl.BlockSpec(memory_space=pl.ANY)] * len(after),
        scratch_shapes=[
            pltpu.VMEM((rows, width), queries.dtype),
            pltpu.VMEM((rows, HEAD), keys.dtype),
            pltpu.VMEM((rows, HEAD), keys.dtype),
            pltpu.VMEM((CHAIN, NODE_TOK, HEAD), keys.dtype),
            pltpu.VMEM((CHAIN, NODE_TOK, HEAD), keys.dtype),
            pltpu.VMEM((side, total, HEAD), keys.dtype),
            pltpu.VMEM((side, total, 2 * HEAD), keys.dtype),
            pltpu.SemaphoreType.DMA((3 + 2 * CHAIN,)),
        ],
        compiler_params=pltpu.CompilerParams(vmem_limit_bytes=ATTEND_LIMIT),
        cost_estimate=LIGHT,
        name="attend",
    )(table, queries, keys, values, got, *after)


def swap(array, axis, distance):
    size = lax.axis_size(axis)
    return lax.ppermute(array, axis, [(i, i ^ distance) for i in range(size)])


def times(rows, weight):
    return lax.dot_general(
        rows, weight, (((1,), (1,)), ((), ())), preferred_element_type=jnp.float32
    )


def is_middle(index):
    return (index == 1) | (index == 2)


def product(rows, weight, outs):
    half = rows[0].shape[0] // 2
    for start in (0, half):
        whole = jnp.concatenate([part[start : start + half, :] for part in rows], 1)
        for order, pair in enumerate(outs):
            out = pair[start // half]
            width = out.shape[1]
            out[...] = times(whole, weight[order * width : (order + 1) * width, :]).astype(out.dtype)


def core_sums(pairs, upper):
    half = pairs[0][0].shape[0] // 2
    rows = slice(half, 2 * half) if upper else slice(0, half)
    return jnp.concatenate(
        [k[rows, :].astype(jnp.float32) + c[rows, :].astype(jnp.float32) for k, c in pairs], 1
    )


def step_body(plan, *refs):
    refs = list(refs)
    take = lambda count: [refs.pop(0) for _ in range(count)]
    rows = [take(count) for count in plan["rows"]]
    weights = [take(count) for count in plan["weights"]]
    cores = [[take(2) for _ in range(count)] for count in plan["cores"]]
    chips = [([take(2) for _ in range(count)], take(1)[0]) for count in plan["chips"]]
    take(plan["after"])
    outs = take(plan["outs"])
    chosen, sem = refs[-2:] if 2 in plan["weights"] else (None, None)
    middle = is_middle(lax.axis_index("node"))
    for out, part in zip(outs[len(outs) - plan["held"] :], [x for parts in rows for x in parts]):
        out[...] = part[...]
    for bundle in weights:
        if len(bundle) == 2:
            for pick, source in zip((middle, jnp.logical_not(middle)), bundle):
                pl.when(pick)(pltpu.make_async_copy(source, chosen, sem).start)
    made = [outs.pop(0) for _ in rows for w in weights for _ in range(2 * plan["split"](w[0]))]
    for bundle in cores:
        out = outs.pop(0)
        out[...] = core_sums(bundle, True).astype(out.dtype)
    for bundle, from_chip in chips:
        out = outs.pop(0)
        out[...] = (core_sums(bundle, False) + from_chip[...].astype(jnp.float32)).astype(out.dtype)
    for weight in weights:
        source = weight[0]
        if len(weight) == 2:
            pltpu.make_async_copy(source, chosen, sem).wait()
            source = chosen
        for parts in rows:
            count = 2 * plan["split"](weight[0])
            product(parts, source, [made[i : i + 2] for i in range(0, count, 2)])
            made = made[count:]


def step(rows=(), weights=(), cores=(), chips=(), after=(), width=0, hold=False):
    weights = [w if isinstance(w, tuple) else (w,) for w in weights]
    plan = {
        "rows": [len(parts) for parts in rows],
        "weights": [len(weight) for weight in weights],
        "cores": [len(bundle) for bundle in cores],
        "chips": [len(bundle) - 1 for bundle in chips],
        "after": len(after),
        "split": lambda weight: weight.shape[0] // width,
    }
    shapes = []
    for weight in weights:
        for parts in rows:
            shapes += [(parts[0].shape[0] // 2, width)] * (2 * plan["split"](weight[0]))
    for bundle in (*cores, *[bundle[:-1] for bundle in chips]):
        features = sum(kept.shape[1] for kept, _ in bundle)
        shapes.append((bundle[0][0].shape[0] // 2, features))
    held = [part.shape for parts in rows for part in parts] if hold else []
    shapes += held
    plan["outs"], plan["held"] = len(shapes), len(held)
    vmem, hbm = pl.BlockSpec(memory_space=pltpu.VMEM), pl.BlockSpec(memory_space=pl.ANY)
    read = [(part, vmem) for parts in rows for part in parts]
    read += [(w, vmem if len(weight) == 1 else hbm) for weight in weights for w in weight]
    read += [(x, vmem) for bundle in cores for pair in bundle for x in pair]
    for bundle in chips:
        read += [(x, vmem) for pair in bundle[:-1] for x in pair] + [(bundle[-1], vmem)]
    read += [(x, hbm) for x in after]
    scratch = []
    if 2 in plan["weights"]:
        shape = [weight[0].shape for weight in weights if len(weight) == 2][0]
        scratch = [pltpu.VMEM(shape, read[0][0].dtype), pltpu.SemaphoreType.DMA]
    return pl.pallas_call(
        functools.partial(step_body, plan),
        out_shape=[jax.ShapeDtypeStruct(shape, read[0][0].dtype) for shape in shapes],
        in_specs=[spec for _, spec in read],
        scratch_shapes=scratch,
        compiler_params=pltpu.CompilerParams(vmem_limit_bytes=VMEM_LIMIT),
        cost_estimate=LIGHT,
        name="step",
    )(*[x for x, _ in read])


PAIRS = [(0, 1), (1, 0), (2, 3), (3, 2)]
MIDDLE = [(1, 2), (2, 1)]
OUTWARD = [(1, 0), (2, 3)]


def relay(piece, exported):
    near = lax.ppermute(piece, "node", PAIRS)
    across = lax.ppermute(piece, "node", MIDDLE)
    near, across, exported = lax.optimization_barrier((near, across, exported))
    across_out = lax.ppermute(across, "node", OUTWARD)
    near_across = lax.ppermute(near, "node", MIDDLE)
    return near, across, near_across, across_out


def place_body(spots, features, *refs):
    out = refs[-1]
    half = features // 2
    device = lax.axis_index("node")
    mine = lax.axis_index("groups")
    last = (core_sums([refs[:2]], False) + refs[2][...].astype(jnp.float32)).astype(out.dtype)
    for source, parts in zip((last, *refs[3:-1]), spots):
        start = 0
        for size, distance, side in parts:
            group = {"own": mine, "other": 1 - mine, "first": 0, "second": 1}[side]
            column = pl.multiple_of((device ^ distance) * features + group * half, HEAD)
            out[:, pl.ds(column, size)] = source[:, start : start + size]
            start += size


def place(last, sources, spots, devices, features):
    return pl.pallas_call(
        functools.partial(place_body, spots, features),
        out_shape=jax.ShapeDtypeStruct((last[2].shape[0], devices * features), last[2].dtype),
        compiler_params=pltpu.CompilerParams(vmem_limit_bytes=VMEM_LIMIT),
        name="place",
    )(*last, *sources)


def cut_body(weight, out, sem):
    half = out.shape[0]
    first = pl.multiple_of(lax.axis_index("groups") * half, half)
    copy = pltpu.make_async_copy(weight.at[pl.ds(first, half), :], out, sem)
    copy.start()
    copy.wait()


def cut(weight):
    return pl.pallas_call(
        cut_body,
        out_shape=jax.ShapeDtypeStruct((weight.shape[0] // 2, weight.shape[1]), weight.dtype),
        in_specs=[pl.BlockSpec(memory_space=pl.ANY)],
        out_specs=pl.BlockSpec(memory_space=pltpu.VMEM),
        scratch_shapes=[pltpu.SemaphoreType.DMA],
        compiler_params=pltpu.CompilerParams(vmem_limit_bytes=ATTEND_LIMIT),
        cost_estimate=LIGHT,
        name="cut",
    )(weight)


def project_split(halves, relayed, out_weight):
    features = out_weight.shape[0]
    half = features // 2
    rows = [part.reshape(-1, part.shape[-1]) for part in halves]
    other = [swap(part, "groups", 1) for part in rows]
    near, across, near_across, across_out = relayed
    second = (near_across, across_out)

    def core(sent):
        return swap(sent, "tensor", 1)

    def chip(away):
        return swap(away, "tensor", 2)

    def multiply(rows, weights, after=(), cores=(), chips=()):
        return step(rows, weights, cores, chips, after, half)

    far = (across, lax.ppermute(near_across, "node", OUTWARD))

    sent_a, kept_a, sent_b, kept_b, *rows = step([rows], [out_weight], width=half, hold=True)
    one = [(kept_a, core(sent_a))]
    (away,) = step(cores=[one])
    one.append(chip(away))
    sent_1, kept_1 = multiply([rows], [near], [away, other[0]])
    sent_2, kept_2, one_done = multiply([rows], [second], [sent_1], (), [one])
    two = [(kept_b, core(sent_b)), (kept_1, core(sent_1)), (kept_2, core(sent_2))]
    (away,) = step(cores=[two])
    two.append(chip(away))
    sent_3, kept_3, sent_4, kept_4 = multiply([other], [near, second], [away])
    three = [(kept_3, core(sent_3)), (kept_4, core(sent_4))]
    away, two_done = step(cores=[three], chips=[two])
    three.append(chip(away))
    sent_5, kept_5 = multiply([other], [far], [away])
    four = [(kept_5, core(sent_5))]
    (three_done,) = step(chips=[three], after=[sent_5])
    three_other = swap(three_done, "groups", 1)
    sent_6, kept_6 = multiply([rows], [far], [three_done])
    five = [(kept_6, core(sent_6))]
    (away,) = step(cores=[four], after=[sent_6])
    four.append(chip(away))
    (away,) = step(cores=[five], after=[away])
    five.append(chip(away))
    (four_done,) = step(chips=[four], after=[three_other])
    four_other = swap(four_done, "groups", 1)
    return place(
        (*five[0], five[1]),
        (one_done, two_done, three_other, four_other),
        (
            ((half, 3, "own"),),
            ((half, 0, "first"),),
            ((half, 0, "second"), (half, 1, "own"), (half, 2, "own")),
            ((half, 1, "other"), (half, 2, "other")),
            ((half, 3, "other"),),
        ),
        lax.axis_size("node"),
        features,
    )


def project_plain(halves, out_weight):
    attended = jnp.concatenate(halves, 2)
    parts, per_part, width = attended.shape
    me = lax.axis_index("tensor")
    order = slot_position(parts, jnp.arange(parts, dtype=jnp.int32) ^ me)
    rows = attended[order].reshape(parts * per_part, width)
    weight = lax.all_gather(out_weight, "node", axis=0, tiled=True)
    terms = times(rows, weight).astype(jnp.bfloat16)
    return lax.psum_scatter(terms, "tensor", scatter_dimension=0, tiled=True)


def local(queries, keys, values, out_weight, slot_nodes, ancestors, depth):
    parts = lax.axis_size("tensor")
    devices = lax.axis_size("node")
    features = out_weight.shape[0]
    kv_count = keys.shape[1] // HEAD
    relayed, after = None, []
    exported, table = prepare(slot_nodes, ancestors, depth, keys, values)
    got = lax.all_gather(exported, "node", axis=0, tiled=True)
    if (
        devices == 4
        and parts == 4
        and lax.axis_size("groups") == 2
        and features % (2 * HEAD) == 0
    ):
        relayed = relay(cut(out_weight), exported)
        after = relayed[:2]
    halves = []
    for kv in range(kv_count):
        halves.append(attend(kv, table, queries, keys, values, got, parts, after))
        after = halves[-1:]
    if relayed is None:
        return project_plain(halves, out_weight)
    return project_split(halves, relayed, out_weight)


def solution(mesh):
    placed = (
        P(("groups", "node"), "tensor"),
        P(("groups", "node"), "tensor"),
        P(("groups", "node"), "tensor"),
        P("node", "tensor"),
        P("groups"),
        P("groups", None),
        P("groups"),
    )
    return jax.shard_map(
        local,
        mesh=mesh,
        in_specs=placed,
        out_specs=P(("groups", "node", "tensor"), None),
        check_vma=False,
    )
```

```python
import functools
import math

import jax
import jax.numpy as jnp
from jax import lax
from jax.experimental import pallas as pl
from jax.experimental.pallas import tpu as pltpu
from jax.sharding import PartitionSpec as P

HEAD = 128
NODE_TOK = 128
A_MAX = 7
CHAIN = A_MAX - 1
EXPORTS = 2
SCALE = math.log2(math.e) / math.sqrt(HEAD)
DEAD = -1e30
LIGHT = pl.CostEstimate(flops=1, bytes_accessed=1, transcendentals=0)
VMEM_LIMIT = 20 * 1024 * 1024
ATTEND_LIMIT = 56 * 1024 * 1024


def prepare_body(nodes, *refs):
    slot_hbm, ancestors_hbm, depth_hbm, keys, values, exported, table_hbm = refs[:7]
    slot_nodes, ancestors, depth, table, holder, within, roots, sem = refs[7:]
    devices = slot_nodes.shape[0] // nodes
    me = lax.axis_index("node")
    fetches = [
        pltpu.make_async_copy(source, target, sem.at[2 * EXPORTS + 1 + order])
        for order, (source, target) in enumerate(
            ((slot_hbm, slot_nodes), (ancestors_hbm, ancestors), (depth_hbm, depth))
        )
    ]
    for fetch in fetches:
        fetch.start()
    for fetch in fetches:
        fetch.wait()

    def place(device, mine):
        root, root_index = jnp.int32(0), jnp.int32(0)
        for index in range(nodes):
            node = slot_nodes[device * nodes + index]
            holder[node] = device
            within[node] = index
            even = (depth[node] & 1) == 0
            root = jnp.where(even, node, root)
            root_index = jnp.where(even, index, root_index)
        roots[device] = root
        return jnp.where(device == me, root_index, mine)

    root = lax.fori_loop(0, devices, place, jnp.int32(0))

    def find_attach(device, attach):
        node = roots[device]
        level = depth[node]
        for step in range(0, CHAIN, 2):
            above = jnp.maximum(ancestors[step, node], 0)
            hit = (step < level) & (holder[above] == me)
            attach = jnp.where(hit, within[above], attach)
        return attach

    attach = lax.fori_loop(0, devices, find_attach, jnp.int32(0))
    copies = []
    for position, (source, index) in enumerate(
        ((keys, root), (keys, attach), (values, root), (values, attach))
    ):
        rows = pl.ds(pl.multiple_of(index * NODE_TOK, NODE_TOK), NODE_TOK)
        copies.append(
            pltpu.make_async_copy(source.at[rows, :], exported.at[position], sem.at[position])
        )
    for copy in copies:
        copy.start()
    root_node = roots[me]
    count = depth[root_node]
    table[0] = root
    table[1] = count
    for step in range(CHAIN):
        above = jnp.maximum(ancestors[step, root_node], 0)
        entry = holder[above] * (2 * EXPORTS) + (1 if step % 2 == 0 else 0)
        table[2 + step] = jnp.where(step < count, entry, 0)
    store = pltpu.make_async_copy(table, table_hbm, sem.at[2 * EXPORTS])
    store.start()
    for copy in (*copies, store):
        copy.wait()


def prepare(slot_nodes, ancestors, depth, keys, values):
    nodes = keys.shape[0] // NODE_TOK
    slots = slot_nodes.shape[0]
    hbm = pl.BlockSpec(memory_space=pltpu.HBM)
    vmem = pl.BlockSpec(memory_space=pltpu.VMEM)
    return pl.pallas_call(
        functools.partial(prepare_body, nodes),
        out_shape=(
            jax.ShapeDtypeStruct((2 * EXPORTS, NODE_TOK, keys.shape[1]), keys.dtype),
            jax.ShapeDtypeStruct((2 + CHAIN,), jnp.int32),
        ),
        in_specs=[hbm, hbm, hbm, vmem, vmem],
        out_specs=(hbm, hbm),
        scratch_shapes=[
            pltpu.SMEM((slots,), jnp.int32),
            pltpu.SMEM((A_MAX, slots), jnp.int32),
            pltpu.SMEM((slots,), jnp.int32),
            pltpu.SMEM((2 + CHAIN,), jnp.int32),
            pltpu.SMEM((slots,), jnp.int32),
            pltpu.SMEM((slots,), jnp.int32),
            pltpu.SMEM((slots // nodes,), jnp.int32),
            pltpu.SemaphoreType.DMA((2 * EXPORTS + 4,)),
        ],
        compiler_params=pltpu.CompilerParams(vmem_limit_bytes=VMEM_LIMIT),
        name="prepare",
    )(slot_nodes, ancestors.T, depth, keys, values)


def attend_body(kv, parts, table, query_hbm, keys_hbm, values_hbm, got, *refs):
    out, query, keys, values, above_keys, above_values, all_keys, all_values, sem = refs[-9:]
    nodes = query.shape[0] // NODE_TOK
    group = query.shape[1] // HEAD
    per_part = query.shape[0] // parts
    side = all_keys.shape[0]
    lanes = pl.ds(kv * HEAD, HEAD)
    pairs = [(keys_hbm.at[:, lanes], keys), (values_hbm.at[:, lanes], values)]
    for step in range(CHAIN):
        entry = table[2 + step]
        pairs.append((got.at[entry, :, lanes], above_keys.at[step]))
        pairs.append((got.at[entry + EXPORTS, :, lanes], above_values.at[step]))
    pairs.append((query_hbm.at[:, pl.ds(kv * group * HEAD, group * HEAD)], query))
    copies = [
        pltpu.make_async_copy(source, target, sem.at[order])
        for order, (source, target) in enumerate(pairs)
    ]
    for copy in copies:
        copy.start()
    ones = jnp.ones((NODE_TOK, HEAD), all_values.dtype)
    nothing = jnp.zeros((NODE_TOK, 2 * HEAD), all_values.dtype)
    query_index = lax.broadcasted_iota(jnp.int32, (NODE_TOK, NODE_TOK), 0)
    key_index = lax.broadcasted_iota(jnp.int32, (NODE_TOK, NODE_TOK), 1)
    own_bias = jnp.where(key_index <= query_index, 0.0, DEAD)
    piece = math.gcd(NODE_TOK, per_part)
    pieces_part = per_part // piece
    me = lax.axis_index("tensor")
    above = (CHAIN + 1) * NODE_TOK
    for copy in copies:
        copy.wait()

    def node_rows(node):
        return pl.ds(pl.multiple_of(node * NODE_TOK, NODE_TOK), NODE_TOK)

    def put(place, order, key_block, value_block):
        rows = pl.ds(order * NODE_TOK, NODE_TOK)
        all_keys[place, rows, :] = key_block
        all_values[place, rows, :HEAD] = value_block
        all_values[place, rows, HEAD:] = ones

    def put_nothing(place, order, first_key):
        rows = pl.ds(order * NODE_TOK, NODE_TOK)
        all_keys[place, rows, :] = jnp.broadcast_to(first_key, (NODE_TOK, HEAD))
        all_values[place, rows, :] = nothing

    for place in range(side):
        for step in range(CHAIN):
            put(place, step, above_keys[step], above_values[step])

    def lay_out(place, node):
        own_key = keys[node_rows(node), :]
        put(place, CHAIN + 1, own_key, values[node_rows(node), :])
        for step in range(CHAIN):
            pl.when(step >= table[1])(functools.partial(put_nothing, place, step, own_key[:1]))
        is_root = node == table[0]
        pl.when(is_root)(functools.partial(put_nothing, place, CHAIN, own_key[:1]))

        @pl.when(jnp.logical_not(is_root))
        def _():
            put(place, CHAIN, keys[node_rows(table[0]), :], values[node_rows(table[0]), :])

    def score(place, node):
        stacked = jnp.concatenate(
            [query[node_rows(node), h * HEAD : (h + 1) * HEAD] for h in range(group)], 0
        )
        return times(stacked, all_keys[place])

    def weigh(scores):
        own = scores[:, above:] + jnp.concatenate([own_bias] * group, 0)
        masked = jnp.concatenate([scores[:, :above], own], 1)
        largest = jnp.max(masked, axis=1, keepdims=True)
        return jnp.exp2((masked - largest) * SCALE).astype(jnp.bfloat16)

    def finish(place, node, expo):
        mixed = jnp.dot(expo, all_values[place], preferred_element_type=jnp.float32)
        result = (mixed[:, :HEAD] / mixed[:, HEAD:]).astype(jnp.bfloat16)
        for part in range(NODE_TOK // piece):
            block = node * (NODE_TOK // piece) + part
            owner = block // pieces_part
            target = slot_position(parts, owner ^ me)
            inner = (block - owner * pieces_part) * piece
            to = pl.ds(pl.multiple_of(inner, piece), piece)
            for h in range(group):
                first = h * NODE_TOK + part * piece
                out[target, to, h * HEAD : (h + 1) * HEAD] = result[first : first + piece]

    def some_nodes(turn, carry):
        mine = [(place, turn * side + place) for place in range(side)]
        for place, node in mine:
            lay_out(place, node)
        scores = [score(place, node) for place, node in mine]
        for (place, node), each in zip(mine, scores):
            finish(place, node, weigh(each))
        return carry

    lax.fori_loop(0, nodes // side, some_nodes, 0)


def slot_position(parts, distance):
    half = parts // 2
    return jnp.where(distance % 2 == 1, distance // 2, half + distance // 2)


def attend(kv, table, queries, keys, values, got, parts, after):
    rows = queries.shape[0]
    width = queries.shape[1] // (keys.shape[1] // HEAD)
    total = (CHAIN + 2) * NODE_TOK
    side = 2 if rows % (2 * NODE_TOK) == 0 else 1
    hbm = pl.BlockSpec(memory_space=pltpu.HBM)
    return pl.pallas_call(
        functools.partial(attend_body, kv, parts),
        out_shape=jax.ShapeDtypeStruct((parts, rows // parts, width), queries.dtype),
        in_specs=[pl.BlockSpec(memory_space=pltpu.SMEM)]
        + [hbm] * 4
        + [pl.BlockSpec(memory_space=pl.ANY)] * len(after),
        scratch_shapes=[
            pltpu.VMEM((rows, width), queries.dtype),
            pltpu.VMEM((rows, HEAD), keys.dtype),
            pltpu.VMEM((rows, HEAD), keys.dtype),
            pltpu.VMEM((CHAIN, NODE_TOK, HEAD), keys.dtype),
            pltpu.VMEM((CHAIN, NODE_TOK, HEAD), keys.dtype),
            pltpu.VMEM((side, total, HEAD), keys.dtype),
            pltpu.VMEM((side, total, 2 * HEAD), keys.dtype),
            pltpu.SemaphoreType.DMA((3 + 2 * CHAIN,)),
        ],
        compiler_params=pltpu.CompilerParams(vmem_limit_bytes=ATTEND_LIMIT),
        cost_estimate=LIGHT,
        name="attend",
    )(table, queries, keys, values, got, *after)


def swap(array, axis, distance):
    size = lax.axis_size(axis)
    return lax.ppermute(array, axis, [(i, i ^ distance) for i in range(size)])


def times(rows, weight):
    return lax.dot_general(
        rows, weight, (((1,), (1,)), ((), ())), preferred_element_type=jnp.float32
    )


def is_middle(index):
    return (index == 1) | (index == 2)


def product(rows, weight, outs):
    half = rows[0].shape[0] // 2
    for start in (0, half):
        whole = jnp.concatenate([part[start : start + half, :] for part in rows], 1)
        for order, pair in enumerate(outs):
            out = pair[start // half]
            width = out.shape[1]
            out[...] = times(whole, weight[order * width : (order + 1) * width, :]).astype(out.dtype)


def core_sums(pairs, upper):
    half = pairs[0][0].shape[0] // 2
    rows = slice(half, 2 * half) if upper else slice(0, half)
    return jnp.concatenate(
        [k[rows, :].astype(jnp.float32) + c[rows, :].astype(jnp.float32) for k, c in pairs], 1
    )


def step_body(plan, *refs):
    refs = list(refs)
    take = lambda count: [refs.pop(0) for _ in range(count)]
    rows = [take(count) for count in plan["rows"]]
    weights = [take(count) for count in plan["weights"]]
    cores = [[take(2) for _ in range(count)] for count in plan["cores"]]
    chips = [([take(2) for _ in range(count)], take(1)[0]) for count in plan["chips"]]
    take(plan["after"])
    outs = take(plan["outs"])
    fetched = 2 in plan["weights"] and not plan["direct"]
    chosen, sem = refs[-2:] if fetched else (None, None)
    middle = is_middle(lax.axis_index("node"))
    for out, part in zip(outs[len(outs) - plan["held"] :], [x for parts in rows for x in parts]):
        out[...] = part[...]
    for bundle in weights:
        if len(bundle) == 2 and fetched:
            for pick, source in zip((middle, jnp.logical_not(middle)), bundle):
                pl.when(pick)(pltpu.make_async_copy(source, chosen, sem).start)
    made = [outs.pop(0) for _ in rows for w in weights for _ in range(2 * plan["split"](w[0]))]
    for bundle in cores:
        out = outs.pop(0)
        out[...] = core_sums(bundle, True).astype(out.dtype)
    for bundle, from_chip in chips:
        out = outs.pop(0)
        out[...] = (core_sums(bundle, False) + from_chip[...].astype(jnp.float32)).astype(out.dtype)
    for weight in weights:
        source = weight[0]
        if len(weight) == 2 and fetched:
            pltpu.make_async_copy(source, chosen, sem).wait()
            source = chosen
        for parts in rows:
            count = 2 * plan["split"](weight[0])
            pairs = [made[i : i + 2] for i in range(0, count, 2)]
            made = made[count:]
            if len(weight) == 2 and not fetched:
                for pick, source in zip((middle, jnp.logical_not(middle)), weight):
                    pl.when(pick)(functools.partial(product, parts, source, pairs))
            else:
                product(parts, source, pairs)


def step(rows=(), weights=(), cores=(), chips=(), after=(), width=0, hold=False, direct=False):
    weights = [w if isinstance(w, tuple) else (w,) for w in weights]
    plan = {
        "rows": [len(parts) for parts in rows],
        "weights": [len(weight) for weight in weights],
        "cores": [len(bundle) for bundle in cores],
        "chips": [len(bundle) - 1 for bundle in chips],
        "after": len(after),
        "direct": direct,
        "split": lambda weight: weight.shape[0] // width,
    }
    shapes = []
    for weight in weights:
        for parts in rows:
            shapes += [(parts[0].shape[0] // 2, width)] * (2 * plan["split"](weight[0]))
    for bundle in (*cores, *[bundle[:-1] for bundle in chips]):
        features = sum(kept.shape[1] for kept, _ in bundle)
        shapes.append((bundle[0][0].shape[0] // 2, features))
    held = [part.shape for parts in rows for part in parts] if hold else []
    shapes += held
    plan["outs"], plan["held"] = len(shapes), len(held)
    vmem, hbm = pl.BlockSpec(memory_space=pltpu.VMEM), pl.BlockSpec(memory_space=pl.ANY)
    read = [(part, vmem) for parts in rows for part in parts]
    where = {1: vmem, 2: vmem if direct else hbm}
    read += [(w, where[len(weight)]) for weight in weights for w in weight]
    read += [(x, vmem) for bundle in cores for pair in bundle for x in pair]
    for bundle in chips:
        read += [(x, vmem) for pair in bundle[:-1] for x in pair] + [(bundle[-1], vmem)]
    read += [(x, hbm) for x in after]
    scratch = []
    if 2 in plan["weights"] and not direct:
        shape = [weight[0].shape for weight in weights if len(weight) == 2][0]
        scratch = [pltpu.VMEM(shape, read[0][0].dtype), pltpu.SemaphoreType.DMA]
    return pl.pallas_call(
        functools.partial(step_body, plan),
        out_shape=[jax.ShapeDtypeStruct(shape, read[0][0].dtype) for shape in shapes],
        in_specs=[spec for _, spec in read],
        scratch_shapes=scratch,
        compiler_params=pltpu.CompilerParams(vmem_limit_bytes=VMEM_LIMIT),
        cost_estimate=LIGHT,
        name="step",
    )(*[x for x, _ in read])


PAIRS = [(0, 1), (1, 0), (2, 3), (3, 2)]
MIDDLE = [(1, 2), (2, 1)]
OUTWARD = [(1, 0), (2, 3)]


def relay(piece, exported):
    near = lax.ppermute(piece, "node", PAIRS)
    across = lax.ppermute(piece, "node", MIDDLE)
    near, across, exported = lax.optimization_barrier((near, across, exported))
    across_out = lax.ppermute(across, "node", OUTWARD)
    near_across = lax.ppermute(near, "node", MIDDLE)
    return near, across, near_across, across_out


def place_body(spots, features, *refs):
    out = refs[-1]
    half = features // 2
    device = lax.axis_index("node")
    mine = lax.axis_index("groups")
    last = (core_sums([refs[:2]], False) + refs[2][...].astype(jnp.float32)).astype(out.dtype)
    for source, parts in zip((last, *refs[3:-1]), spots):
        start = 0
        for size, distance, side in parts:
            group = {"own": mine, "other": 1 - mine, "first": 0, "second": 1}[side]
            column = pl.multiple_of((device ^ distance) * features + group * half, HEAD)
            out[:, pl.ds(column, size)] = source[:, start : start + size]
            start += size


def place(last, sources, spots, devices, features):
    return pl.pallas_call(
        functools.partial(place_body, spots, features),
        out_shape=jax.ShapeDtypeStruct((last[2].shape[0], devices * features), last[2].dtype),
        compiler_params=pltpu.CompilerParams(vmem_limit_bytes=VMEM_LIMIT),
        name="place",
    )(*last, *sources)


def cut_body(weight, out, sem):
    half = out.shape[0]
    first = pl.multiple_of(lax.axis_index("groups") * half, half)
    copy = pltpu.make_async_copy(weight.at[pl.ds(first, half), :], out, sem)
    copy.start()
    copy.wait()


def cut(weight):
    return pl.pallas_call(
        cut_body,
        out_shape=jax.ShapeDtypeStruct((weight.shape[0] // 2, weight.shape[1]), weight.dtype),
        in_specs=[pl.BlockSpec(memory_space=pl.ANY)],
        out_specs=pl.BlockSpec(memory_space=pltpu.VMEM),
        scratch_shapes=[pltpu.SemaphoreType.DMA],
        compiler_params=pltpu.CompilerParams(vmem_limit_bytes=ATTEND_LIMIT),
        cost_estimate=LIGHT,
        name="cut",
    )(weight)


def project_split(halves, relayed, out_weight):
    features = out_weight.shape[0]
    half = features // 2
    rows = [part.reshape(-1, part.shape[-1]) for part in halves]
    other = [swap(part, "groups", 1) for part in rows]
    near, across, near_across, across_out = relayed
    second = (near_across, across_out)

    def core(sent):
        return swap(sent, "tensor", 1)

    def chip(away):
        return swap(away, "tensor", 2)

    def multiply(rows, weights, after=(), cores=(), chips=(), direct=False):
        return step(rows, weights, cores, chips, after, half, direct=direct)

    far = (across, lax.ppermute(near_across, "node", OUTWARD))

    sent_a, kept_a, sent_b, kept_b, *rows = step([rows], [out_weight], width=half, hold=True)
    one = [(kept_a, core(sent_a))]
    (away,) = step(cores=[one])
    one.append(chip(away))
    sent_1, kept_1 = multiply([rows], [near], [away, other[0]])
    sent_2, kept_2, one_done = multiply([rows], [second], [sent_1], (), [one])
    two = [(kept_b, core(sent_b)), (kept_1, core(sent_1)), (kept_2, core(sent_2))]
    (away,) = step(cores=[two])
    two.append(chip(away))
    sent_3, kept_3, sent_4, kept_4 = multiply([other], [near, second], [away])
    three = [(kept_3, core(sent_3))]
    four = [(kept_4, core(sent_4))]
    away, two_done = step(cores=[three], chips=[two])
    three.append(chip(away))
    away, three_done = step(cores=[four], chips=[three])
    four.append(chip(away))
    three_other = swap(three_done, "groups", 1)
    sent_5, kept_5 = multiply([other], [far], [away], direct=True)
    five = [(kept_5, core(sent_5))]
    (four_done,) = step(chips=[four], after=[sent_5, three_other])
    four_other = swap(four_done, "groups", 1)
    sent_6, kept_6 = multiply([rows], [far], [four_done], direct=True)
    six = [(kept_6, core(sent_6))]
    (away,) = step(cores=[five], after=[sent_6])
    five.append(chip(away))
    (away,) = step(cores=[six], after=[away, four_other])
    six.append(chip(away))
    (five_done,) = step(chips=[five])
    five_other = swap(five_done, "groups", 1)
    return place(
        (*six[0], six[1]),
        (one_done, two_done, three_other, four_other, five_other),
        (
            ((half, 3, "own"),),
            ((half, 0, "first"),),
            ((half, 0, "second"), (half, 1, "own"), (half, 2, "own")),
            ((half, 1, "other"),),
            ((half, 2, "other"),),
            ((half, 3, "other"),),
        ),
        lax.axis_size("node"),
        features,
    )


def project_plain(halves, out_weight):
    attended = jnp.concatenate(halves, 2)
    parts, per_part, width = attended.shape
    me = lax.axis_index("tensor")
    order = slot_position(parts, jnp.arange(parts, dtype=jnp.int32) ^ me)
    rows = attended[order].reshape(parts * per_part, width)
    weight = lax.all_gather(out_weight, "node", axis=0, tiled=True)
    terms = times(rows, weight).astype(jnp.bfloat16)
    return lax.psum_scatter(terms, "tensor", scatter_dimension=0, tiled=True)


def local(queries, keys, values, out_weight, slot_nodes, ancestors, depth):
    parts = lax.axis_size("tensor")
    devices = lax.axis_size("node")
    features = out_weight.shape[0]
    kv_count = keys.shape[1] // HEAD
    relayed, after = None, []
    exported, table = prepare(slot_nodes, ancestors, depth, keys, values)
    got = lax.all_gather(exported, "node", axis=0, tiled=True)
    if (
        devices == 4
        and parts == 4
        and lax.axis_size("groups") == 2
        and features % (2 * HEAD) == 0
    ):
        relayed = relay(cut(out_weight), exported)
        after = relayed[:2]
    halves = []
    for kv in range(kv_count):
        halves.append(attend(kv, table, queries, keys, values, got, parts, after))
        after = halves[-1:]
    if relayed is None:
        return project_plain(halves, out_weight)
    return project_split(halves, relayed, out_weight)


def solution(mesh):
    placed = (
        P(("groups", "node"), "tensor"),
        P(("groups", "node"), "tensor"),
        P(("groups", "node"), "tensor"),
        P("node", "tensor"),
        P("groups"),
        P("groups", None),
        P("groups"),
    )
    return jax.shard_map(
        local,
        mesh=mesh,
        in_specs=placed,
        out_specs=P(("groups", "node", "tensor"), None),
        check_vma=False,
    )
```

```python
import functools
import math

import jax
import jax.numpy as jnp
from jax import lax
from jax.experimental import pallas as pl
from jax.experimental.pallas import tpu as pltpu
from jax.sharding import PartitionSpec as P

HEAD = 128
NODE_TOK = 128
A_MAX = 7
CHAIN = A_MAX - 1
EXPORTS = 2
SCALE = math.log2(math.e) / math.sqrt(HEAD)
DEAD = -1e30
LIGHT = pl.CostEstimate(flops=1, bytes_accessed=1, transcendentals=0)
VMEM_LIMIT = 20 * 1024 * 1024
ATTEND_LIMIT = 56 * 1024 * 1024


def prepare_body(nodes, *refs):
    slot_hbm, ancestors_hbm, depth_hbm, keys, values, exported, table_hbm = refs[:7]
    slot_nodes, ancestors, depth, table, holder, within, roots, sem = refs[7:]
    devices = slot_nodes.shape[0] // nodes
    me = lax.axis_index("node")
    fetches = [
        pltpu.make_async_copy(source, target, sem.at[2 * EXPORTS + 1 + order])
        for order, (source, target) in enumerate(
            ((slot_hbm, slot_nodes), (ancestors_hbm, ancestors), (depth_hbm, depth))
        )
    ]
    for fetch in fetches:
        fetch.start()
    for fetch in fetches:
        fetch.wait()

    def place(device, mine):
        root, root_index = jnp.int32(0), jnp.int32(0)
        for index in range(nodes):
            node = slot_nodes[device * nodes + index]
            holder[node] = device
            within[node] = index
            even = (depth[node] & 1) == 0
            root = jnp.where(even, node, root)
            root_index = jnp.where(even, index, root_index)
        roots[device] = root
        return jnp.where(device == me, root_index, mine)

    root = lax.fori_loop(0, devices, place, jnp.int32(0))

    def find_attach(device, attach):
        node = roots[device]
        level = depth[node]
        for step in range(0, CHAIN, 2):
            above = jnp.maximum(ancestors[step, node], 0)
            hit = (step < level) & (holder[above] == me)
            attach = jnp.where(hit, within[above], attach)
        return attach

    attach = lax.fori_loop(0, devices, find_attach, jnp.int32(0))
    copies = []
    for position, (source, index) in enumerate(
        ((keys, root), (keys, attach), (values, root), (values, attach))
    ):
        rows = pl.ds(pl.multiple_of(index * NODE_TOK, NODE_TOK), NODE_TOK)
        copies.append(
            pltpu.make_async_copy(source.at[rows, :], exported.at[position], sem.at[position])
        )
    for copy in copies:
        copy.start()
    root_node = roots[me]
    count = depth[root_node]
    table[0] = root
    table[1] = count
    for step in range(CHAIN):
        above = jnp.maximum(ancestors[step, root_node], 0)
        entry = holder[above] * (2 * EXPORTS) + (1 if step % 2 == 0 else 0)
        table[2 + step] = jnp.where(step < count, entry, 0)
    store = pltpu.make_async_copy(table, table_hbm, sem.at[2 * EXPORTS])
    store.start()
    for copy in (*copies, store):
        copy.wait()


def prepare(slot_nodes, ancestors, depth, keys, values):
    nodes = keys.shape[0] // NODE_TOK
    slots = slot_nodes.shape[0]
    hbm = pl.BlockSpec(memory_space=pltpu.HBM)
    vmem = pl.BlockSpec(memory_space=pltpu.VMEM)
    return pl.pallas_call(
        functools.partial(prepare_body, nodes),
        out_shape=(
            jax.ShapeDtypeStruct((2 * EXPORTS, NODE_TOK, keys.shape[1]), keys.dtype),
            jax.ShapeDtypeStruct((2 + CHAIN,), jnp.int32),
        ),
        in_specs=[hbm, hbm, hbm, vmem, vmem],
        out_specs=(hbm, hbm),
        scratch_shapes=[
            pltpu.SMEM((slots,), jnp.int32),
            pltpu.SMEM((A_MAX, slots), jnp.int32),
            pltpu.SMEM((slots,), jnp.int32),
            pltpu.SMEM((2 + CHAIN,), jnp.int32),
            pltpu.SMEM((slots,), jnp.int32),
            pltpu.SMEM((slots,), jnp.int32),
            pltpu.SMEM((slots // nodes,), jnp.int32),
            pltpu.SemaphoreType.DMA((2 * EXPORTS + 4,)),
        ],
        compiler_params=pltpu.CompilerParams(vmem_limit_bytes=VMEM_LIMIT),
        name="prepare",
    )(slot_nodes, ancestors.T, depth, keys, values)


def attend_body(kv, parts, table, query_hbm, keys_hbm, values_hbm, got, *refs):
    out, query, keys, values, above_keys, above_values, all_keys, all_values, sem = refs[-9:]
    nodes = query.shape[0] // NODE_TOK
    group = query.shape[1] // HEAD
    per_part = query.shape[0] // parts
    side = all_keys.shape[0]
    lanes = pl.ds(kv * HEAD, HEAD)
    pairs = [(keys_hbm.at[:, lanes], keys), (values_hbm.at[:, lanes], values)]
    for step in range(CHAIN):
        entry = table[2 + step]
        pairs.append((got.at[entry, :, lanes], above_keys.at[step]))
        pairs.append((got.at[entry + EXPORTS, :, lanes], above_values.at[step]))
    pairs.append((query_hbm.at[:, pl.ds(kv * group * HEAD, group * HEAD)], query))
    copies = [
        pltpu.make_async_copy(source, target, sem.at[order])
        for order, (source, target) in enumerate(pairs)
    ]
    for copy in copies:
        copy.start()
    ones = jnp.ones((NODE_TOK, HEAD), all_values.dtype)
    nothing = jnp.zeros((NODE_TOK, 2 * HEAD), all_values.dtype)
    query_index = lax.broadcasted_iota(jnp.int32, (NODE_TOK, NODE_TOK), 0)
    key_index = lax.broadcasted_iota(jnp.int32, (NODE_TOK, NODE_TOK), 1)
    own_bias = jnp.where(key_index <= query_index, 0.0, DEAD)
    piece = math.gcd(NODE_TOK, per_part)
    pieces_part = per_part // piece
    me = lax.axis_index("tensor")
    above = (CHAIN + 1) * NODE_TOK
    for copy in copies:
        copy.wait()

    def node_rows(node):
        return pl.ds(pl.multiple_of(node * NODE_TOK, NODE_TOK), NODE_TOK)

    def put(place, order, key_block, value_block):
        rows = pl.ds(order * NODE_TOK, NODE_TOK)
        all_keys[place, rows, :] = key_block
        all_values[place, rows, :HEAD] = value_block
        all_values[place, rows, HEAD:] = ones

    def put_nothing(place, order, first_key):
        rows = pl.ds(order * NODE_TOK, NODE_TOK)
        all_keys[place, rows, :] = jnp.broadcast_to(first_key, (NODE_TOK, HEAD))
        all_values[place, rows, :] = nothing

    for place in range(side):
        for step in range(CHAIN):
            put(place, step, above_keys[step], above_values[step])

    def lay_out(place, node):
        own_key = keys[node_rows(node), :]
        put(place, CHAIN + 1, own_key, values[node_rows(node), :])
        for step in range(CHAIN):
            pl.when(step >= table[1])(functools.partial(put_nothing, place, step, own_key[:1]))
        is_root = node == table[0]
        pl.when(is_root)(functools.partial(put_nothing, place, CHAIN, own_key[:1]))

        @pl.when(jnp.logical_not(is_root))
        def _():
            put(place, CHAIN, keys[node_rows(table[0]), :], values[node_rows(table[0]), :])

    def score(place, node):
        stacked = jnp.concatenate(
            [query[node_rows(node), h * HEAD : (h + 1) * HEAD] for h in range(group)], 0
        )
        return times(stacked, all_keys[place])

    def weigh(scores):
        own = scores[:, above:] + jnp.concatenate([own_bias] * group, 0)
        masked = jnp.concatenate([scores[:, :above], own], 1)
        largest = jnp.max(masked, axis=1, keepdims=True)
        return jnp.exp2((masked - largest) * SCALE).astype(jnp.bfloat16)

    def finish(place, node, expo):
        mixed = jnp.dot(expo, all_values[place], preferred_element_type=jnp.float32)
        result = (mixed[:, :HEAD] / mixed[:, HEAD:]).astype(jnp.bfloat16)
        for part in range(NODE_TOK // piece):
            block = node * (NODE_TOK // piece) + part
            owner = block // pieces_part
            target = slot_position(parts, owner ^ me)
            inner = (block - owner * pieces_part) * piece
            to = pl.ds(pl.multiple_of(inner, piece), piece)
            for h in range(group):
                first = h * NODE_TOK + part * piece
                out[target, to, h * HEAD : (h + 1) * HEAD] = result[first : first + piece]

    def some_nodes(turn, carry):
        mine = [(place, turn * side + place) for place in range(side)]
        for place, node in mine:
            lay_out(place, node)
        scores = [score(place, node) for place, node in mine]
        for (place, node), each in zip(mine, scores):
            finish(place, node, weigh(each))
        return carry

    lax.fori_loop(0, nodes // side, some_nodes, 0)


def slot_position(parts, distance):
    half = parts // 2
    return jnp.where(distance % 2 == 1, distance // 2, half + distance // 2)


def attend(kv, table, queries, keys, values, got, parts, after):
    rows = queries.shape[0]
    width = queries.shape[1] // (keys.shape[1] // HEAD)
    total = (CHAIN + 2) * NODE_TOK
    side = 2 if rows % (2 * NODE_TOK) == 0 else 1
    hbm = pl.BlockSpec(memory_space=pltpu.HBM)
    return pl.pallas_call(
        functools.partial(attend_body, kv, parts),
        out_shape=jax.ShapeDtypeStruct((parts, rows // parts, width), queries.dtype),
        in_specs=[pl.BlockSpec(memory_space=pltpu.SMEM)]
        + [hbm] * 4
        + [pl.BlockSpec(memory_space=pl.ANY)] * len(after),
        scratch_shapes=[
            pltpu.VMEM((rows, width), queries.dtype),
            pltpu.VMEM((rows, HEAD), keys.dtype),
            pltpu.VMEM((rows, HEAD), keys.dtype),
            pltpu.VMEM((CHAIN, NODE_TOK, HEAD), keys.dtype),
            pltpu.VMEM((CHAIN, NODE_TOK, HEAD), keys.dtype),
            pltpu.VMEM((side, total, HEAD), keys.dtype),
            pltpu.VMEM((side, total, 2 * HEAD), keys.dtype),
            pltpu.SemaphoreType.DMA((3 + 2 * CHAIN,)),
        ],
        compiler_params=pltpu.CompilerParams(vmem_limit_bytes=ATTEND_LIMIT),
        cost_estimate=LIGHT,
        name="attend",
    )(table, queries, keys, values, got, *after)


def swap(array, axis, distance):
    size = lax.axis_size(axis)
    return lax.ppermute(array, axis, [(i, i ^ distance) for i in range(size)])


def times(rows, weight):
    return lax.dot_general(
        rows, weight, (((1,), (1,)), ((), ())), preferred_element_type=jnp.float32
    )


def is_middle(index):
    return (index == 1) | (index == 2)


def product(parts, pieces, sent, kept):
    half = parts[0].shape[0] // 2
    for out, start in ((sent, 0), (kept, half)):
        whole = jnp.concatenate([part[start : start + half, :] for part in parts], 1)
        column = 0
        for weight, first, count in pieces:
            out[:, column : column + count] = times(
                whole, weight[first : first + count, :]
            ).astype(out.dtype)
            column += count


def core_sum(pair, upper):
    kept, from_core = pair
    half = kept.shape[0] // 2
    rows = slice(half, 2 * half) if upper else slice(0, half)
    return kept[rows, :].astype(jnp.float32) + from_core[rows, :].astype(jnp.float32)


def step_body(plan, *refs):
    refs = list(refs)

    def take(count):
        return [refs.pop(0) for _ in range(count)]

    rows = [take(count) for count in plan["rows"]]
    arrays = take(plan["arrays"])
    weights = [
        [[(arrays[index], first, count) for index, first, count in pieces] for pieces in weight]
        for weight in plan["weights"]
    ]
    cores = [[take(2) for _ in range(count)] for count in plan["cores"]]
    chips = [([take(2) for _ in range(count)], take(1)[0]) for count in plan["chips"]]
    take(plan["after"])
    outs = take(plan["outs"])
    middle = is_middle(lax.axis_index("node"))
    picks = (middle, jnp.logical_not(middle))
    fetched = None
    for order, weight in enumerate(weights):
        if len(weight) == 2 and not plan["direct"]:
            chosen, sem = refs
            fetched = order
            for pick, pieces in zip(picks, weight):
                column = 0
                for array, first, count in pieces:
                    source = array.at[pl.ds(first, count), :]
                    target = chosen.at[pl.ds(column, count), :]
                    pl.when(pick)(pltpu.make_async_copy(source, target, sem).start)
                    column += count
    made = [[(outs.pop(0), outs.pop(0)) for _ in rows] for _ in weights]
    if plan["hold"]:
        for part in [x for parts in rows for x in parts]:
            out = outs.pop(0)
            out[...] = part[...]
    for bundle in cores:
        out, column = outs.pop(0), 0
        for pair in bundle:
            width = pair[0].shape[1]
            out[:, column : column + width] = core_sum(pair, True).astype(out.dtype)
            column += width
    for bundle, from_chip in chips:
        column = 0
        for pair in bundle:
            out = outs.pop(0)
            width = out.shape[1]
            away = from_chip[:, column : column + width].astype(jnp.float32)
            out[...] = (core_sum(pair, False) + away).astype(out.dtype)
            column += width
    for order, (weight, pairs) in enumerate(zip(weights, made)):
        if order == fetched:
            pltpu.make_async_copy(chosen, chosen, sem).wait()
            weight = [[(chosen, 0, chosen.shape[0])]]
        for parts, (sent, kept) in zip(rows, pairs):
            if len(weight) == 2:
                for pick, pieces in zip(picks, weight):
                    pl.when(pick)(functools.partial(product, parts, pieces, sent, kept))
            else:
                product(parts, weight[0], sent, kept)


def step(rows=(), weights=(), cores=(), chips=(), after=(), hold=False, direct=False):
    weights = [weight if isinstance(weight, tuple) else (weight,) for weight in weights]
    arrays, fetch, plans = [], [], []
    for weight in weights:
        plans.append([])
        for pieces in weight:
            plans[-1].append([])
            for array, first, count in pieces:
                known = [index for index, x in enumerate(arrays) if x is array]
                if not known:
                    known = [len(arrays)]
                    arrays.append(array)
                    fetch.append(len(weight) == 2 and not direct)
                plans[-1][-1].append((known[0], first, count))
    widths = [sum(count for _, _, count in weight[0]) for weight in weights]
    shapes = []
    for width in widths:
        shapes += [(parts[0].shape[0] // 2, width) for parts in rows for _ in range(2)]
    if hold:
        shapes += [part.shape for parts in rows for part in parts]
    for bundle in cores:
        shapes.append((bundle[0][0].shape[0] // 2, sum(kept.shape[1] for kept, _ in bundle)))
    for bundle in chips:
        shapes += [(kept.shape[0] // 2, kept.shape[1]) for kept, _ in bundle[:-1]]
    plan = {
        "rows": [len(parts) for parts in rows],
        "arrays": len(arrays),
        "weights": plans,
        "cores": [len(bundle) for bundle in cores],
        "chips": [len(bundle) - 1 for bundle in chips],
        "after": len(after),
        "outs": len(shapes),
        "hold": hold,
        "direct": direct,
    }
    vmem, hbm = pl.BlockSpec(memory_space=pltpu.VMEM), pl.BlockSpec(memory_space=pl.ANY)
    read = [(part, vmem) for parts in rows for part in parts]
    read += [(array, hbm if far else vmem) for array, far in zip(arrays, fetch)]
    read += [(x, vmem) for bundle in cores for pair in bundle for x in pair]
    for bundle in chips:
        read += [(x, vmem) for pair in bundle[:-1] for x in pair] + [(bundle[-1], vmem)]
    read += [(x, hbm) for x in after]
    dtype = read[0][0].dtype
    scratch = []
    if any(fetch):
        width = [w for w, weight in zip(widths, weights) if len(weight) == 2][0]
        scratch = [
            pltpu.VMEM((width, rows[0][0].shape[1] * len(rows[0])), dtype),
            pltpu.SemaphoreType.DMA,
        ]
    return pl.pallas_call(
        functools.partial(step_body, plan),
        out_shape=[jax.ShapeDtypeStruct(shape, dtype) for shape in shapes],
        in_specs=[spec for _, spec in read],
        scratch_shapes=scratch,
        compiler_params=pltpu.CompilerParams(vmem_limit_bytes=VMEM_LIMIT),
        cost_estimate=LIGHT,
        name="step",
    )(*[x for x, _ in read])


PAIRS = [(0, 1), (1, 0), (2, 3), (3, 2)]
MIDDLE = [(1, 2), (2, 1)]
OUTWARD = [(1, 0), (2, 3)]


def relay(piece, exported):
    near = lax.ppermute(piece, "node", PAIRS)
    across = lax.ppermute(piece, "node", MIDDLE)
    near, across, exported = lax.optimization_barrier((near, across, exported))
    across_out = lax.ppermute(across, "node", OUTWARD)
    near_across = lax.ppermute(near, "node", MIDDLE)
    return near, across, near_across, across_out


def place_body(spots, features, *refs):
    out = refs[-1]
    half = features // 2
    device = lax.axis_index("node")
    mine = lax.axis_index("groups")
    for source, (distance, side) in zip(refs[:-1], spots):
        group = {"own": mine, "other": 1 - mine, "first": 0, "second": 1}[side]
        column = pl.multiple_of((device ^ distance) * features + group * half, HEAD)
        out[:, pl.ds(column, source.shape[1])] = source[...]


def place(sources, spots, devices, features):
    return pl.pallas_call(
        functools.partial(place_body, spots, features),
        out_shape=jax.ShapeDtypeStruct(
            (sources[0].shape[0], devices * features), sources[0].dtype
        ),
        compiler_params=pltpu.CompilerParams(vmem_limit_bytes=VMEM_LIMIT),
        name="place",
    )(*sources)


def cut(weight):
    half = weight.shape[0] // 2
    return lax.dynamic_slice_in_dim(weight, lax.axis_index("groups") * half, half, 0)


def project_split(halves, relayed, out_weight):
    features = out_weight.shape[0]
    half = features // 2
    rows = [part.reshape(-1, part.shape[-1]) for part in halves]
    other = [swap(part, "groups", 1) for part in rows]
    near, across, near_across, across_out = relayed
    far_out = lax.ppermute(near_across, "node", OUTWARD)

    def core(sent):
        return swap(sent, "tensor", 1)

    def chip(away):
        return swap(away, "tensor", 2)

    def back(done):
        return swap(done, "groups", 1)

    def whole(weight):
        return [(weight, 0, weight.shape[0])]

    second = (whole(near_across), whole(across_out))
    far = (whole(across), whole(far_out))

    sent_a, kept_a, sent_b, kept_b, *rows = step(
        [rows], [[(out_weight, 0, half)], [(out_weight, half, half)]], hold=True
    )
    one = [(kept_a, core(sent_a))]
    (away,) = step(cores=[one])
    one.append(chip(away))
    sent_1, kept_1 = step([rows], [whole(near)], after=[away, other[0]])
    sent_2, kept_2, done_a = step([rows], [second], chips=[one], after=[sent_1])
    two = [(kept_b, core(sent_b)), (kept_1, core(sent_1)), (kept_2, core(sent_2))]
    (away,) = step(cores=[two])
    two.append(chip(away))
    sent_3, kept_3, sent_4, kept_4, *other = step(
        [other], [whole(near), second], after=[away], hold=True
    )
    three, four = [(kept_3, core(sent_3))], [(kept_4, core(sent_4))]
    away, done_b, done_1, done_2 = step(cores=[three], chips=[two])
    three.append(chip(away))
    away, done_3 = step(cores=[four], chips=[three])
    four.append(chip(away))
    back_3 = back(done_3)
    sent_5, kept_5 = step([other], [far], after=[away], direct=True)
    five = [(kept_5, core(sent_5))]
    (done_4,) = step(chips=[four], after=[sent_5, back_3])
    back_4 = back(done_4)
    sent_6, kept_6 = step([rows], [far], after=[done_4], direct=True)
    six = [(kept_6, core(sent_6))]
    (away,) = step(cores=[five], after=[sent_6])
    five.append(chip(away))
    (away,) = step(cores=[six], after=[away])
    six.append(chip(away))
    (done_5,) = step(chips=[five], after=[away, back_4])
    back_5 = back(done_5)
    (done_6,) = step(chips=[six], after=[done_5])
    return place(
        (done_a, done_b, done_1, done_2, back_3, back_4, back_5, done_6),
        (
            (0, "first"),
            (0, "second"),
            (1, "own"),
            (2, "own"),
            (1, "other"),
            (2, "other"),
            (3, "other"),
            (3, "own"),
        ),
        lax.axis_size("node"),
        features,
    )


def project_plain(halves, out_weight):
    attended = jnp.concatenate(halves, 2)
    parts, per_part, width = attended.shape
    me = lax.axis_index("tensor")
    order = slot_position(parts, jnp.arange(parts, dtype=jnp.int32) ^ me)
    rows = attended[order].reshape(parts * per_part, width)
    weight = lax.all_gather(out_weight, "node", axis=0, tiled=True)
    terms = times(rows, weight).astype(jnp.bfloat16)
    return lax.psum_scatter(terms, "tensor", scatter_dimension=0, tiled=True)


def local(queries, keys, values, out_weight, slot_nodes, ancestors, depth):
    parts = lax.axis_size("tensor")
    devices = lax.axis_size("node")
    features = out_weight.shape[0]
    kv_count = keys.shape[1] // HEAD
    relayed, after = None, []
    exported, table = prepare(slot_nodes, ancestors, depth, keys, values)
    got = lax.all_gather(exported, "node", axis=0, tiled=True)
    if (
        devices == 4
        and parts == 4
        and lax.axis_size("groups") == 2
        and features % (2 * HEAD) == 0
    ):
        relayed = relay(cut(out_weight), exported)
        after = relayed[:2]
    halves = []
    for kv in range(kv_count):
        halves.append(attend(kv, table, queries, keys, values, got, parts, after))
        after = halves[-1:]
    if relayed is None:
        return project_plain(halves, out_weight)
    return project_split(halves, relayed, out_weight)


def solution(mesh):
    placed = (
        P(("groups", "node"), "tensor"),
        P(("groups", "node"), "tensor"),
        P(("groups", "node"), "tensor"),
        P("node", "tensor"),
        P("groups"),
        P("groups", None),
        P("groups"),
    )
    return jax.shard_map(
        local,
        mesh=mesh,
        in_specs=placed,
        out_specs=P(("groups", "node", "tensor"), None),
        check_vma=False,
    )
```

```python
import functools
import math

import jax
import jax.numpy as jnp
from jax import lax
from jax.experimental import pallas as pl
from jax.experimental.pallas import tpu as pltpu
from jax.sharding import PartitionSpec as P

HEAD = 128
NODE_TOK = 128
A_MAX = 7
CHAIN = A_MAX - 1
EXPORTS = 2
SCALE = math.log2(math.e) / math.sqrt(HEAD)
DEAD = -1e30
LIGHT = pl.CostEstimate(flops=1, bytes_accessed=1, transcendentals=0)
VMEM_LIMIT = 20 * 1024 * 1024
ATTEND_LIMIT = 56 * 1024 * 1024


def prepare_body(nodes, *refs):
    slot_hbm, ancestors_hbm, depth_hbm, keys, values, exported, table_hbm = refs[:7]
    slot_nodes, ancestors, depth, table, holder, within, roots, sem = refs[7:]
    devices = slot_nodes.shape[0] // nodes
    me = lax.axis_index("node")
    fetches = [
        pltpu.make_async_copy(source, target, sem.at[2 * EXPORTS + 1 + order])
        for order, (source, target) in enumerate(
            ((slot_hbm, slot_nodes), (ancestors_hbm, ancestors), (depth_hbm, depth))
        )
    ]
    for fetch in fetches:
        fetch.start()
    for fetch in fetches:
        fetch.wait()

    def place(device, mine):
        root, root_index = jnp.int32(0), jnp.int32(0)
        for index in range(nodes):
            node = slot_nodes[device * nodes + index]
            holder[node] = device
            within[node] = index
            even = (depth[node] & 1) == 0
            root = jnp.where(even, node, root)
            root_index = jnp.where(even, index, root_index)
        roots[device] = root
        return jnp.where(device == me, root_index, mine)

    root = lax.fori_loop(0, devices, place, jnp.int32(0))

    def find_attach(device, attach):
        node = roots[device]
        level = depth[node]
        for step in range(0, CHAIN, 2):
            above = jnp.maximum(ancestors[step, node], 0)
            hit = (step < level) & (holder[above] == me)
            attach = jnp.where(hit, within[above], attach)
        return attach

    attach = lax.fori_loop(0, devices, find_attach, jnp.int32(0))
    copies = []
    for position, (source, index) in enumerate(
        ((keys, root), (keys, attach), (values, root), (values, attach))
    ):
        rows = pl.ds(pl.multiple_of(index * NODE_TOK, NODE_TOK), NODE_TOK)
        copies.append(
            pltpu.make_async_copy(source.at[rows, :], exported.at[position], sem.at[position])
        )
    for copy in copies:
        copy.start()
    root_node = roots[me]
    count = depth[root_node]
    table[0] = root
    table[1] = count
    for step in range(CHAIN):
        above = jnp.maximum(ancestors[step, root_node], 0)
        entry = holder[above] * (2 * EXPORTS) + (1 if step % 2 == 0 else 0)
        table[2 + step] = jnp.where(step < count, entry, 0)
    store = pltpu.make_async_copy(table, table_hbm, sem.at[2 * EXPORTS])
    store.start()
    for copy in (*copies, store):
        copy.wait()


def prepare(slot_nodes, ancestors, depth, keys, values):
    nodes = keys.shape[0] // NODE_TOK
    slots = slot_nodes.shape[0]
    hbm = pl.BlockSpec(memory_space=pltpu.HBM)
    vmem = pl.BlockSpec(memory_space=pltpu.VMEM)
    return pl.pallas_call(
        functools.partial(prepare_body, nodes),
        out_shape=(
            jax.ShapeDtypeStruct((2 * EXPORTS, NODE_TOK, keys.shape[1]), keys.dtype),
            jax.ShapeDtypeStruct((2 + CHAIN,), jnp.int32),
        ),
        in_specs=[hbm, hbm, hbm, vmem, vmem],
        out_specs=(hbm, hbm),
        scratch_shapes=[
            pltpu.SMEM((slots,), jnp.int32),
            pltpu.SMEM((A_MAX, slots), jnp.int32),
            pltpu.SMEM((slots,), jnp.int32),
            pltpu.SMEM((2 + CHAIN,), jnp.int32),
            pltpu.SMEM((slots,), jnp.int32),
            pltpu.SMEM((slots,), jnp.int32),
            pltpu.SMEM((slots // nodes,), jnp.int32),
            pltpu.SemaphoreType.DMA((2 * EXPORTS + 4,)),
        ],
        compiler_params=pltpu.CompilerParams(vmem_limit_bytes=VMEM_LIMIT),
        name="prepare",
    )(slot_nodes, ancestors.T, depth, keys, values)


def attend_body(kv, parts, table, query_hbm, keys_hbm, values_hbm, got, *refs):
    out, query, keys, values, above_keys, above_values, all_keys, all_values, sem = refs[-9:]
    nodes = query.shape[0] // NODE_TOK
    group = query.shape[1] // HEAD
    per_part = query.shape[0] // parts
    side = all_keys.shape[0]
    lanes = pl.ds(kv * HEAD, HEAD)
    pairs = [(keys_hbm.at[:, lanes], keys), (values_hbm.at[:, lanes], values)]
    for step in range(CHAIN):
        entry = table[2 + step]
        pairs.append((got.at[entry, :, lanes], above_keys.at[step]))
        pairs.append((got.at[entry + EXPORTS, :, lanes], above_values.at[step]))
    pairs.append((query_hbm.at[:, pl.ds(kv * group * HEAD, group * HEAD)], query))
    copies = [
        pltpu.make_async_copy(source, target, sem.at[order])
        for order, (source, target) in enumerate(pairs)
    ]
    for copy in copies:
        copy.start()
    ones = jnp.ones((NODE_TOK, HEAD), all_values.dtype)
    nothing = jnp.zeros((NODE_TOK, 2 * HEAD), all_values.dtype)
    query_index = lax.broadcasted_iota(jnp.int32, (NODE_TOK, NODE_TOK), 0)
    key_index = lax.broadcasted_iota(jnp.int32, (NODE_TOK, NODE_TOK), 1)
    own_bias = jnp.where(key_index <= query_index, 0.0, DEAD)
    piece = math.gcd(NODE_TOK, per_part)
    pieces_part = per_part // piece
    me = lax.axis_index("tensor")
    above = (CHAIN + 1) * NODE_TOK
    for copy in copies:
        copy.wait()

    def node_rows(node):
        return pl.ds(pl.multiple_of(node * NODE_TOK, NODE_TOK), NODE_TOK)

    def put(place, order, key_block, value_block):
        rows = pl.ds(order * NODE_TOK, NODE_TOK)
        all_keys[place, rows, :] = key_block
        all_values[place, rows, :HEAD] = value_block
        all_values[place, rows, HEAD:] = ones

    def put_nothing(place, order, first_key):
        rows = pl.ds(order * NODE_TOK, NODE_TOK)
        all_keys[place, rows, :] = jnp.broadcast_to(first_key, (NODE_TOK, HEAD))
        all_values[place, rows, :] = nothing

    for place in range(side):
        for step in range(CHAIN):
            put(place, step, above_keys[step], above_values[step])

    def lay_out(place, node):
        own_key = keys[node_rows(node), :]
        put(place, CHAIN + 1, own_key, values[node_rows(node), :])
        for step in range(CHAIN):
            pl.when(step >= table[1])(functools.partial(put_nothing, place, step, own_key[:1]))
        is_root = node == table[0]
        pl.when(is_root)(functools.partial(put_nothing, place, CHAIN, own_key[:1]))

        @pl.when(jnp.logical_not(is_root))
        def _():
            put(place, CHAIN, keys[node_rows(table[0]), :], values[node_rows(table[0]), :])

    def score(place, node):
        stacked = jnp.concatenate(
            [query[node_rows(node), h * HEAD : (h + 1) * HEAD] for h in range(group)], 0
        )
        return times(stacked, all_keys[place])

    def weigh(scores):
        own = scores[:, above:] + jnp.concatenate([own_bias] * group, 0)
        masked = jnp.concatenate([scores[:, :above], own], 1)
        largest = jnp.max(masked, axis=1, keepdims=True)
        return jnp.exp2((masked - largest) * SCALE).astype(jnp.bfloat16)

    def finish(place, node, expo):
        mixed = jnp.dot(expo, all_values[place], preferred_element_type=jnp.float32)
        result = (mixed[:, :HEAD] / mixed[:, HEAD:]).astype(jnp.bfloat16)
        for part in range(NODE_TOK // piece):
            block = node * (NODE_TOK // piece) + part
            owner = block // pieces_part
            target = slot_position(parts, owner ^ me)
            inner = (block - owner * pieces_part) * piece
            to = pl.ds(pl.multiple_of(inner, piece), piece)
            for h in range(group):
                first = h * NODE_TOK + part * piece
                out[target, to, h * HEAD : (h + 1) * HEAD] = result[first : first + piece]

    def some_nodes(turn, carry):
        mine = [(place, turn * side + place) for place in range(side)]
        for place, node in mine:
            lay_out(place, node)
        scores = [score(place, node) for place, node in mine]
        for (place, node), each in zip(mine, scores):
            finish(place, node, weigh(each))
        return carry

    lax.fori_loop(0, nodes // side, some_nodes, 0)


def slot_position(parts, distance):
    half = parts // 2
    return jnp.where(distance % 2 == 1, distance // 2, half + distance // 2)


def attend(kv, table, queries, keys, values, got, parts, after):
    rows = queries.shape[0]
    width = queries.shape[1] // (keys.shape[1] // HEAD)
    total = (CHAIN + 2) * NODE_TOK
    side = 2 if rows % (2 * NODE_TOK) == 0 else 1
    hbm = pl.BlockSpec(memory_space=pltpu.HBM)
    return pl.pallas_call(
        functools.partial(attend_body, kv, parts),
        out_shape=jax.ShapeDtypeStruct((parts, rows // parts, width), queries.dtype),
        in_specs=[pl.BlockSpec(memory_space=pltpu.SMEM)]
        + [hbm] * 4
        + [pl.BlockSpec(memory_space=pl.ANY)] * len(after),
        scratch_shapes=[
            pltpu.VMEM((rows, width), queries.dtype),
            pltpu.VMEM((rows, HEAD), keys.dtype),
            pltpu.VMEM((rows, HEAD), keys.dtype),
            pltpu.VMEM((CHAIN, NODE_TOK, HEAD), keys.dtype),
            pltpu.VMEM((CHAIN, NODE_TOK, HEAD), keys.dtype),
            pltpu.VMEM((side, total, HEAD), keys.dtype),
            pltpu.VMEM((side, total, 2 * HEAD), keys.dtype),
            pltpu.SemaphoreType.DMA((3 + 2 * CHAIN,)),
        ],
        compiler_params=pltpu.CompilerParams(vmem_limit_bytes=ATTEND_LIMIT),
        cost_estimate=LIGHT,
        name="attend",
    )(table, queries, keys, values, got, *after)


def swap(array, axis, distance):
    size = lax.axis_size(axis)
    return lax.ppermute(array, axis, [(i, i ^ distance) for i in range(size)])


def times(rows, weight):
    return lax.dot_general(
        rows, weight, (((1,), (1,)), ((), ())), preferred_element_type=jnp.float32
    )


def is_middle(index):
    return (index == 1) | (index == 2)


def product(parts, pieces, sent, kept):
    half = parts[0].shape[0] // 2
    for out, start in ((sent, 0), (kept, half)):
        whole = jnp.concatenate([part[start : start + half, :] for part in parts], 1)
        column = 0
        for weight, first, count in pieces:
            out[:, column : column + count] = times(
                whole, weight[first : first + count, :]
            ).astype(out.dtype)
            column += count


def core_sum(pair, upper):
    kept, from_core = pair
    half = kept.shape[0] // 2
    rows = slice(half, 2 * half) if upper else slice(0, half)
    return kept[rows, :].astype(jnp.float32) + from_core[rows, :].astype(jnp.float32)


def step_body(plan, *refs):
    refs = list(refs)

    def take(count):
        return [refs.pop(0) for _ in range(count)]

    rows = [take(count) for count in plan["rows"]]
    arrays = take(plan["arrays"])
    weights = [
        [[(arrays[index], first, count) for index, first, count in pieces] for pieces in weight]
        for weight in plan["weights"]
    ]
    cores = [[take(2) for _ in range(count)] for count in plan["cores"]]
    chips = [([take(2) for _ in range(count)], take(1)[0]) for count in plan["chips"]]
    take(plan["after"])
    outs = take(plan["outs"])
    middle = is_middle(lax.axis_index("node"))
    picks = (middle, jnp.logical_not(middle))
    fetched = None
    for order, weight in enumerate(weights):
        if len(weight) == 2 and not plan["direct"]:
            chosen, sem = refs
            fetched = order
            for pick, pieces in zip(picks, weight):
                column = 0
                for array, first, count in pieces:
                    source = array.at[pl.ds(first, count), :]
                    target = chosen.at[pl.ds(column, count), :]
                    pl.when(pick)(pltpu.make_async_copy(source, target, sem).start)
                    column += count
    made = [[(outs.pop(0), outs.pop(0)) for _ in rows] for _ in weights]
    if plan["hold"]:
        for part in [x for parts in rows for x in parts]:
            out = outs.pop(0)
            out[...] = part[...]
    for bundle in cores:
        out, column = outs.pop(0), 0
        for pair in bundle:
            width = pair[0].shape[1]
            out[:, column : column + width] = core_sum(pair, True).astype(out.dtype)
            column += width
    for bundle, from_chip in chips:
        column = start = 0
        for order, pair in enumerate(bundle):
            if order == 0 or not plan["join"]:
                out, start = outs.pop(0), column
            width = pair[0].shape[1]
            away = from_chip[:, column : column + width].astype(jnp.float32)
            total = (core_sum(pair, False) + away).astype(out.dtype)
            out[:, column - start : column - start + width] = total
            column += width
    for order, (weight, pairs) in enumerate(zip(weights, made)):
        if order == fetched:
            pltpu.make_async_copy(chosen, chosen, sem).wait()
            weight = [[(chosen, 0, chosen.shape[0])]]
        for parts, (sent, kept) in zip(rows, pairs):
            if len(weight) == 2:
                for pick, pieces in zip(picks, weight):
                    pl.when(pick)(functools.partial(product, parts, pieces, sent, kept))
            else:
                product(parts, weight[0], sent, kept)


def step(rows=(), weights=(), cores=(), chips=(), after=(), hold=False, direct=False, join=False):
    weights = [weight if isinstance(weight, tuple) else (weight,) for weight in weights]
    arrays, fetch, plans = [], [], []
    for weight in weights:
        plans.append([])
        for pieces in weight:
            plans[-1].append([])
            for array, first, count in pieces:
                known = [index for index, x in enumerate(arrays) if x is array]
                if not known:
                    known = [len(arrays)]
                    arrays.append(array)
                    fetch.append(len(weight) == 2 and not direct)
                plans[-1][-1].append((known[0], first, count))
    widths = [sum(count for _, _, count in weight[0]) for weight in weights]
    shapes = []
    for width in widths:
        shapes += [(parts[0].shape[0] // 2, width) for parts in rows for _ in range(2)]
    if hold:
        shapes += [part.shape for parts in rows for part in parts]
    for bundle in cores:
        shapes.append((bundle[0][0].shape[0] // 2, sum(kept.shape[1] for kept, _ in bundle)))
    for bundle in chips:
        each = [kept.shape[1] for kept, _ in bundle[:-1]]
        shapes += [(bundle[0][0].shape[0] // 2, w) for w in ([sum(each)] if join else each)]
    plan = {
        "rows": [len(parts) for parts in rows],
        "arrays": len(arrays),
        "weights": plans,
        "cores": [len(bundle) for bundle in cores],
        "chips": [len(bundle) - 1 for bundle in chips],
        "after": len(after),
        "outs": len(shapes),
        "hold": hold,
        "direct": direct,
        "join": join,
    }
    vmem, hbm = pl.BlockSpec(memory_space=pltpu.VMEM), pl.BlockSpec(memory_space=pl.ANY)
    read = [(part, vmem) for parts in rows for part in parts]
    read += [(array, hbm if far else vmem) for array, far in zip(arrays, fetch)]
    read += [(x, vmem) for bundle in cores for pair in bundle for x in pair]
    for bundle in chips:
        read += [(x, vmem) for pair in bundle[:-1] for x in pair] + [(bundle[-1], vmem)]
    read += [(x, hbm) for x in after]
    dtype = read[0][0].dtype
    scratch = []
    if any(fetch):
        width = [w for w, weight in zip(widths, weights) if len(weight) == 2][0]
        scratch = [
            pltpu.VMEM((width, rows[0][0].shape[1] * len(rows[0])), dtype),
            pltpu.SemaphoreType.DMA,
        ]
    return pl.pallas_call(
        functools.partial(step_body, plan),
        out_shape=[jax.ShapeDtypeStruct(shape, dtype) for shape in shapes],
        in_specs=[spec for _, spec in read],
        scratch_shapes=scratch,
        compiler_params=pltpu.CompilerParams(vmem_limit_bytes=VMEM_LIMIT),
        cost_estimate=LIGHT,
        name="step",
    )(*[x for x, _ in read])


PAIRS = [(0, 1), (1, 0), (2, 3), (3, 2)]
MIDDLE = [(1, 2), (2, 1)]
OUTWARD = [(1, 0), (2, 3)]


def relay(piece, exported):
    near = lax.ppermute(piece, "node", PAIRS)
    across = lax.ppermute(piece, "node", MIDDLE)
    near, across, exported = lax.optimization_barrier((near, across, exported))
    across_out = lax.ppermute(across, "node", OUTWARD)
    near_across = lax.ppermute(near, "node", MIDDLE)
    return near, across, near_across, across_out


def place_body(spots, features, *refs):
    out = refs[-1]
    half = features // 2
    device = lax.axis_index("node")
    mine = lax.axis_index("groups")
    for source, (distance, side) in zip(refs[:-1], spots):
        group = {"own": mine, "other": 1 - mine, "first": 0, "second": 1}[side]
        column = pl.multiple_of((device ^ distance) * features + group * half, HEAD)
        out[:, pl.ds(column, source.shape[1])] = source[...]


def place(sources, spots, devices, features):
    return pl.pallas_call(
        functools.partial(place_body, spots, features),
        out_shape=jax.ShapeDtypeStruct(
            (sources[0].shape[0], devices * features), sources[0].dtype
        ),
        compiler_params=pltpu.CompilerParams(vmem_limit_bytes=VMEM_LIMIT),
        name="place",
    )(*sources)


def cut(weight):
    half = weight.shape[0] // 2
    return lax.dynamic_slice_in_dim(weight, lax.axis_index("groups") * half, half, 0)


def project_split(halves, relayed, out_weight):
    features = out_weight.shape[0]
    half = features // 2
    rows = [part.reshape(-1, part.shape[-1]) for part in halves]
    other = [swap(part, "groups", 1) for part in rows]
    near, across, near_across, across_out = relayed
    far_out = lax.ppermute(near_across, "node", OUTWARD)

    def core(sent):
        return swap(sent, "tensor", 1)

    def chip(away):
        return swap(away, "tensor", 2)

    def back(done):
        return swap(done, "groups", 1)

    def whole(weight):
        return [(weight, 0, weight.shape[0])]

    second = (whole(near_across), whole(across_out))
    far = (whole(across), whole(far_out))

    sent_a, kept_a, sent_b, kept_b, *rows = step(
        [rows], [[(out_weight, 0, half)], [(out_weight, half, half)]], hold=True
    )
    one = [(kept_a, core(sent_a)), (kept_b, core(sent_b))]
    (away,) = step(cores=[one])
    one.append(chip(away))
    sent_1, kept_1 = step([rows], [whole(near)], after=[away, other[0]])
    sent_2, kept_2, done_a, done_b = step([rows], [second], chips=[one], after=[sent_1])
    two = [(kept_1, core(sent_1)), (kept_2, core(sent_2))]
    (away,) = step(cores=[two])
    two.append(chip(away))
    first = (half // HEAD + 1) // 2 * HEAD
    sent_3, kept_3, sent_c, kept_c, sent_4, kept_4, *other = step(
        [other],
        [[(near, 0, first)], [(near, first, half - first)], second],
        after=[away],
        hold=True,
    )
    three = [(kept_3, core(sent_3)), (kept_c, core(sent_c))]
    four = [(kept_4, core(sent_4))]
    away, done_1, done_2 = step(cores=[three], chips=[two])
    three.append(chip(away))
    away, done_3 = step(cores=[four], chips=[three], join=True)
    four.append(chip(away))
    back_3 = back(done_3)
    sent_5, kept_5 = step([other], [far], after=[away, back_3], direct=True)
    five = [(kept_5, core(sent_5))]
    (done_4,) = step(chips=[four], after=[sent_5])
    back_4 = back(done_4)
    sent_6, kept_6 = step([rows], [far], after=[done_4], direct=True)
    six = [(kept_6, core(sent_6))]
    (away,) = step(cores=[five], after=[sent_6])
    five.append(chip(away))
    (away,) = step(cores=[six], after=[away])
    six.append(chip(away))
    (done_5,) = step(chips=[five], after=[away, back_4])
    back_5 = back(done_5)
    (done_6,) = step(chips=[six], after=[done_5])
    return place(
        (done_a, done_b, done_1, done_2, back_3, back_4, back_5, done_6),
        (
            (0, "first"),
            (0, "second"),
            (1, "own"),
            (2, "own"),
            (1, "other"),
            (2, "other"),
            (3, "other"),
            (3, "own"),
        ),
        lax.axis_size("node"),
        features,
    )


def project_plain(halves, out_weight):
    attended = jnp.concatenate(halves, 2)
    parts, per_part, width = attended.shape
    me = lax.axis_index("tensor")
    order = slot_position(parts, jnp.arange(parts, dtype=jnp.int32) ^ me)
    rows = attended[order].reshape(parts * per_part, width)
    weight = lax.all_gather(out_weight, "node", axis=0, tiled=True)
    terms = times(rows, weight).astype(jnp.bfloat16)
    return lax.psum_scatter(terms, "tensor", scatter_dimension=0, tiled=True)


def local(queries, keys, values, out_weight, slot_nodes, ancestors, depth):
    parts = lax.axis_size("tensor")
    devices = lax.axis_size("node")
    features = out_weight.shape[0]
    kv_count = keys.shape[1] // HEAD
    relayed, after = None, []
    exported, table = prepare(slot_nodes, ancestors, depth, keys, values)
    got = lax.all_gather(exported, "node", axis=0, tiled=True)
    if (
        devices == 4
        and parts == 4
        and lax.axis_size("groups") == 2
        and features % (2 * HEAD) == 0
    ):
        relayed = relay(cut(out_weight), exported)
        after = relayed[:2]
    halves = []
    for kv in range(kv_count):
        halves.append(attend(kv, table, queries, keys, values, got, parts, after))
        after = halves[-1:]
    if relayed is None:
        return project_plain(halves, out_weight)
    return project_split(halves, relayed, out_weight)


def solution(mesh):
    placed = (
        P(("groups", "node"), "tensor"),
        P(("groups", "node"), "tensor"),
        P(("groups", "node"), "tensor"),
        P("node", "tensor"),
        P("groups"),
        P("groups", None),
        P("groups"),
    )
    return jax.shard_map(
        local,
        mesh=mesh,
        in_specs=placed,
        out_specs=P(("groups", "node", "tensor"), None),
        check_vma=False,
    )
```

```python
import functools
import math

import jax
import jax.numpy as jnp
from jax import lax
from jax.experimental import pallas as pl
from jax.experimental.pallas import tpu as pltpu
from jax.sharding import PartitionSpec as P

HEAD = 128
NODE_TOK = 128
A_MAX = 7
CHAIN = A_MAX - 1
EXPORTS = 2
SCALE = math.log2(math.e) / math.sqrt(HEAD)
DEAD = -1e30
LIGHT = pl.CostEstimate(flops=1, bytes_accessed=1, transcendentals=0)
VMEM_LIMIT = 20 * 1024 * 1024
ATTEND_LIMIT = 24 * 1024 * 1024


def prepare_body(nodes, *refs):
    slot_hbm, ancestors_hbm, depth_hbm, keys, values, exported, table_hbm = refs[:7]
    slot_nodes, ancestors, depth, table, holder, within, roots, sem = refs[7:]
    devices = slot_nodes.shape[0] // nodes
    me = lax.axis_index("node")
    fetches = [
        pltpu.make_async_copy(source, target, sem.at[2 * EXPORTS + 1 + order])
        for order, (source, target) in enumerate(
            ((slot_hbm, slot_nodes), (ancestors_hbm, ancestors), (depth_hbm, depth))
        )
    ]
    for fetch in fetches:
        fetch.start()
    for fetch in fetches:
        fetch.wait()

    def place(device, mine):
        root, root_index = jnp.int32(0), jnp.int32(0)
        for index in range(nodes):
            node = slot_nodes[device * nodes + index]
            holder[node] = device
            within[node] = index
            even = (depth[node] & 1) == 0
            root = jnp.where(even, node, root)
            root_index = jnp.where(even, index, root_index)
        roots[device] = root
        return jnp.where(device == me, root_index, mine)

    root = lax.fori_loop(0, devices, place, jnp.int32(0))

    def find_attach(device, attach):
        node = roots[device]
        level = depth[node]
        for step in range(0, CHAIN, 2):
            above = jnp.maximum(ancestors[step, node], 0)
            hit = (step < level) & (holder[above] == me)
            attach = jnp.where(hit, within[above], attach)
        return attach

    attach = lax.fori_loop(0, devices, find_attach, jnp.int32(0))
    copies = []
    for position, (source, index) in enumerate(
        ((keys, root), (keys, attach), (values, root), (values, attach))
    ):
        rows = pl.ds(pl.multiple_of(index * NODE_TOK, NODE_TOK), NODE_TOK)
        copies.append(
            pltpu.make_async_copy(source.at[rows, :], exported.at[position], sem.at[position])
        )
    for copy in copies:
        copy.start()
    root_node = roots[me]
    count = depth[root_node]
    table[0] = root
    table[1] = count
    for step in range(CHAIN):
        above = jnp.maximum(ancestors[step, root_node], 0)
        entry = holder[above] * (2 * EXPORTS) + (1 if step % 2 == 0 else 0)
        table[2 + step] = jnp.where(step < count, entry, 0)
    store = pltpu.make_async_copy(table, table_hbm, sem.at[2 * EXPORTS])
    store.start()
    for copy in (*copies, store):
        copy.wait()


def prepare(slot_nodes, ancestors, depth, keys, values):
    nodes = keys.shape[0] // NODE_TOK
    slots = slot_nodes.shape[0]
    hbm = pl.BlockSpec(memory_space=pltpu.HBM)
    vmem = pl.BlockSpec(memory_space=pltpu.VMEM)
    return pl.pallas_call(
        functools.partial(prepare_body, nodes),
        out_shape=(
            jax.ShapeDtypeStruct((2 * EXPORTS, NODE_TOK, keys.shape[1]), keys.dtype),
            jax.ShapeDtypeStruct((2 + CHAIN,), jnp.int32),
        ),
        in_specs=[hbm, hbm, hbm, vmem, vmem],
        out_specs=(hbm, hbm),
        scratch_shapes=[
            pltpu.SMEM((slots,), jnp.int32),
            pltpu.SMEM((A_MAX, slots), jnp.int32),
            pltpu.SMEM((slots,), jnp.int32),
            pltpu.SMEM((2 + CHAIN,), jnp.int32),
            pltpu.SMEM((slots,), jnp.int32),
            pltpu.SMEM((slots,), jnp.int32),
            pltpu.SMEM((slots // nodes,), jnp.int32),
            pltpu.SemaphoreType.DMA((2 * EXPORTS + 4,)),
        ],
        compiler_params=pltpu.CompilerParams(vmem_limit_bytes=VMEM_LIMIT),
        name="prepare",
    )(slot_nodes, ancestors.T, depth, keys, values)


def attend_body(kv, parts, table, query_hbm, keys_hbm, values_hbm, got, *refs):
    out, query, keys, values, above_keys, above_values, all_keys, all_values, sem = refs[-9:]
    nodes = query.shape[0] // NODE_TOK
    group = query.shape[1] // HEAD
    per_part = query.shape[0] // parts
    side = all_keys.shape[0]
    lanes = pl.ds(kv * HEAD, HEAD)
    pairs = [(keys_hbm.at[:, lanes], keys), (values_hbm.at[:, lanes], values)]
    for step in range(CHAIN):
        entry = table[2 + step]
        pairs.append((got.at[entry, :, lanes], above_keys.at[step]))
        pairs.append((got.at[entry + EXPORTS, :, lanes], above_values.at[step]))
    pairs.append((query_hbm.at[:, pl.ds(kv * group * HEAD, group * HEAD)], query))
    copies = [
        pltpu.make_async_copy(source, target, sem.at[order])
        for order, (source, target) in enumerate(pairs)
    ]
    for copy in copies:
        copy.start()
    ones = jnp.ones((NODE_TOK, HEAD), all_values.dtype)
    nothing = jnp.zeros((NODE_TOK, 2 * HEAD), all_values.dtype)
    query_index = lax.broadcasted_iota(jnp.int32, (NODE_TOK, NODE_TOK), 0)
    key_index = lax.broadcasted_iota(jnp.int32, (NODE_TOK, NODE_TOK), 1)
    own_bias = jnp.where(key_index <= query_index, 0.0, DEAD)
    piece = math.gcd(NODE_TOK, per_part)
    pieces_part = per_part // piece
    me = lax.axis_index("tensor")
    above = (CHAIN + 1) * NODE_TOK
    for copy in copies:
        copy.wait()

    def node_rows(node):
        return pl.ds(pl.multiple_of(node * NODE_TOK, NODE_TOK), NODE_TOK)

    def put(place, order, key_block, value_block):
        rows = pl.ds(order * NODE_TOK, NODE_TOK)
        all_keys[place, rows, :] = key_block
        all_values[place, rows, :HEAD] = value_block
        all_values[place, rows, HEAD:] = ones

    def put_nothing(place, order, first_key):
        rows = pl.ds(order * NODE_TOK, NODE_TOK)
        all_keys[place, rows, :] = jnp.broadcast_to(first_key, (NODE_TOK, HEAD))
        all_values[place, rows, :] = nothing

    for place in range(side):
        for step in range(CHAIN):
            put(place, step, above_keys[step], above_values[step])

    def lay_out(place, node):
        own_key = keys[node_rows(node), :]
        put(place, CHAIN + 1, own_key, values[node_rows(node), :])
        for step in range(CHAIN):
            pl.when(step >= table[1])(functools.partial(put_nothing, place, step, own_key[:1]))
        is_root = node == table[0]
        pl.when(is_root)(functools.partial(put_nothing, place, CHAIN, own_key[:1]))

        @pl.when(jnp.logical_not(is_root))
        def _():
            put(place, CHAIN, keys[node_rows(table[0]), :], values[node_rows(table[0]), :])

    def score(place, node):
        stacked = jnp.concatenate(
            [query[node_rows(node), h * HEAD : (h + 1) * HEAD] for h in range(group)], 0
        )
        return times(stacked, all_keys[place])

    def weigh(scores):
        own = scores[:, above:] + jnp.concatenate([own_bias] * group, 0)
        masked = jnp.concatenate([scores[:, :above], own], 1)
        largest = jnp.max(masked, axis=1, keepdims=True)
        return jnp.exp2((masked - largest) * SCALE).astype(jnp.bfloat16)

    def finish(place, node, expo):
        mixed = jnp.dot(expo, all_values[place], preferred_element_type=jnp.float32)
        result = (mixed[:, :HEAD] / mixed[:, HEAD:]).astype(jnp.bfloat16)
        for part in range(NODE_TOK // piece):
            block = node * (NODE_TOK // piece) + part
            owner = block // pieces_part
            target = slot_position(parts, owner ^ me)
            inner = (block - owner * pieces_part) * piece
            to = pl.ds(pl.multiple_of(inner, piece), piece)
            for h in range(group):
                first = h * NODE_TOK + part * piece
                out[target, to, h * HEAD : (h + 1) * HEAD] = result[first : first + piece]

    def some_nodes(turn, carry):
        mine = [(place, turn * side + place) for place in range(side)]
        for place, node in mine:
            lay_out(place, node)
        scores = [score(place, node) for place, node in mine]
        for (place, node), each in zip(mine, scores):
            finish(place, node, weigh(each))
        return carry

    lax.fori_loop(0, nodes // side, some_nodes, 0)


def slot_position(parts, distance):
    half = parts // 2
    return jnp.where(distance % 2 == 1, distance // 2, half + distance // 2)


def in_hbm(array):
    return pltpu.with_memory_space_constraint(array, pltpu.HBM)


def attend(kv, table, queries, keys, values, got, parts, after):
    rows = queries.shape[0]
    width = queries.shape[1] // (keys.shape[1] // HEAD)
    total = (CHAIN + 2) * NODE_TOK
    side = 2 if rows % (2 * NODE_TOK) == 0 else 1
    hbm = pl.BlockSpec(memory_space=pltpu.HBM)
    return pl.pallas_call(
        functools.partial(attend_body, kv, parts),
        out_shape=jax.ShapeDtypeStruct((parts, rows // parts, width), queries.dtype),
        in_specs=[pl.BlockSpec(memory_space=pltpu.SMEM)]
        + [hbm] * 4
        + [pl.BlockSpec(memory_space=pl.ANY)] * len(after),
        scratch_shapes=[
            pltpu.VMEM((rows, width), queries.dtype),
            pltpu.VMEM((rows, HEAD), keys.dtype),
            pltpu.VMEM((rows, HEAD), keys.dtype),
            pltpu.VMEM((CHAIN, NODE_TOK, HEAD), keys.dtype),
            pltpu.VMEM((CHAIN, NODE_TOK, HEAD), keys.dtype),
            pltpu.VMEM((side, total, HEAD), keys.dtype),
            pltpu.VMEM((side, total, 2 * HEAD), keys.dtype),
            pltpu.SemaphoreType.DMA((3 + 2 * CHAIN,)),
        ],
        compiler_params=pltpu.CompilerParams(vmem_limit_bytes=ATTEND_LIMIT),
        cost_estimate=LIGHT,
        name="attend",
    )(table, *[in_hbm(x) for x in (queries, keys, values, got)], *after)


def swap(array, axis, distance):
    size = lax.axis_size(axis)
    return lax.ppermute(array, axis, [(i, i ^ distance) for i in range(size)])


def times(rows, weight):
    return lax.dot_general(
        rows, weight, (((1,), (1,)), ((), ())), preferred_element_type=jnp.float32
    )


def is_middle(index):
    return (index == 1) | (index == 2)


def product(parts, pieces, sent, kept):
    half = parts[0].shape[0] // 2
    for out, start in ((sent, 0), (kept, half)):
        whole = jnp.concatenate([part[start : start + half, :] for part in parts], 1)
        column = 0
        for weight, first, count in pieces:
            out[:, column : column + count] = times(
                whole, weight[first : first + count, :]
            ).astype(out.dtype)
            column += count


def core_sum(pair, upper):
    kept, from_core = pair
    half = kept.shape[0] // 2
    rows = slice(half, 2 * half) if upper else slice(0, half)
    return kept[rows, :].astype(jnp.float32) + from_core[rows, :].astype(jnp.float32)


def step_body(plan, *refs):
    refs = list(refs)

    def take(count):
        return [refs.pop(0) for _ in range(count)]

    rows = [take(count) for count in plan["rows"]]
    arrays = take(plan["arrays"])
    weights = [
        [[(arrays[index], first, count) for index, first, count in pieces] for pieces in weight]
        for weight in plan["weights"]
    ]
    cores = [[take(2) for _ in range(count)] for count in plan["cores"]]
    chips = [([take(2) for _ in range(count)], take(1)[0]) for count in plan["chips"]]
    take(plan["after"])
    outs = take(plan["outs"])
    middle = is_middle(lax.axis_index("node"))
    picks = (middle, jnp.logical_not(middle))
    fetched = None
    for order, weight in enumerate(weights):
        if len(weight) == 2 and not plan["direct"]:
            chosen, sem = refs
            fetched = order
            for pick, pieces in zip(picks, weight):
                column = 0
                for array, first, count in pieces:
                    source = array.at[pl.ds(first, count), :]
                    target = chosen.at[pl.ds(column, count), :]
                    pl.when(pick)(pltpu.make_async_copy(source, target, sem).start)
                    column += count
    made = [[(outs.pop(0), outs.pop(0)) for _ in rows] for _ in weights]
    for bundle in cores:
        out, column = outs.pop(0), 0
        for pair in bundle:
            width = pair[0].shape[1]
            out[:, column : column + width] = core_sum(pair, True).astype(out.dtype)
            column += width
    for bundle, from_chip in chips:
        column = 0
        for pair in bundle:
            out = outs.pop(0)
            width = out.shape[1]
            away = from_chip[:, column : column + width].astype(jnp.float32)
            out[...] = (core_sum(pair, False) + away).astype(out.dtype)
            column += width
    for order, (weight, pairs) in enumerate(zip(weights, made)):
        if order == fetched:
            pltpu.make_async_copy(chosen, chosen, sem).wait()
            weight = [[(chosen, 0, chosen.shape[0])]]
        for parts, (sent, kept) in zip(rows, pairs):
            if len(weight) == 2:
                for pick, pieces in zip(picks, weight):
                    pl.when(pick)(functools.partial(product, parts, pieces, sent, kept))
            else:
                product(parts, weight[0], sent, kept)


def step(rows=(), weights=(), cores=(), chips=(), after=(), direct=False):
    weights = [weight if isinstance(weight, tuple) else (weight,) for weight in weights]
    arrays, fetch, plans = [], [], []
    for weight in weights:
        plans.append([])
        for pieces in weight:
            plans[-1].append([])
            for array, first, count in pieces:
                known = [index for index, x in enumerate(arrays) if x is array]
                if not known:
                    known = [len(arrays)]
                    arrays.append(array)
                    fetch.append(len(weight) == 2 and not direct)
                plans[-1][-1].append((known[0], first, count))
    widths = [sum(count for _, _, count in weight[0]) for weight in weights]
    shapes = []
    for width in widths:
        shapes += [(parts[0].shape[0] // 2, width) for parts in rows for _ in range(2)]
    for bundle in cores:
        shapes.append((bundle[0][0].shape[0] // 2, sum(kept.shape[1] for kept, _ in bundle)))
    for bundle in chips:
        shapes += [(kept.shape[0] // 2, kept.shape[1]) for kept, _ in bundle[:-1]]
    plan = {
        "rows": [len(parts) for parts in rows],
        "arrays": len(arrays),
        "weights": plans,
        "cores": [len(bundle) for bundle in cores],
        "chips": [len(bundle) - 1 for bundle in chips],
        "after": len(after),
        "outs": len(shapes),
        "direct": direct,
    }
    vmem, hbm = pl.BlockSpec(memory_space=pltpu.VMEM), pl.BlockSpec(memory_space=pl.ANY)
    read = [(part, vmem) for parts in rows for part in parts]
    read += [(array, hbm if far else vmem) for array, far in zip(arrays, fetch)]
    read += [(x, vmem) for bundle in cores for pair in bundle for x in pair]
    for bundle in chips:
        read += [(x, vmem) for pair in bundle[:-1] for x in pair] + [(bundle[-1], vmem)]
    read += [(x, hbm) for x in after]
    dtype = read[0][0].dtype
    scratch = []
    if any(fetch):
        width = [w for w, weight in zip(widths, weights) if len(weight) == 2][0]
        scratch = [
            pltpu.VMEM((width, rows[0][0].shape[1] * len(rows[0])), dtype),
            pltpu.SemaphoreType.DMA,
        ]
    return pl.pallas_call(
        functools.partial(step_body, plan),
        out_shape=[jax.ShapeDtypeStruct(shape, dtype) for shape in shapes],
        in_specs=[spec for _, spec in read],
        scratch_shapes=scratch,
        compiler_params=pltpu.CompilerParams(vmem_limit_bytes=VMEM_LIMIT),
        cost_estimate=LIGHT,
        name="step",
    )(*[x for x, _ in read])


PAIRS = [(0, 1), (1, 0), (2, 3), (3, 2)]
MIDDLE = [(1, 2), (2, 1)]
OUTWARD = [(1, 0), (2, 3)]


def relay(piece, exported):
    near = lax.ppermute(piece, "node", PAIRS)
    across = lax.ppermute(piece, "node", MIDDLE)
    near, across, exported = lax.optimization_barrier((near, across, exported))
    across_out = lax.ppermute(across, "node", OUTWARD)
    near_across = lax.ppermute(near, "node", MIDDLE)
    return near, across, near_across, across_out


def place_body(spots, features, *refs):
    out = refs[-1]
    half = features // 2
    device = lax.axis_index("node")
    mine = lax.axis_index("groups")
    for source, (distance, side) in zip(refs[:-1], spots):
        group = {"own": mine, "other": 1 - mine, "first": 0, "second": 1}[side]
        column = pl.multiple_of((device ^ distance) * features + group * half, HEAD)
        out[:, pl.ds(column, source.shape[1])] = source[...]


def place(sources, spots, devices, features):
    return pl.pallas_call(
        functools.partial(place_body, spots, features),
        out_shape=jax.ShapeDtypeStruct(
            (sources[0].shape[0], devices * features), sources[0].dtype
        ),
        compiler_params=pltpu.CompilerParams(vmem_limit_bytes=VMEM_LIMIT),
        name="place",
    )(*sources)


def cut(weight):
    half = weight.shape[0] // 2
    return lax.dynamic_slice_in_dim(weight, lax.axis_index("groups") * half, half, 0)


def project_split(halves, relayed, out_weight):
    features = out_weight.shape[0]
    half = features // 2
    rows = [part.reshape(-1, part.shape[-1]) for part in halves]
    other = [swap(part, "groups", 1) for part in rows]
    near, across, near_across, across_out = relayed
    far_out = lax.ppermute(near_across, "node", OUTWARD)

    def core(sent):
        return swap(sent, "tensor", 1)

    def chip(away):
        return swap(away, "tensor", 2)

    def back(done):
        return swap(done, "groups", 1)

    def whole(weight):
        return [(weight, 0, weight.shape[0])]

    second = (whole(near_across), whole(across_out))
    far = (whole(across), whole(far_out))

    sent_a, kept_a, sent_b, kept_b = step(
        [rows], [[(out_weight, 0, half)], [(out_weight, half, half)]]
    )
    one = [(kept_a, core(sent_a))]
    (away,) = step(cores=[one])
    one.append(chip(away))
    sent_1, kept_1 = step([rows], [whole(near)], after=[away, other[0]])
    sent_2, kept_2, done_a = step([rows], [second], chips=[one], after=[sent_1])
    two = [(kept_b, core(sent_b)), (kept_1, core(sent_1)), (kept_2, core(sent_2))]
    (away,) = step(cores=[two])
    two.append(chip(away))
    sent_3, kept_3, sent_4, kept_4 = step([other], [whole(near), second], after=[away])
    three, four = [(kept_3, core(sent_3))], [(kept_4, core(sent_4))]
    away, done_b, done_1, done_2 = step(cores=[three], chips=[two])
    three.append(chip(away))
    away, done_3 = step(cores=[four], chips=[three])
    four.append(chip(away))
    back_3 = back(done_3)
    sent_5, kept_5 = step([other], [far], after=[away], direct=True)
    five = [(kept_5, core(sent_5))]
    (done_4,) = step(chips=[four], after=[sent_5, back_3])
    back_4 = back(done_4)
    sent_6, kept_6 = step([rows], [far], after=[done_4], direct=True)
    six = [(kept_6, core(sent_6))]
    (away,) = step(cores=[five], after=[sent_6])
    five.append(chip(away))
    (away,) = step(cores=[six], after=[away])
    six.append(chip(away))
    (done_5,) = step(chips=[five], after=[away, back_4])
    back_5 = back(done_5)
    (done_6,) = step(chips=[six], after=[done_5])
    return place(
        (done_a, done_b, done_1, done_2, back_3, back_4, back_5, done_6),
        (
            (0, "first"),
            (0, "second"),
            (1, "own"),
            (2, "own"),
            (1, "other"),
            (2, "other"),
            (3, "other"),
            (3, "own"),
        ),
        lax.axis_size("node"),
        features,
    )


def project_plain(halves, out_weight):
    attended = jnp.concatenate(halves, 2)
    parts, per_part, width = attended.shape
    me = lax.axis_index("tensor")
    order = slot_position(parts, jnp.arange(parts, dtype=jnp.int32) ^ me)
    rows = attended[order].reshape(parts * per_part, width)
    weight = lax.all_gather(out_weight, "node", axis=0, tiled=True)
    terms = times(rows, weight).astype(jnp.bfloat16)
    return lax.psum_scatter(terms, "tensor", scatter_dimension=0, tiled=True)


def local(queries, keys, values, out_weight, slot_nodes, ancestors, depth):
    parts = lax.axis_size("tensor")
    devices = lax.axis_size("node")
    features = out_weight.shape[0]
    kv_count = keys.shape[1] // HEAD
    relayed, after = None, []
    exported, table = prepare(slot_nodes, ancestors, depth, keys, values)
    got = lax.all_gather(exported, "node", axis=0, tiled=True)
    if (
        devices == 4
        and parts == 4
        and lax.axis_size("groups") == 2
        and features % (2 * HEAD) == 0
    ):
        relayed = relay(cut(out_weight), exported)
        after = relayed[:2]
    halves = []
    for kv in range(kv_count):
        halves.append(attend(kv, table, queries, keys, values, got, parts, after))
        after = halves[-1:]
    if relayed is None:
        return project_plain(halves, out_weight)
    return project_split(halves, relayed, out_weight)


def solution(mesh):
    placed = (
        P(("groups", "node"), "tensor"),
        P(("groups", "node"), "tensor"),
        P(("groups", "node"), "tensor"),
        P("node", "tensor"),
        P("groups"),
        P("groups", None),
        P("groups"),
    )
    return jax.shard_map(
        local,
        mesh=mesh,
        in_specs=placed,
        out_specs=P(("groups", "node", "tensor"), None),
        check_vma=False,
    )
```

```python
import functools
import math

import jax
import jax.numpy as jnp
from jax import lax
from jax.experimental import pallas as pl
from jax.experimental.pallas import tpu as pltpu
from jax.sharding import PartitionSpec as P

HEAD = 128
NODE_TOK = 128
A_MAX = 7
CHAIN = A_MAX - 1
EXPORTS = 2
SCALE = math.log2(math.e) / math.sqrt(HEAD)
DEAD = -1e30
LIGHT = pl.CostEstimate(flops=1, bytes_accessed=1, transcendentals=0)
VMEM_LIMIT = 20 * 1024 * 1024
ATTEND_LIMIT = 24 * 1024 * 1024


def prepare_body(nodes, *refs):
    slot_hbm, ancestors_hbm, depth_hbm, keys, values, exported, table_hbm = refs[:7]
    slot_nodes, ancestors, depth, table, holder, within, roots, sem = refs[7:]
    devices = slot_nodes.shape[0] // nodes
    me = lax.axis_index("node")
    fetches = [
        pltpu.make_async_copy(source, target, sem.at[2 * EXPORTS + 1 + order])
        for order, (source, target) in enumerate(
            ((slot_hbm, slot_nodes), (ancestors_hbm, ancestors), (depth_hbm, depth))
        )
    ]
    for fetch in fetches:
        fetch.start()
    for fetch in fetches:
        fetch.wait()

    def place(device, mine):
        root, root_index = jnp.int32(0), jnp.int32(0)
        for index in range(nodes):
            node = slot_nodes[device * nodes + index]
            holder[node] = device
            within[node] = index
            even = (depth[node] & 1) == 0
            root = jnp.where(even, node, root)
            root_index = jnp.where(even, index, root_index)
        roots[device] = root
        return jnp.where(device == me, root_index, mine)

    root = lax.fori_loop(0, devices, place, jnp.int32(0))

    def find_attach(device, attach):
        node = roots[device]
        level = depth[node]
        for step in range(0, CHAIN, 2):
            above = jnp.maximum(ancestors[step, node], 0)
            hit = (step < level) & (holder[above] == me)
            attach = jnp.where(hit, within[above], attach)
        return attach

    attach = lax.fori_loop(0, devices, find_attach, jnp.int32(0))
    copies = []
    for position, (source, index) in enumerate(
        ((keys, root), (keys, attach), (values, root), (values, attach))
    ):
        rows = pl.ds(pl.multiple_of(index * NODE_TOK, NODE_TOK), NODE_TOK)
        copies.append(
            pltpu.make_async_copy(source.at[rows, :], exported.at[position], sem.at[position])
        )
    for copy in copies:
        copy.start()
    root_node = roots[me]
    count = depth[root_node]
    table[0] = root
    table[1] = count
    for step in range(CHAIN):
        above = jnp.maximum(ancestors[step, root_node], 0)
        entry = holder[above] * (2 * EXPORTS) + (1 if step % 2 == 0 else 0)
        table[2 + step] = jnp.where(step < count, entry, 0)
    store = pltpu.make_async_copy(table, table_hbm, sem.at[2 * EXPORTS])
    store.start()
    for copy in (*copies, store):
        copy.wait()


def prepare(slot_nodes, ancestors, depth, keys, values):
    nodes = keys.shape[0] // NODE_TOK
    slots = slot_nodes.shape[0]
    hbm = pl.BlockSpec(memory_space=pltpu.HBM)
    vmem = pl.BlockSpec(memory_space=pltpu.VMEM)
    return pl.pallas_call(
        functools.partial(prepare_body, nodes),
        out_shape=(
            jax.ShapeDtypeStruct((2 * EXPORTS, NODE_TOK, keys.shape[1]), keys.dtype),
            jax.ShapeDtypeStruct((2 + CHAIN,), jnp.int32),
        ),
        in_specs=[hbm, hbm, hbm, vmem, vmem],
        out_specs=(hbm, hbm),
        scratch_shapes=[
            pltpu.SMEM((slots,), jnp.int32),
            pltpu.SMEM((A_MAX, slots), jnp.int32),
            pltpu.SMEM((slots,), jnp.int32),
            pltpu.SMEM((2 + CHAIN,), jnp.int32),
            pltpu.SMEM((slots,), jnp.int32),
            pltpu.SMEM((slots,), jnp.int32),
            pltpu.SMEM((slots // nodes,), jnp.int32),
            pltpu.SemaphoreType.DMA((2 * EXPORTS + 4,)),
        ],
        compiler_params=pltpu.CompilerParams(vmem_limit_bytes=VMEM_LIMIT),
        name="prepare",
    )(slot_nodes, ancestors.T, depth, keys, values)


def attend_body(kv, parts, table, query_hbm, keys_hbm, values_hbm, got, *refs):
    out, query, keys, values, above_keys, above_values, all_keys, all_values, sem = refs[-9:]
    nodes = query.shape[0] // NODE_TOK
    group = query.shape[1] // HEAD
    per_part = query.shape[0] // parts
    side = all_keys.shape[0]
    lanes = pl.ds(kv * HEAD, HEAD)
    pairs = [(keys_hbm.at[:, lanes], keys), (values_hbm.at[:, lanes], values)]
    for step in range(CHAIN):
        entry = table[2 + step]
        pairs.append((got.at[entry, :, lanes], above_keys.at[step]))
        pairs.append((got.at[entry + EXPORTS, :, lanes], above_values.at[step]))
    pairs.append((query_hbm.at[:, pl.ds(kv * group * HEAD, group * HEAD)], query))
    copies = [
        pltpu.make_async_copy(source, target, sem.at[order])
        for order, (source, target) in enumerate(pairs)
    ]
    for copy in copies:
        copy.start()
    ones = jnp.ones((NODE_TOK, HEAD), all_values.dtype)
    nothing = jnp.zeros((NODE_TOK, 2 * HEAD), all_values.dtype)
    query_index = lax.broadcasted_iota(jnp.int32, (NODE_TOK, NODE_TOK), 0)
    key_index = lax.broadcasted_iota(jnp.int32, (NODE_TOK, NODE_TOK), 1)
    own_bias = jnp.where(key_index <= query_index, 0.0, DEAD)
    piece = math.gcd(NODE_TOK, per_part)
    pieces_part = per_part // piece
    me = lax.axis_index("tensor")
    above = (CHAIN + 1) * NODE_TOK
    for copy in copies:
        copy.wait()

    def node_rows(node):
        return pl.ds(pl.multiple_of(node * NODE_TOK, NODE_TOK), NODE_TOK)

    def put(place, order, key_block, value_block):
        rows = pl.ds(order * NODE_TOK, NODE_TOK)
        all_keys[place, rows, :] = key_block
        all_values[place, rows, :HEAD] = value_block
        all_values[place, rows, HEAD:] = ones

    def put_nothing(place, order, first_key):
        rows = pl.ds(order * NODE_TOK, NODE_TOK)
        all_keys[place, rows, :] = jnp.broadcast_to(first_key, (NODE_TOK, HEAD))
        all_values[place, rows, :] = nothing

    for place in range(side):
        for step in range(CHAIN):
            put(place, step, above_keys[step], above_values[step])

    def lay_out(place, node):
        own_key = keys[node_rows(node), :]
        put(place, CHAIN + 1, own_key, values[node_rows(node), :])
        for step in range(CHAIN):
            pl.when(step >= table[1])(functools.partial(put_nothing, place, step, own_key[:1]))
        is_root = node == table[0]
        pl.when(is_root)(functools.partial(put_nothing, place, CHAIN, own_key[:1]))

        @pl.when(jnp.logical_not(is_root))
        def _():
            put(place, CHAIN, keys[node_rows(table[0]), :], values[node_rows(table[0]), :])

    def score(place, node):
        stacked = jnp.concatenate(
            [query[node_rows(node), h * HEAD : (h + 1) * HEAD] for h in range(group)], 0
        )
        return times(stacked, all_keys[place])

    def weigh(scores):
        own = scores[:, above:] + jnp.concatenate([own_bias] * group, 0)
        masked = jnp.concatenate([scores[:, :above], own], 1)
        largest = jnp.max(masked, axis=1, keepdims=True)
        return jnp.exp2((masked - largest) * SCALE).astype(jnp.bfloat16)

    def finish(place, node, expo):
        mixed = jnp.dot(expo, all_values[place], preferred_element_type=jnp.float32)
        result = (mixed[:, :HEAD] / mixed[:, HEAD:]).astype(jnp.bfloat16)
        for part in range(NODE_TOK // piece):
            block = node * (NODE_TOK // piece) + part
            owner = block // pieces_part
            target = slot_position(parts, owner ^ me)
            inner = (block - owner * pieces_part) * piece
            to = pl.ds(pl.multiple_of(inner, piece), piece)
            for h in range(group):
                first = h * NODE_TOK + part * piece
                out[target, to, h * HEAD : (h + 1) * HEAD] = result[first : first + piece]

    def some_nodes(turn, carry):
        mine = [(place, turn * side + place) for place in range(side)]
        for place, node in mine:
            lay_out(place, node)
        scores = [score(place, node) for place, node in mine]
        for (place, node), each in zip(mine, scores):
            finish(place, node, weigh(each))
        return carry

    lax.fori_loop(0, nodes // side, some_nodes, 0)


def slot_position(parts, distance):
    half = parts // 2
    return jnp.where(distance % 2 == 1, distance // 2, half + distance // 2)


def in_hbm(array):
    return pltpu.with_memory_space_constraint(array, pltpu.HBM)


def attend(kv, table, queries, keys, values, got, parts, after):
    rows = queries.shape[0]
    width = queries.shape[1] // (keys.shape[1] // HEAD)
    total = (CHAIN + 2) * NODE_TOK
    side = 2 if rows % (2 * NODE_TOK) == 0 else 1
    hbm = pl.BlockSpec(memory_space=pltpu.HBM)
    return pl.pallas_call(
        functools.partial(attend_body, kv, parts),
        out_shape=jax.ShapeDtypeStruct((parts, rows // parts, width), queries.dtype),
        in_specs=[pl.BlockSpec(memory_space=pltpu.SMEM)]
        + [hbm] * 4
        + [pl.BlockSpec(memory_space=pl.ANY)] * len(after),
        scratch_shapes=[
            pltpu.VMEM((rows, width), queries.dtype),
            pltpu.VMEM((rows, HEAD), keys.dtype),
            pltpu.VMEM((rows, HEAD), keys.dtype),
            pltpu.VMEM((CHAIN, NODE_TOK, HEAD), keys.dtype),
            pltpu.VMEM((CHAIN, NODE_TOK, HEAD), keys.dtype),
            pltpu.VMEM((side, total, HEAD), keys.dtype),
            pltpu.VMEM((side, total, 2 * HEAD), keys.dtype),
            pltpu.SemaphoreType.DMA((3 + 2 * CHAIN,)),
        ],
        compiler_params=pltpu.CompilerParams(vmem_limit_bytes=ATTEND_LIMIT),
        cost_estimate=LIGHT,
        name="attend",
    )(table, *[in_hbm(x) for x in (queries, keys, values, got)], *after)


def swap(array, axis, distance):
    size = lax.axis_size(axis)
    return lax.ppermute(array, axis, [(i, i ^ distance) for i in range(size)])


def times(rows, weight):
    return lax.dot_general(
        rows, weight, (((1,), (1,)), ((), ())), preferred_element_type=jnp.float32
    )


def is_middle(index):
    return (index == 1) | (index == 2)


def product(parts, pieces, sent, kept):
    half = parts[0].shape[0] // 2
    for out, start in ((sent, 0), (kept, half)):
        whole = jnp.concatenate([part[start : start + half, :] for part in parts], 1)
        column = 0
        for weight, first, count in pieces:
            out[:, column : column + count] = times(
                whole, weight[first : first + count, :]
            ).astype(out.dtype)
            column += count


def core_sum(pair, upper):
    kept, from_core = pair
    half = kept.shape[0] // 2
    rows = slice(half, 2 * half) if upper else slice(0, half)
    return kept[rows, :].astype(jnp.float32) + from_core[rows, :].astype(jnp.float32)


def step_body(plan, *refs):
    refs = list(refs)

    def take(count):
        return [refs.pop(0) for _ in range(count)]

    rows = [take(count) for count in plan["rows"]]
    arrays = take(plan["arrays"])
    weights = [
        [[(arrays[index], first, count) for index, first, count in pieces] for pieces in weight]
        for weight in plan["weights"]
    ]
    cores = [[take(2) for _ in range(count)] for count in plan["cores"]]
    chips = [([take(2) for _ in range(count)], take(1)[0]) for count in plan["chips"]]
    take(plan["after"])
    outs = take(plan["outs"])
    middle = is_middle(lax.axis_index("node"))
    picks = (middle, jnp.logical_not(middle))
    fetched = None
    for order, weight in enumerate(weights):
        if len(weight) == 2 and not plan["direct"]:
            chosen, sem = refs
            fetched = order
            for pick, pieces in zip(picks, weight):
                column = 0
                for array, first, count in pieces:
                    source = array.at[pl.ds(first, count), :]
                    target = chosen.at[pl.ds(column, count), :]
                    pl.when(pick)(pltpu.make_async_copy(source, target, sem).start)
                    column += count
    made = [[(outs.pop(0), outs.pop(0)) for _ in rows] for _ in weights]
    for bundle in cores:
        out, column = outs.pop(0), 0
        for pair in bundle:
            width = pair[0].shape[1]
            out[:, column : column + width] = core_sum(pair, True).astype(out.dtype)
            column += width
    for bundle, from_chip in chips:
        column = start = 0
        for order, pair in enumerate(bundle):
            if order == 0 or not plan["join"]:
                out, start = outs.pop(0), column
            width = pair[0].shape[1]
            away = from_chip[:, column : column + width].astype(jnp.float32)
            total = (core_sum(pair, False) + away).astype(out.dtype)
            out[:, column - start : column - start + width] = total
            column += width
    for order, (weight, pairs) in enumerate(zip(weights, made)):
        if order == fetched:
            pltpu.make_async_copy(chosen, chosen, sem).wait()
            weight = [[(chosen, 0, chosen.shape[0])]]
        for parts, (sent, kept) in zip(rows, pairs):
            if len(weight) == 2:
                for pick, pieces in zip(picks, weight):
                    pl.when(pick)(functools.partial(product, parts, pieces, sent, kept))
            else:
                product(parts, weight[0], sent, kept)


def step(rows=(), weights=(), cores=(), chips=(), after=(), direct=False, join=False):
    weights = [weight if isinstance(weight, tuple) else (weight,) for weight in weights]
    arrays, fetch, plans = [], [], []
    for weight in weights:
        plans.append([])
        for pieces in weight:
            plans[-1].append([])
            for array, first, count in pieces:
                known = [index for index, x in enumerate(arrays) if x is array]
                if not known:
                    known = [len(arrays)]
                    arrays.append(array)
                    fetch.append(len(weight) == 2 and not direct)
                plans[-1][-1].append((known[0], first, count))
    widths = [sum(count for _, _, count in weight[0]) for weight in weights]
    shapes = []
    for width in widths:
        shapes += [(parts[0].shape[0] // 2, width) for parts in rows for _ in range(2)]
    for bundle in cores:
        shapes.append((bundle[0][0].shape[0] // 2, sum(kept.shape[1] for kept, _ in bundle)))
    for bundle in chips:
        each = [kept.shape[1] for kept, _ in bundle[:-1]]
        shapes += [(bundle[0][0].shape[0] // 2, w) for w in ([sum(each)] if join else each)]
    plan = {
        "rows": [len(parts) for parts in rows],
        "arrays": len(arrays),
        "weights": plans,
        "cores": [len(bundle) for bundle in cores],
        "chips": [len(bundle) - 1 for bundle in chips],
        "after": len(after),
        "outs": len(shapes),
        "direct": direct,
        "join": join,
    }
    vmem, hbm = pl.BlockSpec(memory_space=pltpu.VMEM), pl.BlockSpec(memory_space=pl.ANY)
    read = [(part, vmem) for parts in rows for part in parts]
    read += [(array, hbm if far else vmem) for array, far in zip(arrays, fetch)]
    read += [(x, vmem) for bundle in cores for pair in bundle for x in pair]
    for bundle in chips:
        read += [(x, vmem) for pair in bundle[:-1] for x in pair] + [(bundle[-1], vmem)]
    read += [(x, hbm) for x in after]
    dtype = read[0][0].dtype
    scratch = []
    if any(fetch):
        width = [w for w, weight in zip(widths, weights) if len(weight) == 2][0]
        scratch = [
            pltpu.VMEM((width, rows[0][0].shape[1] * len(rows[0])), dtype),
            pltpu.SemaphoreType.DMA,
        ]
    return pl.pallas_call(
        functools.partial(step_body, plan),
        out_shape=[jax.ShapeDtypeStruct(shape, dtype) for shape in shapes],
        in_specs=[spec for _, spec in read],
        scratch_shapes=scratch,
        compiler_params=pltpu.CompilerParams(vmem_limit_bytes=VMEM_LIMIT),
        cost_estimate=LIGHT,
        name="step",
    )(*[x for x, _ in read])


PAIRS = [(0, 1), (1, 0), (2, 3), (3, 2)]
MIDDLE = [(1, 2), (2, 1)]
OUTWARD = [(1, 0), (2, 3)]


def relay(piece, exported):
    near = lax.ppermute(piece, "node", PAIRS)
    across = lax.ppermute(piece, "node", MIDDLE)
    near, across, exported = lax.optimization_barrier((near, across, exported))
    across_out = lax.ppermute(across, "node", OUTWARD)
    near_across = lax.ppermute(near, "node", MIDDLE)
    return near, across, near_across, across_out


def place_body(spots, features, *refs):
    out = refs[-1]
    half = features // 2
    device = lax.axis_index("node")
    mine = lax.axis_index("groups")
    for source, (distance, side) in zip(refs[:-1], spots):
        group = {"own": mine, "other": 1 - mine, "first": 0, "second": 1}[side]
        column = pl.multiple_of((device ^ distance) * features + group * half, HEAD)
        out[:, pl.ds(column, source.shape[1])] = source[...]


def place(sources, spots, devices, features):
    return pl.pallas_call(
        functools.partial(place_body, spots, features),
        out_shape=jax.ShapeDtypeStruct(
            (sources[0].shape[0], devices * features), sources[0].dtype
        ),
        compiler_params=pltpu.CompilerParams(vmem_limit_bytes=VMEM_LIMIT),
        name="place",
    )(*sources)


def cut_body(weight, out, sem):
    half = out.shape[0]
    first = pl.multiple_of(lax.axis_index("groups") * half, half)
    copy = pltpu.make_async_copy(weight.at[pl.ds(first, half), :], out, sem)
    copy.start()
    copy.wait()


def cut(weight):
    return pl.pallas_call(
        cut_body,
        out_shape=jax.ShapeDtypeStruct((weight.shape[0] // 2, weight.shape[1]), weight.dtype),
        in_specs=[pl.BlockSpec(memory_space=pltpu.HBM)],
        out_specs=pl.BlockSpec(memory_space=pltpu.VMEM),
        scratch_shapes=[pltpu.SemaphoreType.DMA],
        compiler_params=pltpu.CompilerParams(vmem_limit_bytes=VMEM_LIMIT),
        cost_estimate=LIGHT,
        name="cut",
    )(in_hbm(weight))


def project_split(halves, relayed, out_weight):
    features = out_weight.shape[0]
    half = features // 2
    rows = [part.reshape(-1, part.shape[-1]) for part in halves]
    other = [swap(part, "groups", 1) for part in rows]
    near, across, near_across, across_out = relayed
    far_out = lax.ppermute(near_across, "node", OUTWARD)

    def core(sent):
        return swap(sent, "tensor", 1)

    def chip(away):
        return swap(away, "tensor", 2)

    def back(done):
        return swap(done, "groups", 1)

    def whole(weight):
        return [(weight, 0, weight.shape[0])]

    second = (whole(near_across), whole(across_out))
    far = (whole(across), whole(far_out))

    sent_a, kept_a, sent_b, kept_b = step(
        [rows], [[(out_weight, 0, half)], [(out_weight, half, half)]]
    )
    one = [(kept_a, core(sent_a)), (kept_b, core(sent_b))]
    (away,) = step(cores=[one])
    one.append(chip(away))
    sent_1, kept_1 = step([rows], [whole(near)], after=[away, other[0]])
    sent_2, kept_2, done_a, done_b = step([rows], [second], chips=[one], after=[sent_1])
    two = [(kept_1, core(sent_1)), (kept_2, core(sent_2))]
    (away,) = step(cores=[two])
    two.append(chip(away))
    first = (half // HEAD + 1) // 2 * HEAD
    sent_3, kept_3, sent_c, kept_c, sent_4, kept_4 = step(
        [other], [[(near, 0, first)], [(near, first, half - first)], second], after=[away]
    )
    three = [(kept_3, core(sent_3)), (kept_c, core(sent_c))]
    four = [(kept_4, core(sent_4))]
    away, done_1, done_2 = step(cores=[three], chips=[two])
    three.append(chip(away))
    away, done_3 = step(cores=[four], chips=[three], join=True)
    four.append(chip(away))
    back_3 = back(done_3)
    sent_5, kept_5 = step([other], [far], after=[away, back_3], direct=True)
    five = [(kept_5, core(sent_5))]
    (done_4,) = step(chips=[four], after=[sent_5])
    back_4 = back(done_4)
    sent_6, kept_6 = step([rows], [far], after=[done_4], direct=True)
    six = [(kept_6, core(sent_6))]
    (away,) = step(cores=[five], after=[sent_6])
    five.append(chip(away))
    (away,) = step(cores=[six], after=[away])
    six.append(chip(away))
    (done_5,) = step(chips=[five], after=[away, back_4])
    back_5 = back(done_5)
    (done_6,) = step(chips=[six], after=[done_5])
    return place(
        (done_a, done_b, done_1, done_2, back_3, back_4, back_5, done_6),
        (
            (0, "first"),
            (0, "second"),
            (1, "own"),
            (2, "own"),
            (1, "other"),
            (2, "other"),
            (3, "other"),
            (3, "own"),
        ),
        lax.axis_size("node"),
        features,
    )


def project_plain(halves, out_weight):
    attended = jnp.concatenate(halves, 2)
    parts, per_part, width = attended.shape
    me = lax.axis_index("tensor")
    order = slot_position(parts, jnp.arange(parts, dtype=jnp.int32) ^ me)
    rows = attended[order].reshape(parts * per_part, width)
    weight = lax.all_gather(out_weight, "node", axis=0, tiled=True)
    terms = times(rows, weight).astype(jnp.bfloat16)
    return lax.psum_scatter(terms, "tensor", scatter_dimension=0, tiled=True)


def local(queries, keys, values, out_weight, slot_nodes, ancestors, depth):
    parts = lax.axis_size("tensor")
    devices = lax.axis_size("node")
    features = out_weight.shape[0]
    kv_count = keys.shape[1] // HEAD
    relayed, after = None, []
    exported, table = prepare(slot_nodes, ancestors, depth, keys, values)
    got = lax.all_gather(exported, "node", axis=0, tiled=True)
    if (
        devices == 4
        and parts == 4
        and lax.axis_size("groups") == 2
        and features % (2 * HEAD) == 0
    ):
        relayed = relay(cut(out_weight), exported)
        after = relayed[:2]
    halves = []
    for kv in range(kv_count):
        halves.append(attend(kv, table, queries, keys, values, got, parts, after))
        after = halves[-1:]
    if relayed is None:
        return project_plain(halves, out_weight)
    return project_split(halves, relayed, out_weight)


def solution(mesh):
    placed = (
        P(("groups", "node"), "tensor"),
        P(("groups", "node"), "tensor"),
        P(("groups", "node"), "tensor"),
        P("node", "tensor"),
        P("groups"),
        P("groups", None),
        P("groups"),
    )
    return jax.shard_map(
        local,
        mesh=mesh,
        in_specs=placed,
        out_specs=P(("groups", "node", "tensor"), None),
        check_vma=False,
    )
```

```python
import functools
import math

import jax
import jax.numpy as jnp
from jax import lax
from jax.experimental import pallas as pl
from jax.experimental.pallas import tpu as pltpu
from jax.sharding import PartitionSpec as P

HEAD = 128
NODE_TOK = 128
A_MAX = 7
CHAIN = A_MAX - 1
EXPORTS = 2
SCALE = math.log2(math.e) / math.sqrt(HEAD)
DEAD = -1e30
LIGHT = pl.CostEstimate(flops=1, bytes_accessed=1, transcendentals=0)
VMEM_LIMIT = 20 * 1024 * 1024
ATTEND_LIMIT = 24 * 1024 * 1024


def prepare_body(nodes, *refs):
    slot_hbm, ancestors_hbm, depth_hbm, keys, values, exported, table_hbm = refs[:7]
    slot_nodes, ancestors, depth, table, holder, within, roots, sem = refs[7:]
    devices = slot_nodes.shape[0] // nodes
    me = lax.axis_index("node")
    fetches = [
        pltpu.make_async_copy(source, target, sem.at[2 * EXPORTS + 1 + order])
        for order, (source, target) in enumerate(
            ((slot_hbm, slot_nodes), (ancestors_hbm, ancestors), (depth_hbm, depth))
        )
    ]
    for fetch in fetches:
        fetch.start()
    for fetch in fetches:
        fetch.wait()

    def place(device, mine):
        root, root_index = jnp.int32(0), jnp.int32(0)
        for index in range(nodes):
            node = slot_nodes[device * nodes + index]
            holder[node] = device
            within[node] = index
            even = (depth[node] & 1) == 0
            root = jnp.where(even, node, root)
            root_index = jnp.where(even, index, root_index)
        roots[device] = root
        return jnp.where(device == me, root_index, mine)

    root = lax.fori_loop(0, devices, place, jnp.int32(0))

    def find_attach(device, attach):
        node = roots[device]
        level = depth[node]
        for step in range(0, CHAIN, 2):
            above = jnp.maximum(ancestors[step, node], 0)
            hit = (step < level) & (holder[above] == me)
            attach = jnp.where(hit, within[above], attach)
        return attach

    attach = lax.fori_loop(0, devices, find_attach, jnp.int32(0))
    copies = []
    for position, (source, index) in enumerate(
        ((keys, root), (keys, attach), (values, root), (values, attach))
    ):
        rows = pl.ds(pl.multiple_of(index * NODE_TOK, NODE_TOK), NODE_TOK)
        copies.append(
            pltpu.make_async_copy(source.at[rows, :], exported.at[position], sem.at[position])
        )
    for copy in copies:
        copy.start()
    root_node = roots[me]
    count = depth[root_node]
    table[0] = root
    table[1] = count
    for step in range(CHAIN):
        above = jnp.maximum(ancestors[step, root_node], 0)
        entry = holder[above] * (2 * EXPORTS) + (1 if step % 2 == 0 else 0)
        table[2 + step] = jnp.where(step < count, entry, 0)
    store = pltpu.make_async_copy(table, table_hbm, sem.at[2 * EXPORTS])
    store.start()
    for copy in (*copies, store):
        copy.wait()


def prepare(slot_nodes, ancestors, depth, keys, values):
    nodes = keys.shape[0] // NODE_TOK
    slots = slot_nodes.shape[0]
    hbm = pl.BlockSpec(memory_space=pltpu.HBM)
    vmem = pl.BlockSpec(memory_space=pltpu.VMEM)
    return pl.pallas_call(
        functools.partial(prepare_body, nodes),
        out_shape=(
            jax.ShapeDtypeStruct((2 * EXPORTS, NODE_TOK, keys.shape[1]), keys.dtype),
            jax.ShapeDtypeStruct((2 + CHAIN,), jnp.int32),
        ),
        in_specs=[hbm, hbm, hbm, vmem, vmem],
        out_specs=(hbm, hbm),
        scratch_shapes=[
            pltpu.SMEM((slots,), jnp.int32),
            pltpu.SMEM((A_MAX, slots), jnp.int32),
            pltpu.SMEM((slots,), jnp.int32),
            pltpu.SMEM((2 + CHAIN,), jnp.int32),
            pltpu.SMEM((slots,), jnp.int32),
            pltpu.SMEM((slots,), jnp.int32),
            pltpu.SMEM((slots // nodes,), jnp.int32),
            pltpu.SemaphoreType.DMA((2 * EXPORTS + 4,)),
        ],
        compiler_params=pltpu.CompilerParams(vmem_limit_bytes=VMEM_LIMIT),
        name="prepare",
    )(slot_nodes, ancestors.T, depth, keys, values)


def attend_body(kv, parts, table, query_hbm, keys_hbm, values_hbm, got, *refs):
    out, query, keys, values, above_keys, above_values, all_keys, all_values, sem = refs[-9:]
    nodes = query.shape[0] // NODE_TOK
    group = query.shape[1] // HEAD
    per_part = query.shape[0] // parts
    side = all_keys.shape[0]
    lanes = pl.ds(kv * HEAD, HEAD)
    pairs = [(keys_hbm.at[:, lanes], keys), (values_hbm.at[:, lanes], values)]
    for step in range(CHAIN):
        entry = table[2 + step]
        pairs.append((got.at[entry, :, lanes], above_keys.at[step]))
        pairs.append((got.at[entry + EXPORTS, :, lanes], above_values.at[step]))
    pairs.append((query_hbm.at[:, pl.ds(kv * group * HEAD, group * HEAD)], query))
    copies = [
        pltpu.make_async_copy(source, target, sem.at[order])
        for order, (source, target) in enumerate(pairs)
    ]
    for copy in copies:
        copy.start()
    ones = jnp.ones((NODE_TOK, HEAD), all_values.dtype)
    nothing = jnp.zeros((NODE_TOK, 2 * HEAD), all_values.dtype)
    query_index = lax.broadcasted_iota(jnp.int32, (NODE_TOK, NODE_TOK), 0)
    key_index = lax.broadcasted_iota(jnp.int32, (NODE_TOK, NODE_TOK), 1)
    own_bias = jnp.where(key_index <= query_index, 0.0, DEAD)
    piece = math.gcd(NODE_TOK, per_part)
    pieces_part = per_part // piece
    me = lax.axis_index("tensor")
    above = (CHAIN + 1) * NODE_TOK
    for copy in copies:
        copy.wait()

    def node_rows(node):
        return pl.ds(pl.multiple_of(node * NODE_TOK, NODE_TOK), NODE_TOK)

    def put(place, order, key_block, value_block):
        rows = pl.ds(order * NODE_TOK, NODE_TOK)
        all_keys[place, rows, :] = key_block
        all_values[place, rows, :HEAD] = value_block
        all_values[place, rows, HEAD:] = ones

    def put_nothing(place, order, first_key):
        rows = pl.ds(order * NODE_TOK, NODE_TOK)
        all_keys[place, rows, :] = jnp.broadcast_to(first_key, (NODE_TOK, HEAD))
        all_values[place, rows, :] = nothing

    for place in range(side):
        for step in range(CHAIN):
            put(place, step, above_keys[step], above_values[step])

    def lay_out(place, node):
        own_key = keys[node_rows(node), :]
        put(place, CHAIN + 1, own_key, values[node_rows(node), :])
        for step in range(CHAIN):
            pl.when(step >= table[1])(functools.partial(put_nothing, place, step, own_key[:1]))
        is_root = node == table[0]
        pl.when(is_root)(functools.partial(put_nothing, place, CHAIN, own_key[:1]))

        @pl.when(jnp.logical_not(is_root))
        def _():
            put(place, CHAIN, keys[node_rows(table[0]), :], values[node_rows(table[0]), :])

    def score(place, node):
        stacked = jnp.concatenate(
            [query[node_rows(node), h * HEAD : (h + 1) * HEAD] for h in range(group)], 0
        )
        return times(stacked, all_keys[place])

    def weigh(scores):
        own = scores[:, above:] + jnp.concatenate([own_bias] * group, 0)
        masked = jnp.concatenate([scores[:, :above], own], 1)
        largest = jnp.max(masked, axis=1, keepdims=True)
        return jnp.exp2((masked - largest) * SCALE).astype(jnp.bfloat16)

    def finish(place, node, expo):
        mixed = jnp.dot(expo, all_values[place], preferred_element_type=jnp.float32)
        result = (mixed[:, :HEAD] / mixed[:, HEAD:]).astype(jnp.bfloat16)
        for part in range(NODE_TOK // piece):
            block = node * (NODE_TOK // piece) + part
            owner = block // pieces_part
            target = slot_position(parts, owner ^ me)
            inner = (block - owner * pieces_part) * piece
            to = pl.ds(pl.multiple_of(inner, piece), piece)
            for h in range(group):
                first = h * NODE_TOK + part * piece
                out[target, to, h * HEAD : (h + 1) * HEAD] = result[first : first + piece]

    def some_nodes(turn, carry):
        mine = [(place, turn * side + place) for place in range(side)]
        for place, node in mine:
            lay_out(place, node)
        scores = [score(place, node) for place, node in mine]
        for (place, node), each in zip(mine, scores):
            finish(place, node, weigh(each))
        return carry

    lax.fori_loop(0, nodes // side, some_nodes, 0)


def slot_position(parts, distance):
    half = parts // 2
    return jnp.where(distance % 2 == 1, distance // 2, half + distance // 2)


def in_hbm(array):
    return pltpu.with_memory_space_constraint(array, pltpu.HBM)


def attend(kv, table, queries, keys, values, got, parts, after):
    rows = queries.shape[0]
    width = queries.shape[1] // (keys.shape[1] // HEAD)
    total = (CHAIN + 2) * NODE_TOK
    side = 2 if rows % (2 * NODE_TOK) == 0 else 1
    hbm = pl.BlockSpec(memory_space=pltpu.HBM)
    return pl.pallas_call(
        functools.partial(attend_body, kv, parts),
        out_shape=jax.ShapeDtypeStruct((parts, rows // parts, width), queries.dtype),
        in_specs=[pl.BlockSpec(memory_space=pltpu.SMEM)]
        + [hbm] * 4
        + [pl.BlockSpec(memory_space=pl.ANY)] * len(after),
        scratch_shapes=[
            pltpu.VMEM((rows, width), queries.dtype),
            pltpu.VMEM((rows, HEAD), keys.dtype),
            pltpu.VMEM((rows, HEAD), keys.dtype),
            pltpu.VMEM((CHAIN, NODE_TOK, HEAD), keys.dtype),
            pltpu.VMEM((CHAIN, NODE_TOK, HEAD), keys.dtype),
            pltpu.VMEM((side, total, HEAD), keys.dtype),
            pltpu.VMEM((side, total, 2 * HEAD), keys.dtype),
            pltpu.SemaphoreType.DMA((3 + 2 * CHAIN,)),
        ],
        compiler_params=pltpu.CompilerParams(vmem_limit_bytes=ATTEND_LIMIT),
        cost_estimate=LIGHT,
        name="attend",
    )(table, *[in_hbm(x) for x in (queries, keys, values, got)], *after)


def swap(array, axis, distance):
    size = lax.axis_size(axis)
    return lax.ppermute(array, axis, [(i, i ^ distance) for i in range(size)])


def times(rows, weight):
    return lax.dot_general(
        rows, weight, (((1,), (1,)), ((), ())), preferred_element_type=jnp.float32
    )


def is_middle(index):
    return (index == 1) | (index == 2)


def product(parts, pieces, sent, kept):
    half = parts[0].shape[0] // 2
    for out, start in ((sent, 0), (kept, half)):
        whole = jnp.concatenate([part[start : start + half, :] for part in parts], 1)
        column = 0
        for weight, first, count in pieces:
            out[:, column : column + count] = times(
                whole, weight[first : first + count, :]
            ).astype(out.dtype)
            column += count


def core_sum(pair, upper):
    kept, from_core = pair
    half = kept.shape[0] // 2
    rows = slice(half, 2 * half) if upper else slice(0, half)
    return kept[rows, :].astype(jnp.float32) + from_core[rows, :].astype(jnp.float32)


def step_body(plan, *refs):
    refs = list(refs)

    def take(count):
        return [refs.pop(0) for _ in range(count)]

    rows = [take(count) for count in plan["rows"]]
    arrays = take(plan["arrays"])
    weights = [
        [[(arrays[index], first, count) for index, first, count in pieces] for pieces in weight]
        for weight in plan["weights"]
    ]
    cores = [[take(2) for _ in range(count)] for count in plan["cores"]]
    chips = [([take(2) for _ in range(count)], take(1)[0]) for count in plan["chips"]]
    take(plan["after"])
    outs = take(plan["outs"])
    middle = is_middle(lax.axis_index("node"))
    picks = (middle, jnp.logical_not(middle))
    fetched = None
    for order, weight in enumerate(weights):
        if len(weight) == 2 and not plan["direct"]:
            chosen, sem = refs
            fetched = order
            for pick, pieces in zip(picks, weight):
                column = 0
                for array, first, count in pieces:
                    source = array.at[pl.ds(first, count), :]
                    target = chosen.at[pl.ds(column, count), :]
                    pl.when(pick)(pltpu.make_async_copy(source, target, sem).start)
                    column += count
    made = [[(outs.pop(0), outs.pop(0)) for _ in rows] for _ in weights]
    for bundle in cores:
        out, column = outs.pop(0), 0
        for pair in bundle:
            width = pair[0].shape[1]
            out[:, column : column + width] = core_sum(pair, True).astype(out.dtype)
            column += width
    for bundle, from_chip in chips:
        column = 0
        for pair in bundle:
            out = outs.pop(0)
            width = out.shape[1]
            away = from_chip[:, column : column + width].astype(jnp.float32)
            out[...] = (core_sum(pair, False) + away).astype(out.dtype)
            column += width
    for order, (weight, pairs) in enumerate(zip(weights, made)):
        if order == fetched:
            pltpu.make_async_copy(chosen, chosen, sem).wait()
            weight = [[(chosen, 0, chosen.shape[0])]]
        for parts, (sent, kept) in zip(rows, pairs):
            if len(weight) == 2:
                for pick, pieces in zip(picks, weight):
                    pl.when(pick)(functools.partial(product, parts, pieces, sent, kept))
            else:
                product(parts, weight[0], sent, kept)


def step(rows=(), weights=(), cores=(), chips=(), after=(), direct=False):
    weights = [weight if isinstance(weight, tuple) else (weight,) for weight in weights]
    arrays, fetch, plans = [], [], []
    for weight in weights:
        plans.append([])
        for pieces in weight:
            plans[-1].append([])
            for array, first, count in pieces:
                known = [index for index, x in enumerate(arrays) if x is array]
                if not known:
                    known = [len(arrays)]
                    arrays.append(array)
                    fetch.append(len(weight) == 2 and not direct)
                plans[-1][-1].append((known[0], first, count))
    widths = [sum(count for _, _, count in weight[0]) for weight in weights]
    shapes = []
    for width in widths:
        shapes += [(parts[0].shape[0] // 2, width) for parts in rows for _ in range(2)]
    for bundle in cores:
        shapes.append((bundle[0][0].shape[0] // 2, sum(kept.shape[1] for kept, _ in bundle)))
    for bundle in chips:
        shapes += [(kept.shape[0] // 2, kept.shape[1]) for kept, _ in bundle[:-1]]
    plan = {
        "rows": [len(parts) for parts in rows],
        "arrays": len(arrays),
        "weights": plans,
        "cores": [len(bundle) for bundle in cores],
        "chips": [len(bundle) - 1 for bundle in chips],
        "after": len(after),
        "outs": len(shapes),
        "direct": direct,
    }
    vmem, hbm = pl.BlockSpec(memory_space=pltpu.VMEM), pl.BlockSpec(memory_space=pl.ANY)
    read = [(part, vmem) for parts in rows for part in parts]
    read += [(array, hbm if far else vmem) for array, far in zip(arrays, fetch)]
    read += [(x, vmem) for bundle in cores for pair in bundle for x in pair]
    for bundle in chips:
        read += [(x, vmem) for pair in bundle[:-1] for x in pair] + [(bundle[-1], vmem)]
    read += [(x, hbm) for x in after]
    dtype = read[0][0].dtype
    scratch = []
    if any(fetch):
        width = [w for w, weight in zip(widths, weights) if len(weight) == 2][0]
        scratch = [
            pltpu.VMEM((width, rows[0][0].shape[1] * len(rows[0])), dtype),
            pltpu.SemaphoreType.DMA,
        ]
    return pl.pallas_call(
        functools.partial(step_body, plan),
        out_shape=[jax.ShapeDtypeStruct(shape, dtype) for shape in shapes],
        in_specs=[spec for _, spec in read],
        scratch_shapes=scratch,
        compiler_params=pltpu.CompilerParams(vmem_limit_bytes=VMEM_LIMIT),
        cost_estimate=LIGHT,
        name="step",
    )(*[x for x, _ in read])


PAIRS = [(0, 1), (1, 0), (2, 3), (3, 2)]
MIDDLE = [(1, 2), (2, 1)]
OUTWARD = [(1, 0), (2, 3)]


def relay(piece, exported):
    near = lax.ppermute(piece, "node", PAIRS)
    across = lax.ppermute(piece, "node", MIDDLE)
    near, _ = lax.optimization_barrier((near, exported))
    across, _ = lax.optimization_barrier((across, exported))
    across_out = lax.ppermute(across, "node", OUTWARD)
    near_across = lax.ppermute(near, "node", MIDDLE)
    return near, across, near_across, across_out


def place_body(spots, features, *refs):
    out = refs[-1]
    half = features // 2
    device = lax.axis_index("node")
    mine = lax.axis_index("groups")
    for source, (distance, side, offset) in zip(refs[:-1], spots):
        group = {"own": mine, "other": 1 - mine, "first": 0}[side]
        column = pl.multiple_of((device ^ distance) * features + group * half + offset, HEAD)
        out[:, pl.ds(column, source.shape[1])] = source[...]


def place(sources, spots, devices, features):
    return pl.pallas_call(
        functools.partial(place_body, spots, features),
        out_shape=jax.ShapeDtypeStruct(
            (sources[0].shape[0], devices * features), sources[0].dtype
        ),
        compiler_params=pltpu.CompilerParams(vmem_limit_bytes=VMEM_LIMIT),
        name="place",
    )(*sources)


def cut_body(weight, out, sem):
    half = out.shape[0]
    first = pl.multiple_of(lax.axis_index("groups") * half, half)
    copy = pltpu.make_async_copy(weight.at[pl.ds(first, half), :], out, sem)
    copy.start()
    copy.wait()


def cut(weight):
    return pl.pallas_call(
        cut_body,
        out_shape=jax.ShapeDtypeStruct((weight.shape[0] // 2, weight.shape[1]), weight.dtype),
        in_specs=[pl.BlockSpec(memory_space=pltpu.HBM)],
        out_specs=pl.BlockSpec(memory_space=pltpu.VMEM),
        scratch_shapes=[pltpu.SemaphoreType.DMA],
        compiler_params=pltpu.CompilerParams(vmem_limit_bytes=VMEM_LIMIT),
        cost_estimate=LIGHT,
        name="cut",
    )(in_hbm(weight))


def project_split(halves, relayed, out_weight):
    features = out_weight.shape[0]
    half = features // 2
    rows = [part.reshape(-1, part.shape[-1]) for part in halves]
    other = [swap(part, "groups", 1) for part in rows]
    near, across, near_across, across_out = relayed
    far_out = lax.ppermute(near_across, "node", OUTWARD)

    def core(sent):
        return swap(sent, "tensor", 1)

    def chip(away):
        return swap(away, "tensor", 2)

    def back(done):
        return swap(done, "groups", 1)

    def whole(weight):
        return [(weight, 0, weight.shape[0])]

    second = (whole(near_across), whole(across_out))
    far = (whole(across), whole(far_out))

    last = features - HEAD
    sent_a, kept_a, sent_b, kept_b, sent_c, kept_c = step(
        [rows],
        [[(out_weight, 0, half)], [(out_weight, half, last - half)], [(out_weight, last, HEAD)]],
    )
    one = [(kept_a, core(sent_a)), (kept_b, core(sent_b))]
    (away,) = step(cores=[one])
    one.append(chip(away))
    sent_1, kept_1 = step([rows], [whole(near)], after=[away, other[0]])
    sent_2, kept_2, done_a, done_b = step([rows], [second], chips=[one], after=[sent_1])
    two = [(kept_c, core(sent_c)), (kept_1, core(sent_1)), (kept_2, core(sent_2))]
    (away,) = step(cores=[two])
    two.append(chip(away))
    sent_3, kept_3, sent_4, kept_4 = step([other], [whole(near), second], after=[away])
    three = [(kept_3, core(sent_3))]
    four = [(kept_4, core(sent_4))]
    away, done_c, done_1, done_2 = step(cores=[three], chips=[two])
    three.append(chip(away))
    away, done_3 = step(cores=[four], chips=[three])
    four.append(chip(away))
    back_3 = back(done_3)
    sent_5, kept_5 = step([other], [far], after=[away], direct=True)
    five = [(kept_5, core(sent_5))]
    (done_4,) = step(chips=[four], after=[sent_5, back_3])
    back_4 = back(done_4)
    sent_6, kept_6 = step([rows], [far], after=[done_4], direct=True)
    six = [(kept_6, core(sent_6))]
    (away,) = step(cores=[five], after=[sent_6])
    five.append(chip(away))
    (away,) = step(cores=[six], after=[away])
    six.append(chip(away))
    (done_5,) = step(chips=[five], after=[away, back_4])
    back_5 = back(done_5)
    (done_6,) = step(chips=[six], after=[done_5])
    return place(
        (done_a, done_b, done_c, done_1, done_2, back_3, back_4, back_5, done_6),
        (
            (0, "first", 0),
            (0, "first", half),
            (0, "first", last),
            (1, "own", 0),
            (2, "own", 0),
            (1, "other", 0),
            (2, "other", 0),
            (3, "other", 0),
            (3, "own", 0),
        ),
        lax.axis_size("node"),
        features,
    )


def project_plain(halves, out_weight):
    attended = jnp.concatenate(halves, 2)
    parts, per_part, width = attended.shape
    me = lax.axis_index("tensor")
    order = slot_position(parts, jnp.arange(parts, dtype=jnp.int32) ^ me)
    rows = attended[order].reshape(parts * per_part, width)
    weight = lax.all_gather(out_weight, "node", axis=0, tiled=True)
    terms = times(rows, weight).astype(jnp.bfloat16)
    return lax.psum_scatter(terms, "tensor", scatter_dimension=0, tiled=True)


def local(queries, keys, values, out_weight, slot_nodes, ancestors, depth):
    parts = lax.axis_size("tensor")
    devices = lax.axis_size("node")
    features = out_weight.shape[0]
    kv_count = keys.shape[1] // HEAD
    relayed, after = None, []
    exported, table = prepare(slot_nodes, ancestors, depth, keys, values)
    got = lax.all_gather(exported, "node", axis=0, tiled=True)
    if (
        devices == 4
        and parts == 4
        and lax.axis_size("groups") == 2
        and features % (2 * HEAD) == 0
    ):
        relayed = relay(cut(out_weight), exported)
        after = relayed[:2]
    halves = []
    for kv in range(kv_count):
        halves.append(attend(kv, table, queries, keys, values, got, parts, after))
        after = halves[-1:]
    if relayed is None:
        return project_plain(halves, out_weight)
    return project_split(halves, relayed, out_weight)


def solution(mesh):
    placed = (
        P(("groups", "node"), "tensor"),
        P(("groups", "node"), "tensor"),
        P(("groups", "node"), "tensor"),
        P("node", "tensor"),
        P("groups"),
        P("groups", None),
        P("groups"),
    )
    return jax.shard_map(
        local,
        mesh=mesh,
        in_specs=placed,
        out_specs=P(("groups", "node", "tensor"), None),
        check_vma=False,
    )
```

```python
import functools
import math

import jax
import jax.numpy as jnp
from jax import lax
from jax.experimental import pallas as pl
from jax.experimental.pallas import tpu as pltpu
from jax.sharding import PartitionSpec as P

HEAD = 128
NODE_TOK = 128
A_MAX = 7
CHAIN = A_MAX - 1
EXPORTS = 2
SCALE = math.log2(math.e) / math.sqrt(HEAD)
DEAD = -1e30
LIGHT = pl.CostEstimate(flops=1, bytes_accessed=1, transcendentals=0)
VMEM_LIMIT = 20 * 1024 * 1024
ATTEND_LIMIT = 24 * 1024 * 1024


def prepare_body(nodes, *refs):
    slot_hbm, ancestors_hbm, depth_hbm, keys, values, exported, table_hbm = refs[:7]
    slot_nodes, ancestors, depth, table, holder, within, roots, sem = refs[7:]
    devices = slot_nodes.shape[0] // nodes
    me = lax.axis_index("node")
    fetches = [
        pltpu.make_async_copy(source, target, sem.at[2 * EXPORTS + 1 + order])
        for order, (source, target) in enumerate(
            ((slot_hbm, slot_nodes), (ancestors_hbm, ancestors), (depth_hbm, depth))
        )
    ]
    for fetch in fetches:
        fetch.start()
    for fetch in fetches:
        fetch.wait()

    def place(device, mine):
        root, root_index = jnp.int32(0), jnp.int32(0)
        for index in range(nodes):
            node = slot_nodes[device * nodes + index]
            holder[node] = device
            within[node] = index
            even = (depth[node] & 1) == 0
            root = jnp.where(even, node, root)
            root_index = jnp.where(even, index, root_index)
        roots[device] = root
        return jnp.where(device == me, root_index, mine)

    root = lax.fori_loop(0, devices, place, jnp.int32(0))

    def find_attach(device, attach):
        node = roots[device]
        level = depth[node]
        for step in range(0, CHAIN, 2):
            above = jnp.maximum(ancestors[step, node], 0)
            hit = (step < level) & (holder[above] == me)
            attach = jnp.where(hit, within[above], attach)
        return attach

    attach = lax.fori_loop(0, devices, find_attach, jnp.int32(0))
    copies = []
    for position, (source, index) in enumerate(
        ((keys, root), (keys, attach), (values, root), (values, attach))
    ):
        rows = pl.ds(pl.multiple_of(index * NODE_TOK, NODE_TOK), NODE_TOK)
        copies.append(
            pltpu.make_async_copy(source.at[rows, :], exported.at[position], sem.at[position])
        )
    for copy in copies:
        copy.start()
    root_node = roots[me]
    count = depth[root_node]
    table[0] = root
    table[1] = count
    for step in range(CHAIN):
        above = jnp.maximum(ancestors[step, root_node], 0)
        entry = holder[above] * (2 * EXPORTS) + (1 if step % 2 == 0 else 0)
        table[2 + step] = jnp.where(step < count, entry, 0)
    store = pltpu.make_async_copy(table, table_hbm, sem.at[2 * EXPORTS])
    store.start()
    for copy in (*copies, store):
        copy.wait()


def prepare(slot_nodes, ancestors, depth, keys, values):
    nodes = keys.shape[0] // NODE_TOK
    slots = slot_nodes.shape[0]
    hbm = pl.BlockSpec(memory_space=pltpu.HBM)
    vmem = pl.BlockSpec(memory_space=pltpu.VMEM)
    return pl.pallas_call(
        functools.partial(prepare_body, nodes),
        out_shape=(
            jax.ShapeDtypeStruct((2 * EXPORTS, NODE_TOK, keys.shape[1]), keys.dtype),
            jax.ShapeDtypeStruct((2 + CHAIN,), jnp.int32),
        ),
        in_specs=[hbm, hbm, hbm, vmem, vmem],
        out_specs=(hbm, hbm),
        scratch_shapes=[
            pltpu.SMEM((slots,), jnp.int32),
            pltpu.SMEM((A_MAX, slots), jnp.int32),
            pltpu.SMEM((slots,), jnp.int32),
            pltpu.SMEM((2 + CHAIN,), jnp.int32),
            pltpu.SMEM((slots,), jnp.int32),
            pltpu.SMEM((slots,), jnp.int32),
            pltpu.SMEM((slots // nodes,), jnp.int32),
            pltpu.SemaphoreType.DMA((2 * EXPORTS + 4,)),
        ],
        compiler_params=pltpu.CompilerParams(vmem_limit_bytes=VMEM_LIMIT),
        name="prepare",
    )(slot_nodes, ancestors.T, depth, keys, values)


def attend_body(kv, parts, table, query_hbm, keys_hbm, values_hbm, got, *refs):
    out, query, keys, values, above_keys, above_values, all_keys, all_values, sem = refs[-9:]
    nodes = query.shape[0] // NODE_TOK
    group = query.shape[1] // HEAD
    per_part = query.shape[0] // parts
    side = all_keys.shape[0]
    lanes = pl.ds(kv * HEAD, HEAD)
    pairs = [(keys_hbm.at[:, lanes], keys), (values_hbm.at[:, lanes], values)]
    for step in range(CHAIN):
        entry = table[2 + step]
        pairs.append((got.at[entry, :, lanes], above_keys.at[step]))
        pairs.append((got.at[entry + EXPORTS, :, lanes], above_values.at[step]))
    pairs.append((query_hbm.at[:, pl.ds(kv * group * HEAD, group * HEAD)], query))
    copies = [
        pltpu.make_async_copy(source, target, sem.at[order])
        for order, (source, target) in enumerate(pairs)
    ]
    for copy in copies:
        copy.start()
    ones = jnp.ones((NODE_TOK, HEAD), all_values.dtype)
    nothing = jnp.zeros((NODE_TOK, 2 * HEAD), all_values.dtype)
    query_index = lax.broadcasted_iota(jnp.int32, (NODE_TOK, NODE_TOK), 0)
    key_index = lax.broadcasted_iota(jnp.int32, (NODE_TOK, NODE_TOK), 1)
    own_bias = jnp.where(key_index <= query_index, 0.0, DEAD)
    piece = math.gcd(NODE_TOK, per_part)
    pieces_part = per_part // piece
    me = lax.axis_index("tensor")
    above = (CHAIN + 1) * NODE_TOK
    for copy in copies:
        copy.wait()

    def node_rows(node):
        return pl.ds(pl.multiple_of(node * NODE_TOK, NODE_TOK), NODE_TOK)

    def put(place, order, key_block, value_block):
        rows = pl.ds(order * NODE_TOK, NODE_TOK)
        all_keys[place, rows, :] = key_block
        all_values[place, rows, :HEAD] = value_block
        all_values[place, rows, HEAD:] = ones

    def put_nothing(place, order, first_key):
        rows = pl.ds(order * NODE_TOK, NODE_TOK)
        all_keys[place, rows, :] = jnp.broadcast_to(first_key, (NODE_TOK, HEAD))
        all_values[place, rows, :] = nothing

    for place in range(side):
        for step in range(CHAIN):
            put(place, step, above_keys[step], above_values[step])

    def lay_out(place, node):
        own_key = keys[node_rows(node), :]
        put(place, CHAIN + 1, own_key, values[node_rows(node), :])
        for step in range(CHAIN):
            pl.when(step >= table[1])(functools.partial(put_nothing, place, step, own_key[:1]))
        is_root = node == table[0]
        pl.when(is_root)(functools.partial(put_nothing, place, CHAIN, own_key[:1]))

        @pl.when(jnp.logical_not(is_root))
        def _():
            put(place, CHAIN, keys[node_rows(table[0]), :], values[node_rows(table[0]), :])

    def score(place, node):
        stacked = jnp.concatenate(
            [query[node_rows(node), h * HEAD : (h + 1) * HEAD] for h in range(group)], 0
        )
        return times(stacked, all_keys[place])

    def weigh(scores):
        own = scores[:, above:] + jnp.concatenate([own_bias] * group, 0)
        masked = jnp.concatenate([scores[:, :above], own], 1)
        largest = jnp.max(masked, axis=1, keepdims=True)
        return jnp.exp2((masked - largest) * SCALE).astype(jnp.bfloat16)

    def finish(place, node, expo):
        mixed = jnp.dot(expo, all_values[place], preferred_element_type=jnp.float32)
        result = (mixed[:, :HEAD] / mixed[:, HEAD:]).astype(jnp.bfloat16)
        for part in range(NODE_TOK // piece):
            block = node * (NODE_TOK // piece) + part
            owner = block // pieces_part
            target = slot_position(parts, owner ^ me)
            inner = (block - owner * pieces_part) * piece
            to = pl.ds(pl.multiple_of(inner, piece), piece)
            for h in range(group):
                first = h * NODE_TOK + part * piece
                out[target, to, h * HEAD : (h + 1) * HEAD] = result[first : first + piece]

    def some_nodes(turn, carry):
        mine = [(place, turn * side + place) for place in range(side)]
        for place, node in mine:
            lay_out(place, node)
        scores = [score(place, node) for place, node in mine]
        for (place, node), each in zip(mine, scores):
            finish(place, node, weigh(each))
        return carry

    lax.fori_loop(0, nodes // side, some_nodes, 0)


def slot_position(parts, distance):
    half = parts // 2
    return jnp.where(distance % 2 == 1, distance // 2, half + distance // 2)


def in_hbm(array):
    return pltpu.with_memory_space_constraint(array, pltpu.HBM)


def attend(kv, table, queries, keys, values, got, parts, after):
    rows = queries.shape[0]
    width = queries.shape[1] // (keys.shape[1] // HEAD)
    total = (CHAIN + 2) * NODE_TOK
    side = 2 if rows % (2 * NODE_TOK) == 0 else 1
    hbm = pl.BlockSpec(memory_space=pltpu.HBM)
    return pl.pallas_call(
        functools.partial(attend_body, kv, parts),
        out_shape=jax.ShapeDtypeStruct((parts, rows // parts, width), queries.dtype),
        in_specs=[pl.BlockSpec(memory_space=pltpu.SMEM)]
        + [hbm] * 4
        + [pl.BlockSpec(memory_space=pl.ANY)] * len(after),
        scratch_shapes=[
            pltpu.VMEM((rows, width), queries.dtype),
            pltpu.VMEM((rows, HEAD), keys.dtype),
            pltpu.VMEM((rows, HEAD), keys.dtype),
            pltpu.VMEM((CHAIN, NODE_TOK, HEAD), keys.dtype),
            pltpu.VMEM((CHAIN, NODE_TOK, HEAD), keys.dtype),
            pltpu.VMEM((side, total, HEAD), keys.dtype),
            pltpu.VMEM((side, total, 2 * HEAD), keys.dtype),
            pltpu.SemaphoreType.DMA((3 + 2 * CHAIN,)),
        ],
        compiler_params=pltpu.CompilerParams(vmem_limit_bytes=ATTEND_LIMIT),
        cost_estimate=LIGHT,
        name="attend",
    )(table, *[in_hbm(x) for x in (queries, keys, values, got)], *after)


def swap(array, axis, distance):
    size = lax.axis_size(axis)
    return lax.ppermute(array, axis, [(i, i ^ distance) for i in range(size)])


def times(rows, weight):
    return lax.dot_general(
        rows, weight, (((1,), (1,)), ((), ())), preferred_element_type=jnp.float32
    )


def is_middle(index):
    return (index == 1) | (index == 2)


def product(parts, pieces, sent, kept):
    half = parts[0].shape[0] // 2
    for out, start in ((sent, 0), (kept, half)):
        whole = jnp.concatenate([part[start : start + half, :] for part in parts], 1)
        column = 0
        for weight, first, count in pieces:
            out[:, column : column + count] = times(
                whole, weight[first : first + count, :]
            ).astype(out.dtype)
            column += count


def core_sum(pair, upper):
    kept, from_core = pair
    half = kept.shape[0] // 2
    rows = slice(half, 2 * half) if upper else slice(0, half)
    return kept[rows, :].astype(jnp.float32) + from_core[rows, :].astype(jnp.float32)


def step_body(plan, *refs):
    refs = list(refs)

    def take(count):
        return [refs.pop(0) for _ in range(count)]

    rows = [take(count) for count in plan["rows"]]
    arrays = take(plan["arrays"])
    weights = [
        [[(arrays[index], first, count) for index, first, count in pieces] for pieces in weight]
        for weight in plan["weights"]
    ]
    cores = [[take(2) for _ in range(count)] for count in plan["cores"]]
    chips = [([take(2) for _ in range(count)], take(1)[0]) for count in plan["chips"]]
    take(plan["after"])
    outs = take(plan["outs"])
    middle = is_middle(lax.axis_index("node"))
    picks = (middle, jnp.logical_not(middle))
    fetched = None
    for order, weight in enumerate(weights):
        if len(weight) == 2 and not plan["direct"]:
            chosen, sem = refs
            fetched = order
            for pick, pieces in zip(picks, weight):
                column = 0
                for array, first, count in pieces:
                    source = array.at[pl.ds(first, count), :]
                    target = chosen.at[pl.ds(column, count), :]
                    pl.when(pick)(pltpu.make_async_copy(source, target, sem).start)
                    column += count
    made = [[(outs.pop(0), outs.pop(0)) for _ in rows] for _ in weights]
    for bundle in cores:
        out, column = outs.pop(0), 0
        for pair in bundle:
            width = pair[0].shape[1]
            out[:, column : column + width] = core_sum(pair, True).astype(out.dtype)
            column += width
    for bundle, from_chip in chips:
        column = 0
        for pair in bundle:
            out = outs.pop(0)
            width = out.shape[1]
            away = from_chip[:, column : column + width].astype(jnp.float32)
            out[...] = (core_sum(pair, False) + away).astype(out.dtype)
            column += width
    for order, (weight, pairs) in enumerate(zip(weights, made)):
        if order == fetched:
            pltpu.make_async_copy(chosen, chosen, sem).wait()
            weight = [[(chosen, 0, chosen.shape[0])]]
        for parts, (sent, kept) in zip(rows, pairs):
            if len(weight) == 2:
                for pick, pieces in zip(picks, weight):
                    pl.when(pick)(functools.partial(product, parts, pieces, sent, kept))
            else:
                product(parts, weight[0], sent, kept)


def step(rows=(), weights=(), cores=(), chips=(), after=(), direct=False):
    weights = [weight if isinstance(weight, tuple) else (weight,) for weight in weights]
    arrays, fetch, plans = [], [], []
    for weight in weights:
        plans.append([])
        for pieces in weight:
            plans[-1].append([])
            for array, first, count in pieces:
                known = [index for index, x in enumerate(arrays) if x is array]
                if not known:
                    known = [len(arrays)]
                    arrays.append(array)
                    fetch.append(len(weight) == 2 and not direct)
                plans[-1][-1].append((known[0], first, count))
    widths = [sum(count for _, _, count in weight[0]) for weight in weights]
    shapes = []
    for width in widths:
        shapes += [(parts[0].shape[0] // 2, width) for parts in rows for _ in range(2)]
    for bundle in cores:
        shapes.append((bundle[0][0].shape[0] // 2, sum(kept.shape[1] for kept, _ in bundle)))
    for bundle in chips:
        shapes += [(kept.shape[0] // 2, kept.shape[1]) for kept, _ in bundle[:-1]]
    plan = {
        "rows": [len(parts) for parts in rows],
        "arrays": len(arrays),
        "weights": plans,
        "cores": [len(bundle) for bundle in cores],
        "chips": [len(bundle) - 1 for bundle in chips],
        "after": len(after),
        "outs": len(shapes),
        "direct": direct,
    }
    vmem, hbm = pl.BlockSpec(memory_space=pltpu.VMEM), pl.BlockSpec(memory_space=pl.ANY)
    read = [(part, vmem) for parts in rows for part in parts]
    read += [(array, hbm if far else vmem) for array, far in zip(arrays, fetch)]
    read += [(x, vmem) for bundle in cores for pair in bundle for x in pair]
    for bundle in chips:
        read += [(x, vmem) for pair in bundle[:-1] for x in pair] + [(bundle[-1], vmem)]
    read += [(x, hbm) for x in after]
    dtype = read[0][0].dtype
    scratch = []
    if any(fetch):
        width = [w for w, weight in zip(widths, weights) if len(weight) == 2][0]
        scratch = [
            pltpu.VMEM((width, rows[0][0].shape[1] * len(rows[0])), dtype),
            pltpu.SemaphoreType.DMA,
        ]
    return pl.pallas_call(
        functools.partial(step_body, plan),
        out_shape=[jax.ShapeDtypeStruct(shape, dtype) for shape in shapes],
        in_specs=[spec for _, spec in read],
        scratch_shapes=scratch,
        compiler_params=pltpu.CompilerParams(vmem_limit_bytes=VMEM_LIMIT),
        cost_estimate=LIGHT,
        name="step",
    )(*[x for x, _ in read])


PAIRS = [(0, 1), (1, 0), (2, 3), (3, 2)]
MIDDLE = [(1, 2), (2, 1)]
OUTWARD = [(1, 0), (2, 3)]


def relay(piece, exported):
    near = lax.ppermute(piece, "node", PAIRS)
    across = lax.ppermute(piece, "node", MIDDLE)
    near, _ = lax.optimization_barrier((near, exported))
    across, _ = lax.optimization_barrier((across, exported))
    across_out = lax.ppermute(across, "node", OUTWARD)
    near_across = lax.ppermute(near, "node", MIDDLE)
    return near, across, near_across, across_out


def place_body(spots, features, *refs):
    sources, out, sem = refs[: len(spots)], refs[-2], refs[-1]
    half = features // 2
    device = lax.axis_index("node")
    mine = lax.axis_index("groups")
    copies = []
    for order, (source, (distance, side, offset)) in enumerate(zip(sources, spots)):
        group = {"own": mine, "other": 1 - mine, "first": 0}[side]
        column = pl.multiple_of((device ^ distance) * features + group * half + offset, HEAD)
        target = out.at[:, pl.ds(column, source.shape[1])]
        copies.append(pltpu.make_async_copy(source, target, sem.at[order]))
    for copy in copies:
        copy.start()
    for copy in copies:
        copy.wait()


def place(sources, spots, devices, features, begun=None):
    hbm = pl.BlockSpec(memory_space=pltpu.HBM)
    more = [] if begun is None else [begun]
    return pl.pallas_call(
        functools.partial(place_body, spots, features),
        out_shape=jax.ShapeDtypeStruct(
            (sources[0].shape[0], devices * features), sources[0].dtype
        ),
        in_specs=[pl.BlockSpec(memory_space=pltpu.VMEM)] * len(sources) + [hbm] * len(more),
        out_specs=hbm,
        input_output_aliases={len(sources): 0} if more else {},
        scratch_shapes=[pltpu.SemaphoreType.DMA((len(sources),))],
        compiler_params=pltpu.CompilerParams(vmem_limit_bytes=VMEM_LIMIT),
        cost_estimate=LIGHT,
        name="place",
    )(*sources, *more)


def cut_body(weight, out, sem):
    half = out.shape[0]
    rows = half // sem.shape[0]
    start = lax.axis_index("groups") * half
    copies = []
    for part in range(sem.shape[0]):
        source = weight.at[pl.ds(pl.multiple_of(start + part * rows, rows), rows), :]
        target = out.at[pl.ds(part * rows, rows), :]
        copies.append(pltpu.make_async_copy(source, target, sem.at[part]))
    for copy in copies:
        copy.start()
    for copy in copies:
        copy.wait()


def cut(weight):
    return pl.pallas_call(
        cut_body,
        out_shape=jax.ShapeDtypeStruct((weight.shape[0] // 2, weight.shape[1]), weight.dtype),
        in_specs=[pl.BlockSpec(memory_space=pltpu.HBM)],
        out_specs=pl.BlockSpec(memory_space=pltpu.VMEM),
        scratch_shapes=[pltpu.SemaphoreType.DMA((4,))],
        compiler_params=pltpu.CompilerParams(vmem_limit_bytes=VMEM_LIMIT),
        cost_estimate=LIGHT,
        name="cut",
    )(in_hbm(weight))


def project_split(halves, relayed, out_weight):
    features = out_weight.shape[0]
    half = features // 2
    rows = [part.reshape(-1, part.shape[-1]) for part in halves]
    other = [swap(part, "groups", 1) for part in rows]
    near, across, near_across, across_out = relayed
    far_out = lax.ppermute(near_across, "node", OUTWARD)

    def core(sent):
        return swap(sent, "tensor", 1)

    def chip(away):
        return swap(away, "tensor", 2)

    def back(done):
        return swap(done, "groups", 1)

    def whole(weight):
        return [(weight, 0, weight.shape[0])]

    second = (whole(near_across), whole(across_out))
    far = (whole(across), whole(far_out))

    last = features - HEAD
    sent_a, kept_a, sent_b, kept_b, sent_c, kept_c = step(
        [rows],
        [[(out_weight, 0, half)], [(out_weight, half, last - half)], [(out_weight, last, HEAD)]],
    )
    one = [(kept_a, core(sent_a)), (kept_b, core(sent_b))]
    (away,) = step(cores=[one])
    one.append(chip(away))
    sent_1, kept_1 = step([rows], [whole(near)], after=[away, other[0]])
    sent_2, kept_2, done_a, done_b = step([rows], [second], chips=[one], after=[sent_1])
    two = [(kept_c, core(sent_c)), (kept_1, core(sent_1)), (kept_2, core(sent_2))]
    (away,) = step(cores=[two])
    two.append(chip(away))
    sent_3, kept_3, sent_4, kept_4 = step([other], [whole(near), second], after=[away])
    three = [(kept_3, core(sent_3))]
    four = [(kept_4, core(sent_4))]
    away, done_c, done_1, done_2 = step(cores=[three], chips=[two])
    three.append(chip(away))
    away, done_3 = step(cores=[four], chips=[three])
    four.append(chip(away))
    back_3 = back(done_3)
    sent_5, kept_5 = step([other], [far], after=[away], direct=True)
    five = [(kept_5, core(sent_5))]
    (done_4,) = step(chips=[four], after=[sent_5, back_3])
    back_4 = back(done_4)
    sent_6, kept_6 = step([rows], [far], after=[done_4], direct=True)
    six = [(kept_6, core(sent_6))]
    (away,) = step(cores=[five], after=[sent_6])
    five.append(chip(away))
    (away,) = step(cores=[six], after=[away])
    six.append(chip(away))
    (done_5,) = step(chips=[five], after=[away, back_4])
    back_5 = back(done_5)
    devices = lax.axis_size("node")
    begun = place(
        (done_a, done_b, done_c, done_1, done_2, back_3, back_4),
        (
            (0, "first", 0),
            (0, "first", half),
            (0, "first", last),
            (1, "own", 0),
            (2, "own", 0),
            (1, "other", 0),
            (2, "other", 0),
        ),
        devices,
        features,
    )
    (done_6,) = step(chips=[six], after=[done_5, in_hbm(begun)])
    return place(
        (back_5, done_6), ((3, "other", 0), (3, "own", 0)), devices, features, begun
    )


def project_plain(halves, out_weight):
    attended = jnp.concatenate(halves, 2)
    parts, per_part, width = attended.shape
    me = lax.axis_index("tensor")
    order = slot_position(parts, jnp.arange(parts, dtype=jnp.int32) ^ me)
    rows = attended[order].reshape(parts * per_part, width)
    weight = lax.all_gather(out_weight, "node", axis=0, tiled=True)
    terms = times(rows, weight).astype(jnp.bfloat16)
    return lax.psum_scatter(terms, "tensor", scatter_dimension=0, tiled=True)


def local(queries, keys, values, out_weight, slot_nodes, ancestors, depth):
    parts = lax.axis_size("tensor")
    devices = lax.axis_size("node")
    features = out_weight.shape[0]
    kv_count = keys.shape[1] // HEAD
    relayed, after = None, []
    exported, table = prepare(slot_nodes, ancestors, depth, keys, values)
    got = lax.all_gather(exported, "node", axis=0, tiled=True)
    if (
        devices == 4
        and parts == 4
        and lax.axis_size("groups") == 2
        and features % (2 * HEAD) == 0
    ):
        relayed = relay(cut(out_weight), exported)
        after = relayed[:2]
    halves = []
    for kv in range(kv_count):
        halves.append(attend(kv, table, queries, keys, values, got, parts, after))
        after = halves[-1:]
    if relayed is None:
        return project_plain(halves, out_weight)
    return project_split(halves, relayed, out_weight)


def solution(mesh):
    placed = (
        P(("groups", "node"), "tensor"),
        P(("groups", "node"), "tensor"),
        P(("groups", "node"), "tensor"),
        P("node", "tensor"),
        P("groups"),
        P("groups", None),
        P("groups"),
    )
    return jax.shard_map(
        local,
        mesh=mesh,
        in_specs=placed,
        out_specs=P(("groups", "node", "tensor"), None),
        check_vma=False,
    )
```

```python
import functools
import math

import jax
import jax.numpy as jnp
from jax import lax
from jax.experimental import pallas as pl
from jax.experimental.pallas import tpu as pltpu
from jax.sharding import PartitionSpec as P

HEAD = 128
NODE_TOK = 128
A_MAX = 7
CHAIN = A_MAX - 1
EXPORTS = 2
SCALE = math.log2(math.e) / math.sqrt(HEAD)
DEAD = -1e30
LIGHT = pl.CostEstimate(flops=1, bytes_accessed=1, transcendentals=0)
VMEM_LIMIT = 20 * 1024 * 1024
ATTEND_LIMIT = 24 * 1024 * 1024


def prepare_body(nodes, relative, *refs):
    slot_hbm, ancestors_hbm, depth_hbm, keys, values, exported, table_hbm = refs[:7]
    slot_nodes, ancestors, depth, table, holder, within, roots, sem = refs[7:]
    devices = slot_nodes.shape[0] // nodes
    me = lax.axis_index("node")
    fetches = [
        pltpu.make_async_copy(source, target, sem.at[2 * EXPORTS + 1 + order])
        for order, (source, target) in enumerate(
            ((slot_hbm, slot_nodes), (ancestors_hbm, ancestors), (depth_hbm, depth))
        )
    ]
    for fetch in fetches:
        fetch.start()
    for fetch in fetches:
        fetch.wait()

    def place(device, mine):
        root, root_index = jnp.int32(0), jnp.int32(0)
        for index in range(nodes):
            node = slot_nodes[device * nodes + index]
            holder[node] = device
            within[node] = index
            even = (depth[node] & 1) == 0
            root = jnp.where(even, node, root)
            root_index = jnp.where(even, index, root_index)
        roots[device] = root
        return jnp.where(device == me, root_index, mine)

    root = lax.fori_loop(0, devices, place, jnp.int32(0))

    def find_attach(device, attach):
        node = roots[device]
        level = depth[node]
        for step in range(0, CHAIN, 2):
            above = jnp.maximum(ancestors[step, node], 0)
            hit = (step < level) & (holder[above] == me)
            attach = jnp.where(hit, within[above], attach)
        return attach

    attach = lax.fori_loop(0, devices, find_attach, jnp.int32(0))
    copies = []
    for position, (source, index) in enumerate(
        ((keys, root), (keys, attach), (values, root), (values, attach))
    ):
        rows = pl.ds(pl.multiple_of(index * NODE_TOK, NODE_TOK), NODE_TOK)
        copies.append(
            pltpu.make_async_copy(source.at[rows, :], exported.at[position], sem.at[position])
        )
    for copy in copies:
        copy.start()
    root_node = roots[me]
    count = depth[root_node]
    table[0] = root
    table[1] = count
    for step in range(CHAIN):
        above = jnp.maximum(ancestors[step, root_node], 0)
        where = (holder[above] ^ me) - 1 if relative else holder[above]
        entry = where * (2 * EXPORTS) + (1 if step % 2 == 0 else 0)
        table[2 + step] = jnp.where(step < count, entry, 0)
    store = pltpu.make_async_copy(table, table_hbm, sem.at[2 * EXPORTS])
    store.start()
    for copy in (*copies, store):
        copy.wait()


def prepare(slot_nodes, ancestors, depth, keys, values, relative):
    nodes = keys.shape[0] // NODE_TOK
    slots = slot_nodes.shape[0]
    hbm = pl.BlockSpec(memory_space=pltpu.HBM)
    vmem = pl.BlockSpec(memory_space=pltpu.VMEM)
    return pl.pallas_call(
        functools.partial(prepare_body, nodes, relative),
        out_shape=(
            jax.ShapeDtypeStruct((2 * EXPORTS, NODE_TOK, keys.shape[1]), keys.dtype),
            jax.ShapeDtypeStruct((2 + CHAIN,), jnp.int32),
        ),
        in_specs=[hbm, hbm, hbm, vmem, vmem],
        out_specs=(hbm, hbm),
        scratch_shapes=[
            pltpu.SMEM((slots,), jnp.int32),
            pltpu.SMEM((A_MAX, slots), jnp.int32),
            pltpu.SMEM((slots,), jnp.int32),
            pltpu.SMEM((2 + CHAIN,), jnp.int32),
            pltpu.SMEM((slots,), jnp.int32),
            pltpu.SMEM((slots,), jnp.int32),
            pltpu.SMEM((slots // nodes,), jnp.int32),
            pltpu.SemaphoreType.DMA((2 * EXPORTS + 4,)),
        ],
        compiler_params=pltpu.CompilerParams(vmem_limit_bytes=VMEM_LIMIT),
        name="prepare",
    )(slot_nodes, ancestors.T, depth, keys, values)


def attend_body(kv, parts, count, table, query_hbm, keys_hbm, values_hbm, *refs):
    got = refs[:count]
    out, query, keys, values, above_keys, above_values, all_keys, all_values, sem = refs[-9:]
    nodes = query.shape[0] // NODE_TOK
    group = query.shape[1] // HEAD
    per_part = query.shape[0] // parts
    side = all_keys.shape[0]
    lanes = pl.ds(kv * HEAD, HEAD)
    pairs = [(keys_hbm.at[:, lanes], keys), (values_hbm.at[:, lanes], values)]
    pairs.append((query_hbm.at[:, pl.ds(kv * group * HEAD, group * HEAD)], query))
    copies = [
        pltpu.make_async_copy(source, target, sem.at[order])
        for order, (source, target) in enumerate(pairs)
    ]
    for copy in copies:
        copy.start()
    for step in range(CHAIN):
        each = got[0].shape[0]
        for order, array in enumerate(got):
            entry = table[2 + step] - order * each
            inside = jnp.clip(entry, 0, each - 1 - EXPORTS)
            blocks = (
                (array.at[inside, :, lanes], above_keys.at[step]),
                (array.at[inside + EXPORTS, :, lanes], above_values.at[step]),
            )
            for part, (source, target) in enumerate(blocks):
                copy = pltpu.make_async_copy(source, target, sem.at[3 + 2 * step + part])
                pl.when((entry >= 0) & (entry < each))(copy.start)
                if order == 0:
                    copies.append(copy)
    ones = jnp.ones((NODE_TOK, HEAD), all_values.dtype)
    nothing = jnp.zeros((NODE_TOK, 2 * HEAD), all_values.dtype)
    query_index = lax.broadcasted_iota(jnp.int32, (NODE_TOK, NODE_TOK), 0)
    key_index = lax.broadcasted_iota(jnp.int32, (NODE_TOK, NODE_TOK), 1)
    own_bias = jnp.where(key_index <= query_index, 0.0, DEAD)
    piece = math.gcd(NODE_TOK, per_part)
    pieces_part = per_part // piece
    me = lax.axis_index("tensor")
    above = (CHAIN + 1) * NODE_TOK
    for copy in copies:
        copy.wait()

    def node_rows(node):
        return pl.ds(pl.multiple_of(node * NODE_TOK, NODE_TOK), NODE_TOK)

    def put(place, order, key_block, value_block):
        rows = pl.ds(order * NODE_TOK, NODE_TOK)
        all_keys[place, rows, :] = key_block
        all_values[place, rows, :HEAD] = value_block
        all_values[place, rows, HEAD:] = ones

    def put_nothing(place, order, first_key):
        rows = pl.ds(order * NODE_TOK, NODE_TOK)
        all_keys[place, rows, :] = jnp.broadcast_to(first_key, (NODE_TOK, HEAD))
        all_values[place, rows, :] = nothing

    for place in range(side):
        for step in range(CHAIN):
            put(place, step, above_keys[step], above_values[step])

    def lay_out(place, node):
        own_key = keys[node_rows(node), :]
        put(place, CHAIN + 1, own_key, values[node_rows(node), :])
        for step in range(CHAIN):
            pl.when(step >= table[1])(functools.partial(put_nothing, place, step, own_key[:1]))
        is_root = node == table[0]
        pl.when(is_root)(functools.partial(put_nothing, place, CHAIN, own_key[:1]))

        @pl.when(jnp.logical_not(is_root))
        def _():
            put(place, CHAIN, keys[node_rows(table[0]), :], values[node_rows(table[0]), :])

    def score(place, node):
        stacked = jnp.concatenate(
            [query[node_rows(node), h * HEAD : (h + 1) * HEAD] for h in range(group)], 0
        )
        return times(stacked, all_keys[place])

    def weigh(scores):
        own = scores[:, above:] + jnp.concatenate([own_bias] * group, 0)
        masked = jnp.concatenate([scores[:, :above], own], 1)
        largest = jnp.max(masked, axis=1, keepdims=True)
        return jnp.exp2((masked - largest) * SCALE).astype(jnp.bfloat16)

    def finish(place, node, expo):
        mixed = jnp.dot(expo, all_values[place], preferred_element_type=jnp.float32)
        result = (mixed[:, :HEAD] / mixed[:, HEAD:]).astype(jnp.bfloat16)
        for part in range(NODE_TOK // piece):
            block = node * (NODE_TOK // piece) + part
            owner = block // pieces_part
            target = slot_position(parts, owner ^ me)
            inner = (block - owner * pieces_part) * piece
            to = pl.ds(pl.multiple_of(inner, piece), piece)
            for h in range(group):
                first = h * NODE_TOK + part * piece
                out[target, to, h * HEAD : (h + 1) * HEAD] = result[first : first + piece]

    def some_nodes(turn, carry):
        mine = [(place, turn * side + place) for place in range(side)]
        for place, node in mine:
            lay_out(place, node)
        scores = [score(place, node) for place, node in mine]
        for (place, node), each in zip(mine, scores):
            finish(place, node, weigh(each))
        return carry

    lax.fori_loop(0, nodes // side, some_nodes, 0)


def slot_position(parts, distance):
    half = parts // 2
    return jnp.where(distance % 2 == 1, distance // 2, half + distance // 2)


def in_hbm(array):
    return pltpu.with_memory_space_constraint(array, pltpu.HBM)


def attend(kv, table, queries, keys, values, got, parts, after):
    rows = queries.shape[0]
    width = queries.shape[1] // (keys.shape[1] // HEAD)
    total = (CHAIN + 2) * NODE_TOK
    side = 2 if rows % (2 * NODE_TOK) == 0 else 1
    hbm = pl.BlockSpec(memory_space=pltpu.HBM)
    return pl.pallas_call(
        functools.partial(attend_body, kv, parts, len(got)),
        out_shape=jax.ShapeDtypeStruct((parts, rows // parts, width), queries.dtype),
        in_specs=[pl.BlockSpec(memory_space=pltpu.SMEM)]
        + [hbm] * 3
        + [pl.BlockSpec(memory_space=pl.ANY)] * (len(got) + len(after)),
        scratch_shapes=[
            pltpu.VMEM((rows, width), queries.dtype),
            pltpu.VMEM((rows, HEAD), keys.dtype),
            pltpu.VMEM((rows, HEAD), keys.dtype),
            pltpu.VMEM((CHAIN, NODE_TOK, HEAD), keys.dtype),
            pltpu.VMEM((CHAIN, NODE_TOK, HEAD), keys.dtype),
            pltpu.VMEM((side, total, HEAD), keys.dtype),
            pltpu.VMEM((side, total, 2 * HEAD), keys.dtype),
            pltpu.SemaphoreType.DMA((3 + 2 * CHAIN,)),
        ],
        compiler_params=pltpu.CompilerParams(vmem_limit_bytes=ATTEND_LIMIT),
        cost_estimate=LIGHT,
        name="attend",
    )(table, *[in_hbm(x) for x in (queries, keys, values)], *got, *after)


def swap(array, axis, distance):
    size = lax.axis_size(axis)
    return lax.ppermute(array, axis, [(i, i ^ distance) for i in range(size)])


def times(rows, weight):
    return lax.dot_general(
        rows, weight, (((1,), (1,)), ((), ())), preferred_element_type=jnp.float32
    )


def is_middle(index):
    return (index == 1) | (index == 2)


def product(parts, pieces, sent, kept):
    half = parts[0].shape[0] // 2
    for out, start in ((sent, 0), (kept, half)):
        whole = jnp.concatenate([part[start : start + half, :] for part in parts], 1)
        column = 0
        for weight, first, count in pieces:
            out[:, column : column + count] = times(
                whole, weight[first : first + count, :]
            ).astype(out.dtype)
            column += count


def core_sum(pair, upper):
    kept, from_core = pair
    half = kept.shape[0] // 2
    rows = slice(half, 2 * half) if upper else slice(0, half)
    return kept[rows, :].astype(jnp.float32) + from_core[rows, :].astype(jnp.float32)


def step_body(plan, *refs):
    refs = list(refs)

    def take(count):
        return [refs.pop(0) for _ in range(count)]

    rows = [take(count) for count in plan["rows"]]
    arrays = take(plan["arrays"])
    weights = [
        [[(arrays[index], first, count) for index, first, count in pieces] for pieces in weight]
        for weight in plan["weights"]
    ]
    cores = [[take(2) for _ in range(count)] for count in plan["cores"]]
    chips = [([take(2) for _ in range(count)], take(1)[0]) for count in plan["chips"]]
    take(plan["after"])
    outs = take(plan["outs"])
    middle = is_middle(lax.axis_index("node"))
    picks = (middle, jnp.logical_not(middle))
    fetched = None
    for order, weight in enumerate(weights):
        if len(weight) == 2 and not plan["direct"]:
            chosen, sem = refs
            fetched = order
            for pick, pieces in zip(picks, weight):
                column = 0
                for array, first, count in pieces:
                    source = array.at[pl.ds(first, count), :]
                    target = chosen.at[pl.ds(column, count), :]
                    pl.when(pick)(pltpu.make_async_copy(source, target, sem).start)
                    column += count
    made = [[(outs.pop(0), outs.pop(0)) for _ in rows] for _ in weights]
    for bundle in cores:
        out, column = outs.pop(0), 0
        for pair in bundle:
            width = pair[0].shape[1]
            out[:, column : column + width] = core_sum(pair, True).astype(out.dtype)
            column += width
    for bundle, from_chip in chips:
        column = 0
        for pair in bundle:
            out = outs.pop(0)
            width = out.shape[1]
            away = from_chip[:, column : column + width].astype(jnp.float32)
            out[...] = (core_sum(pair, False) + away).astype(out.dtype)
            column += width
    for order, (weight, pairs) in enumerate(zip(weights, made)):
        if order == fetched:
            pltpu.make_async_copy(chosen, chosen, sem).wait()
            weight = [[(chosen, 0, chosen.shape[0])]]
        for parts, (sent, kept) in zip(rows, pairs):
            if len(weight) == 2:
                for pick, pieces in zip(picks, weight):
                    pl.when(pick)(functools.partial(product, parts, pieces, sent, kept))
            else:
                product(parts, weight[0], sent, kept)


def step(rows=(), weights=(), cores=(), chips=(), after=(), direct=False):
    weights = [weight if isinstance(weight, tuple) else (weight,) for weight in weights]
    arrays, fetch, plans = [], [], []
    for weight in weights:
        plans.append([])
        for pieces in weight:
            plans[-1].append([])
            for array, first, count in pieces:
                known = [index for index, x in enumerate(arrays) if x is array]
                if not known:
                    known = [len(arrays)]
                    arrays.append(array)
                    fetch.append(len(weight) == 2 and not direct)
                plans[-1][-1].append((known[0], first, count))
    widths = [sum(count for _, _, count in weight[0]) for weight in weights]
    shapes = []
    for width in widths:
        shapes += [(parts[0].shape[0] // 2, width) for parts in rows for _ in range(2)]
    for bundle in cores:
        shapes.append((bundle[0][0].shape[0] // 2, sum(kept.shape[1] for kept, _ in bundle)))
    for bundle in chips:
        shapes += [(kept.shape[0] // 2, kept.shape[1]) for kept, _ in bundle[:-1]]
    plan = {
        "rows": [len(parts) for parts in rows],
        "arrays": len(arrays),
        "weights": plans,
        "cores": [len(bundle) for bundle in cores],
        "chips": [len(bundle) - 1 for bundle in chips],
        "after": len(after),
        "outs": len(shapes),
        "direct": direct,
    }
    vmem, hbm = pl.BlockSpec(memory_space=pltpu.VMEM), pl.BlockSpec(memory_space=pl.ANY)
    read = [(part, vmem) for parts in rows for part in parts]
    read += [(array, hbm if far else vmem) for array, far in zip(arrays, fetch)]
    read += [(x, vmem) for bundle in cores for pair in bundle for x in pair]
    for bundle in chips:
        read += [(x, vmem) for pair in bundle[:-1] for x in pair] + [(bundle[-1], vmem)]
    read += [(x, hbm) for x in after]
    dtype = read[0][0].dtype
    scratch = []
    if any(fetch):
        width = [w for w, weight in zip(widths, weights) if len(weight) == 2][0]
        scratch = [
            pltpu.VMEM((width, rows[0][0].shape[1] * len(rows[0])), dtype),
            pltpu.SemaphoreType.DMA,
        ]
    return pl.pallas_call(
        functools.partial(step_body, plan),
        out_shape=[jax.ShapeDtypeStruct(shape, dtype) for shape in shapes],
        in_specs=[spec for _, spec in read],
        scratch_shapes=scratch,
        compiler_params=pltpu.CompilerParams(vmem_limit_bytes=VMEM_LIMIT),
        cost_estimate=LIGHT,
        name="step",
    )(*[x for x, _ in read])


PAIRS = [(0, 1), (1, 0), (2, 3), (3, 2)]
MIDDLE = [(1, 2), (2, 1)]
OUTWARD = [(1, 0), (2, 3)]


def relay(piece, got):
    near = lax.ppermute(piece, "node", PAIRS)
    across = lax.ppermute(piece, "node", MIDDLE)
    near, _ = lax.optimization_barrier((near, got))
    across, _ = lax.optimization_barrier((across, got))
    across_out = lax.ppermute(across, "node", OUTWARD)
    near_across = lax.ppermute(near, "node", MIDDLE)
    return near, across, near_across, across_out


def place_body(spots, features, *refs):
    sources, out, sem = refs[: len(spots)], refs[-2], refs[-1]
    half = features // 2
    device = lax.axis_index("node")
    mine = lax.axis_index("groups")
    copies = []
    for order, (source, (distance, side, offset)) in enumerate(zip(sources, spots)):
        group = {"own": mine, "other": 1 - mine, "first": 0}[side]
        column = pl.multiple_of((device ^ distance) * features + group * half + offset, HEAD)
        target = out.at[:, pl.ds(column, source.shape[1])]
        copies.append(pltpu.make_async_copy(source, target, sem.at[order]))
    for copy in copies:
        copy.start()
    for copy in copies:
        copy.wait()


def place(sources, spots, devices, features, begun=None):
    hbm = pl.BlockSpec(memory_space=pltpu.HBM)
    more = [] if begun is None else [begun]
    return pl.pallas_call(
        functools.partial(place_body, spots, features),
        out_shape=jax.ShapeDtypeStruct(
            (sources[0].shape[0], devices * features), sources[0].dtype
        ),
        in_specs=[pl.BlockSpec(memory_space=pltpu.VMEM)] * len(sources) + [hbm] * len(more),
        out_specs=hbm,
        input_output_aliases={len(sources): 0} if more else {},
        scratch_shapes=[pltpu.SemaphoreType.DMA((len(sources),))],
        compiler_params=pltpu.CompilerParams(vmem_limit_bytes=VMEM_LIMIT),
        cost_estimate=LIGHT,
        name="place",
    )(*sources, *more)


def cut_body(weight, out, sem):
    half = out.shape[0]
    rows = half // sem.shape[0]
    start = lax.axis_index("groups") * half
    copies = []
    for part in range(sem.shape[0]):
        source = weight.at[pl.ds(pl.multiple_of(start + part * rows, rows), rows), :]
        target = out.at[pl.ds(part * rows, rows), :]
        copies.append(pltpu.make_async_copy(source, target, sem.at[part]))
    for copy in copies:
        copy.start()
    for copy in copies:
        copy.wait()


def cut(weight):
    return pl.pallas_call(
        cut_body,
        out_shape=jax.ShapeDtypeStruct((weight.shape[0] // 2, weight.shape[1]), weight.dtype),
        in_specs=[pl.BlockSpec(memory_space=pltpu.HBM)],
        out_specs=pl.BlockSpec(memory_space=pltpu.VMEM),
        scratch_shapes=[pltpu.SemaphoreType.DMA((4,))],
        compiler_params=pltpu.CompilerParams(vmem_limit_bytes=VMEM_LIMIT),
        cost_estimate=LIGHT,
        name="cut",
    )(in_hbm(weight))


def project_split(halves, relayed, out_weight):
    features = out_weight.shape[0]
    half = features // 2
    rows = [part.reshape(-1, part.shape[-1]) for part in halves]
    other = [swap(part, "groups", 1) for part in rows]
    near, across, near_across, across_out = relayed
    far_out = lax.ppermute(near_across, "node", OUTWARD)

    def core(sent):
        return swap(sent, "tensor", 1)

    def chip(away):
        return swap(away, "tensor", 2)

    def back(done):
        return swap(done, "groups", 1)

    def whole(weight):
        return [(weight, 0, weight.shape[0])]

    second = (whole(near_across), whole(across_out))
    far = (whole(across), whole(far_out))

    last = features - HEAD
    sent_a, kept_a, sent_b, kept_b, sent_c, kept_c = step(
        [rows],
        [[(out_weight, 0, half)], [(out_weight, half, last - half)], [(out_weight, last, HEAD)]],
    )
    one = [(kept_a, core(sent_a)), (kept_b, core(sent_b))]
    (away,) = step(cores=[one])
    one.append(chip(away))
    sent_1, kept_1 = step([rows], [whole(near)], after=[away, other[0]])
    sent_2, kept_2, done_a, done_b = step([rows], [second], chips=[one], after=[sent_1])
    two = [(kept_c, core(sent_c)), (kept_1, core(sent_1)), (kept_2, core(sent_2))]
    (away,) = step(cores=[two])
    two.append(chip(away))
    sent_3, kept_3, sent_4, kept_4 = step([other], [whole(near), second], after=[away])
    three = [(kept_3, core(sent_3))]
    four = [(kept_4, core(sent_4))]
    away, done_c, done_1, done_2 = step(cores=[three], chips=[two])
    three.append(chip(away))
    away, done_3 = step(cores=[four], chips=[three])
    four.append(chip(away))
    back_3 = back(done_3)
    sent_5, kept_5 = step([other], [far], after=[away], direct=True)
    five = [(kept_5, core(sent_5))]
    (done_4,) = step(chips=[four], after=[sent_5, back_3])
    back_4 = back(done_4)
    sent_6, kept_6 = step([rows], [far], after=[done_4], direct=True)
    six = [(kept_6, core(sent_6))]
    (away,) = step(cores=[five], after=[sent_6])
    five.append(chip(away))
    (away,) = step(cores=[six], after=[away])
    six.append(chip(away))
    (done_5,) = step(chips=[five], after=[away, back_4])
    back_5 = back(done_5)
    devices = lax.axis_size("node")
    begun = place(
        (done_a, done_b, done_c, done_1, done_2, back_3, back_4),
        (
            (0, "first", 0),
            (0, "first", half),
            (0, "first", last),
            (1, "own", 0),
            (2, "own", 0),
            (1, "other", 0),
            (2, "other", 0),
        ),
        devices,
        features,
    )
    (done_6,) = step(chips=[six], after=[done_5, in_hbm(begun)])
    return place(
        (back_5, done_6), ((3, "other", 0), (3, "own", 0)), devices, features, begun
    )


def project_plain(halves, out_weight):
    attended = jnp.concatenate(halves, 2)
    parts, per_part, width = attended.shape
    me = lax.axis_index("tensor")
    order = slot_position(parts, jnp.arange(parts, dtype=jnp.int32) ^ me)
    rows = attended[order].reshape(parts * per_part, width)
    weight = lax.all_gather(out_weight, "node", axis=0, tiled=True)
    terms = times(rows, weight).astype(jnp.bfloat16)
    return lax.psum_scatter(terms, "tensor", scatter_dimension=0, tiled=True)


def local(queries, keys, values, out_weight, slot_nodes, ancestors, depth):
    parts = lax.axis_size("tensor")
    devices = lax.axis_size("node")
    features = out_weight.shape[0]
    kv_count = keys.shape[1] // HEAD
    relayed, after = None, []
    relative = devices == 4
    exported, table = prepare(slot_nodes, ancestors, depth, keys, values, relative)
    if relative:
        got = [swap(exported, "node", distance) for distance in (1, 2, 3)]
    else:
        got = [lax.all_gather(exported, "node", axis=0, tiled=True)]
    if (
        devices == 4
        and parts == 4
        and lax.axis_size("groups") == 2
        and features % (2 * HEAD) == 0
    ):
        relayed = relay(cut(out_weight), got)
        after = relayed[:2]
    halves = []
    for kv in range(kv_count):
        halves.append(attend(kv, table, queries, keys, values, got, parts, after))
        after = halves[-1:]
    if relayed is None:
        return project_plain(halves, out_weight)
    return project_split(halves, relayed, out_weight)


def solution(mesh):
    placed = (
        P(("groups", "node"), "tensor"),
        P(("groups", "node"), "tensor"),
        P(("groups", "node"), "tensor"),
        P("node", "tensor"),
        P("groups"),
        P("groups", None),
        P("groups"),
    )
    return jax.shard_map(
        local,
        mesh=mesh,
        in_specs=placed,
        out_specs=P(("groups", "node", "tensor"), None),
        check_vma=False,
    )
```

```python
import functools
import math

import jax
import jax.numpy as jnp
from jax import lax
from jax.experimental import pallas as pl
from jax.experimental.pallas import tpu as pltpu
from jax.sharding import PartitionSpec as P

HEAD = 128
NODE_TOK = 128
A_MAX = 7
CHAIN = A_MAX - 1
EXPORTS = 2
SCALE = math.log2(math.e) / math.sqrt(HEAD)
DEAD = -1e30
LIGHT = pl.CostEstimate(flops=1, bytes_accessed=1, transcendentals=0)
VMEM_LIMIT = 20 * 1024 * 1024
ATTEND_LIMIT = 24 * 1024 * 1024


def prepare_body(nodes, relative, *refs):
    slot_hbm, ancestors_hbm, depth_hbm, keys, values, exported, table_hbm = refs[:7]
    slot_nodes, ancestors, depth, table, holder, within, roots, sem = refs[7:]
    devices = slot_nodes.shape[0] // nodes
    me = lax.axis_index("node")
    fetches = [
        pltpu.make_async_copy(source, target, sem.at[2 * EXPORTS + 1 + order])
        for order, (source, target) in enumerate(
            ((slot_hbm, slot_nodes), (ancestors_hbm, ancestors), (depth_hbm, depth))
        )
    ]
    for fetch in fetches:
        fetch.start()
    for fetch in fetches:
        fetch.wait()

    def place(device, mine):
        root, root_index = jnp.int32(0), jnp.int32(0)
        for index in range(nodes):
            node = slot_nodes[device * nodes + index]
            holder[node] = device
            within[node] = index
            even = (depth[node] & 1) == 0
            root = jnp.where(even, node, root)
            root_index = jnp.where(even, index, root_index)
        roots[device] = root
        return jnp.where(device == me, root_index, mine)

    root = lax.fori_loop(0, devices, place, jnp.int32(0))

    def find_attach(device, attach):
        node = roots[device]
        level = depth[node]
        for step in range(0, CHAIN, 2):
            above = jnp.maximum(ancestors[step, node], 0)
            hit = (step < level) & (holder[above] == me)
            attach = jnp.where(hit, within[above], attach)
        return attach

    attach = lax.fori_loop(0, devices, find_attach, jnp.int32(0))
    copies = []
    for position, (source, index) in enumerate(
        ((keys, root), (keys, attach), (values, root), (values, attach))
    ):
        rows = pl.ds(pl.multiple_of(index * NODE_TOK, NODE_TOK), NODE_TOK)
        copies.append(
            pltpu.make_async_copy(source.at[rows, :], exported.at[position], sem.at[position])
        )
    for copy in copies:
        copy.start()
    root_node = roots[me]
    count = depth[root_node]
    table[0] = root
    table[1] = count
    for step in range(CHAIN):
        above = jnp.maximum(ancestors[step, root_node], 0)
        where = (holder[above] ^ me) - 1 if relative else holder[above]
        entry = where * (2 * EXPORTS) + (1 if step % 2 == 0 else 0)
        table[2 + step] = jnp.where(step < count, entry, 0)
    store = pltpu.make_async_copy(table, table_hbm, sem.at[2 * EXPORTS])
    store.start()
    for copy in (*copies, store):
        copy.wait()


def prepare(slot_nodes, ancestors, depth, keys, values, relative):
    nodes = keys.shape[0] // NODE_TOK
    slots = slot_nodes.shape[0]
    hbm = pl.BlockSpec(memory_space=pltpu.HBM)
    vmem = pl.BlockSpec(memory_space=pltpu.VMEM)
    return pl.pallas_call(
        functools.partial(prepare_body, nodes, relative),
        out_shape=(
            jax.ShapeDtypeStruct((2 * EXPORTS, NODE_TOK, keys.shape[1]), keys.dtype),
            jax.ShapeDtypeStruct((2 + CHAIN,), jnp.int32),
        ),
        in_specs=[hbm, hbm, hbm, vmem, vmem],
        out_specs=(hbm, hbm),
        scratch_shapes=[
            pltpu.SMEM((slots,), jnp.int32),
            pltpu.SMEM((A_MAX, slots), jnp.int32),
            pltpu.SMEM((slots,), jnp.int32),
            pltpu.SMEM((2 + CHAIN,), jnp.int32),
            pltpu.SMEM((slots,), jnp.int32),
            pltpu.SMEM((slots,), jnp.int32),
            pltpu.SMEM((slots // nodes,), jnp.int32),
            pltpu.SemaphoreType.DMA((2 * EXPORTS + 4,)),
        ],
        compiler_params=pltpu.CompilerParams(vmem_limit_bytes=VMEM_LIMIT),
        name="prepare",
    )(slot_nodes, ancestors.T, depth, keys, values)


def attend_body(kv, parts, counts, table, query_hbm, keys_hbm, values_hbm, *refs):
    refs = list(refs)
    got = [[refs.pop(0) for _ in range(count)] for count in counts]
    middle = is_middle(lax.axis_index("node"))
    out, query, keys, values, above_keys, above_values, all_keys, all_values, sem = refs[-9:]
    nodes = query.shape[0] // NODE_TOK
    group = query.shape[1] // HEAD
    per_part = query.shape[0] // parts
    side = all_keys.shape[0]
    lanes = pl.ds(kv * HEAD, HEAD)
    pairs = [(keys_hbm.at[:, lanes], keys), (values_hbm.at[:, lanes], values)]
    pairs.append((query_hbm.at[:, pl.ds(kv * group * HEAD, group * HEAD)], query))
    copies = [
        pltpu.make_async_copy(source, target, sem.at[order])
        for order, (source, target) in enumerate(pairs)
    ]
    for copy in copies:
        copy.start()
    for step in range(CHAIN):
        each = got[0][0].shape[0]
        for order, choice in enumerate(got):
            entry = table[2 + step] - order * each
            inside = jnp.clip(entry, 0, each - 1 - EXPORTS)
            here = (entry >= 0) & (entry < each)
            for array, pick in zip(choice, (middle, jnp.logical_not(middle))):
                blocks = (
                    (array.at[inside, :, lanes], above_keys.at[step]),
                    (array.at[inside + EXPORTS, :, lanes], above_values.at[step]),
                )
                for part, (source, target) in enumerate(blocks):
                    copy = pltpu.make_async_copy(source, target, sem.at[3 + 2 * step + part])
                    pl.when(here & pick if len(choice) == 2 else here)(copy.start)
                    if order == 0:
                        copies.append(copy)
    ones = jnp.ones((NODE_TOK, HEAD), all_values.dtype)
    nothing = jnp.zeros((NODE_TOK, 2 * HEAD), all_values.dtype)
    query_index = lax.broadcasted_iota(jnp.int32, (NODE_TOK, NODE_TOK), 0)
    key_index = lax.broadcasted_iota(jnp.int32, (NODE_TOK, NODE_TOK), 1)
    own_bias = jnp.where(key_index <= query_index, 0.0, DEAD)
    piece = math.gcd(NODE_TOK, per_part)
    pieces_part = per_part // piece
    me = lax.axis_index("tensor")
    above = (CHAIN + 1) * NODE_TOK
    for copy in copies:
        copy.wait()

    def node_rows(node):
        return pl.ds(pl.multiple_of(node * NODE_TOK, NODE_TOK), NODE_TOK)

    def put(place, order, key_block, value_block):
        rows = pl.ds(order * NODE_TOK, NODE_TOK)
        all_keys[place, rows, :] = key_block
        all_values[place, rows, :HEAD] = value_block
        all_values[place, rows, HEAD:] = ones

    def put_nothing(place, order, first_key):
        rows = pl.ds(order * NODE_TOK, NODE_TOK)
        all_keys[place, rows, :] = jnp.broadcast_to(first_key, (NODE_TOK, HEAD))
        all_values[place, rows, :] = nothing

    for place in range(side):
        for step in range(CHAIN):
            put(place, step, above_keys[step], above_values[step])

    def lay_out(place, node):
        own_key = keys[node_rows(node), :]
        put(place, CHAIN + 1, own_key, values[node_rows(node), :])
        for step in range(CHAIN):
            pl.when(step >= table[1])(functools.partial(put_nothing, place, step, own_key[:1]))
        is_root = node == table[0]
        pl.when(is_root)(functools.partial(put_nothing, place, CHAIN, own_key[:1]))

        @pl.when(jnp.logical_not(is_root))
        def _():
            put(place, CHAIN, keys[node_rows(table[0]), :], values[node_rows(table[0]), :])

    def score(place, node):
        stacked = jnp.concatenate(
            [query[node_rows(node), h * HEAD : (h + 1) * HEAD] for h in range(group)], 0
        )
        return times(stacked, all_keys[place])

    def weigh(scores):
        own = scores[:, above:] + jnp.concatenate([own_bias] * group, 0)
        masked = jnp.concatenate([scores[:, :above], own], 1)
        largest = jnp.max(masked, axis=1, keepdims=True)
        return jnp.exp2((masked - largest) * SCALE).astype(jnp.bfloat16)

    def finish(place, node, expo):
        mixed = jnp.dot(expo, all_values[place], preferred_element_type=jnp.float32)
        result = (mixed[:, :HEAD] / mixed[:, HEAD:]).astype(jnp.bfloat16)
        for part in range(NODE_TOK // piece):
            block = node * (NODE_TOK // piece) + part
            owner = block // pieces_part
            target = slot_position(parts, owner ^ me)
            inner = (block - owner * pieces_part) * piece
            to = pl.ds(pl.multiple_of(inner, piece), piece)
            for h in range(group):
                first = h * NODE_TOK + part * piece
                out[target, to, h * HEAD : (h + 1) * HEAD] = result[first : first + piece]

    def some_nodes(turn, carry):
        mine = [(place, turn * side + place) for place in range(side)]
        for place, node in mine:
            lay_out(place, node)
        scores = [score(place, node) for place, node in mine]
        for (place, node), each in zip(mine, scores):
            finish(place, node, weigh(each))
        return carry

    lax.fori_loop(0, nodes // side, some_nodes, 0)


def slot_position(parts, distance):
    half = parts // 2
    return jnp.where(distance % 2 == 1, distance // 2, half + distance // 2)


def in_hbm(array):
    return pltpu.with_memory_space_constraint(array, pltpu.HBM)


def attend(kv, table, queries, keys, values, got, parts, after):
    rows = queries.shape[0]
    width = queries.shape[1] // (keys.shape[1] // HEAD)
    total = (CHAIN + 2) * NODE_TOK
    side = 2 if rows % (2 * NODE_TOK) == 0 else 1
    hbm = pl.BlockSpec(memory_space=pltpu.HBM)
    return pl.pallas_call(
        functools.partial(attend_body, kv, parts, [len(choice) for choice in got]),
        out_shape=jax.ShapeDtypeStruct((parts, rows // parts, width), queries.dtype),
        in_specs=[pl.BlockSpec(memory_space=pltpu.SMEM)]
        + [hbm] * 3
        + [pl.BlockSpec(memory_space=pl.ANY)] * (sum(len(x) for x in got) + len(after)),
        scratch_shapes=[
            pltpu.VMEM((rows, width), queries.dtype),
            pltpu.VMEM((rows, HEAD), keys.dtype),
            pltpu.VMEM((rows, HEAD), keys.dtype),
            pltpu.VMEM((CHAIN, NODE_TOK, HEAD), keys.dtype),
            pltpu.VMEM((CHAIN, NODE_TOK, HEAD), keys.dtype),
            pltpu.VMEM((side, total, HEAD), keys.dtype),
            pltpu.VMEM((side, total, 2 * HEAD), keys.dtype),
            pltpu.SemaphoreType.DMA((3 + 2 * CHAIN,)),
        ],
        compiler_params=pltpu.CompilerParams(vmem_limit_bytes=ATTEND_LIMIT),
        cost_estimate=LIGHT,
        name="attend",
    )(table, *[in_hbm(x) for x in (queries, keys, values)], *[x for choice in got for x in choice], *after)


def swap(array, axis, distance):
    size = lax.axis_size(axis)
    return lax.ppermute(array, axis, [(i, i ^ distance) for i in range(size)])


def times(rows, weight):
    return lax.dot_general(
        rows, weight, (((1,), (1,)), ((), ())), preferred_element_type=jnp.float32
    )


def is_middle(index):
    return (index == 1) | (index == 2)


def product(parts, pieces, sent, kept):
    half = parts[0].shape[0] // 2
    for out, start in ((sent, 0), (kept, half)):
        whole = jnp.concatenate([part[start : start + half, :] for part in parts], 1)
        column = 0
        for weight, first, count in pieces:
            out[:, column : column + count] = times(
                whole, weight[first : first + count, :]
            ).astype(out.dtype)
            column += count


def core_sum(pair, upper):
    kept, from_core = pair
    half = kept.shape[0] // 2
    rows = slice(half, 2 * half) if upper else slice(0, half)
    return kept[rows, :].astype(jnp.float32) + from_core[rows, :].astype(jnp.float32)


def step_body(plan, *refs):
    refs = list(refs)

    def take(count):
        return [refs.pop(0) for _ in range(count)]

    rows = [take(count) for count in plan["rows"]]
    arrays = take(plan["arrays"])
    weights = [
        [[(arrays[index], first, count) for index, first, count in pieces] for pieces in weight]
        for weight in plan["weights"]
    ]
    cores = [[take(2) for _ in range(count)] for count in plan["cores"]]
    chips = [([take(2) for _ in range(count)], take(1)[0]) for count in plan["chips"]]
    take(plan["after"])
    outs = take(plan["outs"])
    middle = is_middle(lax.axis_index("node"))
    picks = (middle, jnp.logical_not(middle))
    fetched = None
    for order, weight in enumerate(weights):
        if len(weight) == 2 and not plan["direct"]:
            chosen, sem = refs
            fetched = order
            for pick, pieces in zip(picks, weight):
                column = 0
                for array, first, count in pieces:
                    source = array.at[pl.ds(first, count), :]
                    target = chosen.at[pl.ds(column, count), :]
                    pl.when(pick)(pltpu.make_async_copy(source, target, sem).start)
                    column += count
    made = [[(outs.pop(0), outs.pop(0)) for _ in rows] for _ in weights]
    for bundle in cores:
        out, column = outs.pop(0), 0
        for pair in bundle:
            width = pair[0].shape[1]
            out[:, column : column + width] = core_sum(pair, True).astype(out.dtype)
            column += width
    for bundle, from_chip in chips:
        column = 0
        for pair in bundle:
            out = outs.pop(0)
            width = out.shape[1]
            away = from_chip[:, column : column + width].astype(jnp.float32)
            out[...] = (core_sum(pair, False) + away).astype(out.dtype)
            column += width
    for order, (weight, pairs) in enumerate(zip(weights, made)):
        if order == fetched:
            pltpu.make_async_copy(chosen, chosen, sem).wait()
            weight = [[(chosen, 0, chosen.shape[0])]]
        for parts, (sent, kept) in zip(rows, pairs):
            if len(weight) == 2:
                for pick, pieces in zip(picks, weight):
                    pl.when(pick)(functools.partial(product, parts, pieces, sent, kept))
            else:
                product(parts, weight[0], sent, kept)


def step(rows=(), weights=(), cores=(), chips=(), after=(), direct=False):
    weights = [weight if isinstance(weight, tuple) else (weight,) for weight in weights]
    arrays, fetch, plans = [], [], []
    for weight in weights:
        plans.append([])
        for pieces in weight:
            plans[-1].append([])
            for array, first, count in pieces:
                known = [index for index, x in enumerate(arrays) if x is array]
                if not known:
                    known = [len(arrays)]
                    arrays.append(array)
                    fetch.append(len(weight) == 2 and not direct)
                plans[-1][-1].append((known[0], first, count))
    widths = [sum(count for _, _, count in weight[0]) for weight in weights]
    shapes = []
    for width in widths:
        shapes += [(parts[0].shape[0] // 2, width) for parts in rows for _ in range(2)]
    for bundle in cores:
        shapes.append((bundle[0][0].shape[0] // 2, sum(kept.shape[1] for kept, _ in bundle)))
    for bundle in chips:
        shapes += [(kept.shape[0] // 2, kept.shape[1]) for kept, _ in bundle[:-1]]
    plan = {
        "rows": [len(parts) for parts in rows],
        "arrays": len(arrays),
        "weights": plans,
        "cores": [len(bundle) for bundle in cores],
        "chips": [len(bundle) - 1 for bundle in chips],
        "after": len(after),
        "outs": len(shapes),
        "direct": direct,
    }
    vmem, hbm = pl.BlockSpec(memory_space=pltpu.VMEM), pl.BlockSpec(memory_space=pl.ANY)
    read = [(part, vmem) for parts in rows for part in parts]
    read += [(array, hbm if far else vmem) for array, far in zip(arrays, fetch)]
    read += [(x, vmem) for bundle in cores for pair in bundle for x in pair]
    for bundle in chips:
        read += [(x, vmem) for pair in bundle[:-1] for x in pair] + [(bundle[-1], vmem)]
    read += [(x, hbm) for x in after]
    dtype = read[0][0].dtype
    scratch = []
    if any(fetch):
        width = [w for w, weight in zip(widths, weights) if len(weight) == 2][0]
        scratch = [
            pltpu.VMEM((width, rows[0][0].shape[1] * len(rows[0])), dtype),
            pltpu.SemaphoreType.DMA,
        ]
    return pl.pallas_call(
        functools.partial(step_body, plan),
        out_shape=[jax.ShapeDtypeStruct(shape, dtype) for shape in shapes],
        in_specs=[spec for _, spec in read],
        scratch_shapes=scratch,
        compiler_params=pltpu.CompilerParams(vmem_limit_bytes=VMEM_LIMIT),
        cost_estimate=LIGHT,
        name="step",
    )(*[x for x, _ in read])


PAIRS = [(0, 1), (1, 0), (2, 3), (3, 2)]
MIDDLE = [(1, 2), (2, 1)]
OUTWARD = [(1, 0), (2, 3)]


def relay(piece, got):
    near = lax.ppermute(piece, "node", PAIRS)
    across = lax.ppermute(piece, "node", MIDDLE)
    near, _ = lax.optimization_barrier((near, got))
    across, _ = lax.optimization_barrier((across, got))
    across_out = lax.ppermute(across, "node", OUTWARD)
    near_across = lax.ppermute(near, "node", MIDDLE)
    return near, across, near_across, across_out


def place_body(spots, features, *refs):
    sources, out, sem = refs[: len(spots)], refs[-2], refs[-1]
    half = features // 2
    device = lax.axis_index("node")
    mine = lax.axis_index("groups")
    copies = []
    for order, (source, (distance, side, offset)) in enumerate(zip(sources, spots)):
        group = {"own": mine, "other": 1 - mine, "first": 0}[side]
        column = pl.multiple_of((device ^ distance) * features + group * half + offset, HEAD)
        target = out.at[:, pl.ds(column, source.shape[1])]
        copies.append(pltpu.make_async_copy(source, target, sem.at[order]))
    for copy in copies:
        copy.start()
    for copy in copies:
        copy.wait()


def place(sources, spots, devices, features, begun=None):
    hbm = pl.BlockSpec(memory_space=pltpu.HBM)
    more = [] if begun is None else [begun]
    return pl.pallas_call(
        functools.partial(place_body, spots, features),
        out_shape=jax.ShapeDtypeStruct(
            (sources[0].shape[0], devices * features), sources[0].dtype
        ),
        in_specs=[pl.BlockSpec(memory_space=pltpu.VMEM)] * len(sources) + [hbm] * len(more),
        out_specs=hbm,
        input_output_aliases={len(sources): 0} if more else {},
        scratch_shapes=[pltpu.SemaphoreType.DMA((len(sources),))],
        compiler_params=pltpu.CompilerParams(vmem_limit_bytes=VMEM_LIMIT),
        cost_estimate=LIGHT,
        name="place",
    )(*sources, *more)


def cut_body(weight, out, sem):
    half = out.shape[0]
    rows = half // sem.shape[0]
    start = lax.axis_index("groups") * half
    copies = []
    for part in range(sem.shape[0]):
        source = weight.at[pl.ds(pl.multiple_of(start + part * rows, rows), rows), :]
        target = out.at[pl.ds(part * rows, rows), :]
        copies.append(pltpu.make_async_copy(source, target, sem.at[part]))
    for copy in copies:
        copy.start()
    for copy in copies:
        copy.wait()


def cut(weight):
    return pl.pallas_call(
        cut_body,
        out_shape=jax.ShapeDtypeStruct((weight.shape[0] // 2, weight.shape[1]), weight.dtype),
        in_specs=[pl.BlockSpec(memory_space=pltpu.HBM)],
        out_specs=pl.BlockSpec(memory_space=pltpu.VMEM),
        scratch_shapes=[pltpu.SemaphoreType.DMA((4,))],
        compiler_params=pltpu.CompilerParams(vmem_limit_bytes=VMEM_LIMIT),
        cost_estimate=LIGHT,
        name="cut",
    )(in_hbm(weight))


def project_split(halves, relayed, out_weight):
    features = out_weight.shape[0]
    half = features // 2
    rows = [part.reshape(-1, part.shape[-1]) for part in halves]
    other = [swap(part, "groups", 1) for part in rows]
    near, across, near_across, across_out = relayed
    far_out = lax.ppermute(near_across, "node", OUTWARD)

    def core(sent):
        return swap(sent, "tensor", 1)

    def chip(away):
        return swap(away, "tensor", 2)

    def back(done):
        return swap(done, "groups", 1)

    def whole(weight):
        return [(weight, 0, weight.shape[0])]

    second = (whole(near_across), whole(across_out))
    far = (whole(across), whole(far_out))

    last = features - HEAD
    sent_a, kept_a, sent_b, kept_b, sent_c, kept_c = step(
        [rows],
        [[(out_weight, 0, half)], [(out_weight, half, last - half)], [(out_weight, last, HEAD)]],
    )
    one = [(kept_a, core(sent_a)), (kept_b, core(sent_b))]
    (away,) = step(cores=[one])
    one.append(chip(away))
    sent_1, kept_1 = step([rows], [whole(near)], after=[away, other[0]])
    sent_2, kept_2, done_a, done_b = step([rows], [second], chips=[one], after=[sent_1])
    two = [(kept_c, core(sent_c)), (kept_1, core(sent_1)), (kept_2, core(sent_2))]
    (away,) = step(cores=[two])
    two.append(chip(away))
    sent_3, kept_3, sent_4, kept_4 = step([other], [whole(near), second], after=[away])
    three = [(kept_3, core(sent_3))]
    four = [(kept_4, core(sent_4))]
    away, done_c, done_1, done_2 = step(cores=[three], chips=[two])
    three.append(chip(away))
    away, done_3 = step(cores=[four], chips=[three])
    four.append(chip(away))
    back_3 = back(done_3)
    sent_5, kept_5 = step([other], [far], after=[away], direct=True)
    five = [(kept_5, core(sent_5))]
    (done_4,) = step(chips=[four], after=[sent_5, back_3])
    back_4 = back(done_4)
    sent_6, kept_6 = step([rows], [far], after=[done_4], direct=True)
    six = [(kept_6, core(sent_6))]
    (away,) = step(cores=[five], after=[sent_6])
    five.append(chip(away))
    (away,) = step(cores=[six], after=[away])
    six.append(chip(away))
    (done_5,) = step(chips=[five], after=[away, back_4])
    back_5 = back(done_5)
    devices = lax.axis_size("node")
    begun = place(
        (done_a, done_b, done_c, done_1, done_2, back_3, back_4),
        (
            (0, "first", 0),
            (0, "first", half),
            (0, "first", last),
            (1, "own", 0),
            (2, "own", 0),
            (1, "other", 0),
            (2, "other", 0),
        ),
        devices,
        features,
    )
    (done_6,) = step(chips=[six], after=[done_5, in_hbm(begun)])
    return place(
        (back_5, done_6), ((3, "other", 0), (3, "own", 0)), devices, features, begun
    )


def project_plain(halves, out_weight):
    attended = jnp.concatenate(halves, 2)
    parts, per_part, width = attended.shape
    me = lax.axis_index("tensor")
    order = slot_position(parts, jnp.arange(parts, dtype=jnp.int32) ^ me)
    rows = attended[order].reshape(parts * per_part, width)
    weight = lax.all_gather(out_weight, "node", axis=0, tiled=True)
    terms = times(rows, weight).astype(jnp.bfloat16)
    return lax.psum_scatter(terms, "tensor", scatter_dimension=0, tiled=True)


def spread(exported):
    near = lax.ppermute(exported, "node", PAIRS)
    across = lax.ppermute(exported, "node", MIDDLE)
    near_across = lax.ppermute(near, "node", MIDDLE)
    across_out = lax.ppermute(across, "node", OUTWARD)
    far_out = lax.ppermute(near_across, "node", OUTWARD)
    return [(near,), (near_across, across_out), (across, far_out)]


def local(queries, keys, values, out_weight, slot_nodes, ancestors, depth):
    parts = lax.axis_size("tensor")
    devices = lax.axis_size("node")
    features = out_weight.shape[0]
    kv_count = keys.shape[1] // HEAD
    relayed, after = None, []
    relative = devices == 4
    exported, table = prepare(slot_nodes, ancestors, depth, keys, values, relative)
    if relative:
        got = spread(exported)
    else:
        got = [(lax.all_gather(exported, "node", axis=0, tiled=True),)]
    if (
        devices == 4
        and parts == 4
        and lax.axis_size("groups") == 2
        and features % (2 * HEAD) == 0
    ):
        relayed = relay(cut(out_weight), got)
        after = relayed[:2]
    halves = []
    for kv in range(kv_count):
        halves.append(attend(kv, table, queries, keys, values, got, parts, after))
        after = halves[-1:]
    if relayed is None:
        return project_plain(halves, out_weight)
    return project_split(halves, relayed, out_weight)


def solution(mesh):
    placed = (
        P(("groups", "node"), "tensor"),
        P(("groups", "node"), "tensor"),
        P(("groups", "node"), "tensor"),
        P("node", "tensor"),
        P("groups"),
        P("groups", None),
        P("groups"),
    )
    return jax.shard_map(
        local,
        mesh=mesh,
        in_specs=placed,
        out_specs=P(("groups", "node", "tensor"), None),
        check_vma=False,
    )
```

```python
import functools
import math

import jax
import jax.numpy as jnp
from jax import lax
from jax.experimental import pallas as pl
from jax.experimental.pallas import tpu as pltpu
from jax.sharding import PartitionSpec as P

HEAD = 128
NODE_TOK = 128
A_MAX = 7
CHAIN = A_MAX - 1
EXPORTS = 2
SCALE = math.log2(math.e) / math.sqrt(HEAD)
DEAD = -1e30
LIGHT = pl.CostEstimate(flops=1, bytes_accessed=1, transcendentals=0)
VMEM_LIMIT = 20 * 1024 * 1024
ATTEND_LIMIT = 24 * 1024 * 1024


def prepare_body(nodes, relative, *refs):
    slot_hbm, ancestors_hbm, depth_hbm, keys, values, exported, table_hbm = refs[:7]
    slot_nodes, ancestors, depth, table, holder, within, roots, sem = refs[7:]
    devices = slot_nodes.shape[0] // nodes
    me = lax.axis_index("node")
    fetches = [
        pltpu.make_async_copy(source, target, sem.at[2 * EXPORTS + 1 + order])
        for order, (source, target) in enumerate(
            ((slot_hbm, slot_nodes), (ancestors_hbm, ancestors), (depth_hbm, depth))
        )
    ]
    for fetch in fetches:
        fetch.start()
    for fetch in fetches:
        fetch.wait()

    def place(device, mine):
        root, root_index = jnp.int32(0), jnp.int32(0)
        for index in range(nodes):
            node = slot_nodes[device * nodes + index]
            holder[node] = device
            within[node] = index
            even = (depth[node] & 1) == 0
            root = jnp.where(even, node, root)
            root_index = jnp.where(even, index, root_index)
        roots[device] = root
        return jnp.where(device == me, root_index, mine)

    root = lax.fori_loop(0, devices, place, jnp.int32(0))

    def find_attach(device, attach):
        node = roots[device]
        level = depth[node]
        for step in range(0, CHAIN, 2):
            above = jnp.maximum(ancestors[step, node], 0)
            hit = (step < level) & (holder[above] == me)
            attach = jnp.where(hit, within[above], attach)
        return attach

    attach = lax.fori_loop(0, devices, find_attach, jnp.int32(0))
    copies = []
    for position, (source, index) in enumerate(
        ((keys, root), (keys, attach), (values, root), (values, attach))
    ):
        rows = pl.ds(pl.multiple_of(index * NODE_TOK, NODE_TOK), NODE_TOK)
        copies.append(
            pltpu.make_async_copy(source.at[rows, :], exported.at[position], sem.at[position])
        )
    for copy in copies:
        copy.start()
    root_node = roots[me]
    count = depth[root_node]
    table[0] = root
    table[1] = count
    for step in range(CHAIN):
        above = jnp.maximum(ancestors[step, root_node], 0)
        where = (holder[above] ^ me) - 1 if relative else holder[above]
        entry = where * (2 * EXPORTS) + (1 if step % 2 == 0 else 0)
        table[2 + step] = jnp.where(step < count, entry, 0)
    store = pltpu.make_async_copy(table, table_hbm, sem.at[2 * EXPORTS])
    store.start()
    for copy in (*copies, store):
        copy.wait()


def prepare(slot_nodes, ancestors, depth, keys, values, relative):
    nodes = keys.shape[0] // NODE_TOK
    slots = slot_nodes.shape[0]
    hbm = pl.BlockSpec(memory_space=pltpu.HBM)
    vmem = pl.BlockSpec(memory_space=pltpu.VMEM)
    return pl.pallas_call(
        functools.partial(prepare_body, nodes, relative),
        out_shape=(
            jax.ShapeDtypeStruct((2 * EXPORTS, NODE_TOK, keys.shape[1]), keys.dtype),
            jax.ShapeDtypeStruct((2 + CHAIN,), jnp.int32),
        ),
        in_specs=[hbm, hbm, hbm, vmem, vmem],
        out_specs=(hbm, hbm),
        scratch_shapes=[
            pltpu.SMEM((slots,), jnp.int32),
            pltpu.SMEM((A_MAX, slots), jnp.int32),
            pltpu.SMEM((slots,), jnp.int32),
            pltpu.SMEM((2 + CHAIN,), jnp.int32),
            pltpu.SMEM((slots,), jnp.int32),
            pltpu.SMEM((slots,), jnp.int32),
            pltpu.SMEM((slots // nodes,), jnp.int32),
            pltpu.SemaphoreType.DMA((2 * EXPORTS + 4,)),
        ],
        compiler_params=pltpu.CompilerParams(vmem_limit_bytes=VMEM_LIMIT),
        name="prepare",
    )(slot_nodes, ancestors.T, depth, keys, values)


def attend_body(kv, parts, counts, table, query_hbm, keys_hbm, values_hbm, *refs):
    refs = list(refs)
    got = [[refs.pop(0) for _ in range(count)] for count in counts]
    middle = is_middle(lax.axis_index("node"))
    out, query, keys, values, above_keys, above_values, all_keys, all_values, sem = refs[-9:]
    nodes = query.shape[0] // NODE_TOK
    group = query.shape[1] // HEAD
    per_part = query.shape[0] // parts
    side = all_keys.shape[0]
    lanes = pl.ds(kv * HEAD, HEAD)
    pairs = [(keys_hbm.at[:, lanes], keys), (values_hbm.at[:, lanes], values)]
    pairs.append((query_hbm.at[:, pl.ds(kv * group * HEAD, group * HEAD)], query))
    copies = [
        pltpu.make_async_copy(source, target, sem.at[order])
        for order, (source, target) in enumerate(pairs)
    ]
    for copy in copies:
        copy.start()
    for step in range(CHAIN):
        each = got[0][0].shape[0]
        for order, choice in enumerate(got):
            entry = table[2 + step] - order * each
            inside = jnp.clip(entry, 0, each - 1 - EXPORTS)
            here = (entry >= 0) & (entry < each)
            for array, pick in zip(choice, (middle, jnp.logical_not(middle))):
                blocks = (
                    (array.at[inside, :, lanes], above_keys.at[step]),
                    (array.at[inside + EXPORTS, :, lanes], above_values.at[step]),
                )
                for part, (source, target) in enumerate(blocks):
                    copy = pltpu.make_async_copy(source, target, sem.at[3 + 2 * step + part])
                    pl.when(here & pick if len(choice) == 2 else here)(copy.start)
                    if order == 0:
                        copies.append(copy)
    ones = jnp.ones((NODE_TOK, HEAD), all_values.dtype)
    nothing = jnp.zeros((NODE_TOK, 2 * HEAD), all_values.dtype)
    query_index = lax.broadcasted_iota(jnp.int32, (NODE_TOK, NODE_TOK), 0)
    key_index = lax.broadcasted_iota(jnp.int32, (NODE_TOK, NODE_TOK), 1)
    own_bias = jnp.where(key_index <= query_index, 0.0, DEAD)
    piece = math.gcd(NODE_TOK, per_part)
    pieces_part = per_part // piece
    me = lax.axis_index("tensor")
    above = (CHAIN + 1) * NODE_TOK
    for copy in copies:
        copy.wait()

    def node_rows(node):
        return pl.ds(pl.multiple_of(node * NODE_TOK, NODE_TOK), NODE_TOK)

    def put(place, order, key_block, value_block):
        rows = pl.ds(order * NODE_TOK, NODE_TOK)
        all_keys[place, rows, :] = key_block
        all_values[place, rows, :HEAD] = value_block
        all_values[place, rows, HEAD:] = ones

    def put_nothing(place, order, first_key):
        rows = pl.ds(order * NODE_TOK, NODE_TOK)
        all_keys[place, rows, :] = jnp.broadcast_to(first_key, (NODE_TOK, HEAD))
        all_values[place, rows, :] = nothing

    for place in range(side):
        for step in range(CHAIN):
            put(place, step, above_keys[step], above_values[step])

    def lay_out(place, node):
        own_key = keys[node_rows(node), :]
        put(place, CHAIN + 1, own_key, values[node_rows(node), :])
        for step in range(CHAIN):
            pl.when(step >= table[1])(functools.partial(put_nothing, place, step, own_key[:1]))
        is_root = node == table[0]
        pl.when(is_root)(functools.partial(put_nothing, place, CHAIN, own_key[:1]))

        @pl.when(jnp.logical_not(is_root))
        def _():
            put(place, CHAIN, keys[node_rows(table[0]), :], values[node_rows(table[0]), :])

    def score(place, node):
        stacked = jnp.concatenate(
            [query[node_rows(node), h * HEAD : (h + 1) * HEAD] for h in range(group)], 0
        )
        return times(stacked, all_keys[place])

    def weigh(scores):
        own = scores[:, above:] + jnp.concatenate([own_bias] * group, 0)
        masked = jnp.concatenate([scores[:, :above], own], 1)
        largest = jnp.max(masked, axis=1, keepdims=True)
        return jnp.exp2((masked - largest) * SCALE).astype(jnp.bfloat16)

    def finish(place, node, expo):
        mixed = jnp.dot(expo, all_values[place], preferred_element_type=jnp.float32)
        result = (mixed[:, :HEAD] / mixed[:, HEAD:]).astype(jnp.bfloat16)
        for part in range(NODE_TOK // piece):
            block = node * (NODE_TOK // piece) + part
            owner = block // pieces_part
            target = slot_position(parts, owner ^ me)
            inner = (block - owner * pieces_part) * piece
            to = pl.ds(pl.multiple_of(inner, piece), piece)
            for h in range(group):
                first = h * NODE_TOK + part * piece
                out[target, to, h * HEAD : (h + 1) * HEAD] = result[first : first + piece]

    def some_nodes(turn, carry):
        mine = [(place, turn * side + place) for place in range(side)]
        for place, node in mine:
            lay_out(place, node)
        scores = [score(place, node) for place, node in mine]
        for (place, node), each in zip(mine, scores):
            finish(place, node, weigh(each))
        return carry

    lax.fori_loop(0, nodes // side, some_nodes, 0)


def slot_position(parts, distance):
    half = parts // 2
    return jnp.where(distance % 2 == 1, distance // 2, half + distance // 2)


def in_hbm(array):
    return pltpu.with_memory_space_constraint(array, pltpu.HBM)


def attend(kv, table, queries, keys, values, got, parts, after):
    rows = queries.shape[0]
    width = queries.shape[1] // (keys.shape[1] // HEAD)
    total = (CHAIN + 2) * NODE_TOK
    side = 2 if rows % (2 * NODE_TOK) == 0 else 1
    hbm = pl.BlockSpec(memory_space=pltpu.HBM)
    return pl.pallas_call(
        functools.partial(attend_body, kv, parts, [len(choice) for choice in got]),
        out_shape=jax.ShapeDtypeStruct((parts, rows // parts, width), queries.dtype),
        in_specs=[pl.BlockSpec(memory_space=pltpu.SMEM)]
        + [hbm] * 3
        + [pl.BlockSpec(memory_space=pl.ANY)] * (sum(len(x) for x in got) + len(after)),
        scratch_shapes=[
            pltpu.VMEM((rows, width), queries.dtype),
            pltpu.VMEM((rows, HEAD), keys.dtype),
            pltpu.VMEM((rows, HEAD), keys.dtype),
            pltpu.VMEM((CHAIN, NODE_TOK, HEAD), keys.dtype),
            pltpu.VMEM((CHAIN, NODE_TOK, HEAD), keys.dtype),
            pltpu.VMEM((side, total, HEAD), keys.dtype),
            pltpu.VMEM((side, total, 2 * HEAD), keys.dtype),
            pltpu.SemaphoreType.DMA((3 + 2 * CHAIN,)),
        ],
        compiler_params=pltpu.CompilerParams(vmem_limit_bytes=ATTEND_LIMIT),
        cost_estimate=LIGHT,
        name="attend",
    )(table, *[in_hbm(x) for x in (queries, keys, values)], *[x for choice in got for x in choice], *after)


def swap(array, axis, distance):
    size = lax.axis_size(axis)
    return lax.ppermute(array, axis, [(i, i ^ distance) for i in range(size)])


def times(rows, weight):
    return lax.dot_general(
        rows, weight, (((1,), (1,)), ((), ())), preferred_element_type=jnp.float32
    )


def is_middle(index):
    return (index == 1) | (index == 2)


def product(parts, pieces, sent, kept):
    half = parts[0].shape[0] // 2
    for out, start in ((sent, 0), (kept, half)):
        whole = jnp.concatenate([part[start : start + half, :] for part in parts], 1)
        column = 0
        for weight, first, count in pieces:
            out[:, column : column + count] = times(
                whole, weight[first : first + count, :]
            ).astype(out.dtype)
            column += count


def core_sum(pair, upper):
    kept, from_core = pair
    half = kept.shape[0] // 2
    rows = slice(half, 2 * half) if upper else slice(0, half)
    return kept[rows, :].astype(jnp.float32) + from_core[rows, :].astype(jnp.float32)


def step_body(plan, *refs):
    refs = list(refs)

    def take(count):
        return [refs.pop(0) for _ in range(count)]

    rows = [take(count) for count in plan["rows"]]
    arrays = take(plan["arrays"])
    weights = [
        [[(arrays[index], first, count) for index, first, count in pieces] for pieces in weight]
        for weight in plan["weights"]
    ]
    cores = [[take(2) for _ in range(count)] for count in plan["cores"]]
    chips = [([take(2) for _ in range(count)], take(1)[0]) for count in plan["chips"]]
    take(plan["after"])
    outs = take(plan["outs"])
    middle = is_middle(lax.axis_index("node"))
    picks = (middle, jnp.logical_not(middle))
    fetched = None
    for order, weight in enumerate(weights):
        if len(weight) == 2 and not plan["direct"]:
            chosen, sem = refs
            fetched = order
            for pick, pieces in zip(picks, weight):
                column = 0
                for array, first, count in pieces:
                    source = array.at[pl.ds(first, count), :]
                    target = chosen.at[pl.ds(column, count), :]
                    pl.when(pick)(pltpu.make_async_copy(source, target, sem).start)
                    column += count
    made = [[(outs.pop(0), outs.pop(0)) for _ in rows] for _ in weights]
    for bundle in cores:
        out, column = outs.pop(0), 0
        for pair in bundle:
            width = pair[0].shape[1]
            out[:, column : column + width] = core_sum(pair, True).astype(out.dtype)
            column += width
    for bundle, from_chip in chips:
        column = 0
        for pair in bundle:
            out = outs.pop(0)
            width = out.shape[1]
            away = from_chip[:, column : column + width].astype(jnp.float32)
            out[...] = (core_sum(pair, False) + away).astype(out.dtype)
            column += width
    for order, (weight, pairs) in enumerate(zip(weights, made)):
        if order == fetched:
            pltpu.make_async_copy(chosen, chosen, sem).wait()
            weight = [[(chosen, 0, chosen.shape[0])]]
        for parts, (sent, kept) in zip(rows, pairs):
            if len(weight) == 2:
                for pick, pieces in zip(picks, weight):
                    pl.when(pick)(functools.partial(product, parts, pieces, sent, kept))
            else:
                product(parts, weight[0], sent, kept)


def step(rows=(), weights=(), cores=(), chips=(), after=(), direct=False):
    weights = [weight if isinstance(weight, tuple) else (weight,) for weight in weights]
    arrays, fetch, plans = [], [], []
    for weight in weights:
        plans.append([])
        for pieces in weight:
            plans[-1].append([])
            for array, first, count in pieces:
                known = [index for index, x in enumerate(arrays) if x is array]
                if not known:
                    known = [len(arrays)]
                    arrays.append(array)
                    fetch.append(len(weight) == 2 and not direct)
                plans[-1][-1].append((known[0], first, count))
    widths = [sum(count for _, _, count in weight[0]) for weight in weights]
    shapes = []
    for width in widths:
        shapes += [(parts[0].shape[0] // 2, width) for parts in rows for _ in range(2)]
    for bundle in cores:
        shapes.append((bundle[0][0].shape[0] // 2, sum(kept.shape[1] for kept, _ in bundle)))
    for bundle in chips:
        shapes += [(kept.shape[0] // 2, kept.shape[1]) for kept, _ in bundle[:-1]]
    plan = {
        "rows": [len(parts) for parts in rows],
        "arrays": len(arrays),
        "weights": plans,
        "cores": [len(bundle) for bundle in cores],
        "chips": [len(bundle) - 1 for bundle in chips],
        "after": len(after),
        "outs": len(shapes),
        "direct": direct,
    }
    vmem, hbm = pl.BlockSpec(memory_space=pltpu.VMEM), pl.BlockSpec(memory_space=pl.ANY)
    read = [(part, vmem) for parts in rows for part in parts]
    read += [(array, hbm if far else vmem) for array, far in zip(arrays, fetch)]
    read += [(x, vmem) for bundle in cores for pair in bundle for x in pair]
    for bundle in chips:
        read += [(x, vmem) for pair in bundle[:-1] for x in pair] + [(bundle[-1], vmem)]
    read += [(x, hbm) for x in after]
    dtype = read[0][0].dtype
    scratch = []
    if any(fetch):
        width = [w for w, weight in zip(widths, weights) if len(weight) == 2][0]
        scratch = [
            pltpu.VMEM((width, rows[0][0].shape[1] * len(rows[0])), dtype),
            pltpu.SemaphoreType.DMA,
        ]
    return pl.pallas_call(
        functools.partial(step_body, plan),
        out_shape=[jax.ShapeDtypeStruct(shape, dtype) for shape in shapes],
        in_specs=[spec for _, spec in read],
        scratch_shapes=scratch,
        compiler_params=pltpu.CompilerParams(vmem_limit_bytes=VMEM_LIMIT),
        cost_estimate=LIGHT,
        name="step",
    )(*[x for x, _ in read])


PAIRS = [(0, 1), (1, 0), (2, 3), (3, 2)]
MIDDLE = [(1, 2), (2, 1)]
OUTWARD = [(1, 0), (2, 3)]
ENDS = [(0, 3), (3, 0)]


def relay(piece, got):
    near = lax.ppermute(piece, "node", PAIRS)
    across = lax.ppermute(piece, "node", MIDDLE)
    near, _ = lax.optimization_barrier((near, got))
    across, _ = lax.optimization_barrier((across, got))
    across_out = lax.ppermute(across, "node", OUTWARD)
    near_across = lax.ppermute(near, "node", MIDDLE)
    return near, across, near_across, across_out


def place_body(spots, features, *refs):
    sources, out, sem = refs[: len(spots)], refs[-2], refs[-1]
    half = features // 2
    device = lax.axis_index("node")
    mine = lax.axis_index("groups")
    copies = []
    for order, (source, (distance, side, offset)) in enumerate(zip(sources, spots)):
        group = {"own": mine, "other": 1 - mine, "first": 0}[side]
        column = pl.multiple_of((device ^ distance) * features + group * half + offset, HEAD)
        target = out.at[:, pl.ds(column, source.shape[1])]
        copies.append(pltpu.make_async_copy(source, target, sem.at[order]))
    for copy in copies:
        copy.start()
    for copy in copies:
        copy.wait()


def place(sources, spots, devices, features, begun=None):
    hbm = pl.BlockSpec(memory_space=pltpu.HBM)
    more = [] if begun is None else [begun]
    return pl.pallas_call(
        functools.partial(place_body, spots, features),
        out_shape=jax.ShapeDtypeStruct(
            (sources[0].shape[0], devices * features), sources[0].dtype
        ),
        in_specs=[pl.BlockSpec(memory_space=pltpu.VMEM)] * len(sources) + [hbm] * len(more),
        out_specs=hbm,
        input_output_aliases={len(sources): 0} if more else {},
        scratch_shapes=[pltpu.SemaphoreType.DMA((len(sources),))],
        compiler_params=pltpu.CompilerParams(vmem_limit_bytes=VMEM_LIMIT),
        cost_estimate=LIGHT,
        name="place",
    )(*sources, *more)


def cut_body(weight, out, sem):
    half = out.shape[0]
    rows = half // sem.shape[0]
    start = lax.axis_index("groups") * half
    copies = []
    for part in range(sem.shape[0]):
        source = weight.at[pl.ds(pl.multiple_of(start + part * rows, rows), rows), :]
        target = out.at[pl.ds(part * rows, rows), :]
        copies.append(pltpu.make_async_copy(source, target, sem.at[part]))
    for copy in copies:
        copy.start()
    for copy in copies:
        copy.wait()


def cut(weight):
    return pl.pallas_call(
        cut_body,
        out_shape=jax.ShapeDtypeStruct((weight.shape[0] // 2, weight.shape[1]), weight.dtype),
        in_specs=[pl.BlockSpec(memory_space=pltpu.HBM)],
        out_specs=pl.BlockSpec(memory_space=pltpu.VMEM),
        scratch_shapes=[pltpu.SemaphoreType.DMA((4,))],
        compiler_params=pltpu.CompilerParams(vmem_limit_bytes=VMEM_LIMIT),
        cost_estimate=LIGHT,
        name="cut",
    )(in_hbm(weight))


def project_split(halves, relayed, out_weight):
    features = out_weight.shape[0]
    half = features // 2
    rows = [part.reshape(-1, part.shape[-1]) for part in halves]
    other = [swap(part, "groups", 1) for part in rows]
    near, across, near_across, across_out = relayed
    far_out = lax.ppermute(near_across, "node", OUTWARD)

    def core(sent):
        return swap(sent, "tensor", 1)

    def chip(away):
        return swap(away, "tensor", 2)

    def back(done):
        return swap(done, "groups", 1)

    def whole(weight):
        return [(weight, 0, weight.shape[0])]

    second = (whole(near_across), whole(across_out))
    far = (whole(across), whole(far_out))

    last = features - HEAD
    sent_a, kept_a, sent_b, kept_b, sent_c, kept_c = step(
        [rows],
        [[(out_weight, 0, half)], [(out_weight, half, last - half)], [(out_weight, last, HEAD)]],
    )
    one = [(kept_a, core(sent_a)), (kept_b, core(sent_b))]
    (away,) = step(cores=[one])
    one.append(chip(away))
    sent_1, kept_1 = step([rows], [whole(near)], after=[away, other[0]])
    sent_2, kept_2, done_a, done_b = step([rows], [second], chips=[one], after=[sent_1])
    two = [(kept_c, core(sent_c)), (kept_1, core(sent_1)), (kept_2, core(sent_2))]
    (away,) = step(cores=[two])
    two.append(chip(away))
    sent_3, kept_3, sent_4, kept_4 = step([other], [whole(near), second], after=[away])
    three = [(kept_3, core(sent_3))]
    four = [(kept_4, core(sent_4))]
    away, done_c, done_1, done_2 = step(cores=[three], chips=[two])
    three.append(chip(away))
    away, done_3 = step(cores=[four], chips=[three])
    four.append(chip(away))
    back_3 = back(done_3)
    sent_5, kept_5 = step([other], [far], after=[away], direct=True)
    five = [(kept_5, core(sent_5))]
    (done_4,) = step(chips=[four], after=[sent_5, back_3])
    back_4 = back(done_4)
    sent_6, kept_6 = step([rows], [far], after=[done_4], direct=True)
    six = [(kept_6, core(sent_6))]
    (away,) = step(cores=[five], after=[sent_6])
    five.append(chip(away))
    (away,) = step(cores=[six], after=[away])
    six.append(chip(away))
    (done_5,) = step(chips=[five], after=[away, back_4])
    back_5 = back(done_5)
    devices = lax.axis_size("node")
    begun = place(
        (done_a, done_b, done_c, done_1, done_2, back_3, back_4),
        (
            (0, "first", 0),
            (0, "first", half),
            (0, "first", last),
            (1, "own", 0),
            (2, "own", 0),
            (1, "other", 0),
            (2, "other", 0),
        ),
        devices,
        features,
    )
    (done_6,) = step(chips=[six], after=[done_5, in_hbm(begun)])
    return place(
        (back_5, done_6), ((3, "other", 0), (3, "own", 0)), devices, features, begun
    )


def project_plain(halves, out_weight):
    attended = jnp.concatenate(halves, 2)
    parts, per_part, width = attended.shape
    me = lax.axis_index("tensor")
    order = slot_position(parts, jnp.arange(parts, dtype=jnp.int32) ^ me)
    rows = attended[order].reshape(parts * per_part, width)
    weight = lax.all_gather(out_weight, "node", axis=0, tiled=True)
    terms = times(rows, weight).astype(jnp.bfloat16)
    return lax.psum_scatter(terms, "tensor", scatter_dimension=0, tiled=True)


def spread(exported):
    near = lax.ppermute(exported, "node", PAIRS)
    across = lax.ppermute(exported, "node", MIDDLE)
    near_across = lax.ppermute(near, "node", MIDDLE)
    across_out = lax.ppermute(across, "node", OUTWARD)
    far = lax.ppermute(exported, "node", ENDS)
    return [(near,), (near_across, across_out), (across, far)]


def local(queries, keys, values, out_weight, slot_nodes, ancestors, depth):
    parts = lax.axis_size("tensor")
    devices = lax.axis_size("node")
    features = out_weight.shape[0]
    kv_count = keys.shape[1] // HEAD
    relayed, after = None, []
    relative = devices == 4
    exported, table = prepare(slot_nodes, ancestors, depth, keys, values, relative)
    if relative:
        got = spread(exported)
    else:
        got = [(lax.all_gather(exported, "node", axis=0, tiled=True),)]
    if (
        devices == 4
        and parts == 4
        and lax.axis_size("groups") == 2
        and features % (2 * HEAD) == 0
    ):
        relayed = relay(cut(out_weight), got)
        after = relayed[:2]
    halves = []
    for kv in range(kv_count):
        halves.append(attend(kv, table, queries, keys, values, got, parts, after))
        after = halves[-1:]
    if relayed is None:
        return project_plain(halves, out_weight)
    return project_split(halves, relayed, out_weight)


def solution(mesh):
    placed = (
        P(("groups", "node"), "tensor"),
        P(("groups", "node"), "tensor"),
        P(("groups", "node"), "tensor"),
        P("node", "tensor"),
        P("groups"),
        P("groups", None),
        P("groups"),
    )
    return jax.shard_map(
        local,
        mesh=mesh,
        in_specs=placed,
        out_specs=P(("groups", "node", "tensor"), None),
        check_vma=False,
    )
```

```python
import functools
import math

import jax
import jax.numpy as jnp
from jax import lax
from jax.experimental import pallas as pl
from jax.experimental.pallas import tpu as pltpu
from jax.sharding import PartitionSpec as P

HEAD = 128
NODE_TOK = 128
A_MAX = 7
CHAIN = A_MAX - 1
EXPORTS = 2
SCALE = math.log2(math.e) / math.sqrt(HEAD)
DEAD = -1e30
LIGHT = pl.CostEstimate(flops=1, bytes_accessed=1, transcendentals=0)
VMEM_LIMIT = 20 * 1024 * 1024
ATTEND_LIMIT = 24 * 1024 * 1024


def prepare_body(nodes, relative, *refs):
    slot_hbm, ancestors_hbm, depth_hbm, keys, values, exported, table_hbm = refs[:7]
    slot_nodes, ancestors, depth, table, holder, within, roots, sem = refs[7:]
    devices = slot_nodes.shape[0] // nodes
    me = lax.axis_index("node")
    fetches = [
        pltpu.make_async_copy(source, target, sem.at[2 * EXPORTS + 1 + order])
        for order, (source, target) in enumerate(
            ((slot_hbm, slot_nodes), (ancestors_hbm, ancestors), (depth_hbm, depth))
        )
    ]
    for fetch in fetches:
        fetch.start()
    for fetch in fetches:
        fetch.wait()

    def place(device, mine):
        root, root_index = jnp.int32(0), jnp.int32(0)
        for index in range(nodes):
            node = slot_nodes[device * nodes + index]
            holder[node] = device
            within[node] = index
            even = (depth[node] & 1) == 0
            root = jnp.where(even, node, root)
            root_index = jnp.where(even, index, root_index)
        roots[device] = root
        return jnp.where(device == me, root_index, mine)

    root = lax.fori_loop(0, devices, place, jnp.int32(0))

    def find_attach(device, attach):
        node = roots[device]
        level = depth[node]
        for step in range(0, CHAIN, 2):
            above = jnp.maximum(ancestors[step, node], 0)
            hit = (step < level) & (holder[above] == me)
            attach = jnp.where(hit, within[above], attach)
        return attach

    attach = lax.fori_loop(0, devices, find_attach, jnp.int32(0))
    copies = []
    for position, (source, index) in enumerate(
        ((keys, root), (keys, attach), (values, root), (values, attach))
    ):
        rows = pl.ds(pl.multiple_of(index * NODE_TOK, NODE_TOK), NODE_TOK)
        copies.append(
            pltpu.make_async_copy(source.at[rows, :], exported.at[position], sem.at[position])
        )
    for copy in copies:
        copy.start()
    root_node = roots[me]
    count = depth[root_node]
    table[0] = root
    table[1] = count
    for step in range(CHAIN):
        above = jnp.maximum(ancestors[step, root_node], 0)
        where = (holder[above] ^ me) - 1 if relative else holder[above]
        entry = where * (2 * EXPORTS) + (1 if step % 2 == 0 else 0)
        table[2 + step] = jnp.where(step < count, entry, 0)
    store = pltpu.make_async_copy(table, table_hbm, sem.at[2 * EXPORTS])
    store.start()
    for copy in (*copies, store):
        copy.wait()


def prepare(slot_nodes, ancestors, depth, keys, values, relative):
    nodes = keys.shape[0] // NODE_TOK
    slots = slot_nodes.shape[0]
    hbm = pl.BlockSpec(memory_space=pltpu.HBM)
    vmem = pl.BlockSpec(memory_space=pltpu.VMEM)
    return pl.pallas_call(
        functools.partial(prepare_body, nodes, relative),
        out_shape=(
            jax.ShapeDtypeStruct((2 * EXPORTS, NODE_TOK, keys.shape[1]), keys.dtype),
            jax.ShapeDtypeStruct((2 + CHAIN,), jnp.int32),
        ),
        in_specs=[hbm, hbm, hbm, vmem, vmem],
        out_specs=(hbm, hbm),
        scratch_shapes=[
            pltpu.SMEM((slots,), jnp.int32),
            pltpu.SMEM((A_MAX, slots), jnp.int32),
            pltpu.SMEM((slots,), jnp.int32),
            pltpu.SMEM((2 + CHAIN,), jnp.int32),
            pltpu.SMEM((slots,), jnp.int32),
            pltpu.SMEM((slots,), jnp.int32),
            pltpu.SMEM((slots // nodes,), jnp.int32),
            pltpu.SemaphoreType.DMA((2 * EXPORTS + 4,)),
        ],
        compiler_params=pltpu.CompilerParams(vmem_limit_bytes=VMEM_LIMIT),
        name="prepare",
    )(slot_nodes, ancestors.T, depth, keys, values)


def attend_body(kv, parts, counts, table, query_hbm, keys_hbm, values_hbm, *refs):
    refs = list(refs)
    got = [[refs.pop(0) for _ in range(count)] for count in counts]
    middle = is_middle(lax.axis_index("node"))
    out, query, keys, values, above_keys, above_values, all_keys, all_values, sem = refs[-9:]
    nodes = query.shape[0] // NODE_TOK
    group = query.shape[1] // HEAD
    per_part = query.shape[0] // parts
    side = all_keys.shape[0]
    lanes = pl.ds(kv * HEAD, HEAD)
    pairs = [(keys_hbm.at[:, lanes], keys), (values_hbm.at[:, lanes], values)]
    pairs.append((query_hbm.at[:, pl.ds(kv * group * HEAD, group * HEAD)], query))
    copies = [
        pltpu.make_async_copy(source, target, sem.at[order])
        for order, (source, target) in enumerate(pairs)
    ]
    for copy in copies:
        copy.start()
    for step in range(CHAIN):
        each = got[0][0].shape[0]
        for order, choice in enumerate(got):
            entry = table[2 + step] - order * each
            inside = jnp.clip(entry, 0, each - 1 - EXPORTS)
            here = (entry >= 0) & (entry < each)
            for array, pick in zip(choice, (middle, jnp.logical_not(middle))):
                blocks = (
                    (array.at[inside, :, lanes], above_keys.at[step]),
                    (array.at[inside + EXPORTS, :, lanes], above_values.at[step]),
                )
                for part, (source, target) in enumerate(blocks):
                    copy = pltpu.make_async_copy(source, target, sem.at[3 + 2 * step + part])
                    pl.when(here & pick if len(choice) == 2 else here)(copy.start)
                    if order == 0:
                        copies.append(copy)
    ones = jnp.ones((NODE_TOK, HEAD), all_values.dtype)
    nothing = jnp.zeros((NODE_TOK, 2 * HEAD), all_values.dtype)
    query_index = lax.broadcasted_iota(jnp.int32, (NODE_TOK, NODE_TOK), 0)
    key_index = lax.broadcasted_iota(jnp.int32, (NODE_TOK, NODE_TOK), 1)
    own_bias = jnp.where(key_index <= query_index, 0.0, DEAD)
    piece = math.gcd(NODE_TOK, per_part)
    pieces_part = per_part // piece
    me = lax.axis_index("tensor")
    above = (CHAIN + 1) * NODE_TOK
    for copy in copies:
        copy.wait()

    def node_rows(node):
        return pl.ds(pl.multiple_of(node * NODE_TOK, NODE_TOK), NODE_TOK)

    def put(place, order, key_block, value_block):
        rows = pl.ds(order * NODE_TOK, NODE_TOK)
        all_keys[place, rows, :] = key_block
        all_values[place, rows, :HEAD] = value_block
        all_values[place, rows, HEAD:] = ones

    def put_nothing(place, order, first_key):
        rows = pl.ds(order * NODE_TOK, NODE_TOK)
        all_keys[place, rows, :] = jnp.broadcast_to(first_key, (NODE_TOK, HEAD))
        all_values[place, rows, :] = nothing

    for place in range(side):
        for step in range(CHAIN):
            put(place, step, above_keys[step], above_values[step])

    def lay_out(place, node):
        own_key = keys[node_rows(node), :]
        put(place, CHAIN + 1, own_key, values[node_rows(node), :])
        for step in range(CHAIN):
            pl.when(step >= table[1])(functools.partial(put_nothing, place, step, own_key[:1]))
        is_root = node == table[0]
        pl.when(is_root)(functools.partial(put_nothing, place, CHAIN, own_key[:1]))

        @pl.when(jnp.logical_not(is_root))
        def _():
            put(place, CHAIN, keys[node_rows(table[0]), :], values[node_rows(table[0]), :])

    def score(place, node):
        stacked = jnp.concatenate(
            [query[node_rows(node), h * HEAD : (h + 1) * HEAD] for h in range(group)], 0
        )
        return times(stacked, all_keys[place])

    def weigh(scores):
        own = scores[:, above:] + jnp.concatenate([own_bias] * group, 0)
        masked = jnp.concatenate([scores[:, :above], own], 1)
        largest = jnp.max(masked, axis=1, keepdims=True)
        return jnp.exp2((masked - largest) * SCALE).astype(jnp.bfloat16)

    def finish(place, node, expo):
        mixed = jnp.dot(expo, all_values[place], preferred_element_type=jnp.float32)
        result = (mixed[:, :HEAD] / mixed[:, HEAD:]).astype(jnp.bfloat16)
        for part in range(NODE_TOK // piece):
            block = node * (NODE_TOK // piece) + part
            owner = block // pieces_part
            target = slot_position(parts, owner ^ me)
            inner = (block - owner * pieces_part) * piece
            to = pl.ds(pl.multiple_of(inner, piece), piece)
            for h in range(group):
                first = h * NODE_TOK + part * piece
                out[target, to, h * HEAD : (h + 1) * HEAD] = result[first : first + piece]

    def some_nodes(turn, carry):
        mine = [(place, turn * side + place) for place in range(side)]
        for place, node in mine:
            lay_out(place, node)
        scores = [score(place, node) for place, node in mine]
        for (place, node), each in zip(mine, scores):
            finish(place, node, weigh(each))
        return carry

    lax.fori_loop(0, nodes // side, some_nodes, 0)


def slot_position(parts, distance):
    half = parts // 2
    return jnp.where(distance % 2 == 1, distance // 2, half + distance // 2)


def in_hbm(array):
    return pltpu.with_memory_space_constraint(array, pltpu.HBM)


def attend(kv, table, queries, keys, values, got, parts, after):
    rows = queries.shape[0]
    width = queries.shape[1] // (keys.shape[1] // HEAD)
    total = (CHAIN + 2) * NODE_TOK
    side = 2 if rows % (2 * NODE_TOK) == 0 else 1
    hbm = pl.BlockSpec(memory_space=pltpu.HBM)
    return pl.pallas_call(
        functools.partial(attend_body, kv, parts, [len(choice) for choice in got]),
        out_shape=jax.ShapeDtypeStruct((parts, rows // parts, width), queries.dtype),
        in_specs=[pl.BlockSpec(memory_space=pltpu.SMEM)]
        + [hbm] * 3
        + [pl.BlockSpec(memory_space=pl.ANY)] * (sum(len(x) for x in got) + len(after)),
        scratch_shapes=[
            pltpu.VMEM((rows, width), queries.dtype),
            pltpu.VMEM((rows, HEAD), keys.dtype),
            pltpu.VMEM((rows, HEAD), keys.dtype),
            pltpu.VMEM((CHAIN, NODE_TOK, HEAD), keys.dtype),
            pltpu.VMEM((CHAIN, NODE_TOK, HEAD), keys.dtype),
            pltpu.VMEM((side, total, HEAD), keys.dtype),
            pltpu.VMEM((side, total, 2 * HEAD), keys.dtype),
            pltpu.SemaphoreType.DMA((3 + 2 * CHAIN,)),
        ],
        compiler_params=pltpu.CompilerParams(vmem_limit_bytes=ATTEND_LIMIT),
        cost_estimate=LIGHT,
        name="attend",
    )(table, *[in_hbm(x) for x in (queries, keys, values)], *[x for choice in got for x in choice], *after)


def swap(array, axis, distance):
    size = lax.axis_size(axis)
    return lax.ppermute(array, axis, [(i, i ^ distance) for i in range(size)])


def times(rows, weight):
    return lax.dot_general(
        rows, weight, (((1,), (1,)), ((), ())), preferred_element_type=jnp.float32
    )


def is_middle(index):
    return (index == 1) | (index == 2)


def product(parts, pieces, sent, kept):
    half = parts[0].shape[0] // 2
    for out, start in ((sent, 0), (kept, half)):
        whole = jnp.concatenate([part[start : start + half, :] for part in parts], 1)
        column = 0
        for weight, first, count in pieces:
            out[:, column : column + count] = times(
                whole, weight[first : first + count, :]
            ).astype(out.dtype)
            column += count


def core_sum(pair, upper):
    kept, from_core = pair
    half = kept.shape[0] // 2
    rows = slice(half, 2 * half) if upper else slice(0, half)
    return kept[rows, :].astype(jnp.float32) + from_core[rows, :].astype(jnp.float32)


def step_body(plan, *refs):
    refs = list(refs)

    def take(count):
        return [refs.pop(0) for _ in range(count)]

    rows = [take(count) for count in plan["rows"]]
    arrays = take(plan["arrays"])
    weights = [
        [[(arrays[index], first, count) for index, first, count in pieces] for pieces in weight]
        for weight in plan["weights"]
    ]
    cores = [[take(2) for _ in range(count)] for count in plan["cores"]]
    chips = [([take(2) for _ in range(count)], take(1)[0]) for count in plan["chips"]]
    take(plan["after"])
    outs = take(plan["outs"])
    middle = is_middle(lax.axis_index("node"))
    picks = (middle, jnp.logical_not(middle))
    fetched = None
    for order, weight in enumerate(weights):
        if len(weight) == 2 and not plan["direct"]:
            chosen, sem = refs
            fetched = order
            for pick, pieces in zip(picks, weight):
                column = 0
                for array, first, count in pieces:
                    source = array.at[pl.ds(first, count), :]
                    target = chosen.at[pl.ds(column, count), :]
                    pl.when(pick)(pltpu.make_async_copy(source, target, sem).start)
                    column += count
    made = [[(outs.pop(0), outs.pop(0)) for _ in rows] for _ in weights]
    for bundle in cores:
        out, column = outs.pop(0), 0
        for pair in bundle:
            width = pair[0].shape[1]
            out[:, column : column + width] = core_sum(pair, True).astype(out.dtype)
            column += width
    for bundle, from_chip in chips:
        column = 0
        for pair in bundle:
            out = outs.pop(0)
            width = out.shape[1]
            away = from_chip[:, column : column + width].astype(jnp.float32)
            out[...] = (core_sum(pair, False) + away).astype(out.dtype)
            column += width
    for order, (weight, pairs) in enumerate(zip(weights, made)):
        if order == fetched:
            pltpu.make_async_copy(chosen, chosen, sem).wait()
            weight = [[(chosen, 0, chosen.shape[0])]]
        for parts, (sent, kept) in zip(rows, pairs):
            if len(weight) == 2:
                for pick, pieces in zip(picks, weight):
                    pl.when(pick)(functools.partial(product, parts, pieces, sent, kept))
            else:
                product(parts, weight[0], sent, kept)


def step(rows=(), weights=(), cores=(), chips=(), after=(), direct=False):
    weights = [weight if isinstance(weight, tuple) else (weight,) for weight in weights]
    arrays, fetch, plans = [], [], []
    for weight in weights:
        plans.append([])
        for pieces in weight:
            plans[-1].append([])
            for array, first, count in pieces:
                known = [index for index, x in enumerate(arrays) if x is array]
                if not known:
                    known = [len(arrays)]
                    arrays.append(array)
                    fetch.append(len(weight) == 2 and not direct)
                plans[-1][-1].append((known[0], first, count))
    widths = [sum(count for _, _, count in weight[0]) for weight in weights]
    shapes = []
    for width in widths:
        shapes += [(parts[0].shape[0] // 2, width) for parts in rows for _ in range(2)]
    for bundle in cores:
        shapes.append((bundle[0][0].shape[0] // 2, sum(kept.shape[1] for kept, _ in bundle)))
    for bundle in chips:
        shapes += [(kept.shape[0] // 2, kept.shape[1]) for kept, _ in bundle[:-1]]
    plan = {
        "rows": [len(parts) for parts in rows],
        "arrays": len(arrays),
        "weights": plans,
        "cores": [len(bundle) for bundle in cores],
        "chips": [len(bundle) - 1 for bundle in chips],
        "after": len(after),
        "outs": len(shapes),
        "direct": direct,
    }
    vmem, hbm = pl.BlockSpec(memory_space=pltpu.VMEM), pl.BlockSpec(memory_space=pl.ANY)
    read = [(part, vmem) for parts in rows for part in parts]
    read += [(array, hbm if far else vmem) for array, far in zip(arrays, fetch)]
    read += [(x, vmem) for bundle in cores for pair in bundle for x in pair]
    for bundle in chips:
        read += [(x, vmem) for pair in bundle[:-1] for x in pair] + [(bundle[-1], vmem)]
    read += [(x, hbm) for x in after]
    dtype = read[0][0].dtype
    scratch = []
    if any(fetch):
        width = [w for w, weight in zip(widths, weights) if len(weight) == 2][0]
        scratch = [
            pltpu.VMEM((width, rows[0][0].shape[1] * len(rows[0])), dtype),
            pltpu.SemaphoreType.DMA,
        ]
    return pl.pallas_call(
        functools.partial(step_body, plan),
        out_shape=[jax.ShapeDtypeStruct(shape, dtype) for shape in shapes],
        in_specs=[spec for _, spec in read],
        scratch_shapes=scratch,
        compiler_params=pltpu.CompilerParams(vmem_limit_bytes=VMEM_LIMIT),
        cost_estimate=LIGHT,
        name="step",
    )(*[x for x, _ in read])


PAIRS = [(0, 1), (1, 0), (2, 3), (3, 2)]
MIDDLE = [(1, 2), (2, 1)]
OUTWARD = [(1, 0), (2, 3)]
ENDS = [(0, 3), (3, 0)]


def relay(piece, got):
    near = lax.ppermute(piece, "node", PAIRS)
    across = lax.ppermute(piece, "node", MIDDLE)
    near, _ = lax.optimization_barrier((near, got))
    across, _ = lax.optimization_barrier((across, got))
    across_out = lax.ppermute(across, "node", OUTWARD)
    near_across = lax.ppermute(near, "node", MIDDLE)
    return near, across, near_across, across_out


def place_body(spots, features, *refs):
    sources, out, sem = refs[: len(spots)], refs[-2], refs[-1]
    half = features // 2
    device = lax.axis_index("node")
    mine = lax.axis_index("groups")
    copies = []
    for order, (source, (distance, side, offset)) in enumerate(zip(sources, spots)):
        group = {"own": mine, "other": 1 - mine, "first": 0}[side]
        column = pl.multiple_of((device ^ distance) * features + group * half + offset, HEAD)
        target = out.at[:, pl.ds(column, source.shape[1])]
        copies.append(pltpu.make_async_copy(source, target, sem.at[order]))
    for copy in copies:
        copy.start()
    for copy in copies:
        copy.wait()


def place(sources, spots, devices, features, begun=None):
    hbm = pl.BlockSpec(memory_space=pltpu.HBM)
    more = [] if begun is None else [begun]
    return pl.pallas_call(
        functools.partial(place_body, spots, features),
        out_shape=jax.ShapeDtypeStruct(
            (sources[0].shape[0], devices * features), sources[0].dtype
        ),
        in_specs=[pl.BlockSpec(memory_space=pltpu.VMEM)] * len(sources) + [hbm] * len(more),
        out_specs=hbm,
        input_output_aliases={len(sources): 0} if more else {},
        scratch_shapes=[pltpu.SemaphoreType.DMA((len(sources),))],
        compiler_params=pltpu.CompilerParams(vmem_limit_bytes=VMEM_LIMIT),
        cost_estimate=LIGHT,
        name="place",
    )(*sources, *more)


def cut_body(weight, out, sem):
    half = out.shape[0]
    rows = half // sem.shape[0]
    start = lax.axis_index("groups") * half
    copies = []
    for part in range(sem.shape[0]):
        source = weight.at[pl.ds(pl.multiple_of(start + part * rows, rows), rows), :]
        target = out.at[pl.ds(part * rows, rows), :]
        copies.append(pltpu.make_async_copy(source, target, sem.at[part]))
    for copy in copies:
        copy.start()
    for copy in copies:
        copy.wait()


def cut(weight):
    return pl.pallas_call(
        cut_body,
        out_shape=jax.ShapeDtypeStruct((weight.shape[0] // 2, weight.shape[1]), weight.dtype),
        in_specs=[pl.BlockSpec(memory_space=pltpu.HBM)],
        out_specs=pl.BlockSpec(memory_space=pltpu.VMEM),
        scratch_shapes=[pltpu.SemaphoreType.DMA((4,))],
        compiler_params=pltpu.CompilerParams(vmem_limit_bytes=VMEM_LIMIT),
        cost_estimate=LIGHT,
        name="cut",
    )(in_hbm(weight))


def project_split(halves, relayed, out_weight):
    features = out_weight.shape[0]
    half = features // 2
    rows = [part.reshape(-1, part.shape[-1]) for part in halves]
    other = [swap(part, "groups", 1) for part in rows]
    near, across, near_across, across_out = relayed
    far_out = lax.ppermute(near_across, "node", OUTWARD)

    def core(sent):
        return swap(sent, "tensor", 1)

    def chip(away):
        return swap(away, "tensor", 2)

    def back(done):
        return swap(done, "groups", 1)

    def whole(weight):
        return [(weight, 0, weight.shape[0])]

    second = (whole(near_across), whole(across_out))
    far = (whole(across), whole(far_out))

    last = features - HEAD
    sent_a, kept_a, sent_b, kept_b, sent_c, kept_c = step(
        [rows],
        [[(out_weight, 0, half)], [(out_weight, half, last - half)], [(out_weight, last, HEAD)]],
    )
    one = [(kept_a, core(sent_a)), (kept_b, core(sent_b))]
    (away,) = step(cores=[one])
    one.append(chip(away))
    sent_1, kept_1 = step([rows], [whole(near)], after=[away, other[0]])
    sent_2, kept_2, done_a, done_b = step([rows], [second], chips=[one], after=[sent_1])
    two = [(kept_c, core(sent_c)), (kept_1, core(sent_1)), (kept_2, core(sent_2))]
    (away,) = step(cores=[two])
    two.append(chip(away))
    sent_3, kept_3, sent_4, kept_4 = step([other], [whole(near), second], after=[away])
    three = [(kept_3, core(sent_3))]
    four = [(kept_4, core(sent_4))]
    away, done_c, done_1, done_2 = step(cores=[three], chips=[two])
    three.append(chip(away))
    away, done_3 = step(cores=[four], chips=[three])
    four.append(chip(away))
    back_3 = back(done_3)
    sent_5, kept_5 = step([other], [far], after=[away], direct=True)
    five = [(kept_5, core(sent_5))]
    (done_4,) = step(chips=[four], after=[sent_5, back_3])
    back_4 = back(done_4)
    sent_6, kept_6 = step([rows], [far], after=[done_4], direct=True)
    six = [(kept_6, core(sent_6))]
    (away,) = step(cores=[five], after=[sent_6])
    five.append(chip(away))
    (away,) = step(cores=[six], after=[away, back_4])
    six.append(chip(away))
    (done_5,) = step(chips=[five], after=[away, back_4])
    back_5 = back(done_5)
    devices = lax.axis_size("node")
    begun = place(
        (done_a, done_b, done_c, done_1, done_2, back_3, back_4),
        (
            (0, "first", 0),
            (0, "first", half),
            (0, "first", last),
            (1, "own", 0),
            (2, "own", 0),
            (1, "other", 0),
            (2, "other", 0),
        ),
        devices,
        features,
    )
    (done_6,) = step(chips=[six], after=[done_5, in_hbm(begun)])
    return place(
        (back_5, done_6), ((3, "other", 0), (3, "own", 0)), devices, features, begun
    )


def project_plain(halves, out_weight):
    attended = jnp.concatenate(halves, 2)
    parts, per_part, width = attended.shape
    me = lax.axis_index("tensor")
    order = slot_position(parts, jnp.arange(parts, dtype=jnp.int32) ^ me)
    rows = attended[order].reshape(parts * per_part, width)
    weight = lax.all_gather(out_weight, "node", axis=0, tiled=True)
    terms = times(rows, weight).astype(jnp.bfloat16)
    return lax.psum_scatter(terms, "tensor", scatter_dimension=0, tiled=True)


def spread(exported):
    near = lax.ppermute(exported, "node", PAIRS)
    across = lax.ppermute(exported, "node", MIDDLE)
    near_across = lax.ppermute(near, "node", MIDDLE)
    across_out = lax.ppermute(across, "node", OUTWARD)
    far = lax.ppermute(exported, "node", ENDS)
    return [(near,), (near_across, across_out), (across, far)]


def local(queries, keys, values, out_weight, slot_nodes, ancestors, depth):
    parts = lax.axis_size("tensor")
    devices = lax.axis_size("node")
    features = out_weight.shape[0]
    kv_count = keys.shape[1] // HEAD
    relayed, after = None, []
    relative = devices == 4
    exported, table = prepare(slot_nodes, ancestors, depth, keys, values, relative)
    if relative:
        got = spread(exported)
    else:
        got = [(lax.all_gather(exported, "node", axis=0, tiled=True),)]
    if (
        devices == 4
        and parts == 4
        and lax.axis_size("groups") == 2
        and features % (2 * HEAD) == 0
    ):
        relayed = relay(cut(out_weight), got)
        after = relayed[:2]
    halves = []
    for kv in range(kv_count):
        halves.append(attend(kv, table, queries, keys, values, got, parts, after))
        after = halves[-1:]
    if relayed is None:
        return project_plain(halves, out_weight)
    return project_split(halves, relayed, out_weight)


def solution(mesh):
    placed = (
        P(("groups", "node"), "tensor"),
        P(("groups", "node"), "tensor"),
        P(("groups", "node"), "tensor"),
        P("node", "tensor"),
        P("groups"),
        P("groups", None),
        P("groups"),
    )
    return jax.shard_map(
        local,
        mesh=mesh,
        in_specs=placed,
        out_specs=P(("groups", "node", "tensor"), None),
        check_vma=False,
    )
```
